32 devices in a mesh: groups: 2 (over x), tiles: 8 (over z, y), sub: 2 (over core).
Axes of the slice: x: 2, y: 2, z: 4, core: 2. Of those that a mesh axis runs over, the one named last changes fastest.
Arguments:
- density: float32 [768, 1536], P(('groups', 'tiles'), 'sub'), parts along dimension 0, may hold values from 0.8 to 1.2
- momentum: float32 [3, 768, 1536], P(None, ('groups', 'tiles'), 'sub'), parts along dimension 1, may hold values from -0.4 to 0.4
- stress: float32 [6, 768, 1536], P(None, ('groups', 'tiles'), 'sub'), parts along dimension 1, may hold values from -0.4 to 0.4
- red_density: float32 [768, 1536], P(('groups', 'tiles'), 'sub'), parts along dimension 0, may hold values from 0.1 to 0.8
- solid: int32 [768, 1536], P(('groups', 'tiles'), 'sub'), parts along dimension 0, may hold values 0 or 1
- widths: int32 [16], P('groups'), parts along dimension 0, may hold values from 1 to 3, 16 in all
Outputs:
- density_next: float32 [768, 1536], P(('groups', 'tiles'), 'sub'), parts along dimension 0
- momentum_next: float32 [3, 768, 1536], P(None, ('groups', 'tiles'), 'sub'), parts along dimension 1
- stress_next: float32 [6, 768, 1536], P(None, ('groups', 'tiles'), 'sub'), parts along dimension 1
- red_next: float32 [768, 1536], P(('groups', 'tiles'), 'sub'), parts along dimension 0
The draws below stay inside these ranges and needn't reach their ends.
There are 2 independent parts, one for each index of `groups`. The reference program is written for one: setup_inputs(seed, part) draws one part's arguments, and reference() takes and returns one part's arrays. A program takes and returns all parts, laid end to end along the dimension named above; each array names one. Nothing has to cross between parts.
Inputs may be any that keep to these rules, and one draw needn't show every extreme that they name: Device k along tiles owns the tile columns from widths[0] + ... + widths[k-1] on, widths[k] of them, alike in every part of sub; they sum to 16, and one equals 3. 1 marks a solid cell, 0 a pore cell.
All inputs are finite; a program needn't handle non-finite values. No bound on the sum of `solid` on one device may be relied on, other than what follows from the above.
Results may differ from the reference program's by a relative error of at most 0.0003.
Values sent between devices are 32-bit elements; how exact they have to be, the bound alone decides.
No kernel may reach another device: no remote copies, remote signals or barrier semaphores. Data moves between devices by JAX's collectives and lax.ppermute only.
A program may use at most 64 MiB of HBM per device.

```python
import math
import jax
import jax.numpy as jnp
import numpy as np
from jax import lax

TILE = 16
COLS_DEV = 2
STEPS = 2
NXP = 384
NX = 256
NYZ = 1536
N_TILES = 8


def with_ends(values, own_key, smallest, high):
    spot = [jax.random.randint(jax.random.fold_in(own_key, axis), (), 0, length) for axis, length in enumerate(values.shape)]
    longest = values.shape.index(max(values.shape))
    next_to = spot[:longest] + [(spot[longest] + 1) % values.shape[longest]] + spot[longest + 1:]
    return values.at[tuple(spot)].set(smallest).at[tuple(next_to)].set(high)


def level_of(key, shape, pieces, smallest, largest):
    level = 1.0
    for axis_at, parts in pieces:
        heights = jax.random.uniform(jax.random.fold_in(jax.random.fold_in(key, 6), axis_at), (parts,), jnp.float32, smallest / len(pieces), largest / len(pieces))
        level = level * jnp.repeat(jnp.exp(heights), shape[axis_at] // parts).reshape((-1,) + (1,) * (len(shape) - 1 - axis_at))
    return level


def length_profile(count, total, limit, lean):
    weights = [(1 << 20) // math.isqrt(standing ** lean) + 1 for standing in range(2, count + 1)]
    rest, given = total - limit - (count - 1), [1] * (count - 1)
    while rest > 0:
        candidates = [i for i in range(count - 1) if given[i] < limit]
        mass, budget = sum([weights[i] for i in candidates]), rest
        for i in candidates:
            more = min(limit - given[i], max(1, budget * weights[i] // mass), rest)
            given[i] = given[i] + more
            rest = rest - more
    return np.array([limit] + given)


def ragged_sizes(key, number_of, total, bound, lean):
    if number_of == 2:
        one = jax.random.randint(key, (), max(1, total - bound), min(bound, total - 1) + 1)
        return jnp.stack([one, total - one])
    sizes = jnp.asarray(length_profile(number_of, total, bound, lean), jnp.int32)
    couples = (number_of - 1) // 2
    source_of, taker = sizes[1:1 + 2 * couples:2], sizes[2:2 + 2 * couples:2]
    margin = jnp.minimum(source_of - 1, bound - taker)
    passed = jax.random.randint(jax.random.fold_in(key, 1), (couples,), 0, 1 << 20) % (margin + 1)
    sizes = sizes.at[1:1 + 2 * couples:2].set(source_of - passed).at[2:2 + 2 * couples:2].set(taker + passed)
    return sizes[jax.random.permutation(jax.random.fold_in(key, 2), number_of)]


def bell_draw(key, extent, scale, limit, split=(), held_as=jnp.bfloat16):
    values = scale * jax.random.normal(key, extent, jnp.float32)
    if split:
        values = values * level_of(key, extent, split, -0.22, 0.18)
    return jnp.clip(values, -limit, limit).astype(held_as)


def setup_inputs(seed: int = 0, part: int = 0) -> dict:
    keys = jax.random.split(jax.random.key(seed), 7)
    part_splits = jax.random.split(jax.random.fold_in(keys[6], part), 7)
    return {
        "density": jnp.clip(0.8 + 0.40000004 * jax.random.uniform(part_splits[0], (NXP, NYZ), jnp.float32) ** level_of(part_splits[0], (NXP, NYZ), ((0, 8), (1, 2)), -0.2, 0.2), 0.8, 1.2),
        "momentum": bell_draw(part_splits[1], (3, NXP, NYZ), 0.1, 0.4, ((1, 8), (2, 2)), jnp.float32),
        "stress": bell_draw(part_splits[2], (6, NXP, NYZ), 0.1, 0.4, ((1, 8), (2, 2)), jnp.float32),
        "red_density": jnp.clip(0.1 + 0.7 * jax.random.uniform(part_splits[3], (NXP, NYZ), jnp.float32) ** level_of(part_splits[3], (NXP, NYZ), ((0, 8), (1, 2)), -0.2, 0.2), 0.1, 0.8),
        "solid": with_ends((jax.random.randint(part_splits[4], (NXP, NYZ), 0, 5) < 2).astype(jnp.int32), jax.random.fold_in(part_splits[4], 1), 0, 1),
        "widths": ragged_sizes(part_splits[5], N_TILES, COLS_DEV * N_TILES, COLS_DEV + 1, 2).astype(jnp.int32),
    }


RELAX_TIME = 0.8
SURFACE = 0.1
SEPARATION = 0.7
VELOCITIES = ((0, 0, 0), (1, 0, 0), (-1, 0, 0), (0, 1, 0), (0, -1, 0), (0, 0, 1), (0, 0, -1), (1, 1, 0), (-1, -1, 0), (1, -1, 0), (-1, 1, 0), (1, 0, 1), (-1, 0, -1), (1, 0, -1), (-1, 0, 1), (0, 1, 1), (0, -1, -1), (0, 1, -1), (0, -1, 1))
WEIGHTS = (1.0 / 3.0,) + (1.0 / 18.0,) * 6 + (1.0 / 36.0,) * 12
OPPOSITE = (0, 2, 1, 4, 3, 6, 5, 8, 7, 10, 9, 12, 11, 14, 13, 16, 15, 18, 17)

def rebuild_row(velocity):
    vel_x, vel_y, vel_z = velocity
    one_third = 1.0 / 3.0
    return (1.0, 3.0 * vel_x, 3.0 * vel_y, 3.0 * vel_z, 4.5 * (vel_x * vel_x - one_third), 4.5 * (vel_y * vel_y - one_third), 4.5 * (vel_z * vel_z - one_third), 9.0 * vel_x * vel_y, 9.0 * vel_x * vel_z, 9.0 * vel_y * vel_z)

def project_row(velocity):
    vel_x, vel_y, vel_z = velocity
    one_third = 1.0 / 3.0
    return (1.0, 1.0 * vel_x, 1.0 * vel_y, 1.0 * vel_z, vel_x * vel_x - one_third, vel_y * vel_y - one_third, vel_z * vel_z - one_third, 1.0 * vel_x * vel_y, 1.0 * vel_x * vel_z, 1.0 * vel_y * vel_z)

def combine(factors, operands):
    summed = None
    for factor, operand in zip(factors, operands):
        if factor != 0.0:
            product = factor * operand
            summed = product if summed is None else summed + product
    return summed

def population(direction, moments):
    return WEIGHTS[direction] * combine(rebuild_row(VELOCITIES[direction]), moments[:10])

def red_population(direction, moments):
    vel_x, vel_y, vel_z = VELOCITIES[direction]
    return WEIGHTS[direction] * combine((1.0, 3.0 * vel_x, 3.0 * vel_y, 3.0 * vel_z), moments[10:14])

def collide(fields, fluid_cells, gradient):
    density, flux_x, flux_y, flux_z = (fields[0], fields[1], fields[2], fields[3])
    stress = fields[4:10]
    red_density = fields[10]
    grad_x, grad_y, grad_z = gradient
    square = grad_x * grad_x + grad_y * grad_y + grad_z * grad_z
    inverse = lax.rsqrt(1.0 + square)
    strength = SURFACE * inverse
    trace_part = square / 3.0
    surface = (grad_x * grad_x - trace_part, grad_y * grad_y - trace_part, grad_z * grad_z - trace_part, grad_x * grad_y, grad_x * grad_z, grad_y * grad_z)
    relaxing = 1.0 - 1.0 / RELAX_TIME
    post_stress = [jnp.where(fluid_cells, relaxing * before + strength * addend, before) for before, addend in zip(stress, surface)]
    post_x = jnp.where(fluid_cells, flux_x, -flux_x)
    post_y = jnp.where(fluid_cells, flux_y, -flux_y)
    post_z = jnp.where(fluid_cells, flux_z, -flux_z)
    mixing = SEPARATION * red_density * (density - red_density) * inverse
    charge_x = jnp.where(fluid_cells, 0.5 * flux_x + mixing * grad_x, -0.5 * flux_x)
    charge_y = jnp.where(fluid_cells, 0.5 * flux_y + mixing * grad_y, -0.5 * flux_y)
    charge_z = jnp.where(fluid_cells, 0.5 * flux_z + mixing * grad_z, -0.5 * flux_z)
    second = [post_x * post_x + post_stress[0], post_y * post_y + post_stress[1], post_z * post_z + post_stress[2], post_x * post_y + post_stress[3], post_x * post_z + post_stress[4], post_y * post_z + post_stress[5]]
    return [density, post_x, post_y, post_z] + second + [red_density, charge_x, charge_y, charge_z]

def accumulate(totals, direction, arrived, red_arrived):
    updated = []
    for position, factor in enumerate(project_row(VELOCITIES[direction])):
        if factor != 0.0:
            contribution = factor * arrived
            updated.append(contribution if totals[position] is None else totals[position] + contribution)
        else:
            updated.append(totals[position])
    updated.append(red_arrived if totals[10] is None else totals[10] + red_arrived)
    return updated

def finish(totals):
    flux_x, flux_y, flux_z = (totals[1], totals[2], totals[3])
    return [totals[0], flux_x, flux_y, flux_z, totals[4] - flux_x * flux_x, totals[5] - flux_y * flux_y, totals[6] - flux_z * flux_z, totals[7] - flux_x * flux_y, totals[8] - flux_x * flux_z, totals[9] - flux_y * flux_z, totals[10]]

def live_source(widths):
    capacity = (COLS_DEV + 1) * TILE
    row_ends = (jnp.cumsum(widths) * TILE).astype(jnp.int32)
    starts = (row_ends - widths * TILE).astype(jnp.int32)
    rows_all = jnp.arange(NX, dtype=jnp.int32)
    owners = lax.optimization_barrier(jnp.sum((rows_all[:, None] >= row_ends[None, :]).astype(jnp.int32), axis=1)).astype(jnp.int32)
    chosen = owners[:, None] == jnp.arange(N_TILES, dtype=jnp.int32)[None, :]
    first_row = lax.optimization_barrier(jnp.sum(jnp.where(chosen, starts[None, :], 0), axis=1)).astype(jnp.int32)
    return (owners * capacity + rows_all - first_row).astype(jnp.int32)

def advance(fields, fluid_cells, inside):
    colour = 2.0 * fields[10] - fields[0]
    gradient = [jnp.zeros_like(colour) for component in range(3)]
    for direction in range(1, 19):
        velocity = VELOCITIES[direction]
        rolled = jnp.roll(colour, (-velocity[0], -velocity[1], -velocity[2]), axis=(0, 1, 2))
        neighbour = jnp.where(inside(velocity), rolled, colour)
        for component in range(3):
            if velocity[component] != 0:
                gradient[component] = gradient[component] + 3.0 * WEIGHTS[direction] * velocity[component] * neighbour
    post = collide(fields, fluid_cells, gradient)
    totals = [None] * 11
    for direction in range(19):
        velocity = VELOCITIES[direction]
        reverse = OPPOSITE[direction]
        inward = inside((-velocity[0], -velocity[1], -velocity[2]))
        outgoing = population(direction, post)
        arrived = jnp.where(inward, jnp.roll(outgoing, velocity, axis=(0, 1, 2)), population(reverse, post))
        red_out = red_population(direction, post)
        red_arrived = jnp.where(inward, jnp.roll(red_out, velocity, axis=(0, 1, 2)), red_population(reverse, post))
        totals = accumulate(totals, direction, arrived, red_arrived)
    return finish(totals)

def reference(density, momentum, stress, red_density, solid, widths):
    source = live_source(widths)
    width_cells = NYZ // TILE

    def compact(array):
        return jnp.take(array, source, axis=0).reshape(NX, width_cells, TILE)
    fields = [compact(density)] + [compact(momentum[component]) for component in range(3)]
    fields = fields + [compact(stress[component]) for component in range(6)] + [compact(red_density)]
    fluid_cells = compact(solid) == 0
    row_ids = jnp.arange(NX, dtype=jnp.int32)[:, None, None]
    lane_ids = jnp.arange(width_cells, dtype=jnp.int32)[None, :, None]
    depth_ids = jnp.arange(TILE, dtype=jnp.int32)[None, None, :]

    def inside(step):
        moved_x = row_ids + step[0]
        moved_y = lane_ids + step[1]
        moved_z = depth_ids + step[2]
        return (moved_x >= 0) & (moved_x < NX) & (moved_y >= 0) & (moved_y < width_cells) & (moved_z >= 0) & (moved_z < TILE)
    for repeat in range(STEPS):
        fields = advance(fields, fluid_cells, inside)

    def spread(grid):
        return jnp.zeros((NXP, NYZ), jnp.float32).at[source].set(grid.reshape(NX, NYZ).astype(jnp.float32))
    results = [spread(grid) for grid in fields]
    return (results[0], jnp.stack(results[1:4]), jnp.stack(results[4:10]), results[10])
```

```python
import functools

import jax
import jax.numpy as jnp
from jax import lax
from jax.experimental import pallas as pl
from jax.experimental.pallas import tpu as pltpu
from jax.sharding import PartitionSpec as P

TILE = 16
STEPS = 2
RELAX_TIME = 0.8
SURFACE = 0.1
SEPARATION = 0.7

LANES = 128
SUBLANES = 8
HALO = 4
CELLS_Y = LANES // TILE


def roll_lanes(values, amount):
    return pltpu.roll(values, amount % LANES, 2)


class Geometry:
    def __init__(self, sub_index, own_tiles):
        shape = (1, SUBLANES, LANES)
        lane = lax.broadcasted_iota(jnp.int32, shape, 2)
        tile = lax.broadcasted_iota(jnp.int32, shape, 1)
        depth = lane & (TILE - 1)
        self.z_low = depth == 0
        self.z_high = depth == TILE - 1
        low_part = sub_index == 0
        high_part = sub_index == 1
        self.y_low = (tile == 1) & (lane < TILE) & low_part
        self.y_high = (tile == own_tiles) & (lane >= LANES - TILE) & high_part
        own = (tile >= 1) & (tile <= own_tiles)
        self.domain = own | ((tile == own_tiles + 1) & low_part) | ((tile == 0) & high_part)
        self.first_lanes = lane < TILE
        self.last_lanes = lane >= LANES - TILE

    def from_low_y(self, values, depth_shift=0):
        crossed = jnp.where(self.last_lanes, pltpu.roll(values, 1, 1), values)
        return roll_lanes(crossed, TILE + depth_shift)

    def from_high_y(self, values, depth_shift=0):
        crossed = jnp.where(self.first_lanes, pltpu.roll(values, SUBLANES - 1, 1), values)
        return roll_lanes(crossed, -TILE + depth_shift)

    def from_low_z(self, values):
        return jnp.where(self.z_low, 0.0, roll_lanes(values, 1))

    def from_high_z(self, values):
        return jnp.where(self.z_high, 0.0, roll_lanes(values, -1))


def load_rows(ref, index, row, count):
    start = row * SUBLANES
    if not isinstance(start, int):
        start = pl.multiple_of(start, SUBLANES)
    return ref[index, pl.ds(start, count * SUBLANES), :].reshape(count, SUBLANES, LANES)


def store_rows(ref, index, row, values):
    count = values.shape[0]
    start = row * SUBLANES
    if not isinstance(start, int):
        start = pl.multiple_of(start, SUBLANES)
    ref[index, pl.ds(start, count * SUBLANES), :] = values.reshape(count * SUBLANES, LANES)


def fill_wall_table(walls, geometry):
    one = jnp.ones((1, SUBLANES, LANES), jnp.float32)
    up_y = jnp.where(geometry.y_high, 0.0, one)
    down_y = jnp.where(geometry.y_low, 0.0, one)
    up_z = jnp.where(geometry.z_high, 0.0, one)
    down_z = jnp.where(geometry.z_low, 0.0, one)
    sum_y, sum_z = up_y + down_y, up_z + down_z
    for kind, (up_x, down_x) in enumerate(((1.0, 1.0), (1.0, 0.0), (0.0, 1.0))):
        sum_x = up_x + down_x
        around_x = 2.0 + sum_y + sum_z
        total = 12.0 + 2.0 * (sum_x + sum_y + sum_z) + sum_x * (sum_y + sum_z) + sum_y * sum_z
        rows = (
            (up_x - down_x) * around_x,
            (up_y - down_y) * (2.0 + sum_x + sum_z),
            (up_z - down_z) * (2.0 + sum_x + sum_y),
            36.0 - total,
        )
        for position, row in enumerate(rows):
            store_rows(walls, position, kind, row)


def wall_rows(walls, position, kinds):
    return jnp.concatenate([load_rows(walls, position, kind, 1) for kind in kinds], axis=0)


def colour_pass(fields, colours, geometry, rows, first_row, count, block):
    def step(index, carry):
        row = first_row + index * block
        at = row + HALO
        density = load_rows(fields, 0, at, block)
        red = load_rows(fields, 10, at, block)
        ids = row + lax.broadcasted_iota(jnp.int32, (block, SUBLANES, LANES), 0)
        valid = geometry.domain & (ids >= rows[0]) & (ids < rows[1])
        colour = jnp.where(valid, 2.0 * red - density, 0.0)
        along_y = geometry.from_low_y(colour) + geometry.from_high_y(colour)
        along_z = geometry.from_low_z(colour) + geometry.from_high_z(colour)
        store_rows(colours, 0, at, colour)
        store_rows(colours, 1, at, 2.0 * colour + (along_y + along_z))
        store_rows(colours, 2, at, along_y)
        store_rows(colours, 3, at, along_z)
        return carry

    lax.fori_loop(0, pl.cdiv(count, block), step, 0)


def collide_pass(fields, colours, walls, moved, reds, geometry, rows, first_row, count, block):
    relaxing = 1.0 - 1.0 / RELAX_TIME
    third = 1.0 / 3.0

    def step(index, carry):
        row = first_row + index * block
        at = row + HALO
        kinds = []
        for extra in range(block):
            here = row + extra
            kinds.append(
                jnp.where(here == rows[0], 1, 0) + jnp.where(here == rows[1] - 1, 2, 0)
            )
        colour = load_rows(colours, 0, at, block)
        doubled = 2.0 * colour + (
            load_rows(colours, 0, at - 1, block) + load_rows(colours, 0, at + 1, block)
        )
        term_y = doubled + load_rows(colours, 3, at, block)
        term_z = doubled + load_rows(colours, 2, at, block)
        grad_x = load_rows(colours, 1, at + 1, block) - load_rows(colours, 1, at - 1, block)
        grad_y = geometry.from_high_y(term_y) - geometry.from_low_y(term_y)
        grad_z = geometry.from_high_z(term_z) - geometry.from_low_z(term_z)
        grad_x = (grad_x - wall_rows(walls, 0, kinds) * colour) * (1.0 / 12.0)
        grad_y = (grad_y - wall_rows(walls, 1, kinds) * colour) * (1.0 / 12.0)
        grad_z = (grad_z - wall_rows(walls, 2, kinds) * colour) * (1.0 / 12.0)

        fluid = load_rows(fields, 11, at, block) == 0.0
        density = load_rows(fields, 0, at, block)
        red = load_rows(fields, 10, at, block)
        flux = [load_rows(fields, 1 + axis, at, block) for axis in range(3)]
        stress = [load_rows(fields, 4 + part, at, block) for part in range(6)]
        square_xx, square_yy, square_zz = grad_x * grad_x, grad_y * grad_y, grad_z * grad_z
        square = square_xx + square_yy + square_zz
        inverse = jnp.where(fluid, lax.rsqrt(1.0 + square), 0.0)
        strength = SURFACE * inverse
        keep = jnp.where(fluid, relaxing, 1.0)
        sign = jnp.where(fluid, 1.0, -1.0)
        trace = third * square
        surface = (
            square_xx - trace,
            square_yy - trace,
            square_zz - trace,
            grad_x * grad_y,
            grad_x * grad_z,
            grad_y * grad_z,
        )
        pairs = ((0, 0), (1, 1), (2, 2), (0, 1), (0, 2), (1, 2))
        second = [
            flux[a] * flux[b] + (keep * before + strength * addend)
            for (a, b), before, addend in zip(pairs, stress, surface)
        ]
        flux = [sign * part for part in flux]
        mixing = (SEPARATION * red) * (density - red) * inverse
        charge = [
            0.5 * part + mixing * grad for part, grad in zip(flux, (grad_x, grad_y, grad_z))
        ]

        base = (density - 1.5 * (second[0] + second[1] + second[2])) * (1.0 / 36.0)
        run = [part * (1.0 / 12.0) for part in flux]
        own = [part * 0.125 for part in second[:3]]
        cross = [part * 0.25 for part in second[3:]]
        store_rows(moved, 0, at, 12.0 * base)
        straight = [base + part for part in own]
        for axis in range(3):
            middle = 2.0 * straight[axis]
            swing = 2.0 * run[axis]
            store_rows(moved, 1 + 2 * axis, at, middle + swing)
            store_rows(moved, 2 + 2 * axis, at, middle - swing)
        for plane, (a, b) in enumerate(((0, 1), (0, 2), (1, 2))):
            middle = straight[a] + own[b]
            same, other = middle + cross[plane], middle - cross[plane]
            along, against = run[a] + run[b], run[a] - run[b]
            first = 7 + 4 * plane
            store_rows(moved, first, at, same + along)
            store_rows(moved, first + 1, at, same - along)
            store_rows(moved, first + 2, at, other + against)
            store_rows(moved, first + 3, at, other - against)

        ids = row + lax.broadcasted_iota(jnp.int32, (block, SUBLANES, LANES), 0)
        valid = geometry.domain & (ids >= rows[0]) & (ids < rows[1])
        scale = jnp.where(valid, 1.0 / 12.0, 0.0)
        red_base = red * (scale * third)
        red_run = [part * scale for part in charge]
        store_rows(reds, 0, at, red_base)
        store_rows(reds, 1, at, red_base + red_run[0])
        store_rows(reds, 2, at, red_base - red_run[0])
        store_rows(reds, 3, at, red_run[1])
        store_rows(reds, 4, at, red_run[2])
        return carry

    lax.fori_loop(0, pl.cdiv(count, block), step, 0)


def arrive_pass(fields, walls, moved, reds, geometry, rows, first_row, count, block):
    third = 1.0 / 3.0

    def step(index, carry):
        row = first_row + index * block
        at = row + HALO
        kinds = []
        for extra in range(block):
            here = row + extra
            kinds.append(
                jnp.where(here == rows[0], 1, 0) + jnp.where(here == rows[1] - 1, 2, 0)
            )
        ids = row + lax.broadcasted_iota(jnp.int32, (block, SUBLANES, LANES), 0)
        x_low = ids == rows[0]
        x_high = ids == rows[1] - 1
        own = [None] * 19

        def here(direction):
            if own[direction] is None:
                own[direction] = load_rows(moved, direction, at, block)
            return own[direction]

        def arrived(direction, opposite, velocity):
            vel_x, vel_y, vel_z = velocity
            values = here(direction) if vel_x == 0 else load_rows(moved, direction, at - vel_x, block)
            if vel_y == 1:
                values = geometry.from_low_y(values, vel_z)
            elif vel_y == -1:
                values = geometry.from_high_y(values, vel_z)
            elif vel_z != 0:
                values = roll_lanes(values, vel_z)
            masks = []
            if vel_x != 0:
                masks.append(x_low if vel_x == 1 else x_high)
            if vel_y != 0:
                masks.append(geometry.y_low if vel_y == 1 else geometry.y_high)
            if vel_z != 0:
                masks.append(geometry.z_low if vel_z == 1 else geometry.z_high)
            wall = functools.reduce(lambda one, two: one | two, masks)
            return jnp.where(wall, here(opposite), values)

        rest = here(0)
        sums, diffs = [], []
        for axis in range(3):
            velocity = [0, 0, 0]
            velocity[axis] = 1
            up = arrived(1 + 2 * axis, 2 + 2 * axis, velocity)
            velocity[axis] = -1
            down = arrived(2 + 2 * axis, 1 + 2 * axis, velocity)
            sums.append(up + down)
            diffs.append(up - down)
        total = rest + sums[0] + sums[1] + sums[2]
        cross = []
        for plane, (a, b) in enumerate(((0, 1), (0, 2), (1, 2))):
            first = 7 + 4 * plane
            parts = []
            for offset, (vel_a, vel_b) in enumerate(((1, 1), (-1, -1), (1, -1), (-1, 1))):
                velocity = [0, 0, 0]
                velocity[a], velocity[b] = vel_a, vel_b
                parts.append(arrived(first + offset, first + (offset ^ 1), velocity))
            same, other = parts[0] + parts[1], parts[2] + parts[3]
            along, against = parts[0] - parts[1], parts[2] - parts[3]
            both = same + other
            cross.append(same - other)
            total = total + both
            sums[a], sums[b] = sums[a] + both, sums[b] + both
            diffs[a], diffs[b] = diffs[a] + (along + against), diffs[b] + (along - against)
        shared = third * total
        store_rows(fields, 0, at, total)
        for axis in range(3):
            store_rows(fields, 1 + axis, at, diffs[axis])
            store_rows(fields, 4 + axis, at, sums[axis] - shared - diffs[axis] * diffs[axis])
        for plane, (a, b) in enumerate(((0, 1), (0, 2), (1, 2))):
            store_rows(fields, 7 + plane, at, cross[plane] - diffs[a] * diffs[b])

        red = load_rows(reds, 0, at, block)
        red_x_up = load_rows(reds, 1, at, block)
        red_y = load_rows(reds, 3, at, block)
        red_z = load_rows(reds, 4, at, block)
        from_x = load_rows(reds, 1, at - 1, block) + load_rows(reds, 2, at + 1, block)
        spread = 2.0 * red + from_x
        spread_y = 2.0 * red_y + (load_rows(reds, 3, at - 1, block) + load_rows(reds, 3, at + 1, block))
        spread_z = 2.0 * red_z + (load_rows(reds, 4, at - 1, block) + load_rows(reds, 4, at + 1, block))
        up_y, down_y = red + red_y, red - red_y
        low_y = (
            (spread + spread_y)
            + geometry.from_low_z(up_y + red_z)
            + geometry.from_high_z(up_y - red_z)
        )
        high_y = (
            (spread - spread_y)
            + geometry.from_low_z(down_y + red_z)
            + geometry.from_high_z(down_y - red_z)
        )
        bounced = (
            wall_rows(walls, 3, kinds) * red
            - wall_rows(walls, 0, kinds) * (red_x_up - red)
            - wall_rows(walls, 1, kinds) * red_y
            - wall_rows(walls, 2, kinds) * red_z
        )
        red_total = (
            12.0 * red
            + 2.0 * from_x
            + geometry.from_low_z(spread + spread_z)
            + geometry.from_high_z(spread - spread_z)
            + geometry.from_low_y(low_y)
            + geometry.from_high_y(high_y)
            + bounced
        )
        store_rows(fields, 10, at, red_total)
        return carry

    lax.fori_loop(0, pl.cdiv(count, block), step, 0)


def spread_tiles(source, target, index, own_tiles, row_tiles):
    for row_tile in range(row_tiles):
        for tile in range(own_tiles):
            start = (HALO + row_tile * SUBLANES) * SUBLANES + 1 + tile
            target[index, pl.ds(start, SUBLANES, stride=SUBLANES), :] = source(row_tile, tile)


def steps_kernel(
    info, density, momentum, stress, red, solid, side, low, high,
    density_out, momentum_out, stress_out, red_out,
    fields, colours, walls, moved, reds,
):
    live, first, last, sub_index = info[0], info[1], info[2], info[3]
    row_count, flat_count = density.shape
    own_tiles = flat_count // LANES
    row_tiles = row_count // SUBLANES
    geometry = Geometry(sub_index, own_tiles)
    rows = (jnp.where(first == 1, 0, -1000), jnp.where(last == 1, live, 1000))
    fill_wall_table(walls, geometry)

    sources = [density] + [momentum.at[axis] for axis in range(3)]
    sources = sources + [stress.at[part] for part in range(6)] + [red, solid]
    low_part = sub_index == 0
    for index, source in enumerate(sources):

        def piece(row_tile, tile, source=source):
            values = source[pl.ds(row_tile * SUBLANES, SUBLANES), pl.ds(tile * LANES, LANES)]
            return values.astype(jnp.float32)

        spread_tiles(piece, fields, index, own_tiles, row_tiles)
        for row_tile in range(row_tiles):
            start = (HALO + row_tile * SUBLANES) * SUBLANES
            values = side[index, pl.ds(row_tile * SUBLANES, SUBLANES), :]
            below = jnp.where(low_part, 0.0, values)
            above = jnp.where(low_part, values, 0.0)
            fields[index, pl.ds(start, SUBLANES, stride=SUBLANES), :] = below
            fields[index, pl.ds(start + own_tiles + 1, SUBLANES, stride=SUBLANES), :] = above
        fields[index, pl.ds(0, HALO * SUBLANES), :] = low[index]
        end = pl.multiple_of((HALO + live) * SUBLANES, SUBLANES)
        fields[index, pl.ds(end, HALO * SUBLANES), :] = high[index]

    for repeat in range(STEPS):
        rim = 2 * (STEPS - 1 - repeat)
        colour_pass(fields, colours, geometry, rows, -rim - 2, live + 2 * rim + 4, 4)
        collide_pass(
            fields, colours, walls, moved, reds, geometry, rows, -rim - 1, live + 2 * rim + 2, 2
        )
        arrive_pass(fields, walls, moved, reds, geometry, rows, -rim, live + 2 * rim, 2)

    targets = [density_out] + [momentum_out.at[axis] for axis in range(3)]
    targets = targets + [stress_out.at[part] for part in range(6)] + [red_out]
    for index, target in enumerate(targets):
        for row_tile in range(row_tiles):
            alive = row_tile * SUBLANES < live
            for tile in range(own_tiles):
                start = (HALO + row_tile * SUBLANES) * SUBLANES + 1 + tile
                values = fields[index, pl.ds(start, SUBLANES, stride=SUBLANES), :]
                target[pl.ds(row_tile * SUBLANES, SUBLANES), pl.ds(tile * LANES, LANES)] = (
                    jnp.where(alive, values, 0.0)
                )


def run_steps(info, arrays, side, low, high):
    density = arrays[0]
    row_count, flat_count = density.shape
    scratch_rows = (row_count + 2 * HALO + SUBLANES) * SUBLANES
    shapes = [jax.ShapeDtypeStruct(array.shape, jnp.float32) for array in arrays[:4]]
    return pl.pallas_call(
        steps_kernel,
        out_shape=shapes,
        in_specs=[pl.BlockSpec(memory_space=pltpu.SMEM)]
        + [pl.BlockSpec(memory_space=pltpu.VMEM)] * 8,
        out_specs=[pl.BlockSpec(memory_space=pltpu.VMEM)] * 4,
        scratch_shapes=[
            pltpu.VMEM((12, scratch_rows, LANES), jnp.float32),
            pltpu.VMEM((4, scratch_rows, LANES), jnp.float32),
            pltpu.VMEM((4, 3 * SUBLANES, LANES), jnp.float32),
            pltpu.VMEM((19, scratch_rows, LANES), jnp.float32),
            pltpu.VMEM((5, scratch_rows, LANES), jnp.float32),
        ],
        compiler_params=pltpu.CompilerParams(vmem_limit_bytes=40 * 1024 * 1024),
    )(info, *arrays, side, low, high)


def body(density, momentum, stress, red_density, solid, widths):
    row_count, flat_count = density.shape
    tiles_index = lax.axis_index("tiles")
    tiles_count = lax.axis_size("tiles")
    sub_index = lax.axis_index("sub")
    chosen = lax.iota(jnp.int32, widths.shape[0]) == tiles_index
    live_rows = jnp.sum(jnp.where(chosen, widths, 0)) * TILE
    info = jnp.stack(
        [
            live_rows,
            (tiles_index == 0).astype(jnp.int32),
            (tiles_index == tiles_count - 1).astype(jnp.int32),
            sub_index.astype(jnp.int32),
        ]
    )
    planes = [density[None], momentum, stress, red_density[None], solid.astype(jnp.float32)[None]]
    low_part = sub_index == 0

    edge = jnp.concatenate(
        [jnp.where(low_part, plane[:, :, -LANES:], plane[:, :, :LANES]) for plane in planes], axis=0
    )
    side = lax.ppermute(edge, "sub", [(0, 1), (1, 0)])

    def send_rows(start):
        own = jnp.concatenate(
            [lax.dynamic_slice_in_dim(plane, start, HALO, axis=1) for plane in planes], axis=0
        )
        beside = lax.dynamic_slice_in_dim(side, start, HALO, axis=1)
        below = jnp.where(low_part, 0.0, beside)
        above = jnp.where(low_part, beside, 0.0)
        whole = jnp.concatenate([below, own, above], axis=2)
        return whole.reshape(12, HALO * SUBLANES, LANES)

    ends = tiles_count - 1
    low = lax.ppermute(
        send_rows(live_rows - HALO), "tiles", [(i, i + 1) for i in range(ends)]
    )
    high = lax.ppermute(send_rows(0), "tiles", [(i + 1, i) for i in range(ends)])
    outs = run_steps(
        info, (density, momentum, stress, red_density, solid), side, low, high
    )
    return tuple(outs)


def solution(mesh):
    in_specs = (
        P(("groups", "tiles"), "sub"),
        P(None, ("groups", "tiles"), "sub"),
        P(None, ("groups", "tiles"), "sub"),
        P(("groups", "tiles"), "sub"),
        P(("groups", "tiles"), "sub"),
        P("groups"),
    )
    out_specs = (
        P(("groups", "tiles"), "sub"),
        P(None, ("groups", "tiles"), "sub"),
        P(None, ("groups", "tiles"), "sub"),
        P(("groups", "tiles"), "sub"),
    )
    return jax.shard_map(body, mesh=mesh, in_specs=in_specs, out_specs=out_specs, check_vma=False)
```

```python
import functools

import jax
import jax.numpy as jnp
from jax import lax
from jax.experimental import pallas as pl
from jax.experimental.pallas import tpu as pltpu
from jax.sharding import PartitionSpec as P

TILE = 16
STEPS = 2
RELAX_TIME = 0.8
SURFACE = 0.1
SEPARATION = 0.7

LANES = 128
SUBLANES = 8
FULL = 3
HALO = FULL + 1
FIELDS = 11
PLANES = FIELDS + 1
MOVED = 19
REDS = 5
RIM = 4
SLAB = HALO + 2 * RIM
COLOUR_BLOCK = 8
COLLIDE_BLOCK = 4
ARRIVE_BLOCK = 4
VMEM = pl.BlockSpec(memory_space=pltpu.VMEM)
SMEM = pl.BlockSpec(memory_space=pltpu.SMEM)
ANY = pl.BlockSpec(memory_space=pl.ANY)
HBM = pl.BlockSpec(memory_space=pltpu.HBM)


def roll_lanes(values, amount):
    return pltpu.roll(values, amount % LANES, 2)


class Geometry:
    def __init__(self, info, own_tiles):
        live, first, last, sub_index = info[0], info[1], info[2], info[3]
        self.live = live
        self.low_row = jnp.where(first == 1, 0, -1000)
        self.high_row = jnp.where(last == 1, live, 1000)
        shape = (1, SUBLANES, LANES)
        lane = lax.broadcasted_iota(jnp.int32, shape, 2)
        tile = lax.broadcasted_iota(jnp.int32, shape, 1)
        depth = lane & (TILE - 1)
        self.z_low = depth == 0
        self.z_high = depth == TILE - 1
        low_part = sub_index == 0
        high_part = sub_index == 1
        self.y_low = (tile == 1) & (lane < TILE) & low_part
        self.y_high = (tile == own_tiles) & (lane >= LANES - TILE) & high_part
        own = (tile >= 1) & (tile <= own_tiles)
        self.domain = own | ((tile == own_tiles + 1) & low_part) | ((tile == 0) & high_part)
        self.first_lanes = lane < TILE
        self.last_lanes = lane >= LANES - TILE

    def from_low_y(self, values, depth_shift=0):
        crossed = jnp.where(self.last_lanes, pltpu.roll(values, 1, 1), values)
        return roll_lanes(crossed, TILE + depth_shift)

    def from_high_y(self, values, depth_shift=0):
        crossed = jnp.where(self.first_lanes, pltpu.roll(values, SUBLANES - 1, 1), values)
        return roll_lanes(crossed, -TILE + depth_shift)

    def from_low_z(self, values):
        return jnp.where(self.z_low, 0.0, roll_lanes(values, 1))

    def from_high_z(self, values):
        return jnp.where(self.z_high, 0.0, roll_lanes(values, -1))


def flat_rows(row, count):
    start = row * SUBLANES
    if not isinstance(start, int):
        start = pl.multiple_of(start, SUBLANES)
    return pl.ds(start, count * SUBLANES)


class Block:
    def __init__(self, geometry, spans, inner=False):
        self.spans = spans
        rows = [row + extra for row, local, count in spans for extra in range(count)]
        if inner:
            self.x_low = self.x_high = None
            self.valid = geometry.domain
            self.kinds = [0]
            return
        shape = (1, SUBLANES, LANES)
        ids = jnp.concatenate([row + jnp.zeros(shape, jnp.int32) for row in rows], axis=0)
        self.x_low = ids == geometry.low_row
        self.x_high = ids == geometry.high_row - 1
        self.valid = geometry.domain & (ids >= geometry.low_row) & (ids < geometry.high_row)
        self.kinds = [
            jnp.where(row == geometry.low_row, 1, 0) + jnp.where(row == geometry.high_row - 1, 2, 0)
            for row in rows
        ]

    def load(self, ref, index, offset=0):
        parts = [
            ref[index, flat_rows(local + offset, count), :].reshape(count, SUBLANES, LANES)
            for row, local, count in self.spans
        ]
        return parts[0] if len(parts) == 1 else jnp.concatenate(parts, axis=0)

    def store(self, ref, index, values):
        done = 0
        for row, local, count in self.spans:
            part = values[done : done + count].reshape(count * SUBLANES, LANES)
            ref[index, flat_rows(local, count), :] = part
            done += count

    def walls(self, walls, position):
        parts = [walls[position, flat_rows(kind, 1), :][None] for kind in self.kinds]
        return jnp.concatenate(parts, axis=0)


def fill_wall_table(walls, geometry):
    one = jnp.ones((1, SUBLANES, LANES), jnp.float32)
    up_y = jnp.where(geometry.y_high, 0.0, one)
    down_y = jnp.where(geometry.y_low, 0.0, one)
    up_z = jnp.where(geometry.z_high, 0.0, one)
    down_z = jnp.where(geometry.z_low, 0.0, one)
    sum_y, sum_z = up_y + down_y, up_z + down_z
    for kind, (up_x, down_x) in enumerate(((1.0, 1.0), (1.0, 0.0), (0.0, 1.0))):
        sum_x = up_x + down_x
        around_x = 2.0 + sum_y + sum_z
        total = 12.0 + 2.0 * (sum_x + sum_y + sum_z) + sum_x * (sum_y + sum_z) + sum_y * sum_z
        rows = (
            (up_x - down_x) * around_x,
            (up_y - down_y) * (2.0 + sum_x + sum_z),
            (up_z - down_z) * (2.0 + sum_x + sum_y),
            36.0 - total,
        )
        for position, row in enumerate(rows):
            walls[position, flat_rows(kind, 1), :] = row[0]


def colour_stage(block, geometry, fields, colours):
    density = block.load(fields, 0)
    red = block.load(fields, 10)
    colour = jnp.where(block.valid, 2.0 * red - density, 0.0)
    along_y = geometry.from_low_y(colour) + geometry.from_high_y(colour)
    along_z = geometry.from_low_z(colour) + geometry.from_high_z(colour)
    block.store(colours, 0, colour)
    block.store(colours, 1, 2.0 * colour + (along_y + along_z))
    block.store(colours, 2, along_y)
    block.store(colours, 3, along_z)


def collide_stage(block, geometry, fields, solids, colours, walls, moved, reds):
    relaxing = 1.0 - 1.0 / RELAX_TIME
    third = 1.0 / 3.0
    colour = block.load(colours, 0)
    doubled = 2.0 * colour + (block.load(colours, 0, -1) + block.load(colours, 0, 1))
    term_y = doubled + block.load(colours, 3)
    term_z = doubled + block.load(colours, 2)
    grad_x = block.load(colours, 1, 1) - block.load(colours, 1, -1)
    grad_y = geometry.from_high_y(term_y) - geometry.from_low_y(term_y)
    grad_z = geometry.from_high_z(term_z) - geometry.from_low_z(term_z)
    grad_x = (grad_x - block.walls(walls, 0) * colour) * (1.0 / 12.0)
    grad_y = (grad_y - block.walls(walls, 1) * colour) * (1.0 / 12.0)
    grad_z = (grad_z - block.walls(walls, 2) * colour) * (1.0 / 12.0)

    fluid = block.load(solids, PLANES - 1) == 0.0
    density = block.load(fields, 0)
    red = block.load(fields, 10)
    flux = [block.load(fields, 1 + axis) for axis in range(3)]
    stress = [block.load(fields, 4 + part) for part in range(6)]
    square_xx, square_yy, square_zz = grad_x * grad_x, grad_y * grad_y, grad_z * grad_z
    square = square_xx + square_yy + square_zz
    inverse = jnp.where(fluid, lax.rsqrt(1.0 + square), 0.0)
    strength = SURFACE * inverse
    keep = jnp.where(fluid, relaxing, 1.0)
    sign = jnp.where(fluid, 1.0, -1.0)
    trace = third * square
    surface = (
        square_xx - trace,
        square_yy - trace,
        square_zz - trace,
        grad_x * grad_y,
        grad_x * grad_z,
        grad_y * grad_z,
    )
    pairs = ((0, 0), (1, 1), (2, 2), (0, 1), (0, 2), (1, 2))
    second = [
        flux[a] * flux[b] + (keep * before + strength * addend)
        for (a, b), before, addend in zip(pairs, stress, surface)
    ]
    flux = [sign * part for part in flux]
    mixing = (SEPARATION * red) * (density - red) * inverse
    charge = [0.5 * part + mixing * grad for part, grad in zip(flux, (grad_x, grad_y, grad_z))]

    base = (density - 1.5 * (second[0] + second[1] + second[2])) * (1.0 / 36.0)
    run = [part * (1.0 / 12.0) for part in flux]
    own = [part * 0.125 for part in second[:3]]
    cross = [part * 0.25 for part in second[3:]]
    block.store(moved, 0, 12.0 * base)
    straight = [base + part for part in own]
    for axis in range(3):
        middle = 2.0 * straight[axis]
        swing = 2.0 * run[axis]
        block.store(moved, 1 + 2 * axis, middle + swing)
        block.store(moved, 2 + 2 * axis, middle - swing)
    for plane, (a, b) in enumerate(((0, 1), (0, 2), (1, 2))):
        middle = straight[a] + own[b]
        same, other = middle + cross[plane], middle - cross[plane]
        along, against = run[a] + run[b], run[a] - run[b]
        first = 7 + 4 * plane
        block.store(moved, first, same + along)
        block.store(moved, first + 1, same - along)
        block.store(moved, first + 2, other + against)
        block.store(moved, first + 3, other - against)

    scale = jnp.where(block.valid, 1.0 / 12.0, 0.0)
    red_base = red * (scale * third)
    red_run = [part * scale for part in charge]
    block.store(reds, 0, red_base)
    block.store(reds, 1, red_base + red_run[0])
    block.store(reds, 2, red_base - red_run[0])
    block.store(reds, 3, red_run[1])
    block.store(reds, 4, red_run[2])


def arrive_stage(block, geometry, walls, moved, reds, fields):
    third = 1.0 / 3.0
    own = [None] * MOVED

    def here(direction):
        if own[direction] is None:
            own[direction] = block.load(moved, direction)
        return own[direction]

    def arrived(direction, opposite, velocity):
        vel_x, vel_y, vel_z = velocity
        values = here(direction) if vel_x == 0 else block.load(moved, direction, -vel_x)
        if vel_y == 1:
            values = geometry.from_low_y(values, vel_z)
        elif vel_y == -1:
            values = geometry.from_high_y(values, vel_z)
        elif vel_z != 0:
            values = roll_lanes(values, vel_z)
        masks = []
        if vel_x != 0 and block.x_low is not None:
            masks.append(block.x_low if vel_x == 1 else block.x_high)
        if vel_y != 0:
            masks.append(geometry.y_low if vel_y == 1 else geometry.y_high)
        if vel_z != 0:
            masks.append(geometry.z_low if vel_z == 1 else geometry.z_high)
        if not masks:
            return values
        wall = functools.reduce(lambda one, two: one | two, masks)
        return jnp.where(wall, here(opposite), values)

    rest = here(0)
    sums, diffs = [], []
    for axis in range(3):
        velocity = [0, 0, 0]
        velocity[axis] = 1
        up = arrived(1 + 2 * axis, 2 + 2 * axis, velocity)
        velocity[axis] = -1
        down = arrived(2 + 2 * axis, 1 + 2 * axis, velocity)
        sums.append(up + down)
        diffs.append(up - down)
    total = rest + sums[0] + sums[1] + sums[2]
    cross = []
    for plane, (a, b) in enumerate(((0, 1), (0, 2), (1, 2))):
        first = 7 + 4 * plane
        parts = []
        for offset, (vel_a, vel_b) in enumerate(((1, 1), (-1, -1), (1, -1), (-1, 1))):
            velocity = [0, 0, 0]
            velocity[a], velocity[b] = vel_a, vel_b
            parts.append(arrived(first + offset, first + (offset ^ 1), velocity))
        same, other = parts[0] + parts[1], parts[2] + parts[3]
        along, against = parts[0] - parts[1], parts[2] - parts[3]
        both = same + other
        cross.append(same - other)
        total = total + both
        sums[a], sums[b] = sums[a] + both, sums[b] + both
        diffs[a], diffs[b] = diffs[a] + (along + against), diffs[b] + (along - against)
    shared = third * total
    block.store(fields, 0, total)
    for axis in range(3):
        block.store(fields, 1 + axis, diffs[axis])
        block.store(fields, 4 + axis, sums[axis] - shared - diffs[axis] * diffs[axis])
    for plane, (a, b) in enumerate(((0, 1), (0, 2), (1, 2))):
        block.store(fields, 7 + plane, cross[plane] - diffs[a] * diffs[b])

    red = block.load(reds, 0)
    red_x_up = block.load(reds, 1)
    red_y = block.load(reds, 3)
    red_z = block.load(reds, 4)
    from_x = block.load(reds, 1, -1) + block.load(reds, 2, 1)
    spread = 2.0 * red + from_x
    spread_y = 2.0 * red_y + (block.load(reds, 3, -1) + block.load(reds, 3, 1))
    spread_z = 2.0 * red_z + (block.load(reds, 4, -1) + block.load(reds, 4, 1))
    up_y, down_y = red + red_y, red - red_y
    low_y = (
        (spread + spread_y)
        + geometry.from_low_z(up_y + red_z)
        + geometry.from_high_z(up_y - red_z)
    )
    high_y = (
        (spread - spread_y)
        + geometry.from_low_z(down_y + red_z)
        + geometry.from_high_z(down_y - red_z)
    )
    bounced = (
        block.walls(walls, 3) * red
        - block.walls(walls, 0) * (red_x_up - red)
        - block.walls(walls, 1) * red_y
        - block.walls(walls, 2) * red_z
    )
    red_total = (
        12.0 * red
        + 2.0 * from_x
        + geometry.from_low_z(spread + spread_z)
        + geometry.from_high_z(spread - spread_z)
        + geometry.from_low_y(low_y)
        + geometry.from_high_y(high_y)
        + bounced
    )
    block.store(fields, 10, red_total)


def over_rows(geometry, first, end, size, stage):
    def step(index, carry):
        row = jnp.minimum(first + index * size, end - size)
        stage(Block(geometry, [(row, row, size)], inner=True))
        return carry

    lax.fori_loop(0, (end - first + size - 1) // size, step, 0)


def edge_kernel(density, momentum, stress, red, solid, edge, solid_edge, sems):
    own_tiles = density.shape[1] // LANES
    start = jnp.where(lax.axis_index("sub") == 0, (own_tiles - 1) * LANES, 0)
    lanes = pl.ds(pl.multiple_of(start, LANES), LANES)
    copies = [
        pltpu.make_async_copy(density.at[:, lanes], edge.at[0], sems.at[0]),
        pltpu.make_async_copy(momentum.at[:, :, lanes], edge.at[pl.ds(1, 3)], sems.at[1]),
        pltpu.make_async_copy(stress.at[:, :, lanes], edge.at[pl.ds(4, 6)], sems.at[2]),
        pltpu.make_async_copy(red.at[:, lanes], edge.at[10], sems.at[3]),
        pltpu.make_async_copy(solid.at[:, lanes], solid_edge, sems.at[4]),
    ]
    for copy in copies:
        copy.start()
    for copy in copies:
        copy.wait()
    edge[PLANES - 1] = solid_edge[...].astype(jnp.float32)


def take_edge(arrays):
    row_count = arrays[0].shape[0]
    return pl.pallas_call(
        edge_kernel,
        out_shape=jax.ShapeDtypeStruct((PLANES, row_count, LANES), jnp.float32),
        in_specs=[HBM] * 5,
        out_specs=VMEM,
        scratch_shapes=[pltpu.VMEM((row_count, LANES), jnp.int32), pltpu.SemaphoreType.DMA((5,))],
        name="edge",
    )(*arrays)


def spread_kernel(density, momentum, stress, red, solid, spread):
    row_count, flat_count = density.shape
    sources = [density] + [momentum.at[axis] for axis in range(3)]
    sources = sources + [stress.at[part] for part in range(6)] + [red, solid]
    for index, source in enumerate(sources):
        for row in range(0, row_count, SUBLANES):
            for tile in range(flat_count // LANES):
                values = source[pl.ds(row, SUBLANES), pl.ds(tile * LANES, LANES)]
                start = row * SUBLANES + 1 + tile
                spread[index, pl.ds(start, SUBLANES, stride=SUBLANES), :] = values.astype(jnp.float32)


def spread_rows(arrays):
    row_count = arrays[0].shape[0]
    return pl.pallas_call(
        spread_kernel,
        out_shape=jax.ShapeDtypeStruct((PLANES, row_count * SUBLANES, LANES), jnp.float32),
        in_specs=[VMEM] * 5,
        out_specs=VMEM,
        compiler_params=pltpu.CompilerParams(vmem_limit_bytes=16 * 1024 * 1024),
        name="spread",
    )(*arrays)


def ends_kernel(info, spread, side, whole, low_end, high_end):
    live, low_part = info[0], info[3] == 0
    row_count = side.shape[1]
    for index in range(PLANES):
        whole[index] = spread[index]
        for row in range(0, row_count, SUBLANES):
            values = side[index, pl.ds(row, SUBLANES), :]
            start = row * SUBLANES
            below = jnp.where(low_part, 0.0, values)
            above = jnp.where(low_part, values, 0.0)
            whole[index, pl.ds(start, SUBLANES, stride=SUBLANES), :] = below
            whole[index, pl.ds(start + SUBLANES - 1, SUBLANES, stride=SUBLANES), :] = above
    for index in range(PLANES):
        target = pl.ds((1 + FULL * index) * SUBLANES, FULL * SUBLANES)
        low_end[target, :] = whole[index, pl.ds(0, FULL * SUBLANES), :]
        high_end[target, :] = whole[index, flat_rows(live - FULL, FULL), :]
    for end, row in ((low_end, FULL), (high_end, live - HALO)):
        rows = flat_rows(row, 1)
        end[pl.ds(0, SUBLANES), :] = 2.0 * whole[10, rows, :] - whole[0, rows, :]


def take_ends(info, spread, side):
    end = jax.ShapeDtypeStruct(((1 + FULL * PLANES) * SUBLANES, LANES), jnp.float32)
    return pl.pallas_call(
        ends_kernel,
        out_shape=[jax.ShapeDtypeStruct(spread.shape, jnp.float32), end, end],
        in_specs=[SMEM, VMEM, VMEM],
        out_specs=[VMEM] * 3,
        compiler_params=pltpu.CompilerParams(vmem_limit_bytes=16 * 1024 * 1024),
        name="ends",
    )(info, spread, side)


def inner_kernel(
    info, whole,
    density_out, momentum_out, stress_out, red_out, moved_rim, fields_rim, final_rim,
    colours, walls, moved, reds, fields, moved_later, reds_later, final,
):
    row_count, flat_count = density_out.shape
    own_tiles = flat_count // LANES
    geometry = Geometry(info, own_tiles)
    live = geometry.live
    fill_wall_table(walls, geometry)

    def colour(source, first, end):
        over_rows(geometry, first, end, COLOUR_BLOCK, lambda block: colour_stage(
            block, geometry, source, colours))

    def collide(source, target, target_reds, first, end):
        over_rows(geometry, first, end, COLLIDE_BLOCK, lambda block: collide_stage(
            block, geometry, source, whole, colours, walls, target, target_reds))

    def arrive(source, source_reds, target, first, end):
        over_rows(geometry, first, end, ARRIVE_BLOCK, lambda block: arrive_stage(
            block, geometry, walls, source, source_reds, target))

    colour(whole, 0, live)
    collide(whole, moved, reds, 1, live - 1)
    arrive(moved, reds, fields, 2, live - 2)
    colour(fields, 2, live - 2)
    collide(fields, moved_later, reds_later, 3, live - 3)
    arrive(moved_later, reds_later, final, 4, live - 4)

    def keep(target, target_index, source, index, rows, size):
        for place, row in enumerate(rows):
            target[target_index, flat_rows(place * size, size), :] = source[
                index, flat_rows(row, size), :
            ]

    for index in range(MOVED + REDS):
        first, later, at = moved, moved_later, index
        if index >= MOVED:
            first, later, at = reds, reds_later, index - MOVED
        keep(moved_rim, index, first, at, (1, live - 3), 2)
        keep(moved_rim, MOVED + REDS + index, later, at, (3, live - 5), 2)
    for index in range(FIELDS):
        keep(fields_rim, index, fields, index, (2, live - 4), 2)
        keep(final_rim, index, final, index, (RIM, live - 2 * RIM), RIM)

    targets = [density_out] + [momentum_out.at[axis] for axis in range(3)]
    targets = targets + [stress_out.at[part] for part in range(6)] + [red_out]
    for index, target in enumerate(targets):
        for row in range(0, row_count, SUBLANES):
            alive = row < live
            for tile in range(own_tiles):
                start = row * SUBLANES + 1 + tile
                values = final[index, pl.ds(start, SUBLANES, stride=SUBLANES), :]
                target[pl.ds(row, SUBLANES), pl.ds(tile * LANES, LANES)] = jnp.where(
                    alive, values, 0.0
                )


def run_inner(info, whole, arrays):
    flat = whole.shape[1]
    rim = lambda count, rows: jax.ShapeDtypeStruct((count, rows * SUBLANES, LANES), jnp.float32)
    shapes = [jax.ShapeDtypeStruct(array.shape, jnp.float32) for array in arrays[:4]]
    shapes = shapes + [rim(2 * (MOVED + REDS), 4), rim(FIELDS, 4), rim(FIELDS, 2 * RIM)]
    return pl.pallas_call(
        inner_kernel,
        out_shape=shapes,
        in_specs=[SMEM, VMEM],
        out_specs=[VMEM] * len(shapes),
        scratch_shapes=[
            pltpu.VMEM((4, flat, LANES), jnp.float32),
            pltpu.VMEM((4, 3 * SUBLANES, LANES), jnp.float32),
            pltpu.VMEM((MOVED, flat, LANES), jnp.float32),
            pltpu.VMEM((REDS, flat, LANES), jnp.float32),
            pltpu.VMEM((FIELDS, flat, LANES), jnp.float32),
            pltpu.VMEM((MOVED, flat, LANES), jnp.float32),
            pltpu.VMEM((REDS, flat, LANES), jnp.float32),
            pltpu.VMEM((FIELDS, flat, LANES), jnp.float32),
        ],
        compiler_params=pltpu.CompilerParams(vmem_limit_bytes=32 * 1024 * 1024),
        cost_estimate=pl.CostEstimate(flops=40_000_000, bytes_accessed=8_000_000, transcendentals=0),
        name="inner",
    )(info, whole)


def outer_kernel(
    info, whole, low, high, moved_rim, fields_rim, final_rim, *refs,
):
    outs = refs[4:8]
    start_fields, colours, walls, moved, reds, fields, moved_later, reds_later, final = refs[8:17]
    pieces, sems = refs[17:]
    row_count, flat_count = outs[0].shape
    own_tiles = flat_count // LANES
    geometry = Geometry(info, own_tiles)
    live = geometry.live
    fill_wall_table(walls, geometry)

    def spans(first, count):
        mirrored = SLAB - first - count
        return [
            (first - HALO, first, count),
            (live - 2 * RIM + mirrored, SLAB + mirrored, count),
        ]

    for index in range(PLANES):
        place = pl.ds((1 + FULL * index) * SUBLANES, FULL * SUBLANES)
        start_fields[index, flat_rows(1, FULL), :] = low[place, :]
        start_fields[index, flat_rows(2 * SLAB - HALO, FULL), :] = high[place, :]
        start_fields[index, flat_rows(HALO, 2), :] = whole[index, flat_rows(0, 2), :]
        start_fields[index, flat_rows(2 * SLAB - HALO - 2, 2), :] = whole[
            index, flat_rows(live - 2, 2), :
        ]
    for row, end in ((0, low), (2 * SLAB - 1, high)):
        start_fields[0, flat_rows(row, 1), :] = jnp.zeros((SUBLANES, LANES), jnp.float32)
        start_fields[10, flat_rows(row, 1), :] = 0.5 * end[pl.ds(0, SUBLANES), :]

    def place(target, index, source, at, first, size):
        for place, (row, local, count) in enumerate(spans(first, size)):
            target[index, flat_rows(local, size), :] = source[at, flat_rows(place * size, size), :]

    for index in range(MOVED + REDS):
        target, later, at = moved, moved_later, index
        if index >= MOVED:
            target, later, at = reds, reds_later, index - MOVED
        place(target, at, moved_rim, index, HALO + 1, 2)
        place(later, at, moved_rim, MOVED + REDS + index, HALO + 3, 2)
    for index in range(FIELDS):
        place(fields, index, fields_rim, index, HALO + 2, 2)
        place(final, index, final_rim, index, HALO + RIM, RIM)

    block = lambda first, count: Block(geometry, spans(first, count))
    colour_stage(block(0, 6), geometry, start_fields, colours)
    collide_stage(block(1, 4), geometry, start_fields, start_fields, colours, walls, moved, reds)
    arrive_stage(block(2, 4), geometry, walls, moved, reds, fields)
    start_fields[PLANES - 1, flat_rows(HALO + 2, 1), :] = whole[PLANES - 1, flat_rows(2, 1), :]
    start_fields[PLANES - 1, flat_rows(2 * SLAB - HALO - 3, 1), :] = whole[
        PLANES - 1, flat_rows(live - 3, 1), :
    ]
    colour_stage(block(2, 6), geometry, fields, colours)
    collide_stage(
        block(3, 4), geometry, fields, start_fields, colours, walls, moved_later, reds_later
    )
    arrive_stage(block(4, 4), geometry, walls, moved_later, reds_later, final)

    for index in range(FIELDS):
        for side, row in ((0, HALO), (1, SLAB)):
            for tile in range(own_tiles):
                start = row * SUBLANES + 1 + tile
                pieces[index, pl.ds(side * SUBLANES, SUBLANES), pl.ds(tile * LANES, LANES)] = final[
                    index, pl.ds(start, SUBLANES, stride=SUBLANES), :
                ]
    copies = []
    for side, row in ((0, 0), (1, pl.multiple_of(live - SUBLANES, SUBLANES))):
        rows = pl.ds(row, SUBLANES)
        held = pl.ds(side * SUBLANES, SUBLANES)
        for number, (out, source) in enumerate(
            (
                (outs[0].at[rows], pieces.at[0, held]),
                (outs[1].at[:, rows], pieces.at[pl.ds(1, 3), held]),
                (outs[2].at[:, rows], pieces.at[pl.ds(4, 6), held]),
                (outs[3].at[rows], pieces.at[10, held]),
            )
        ):
            copies.append(pltpu.make_async_copy(source, out, sems.at[side, number]))
    for copy in copies:
        copy.start()
    for copy in copies:
        copy.wait()


def run_outer(info, whole, low, high, rims, outs):
    flat = 2 * SLAB * SUBLANES
    flat_count = outs[0].shape[1]
    return pl.pallas_call(
        outer_kernel,
        out_shape=[jax.ShapeDtypeStruct(out.shape, jnp.float32) for out in outs],
        in_specs=[SMEM] + [VMEM] * 6 + [ANY] * 4,
        out_specs=[ANY] * 4,
        scratch_shapes=[
            pltpu.VMEM((PLANES, flat, LANES), jnp.float32),
            pltpu.VMEM((4, flat, LANES), jnp.float32),
            pltpu.VMEM((4, 3 * SUBLANES, LANES), jnp.float32),
            pltpu.VMEM((MOVED, flat, LANES), jnp.float32),
            pltpu.VMEM((REDS, flat, LANES), jnp.float32),
            pltpu.VMEM((FIELDS, flat, LANES), jnp.float32),
            pltpu.VMEM((MOVED, flat, LANES), jnp.float32),
            pltpu.VMEM((REDS, flat, LANES), jnp.float32),
            pltpu.VMEM((FIELDS, flat, LANES), jnp.float32),
            pltpu.VMEM((FIELDS, 2 * SUBLANES, flat_count), jnp.float32),
            pltpu.SemaphoreType.DMA((2, 4)),
        ],
        input_output_aliases={7: 0, 8: 1, 9: 2, 10: 3},
        compiler_params=pltpu.CompilerParams(vmem_limit_bytes=32 * 1024 * 1024),
        name="outer",
    )(info, whole, low, high, *rims, *outs)


def body(density, momentum, stress, red_density, solid, widths):
    tiles_index = lax.axis_index("tiles")
    tiles_count = lax.axis_size("tiles")
    chosen = lax.iota(jnp.int32, widths.shape[0]) == tiles_index
    live_rows = jnp.sum(jnp.where(chosen, widths, 0)) * TILE
    info = jnp.stack(
        [
            live_rows,
            (tiles_index == 0).astype(jnp.int32),
            (tiles_index == tiles_count - 1).astype(jnp.int32),
            lax.axis_index("sub").astype(jnp.int32),
        ]
    )
    arrays = (density, momentum, stress, red_density, solid)
    side = lax.ppermute(take_edge(arrays), "sub", [(0, 1), (1, 0)])
    whole, low_end, high_end = take_ends(info, spread_rows(arrays), side)
    ends = tiles_count - 1
    low = lax.ppermute(high_end, "tiles", [(i, i + 1) for i in range(ends)])
    high = lax.ppermute(low_end, "tiles", [(i + 1, i) for i in range(ends)])
    results = run_inner(info, whole, arrays)
    return tuple(run_outer(info, whole, low, high, results[4:], results[:4]))


def solution(mesh):
    in_specs = (
        P(("groups", "tiles"), "sub"),
        P(None, ("groups", "tiles"), "sub"),
        P(None, ("groups", "tiles"), "sub"),
        P(("groups", "tiles"), "sub"),
        P(("groups", "tiles"), "sub"),
        P("groups"),
    )
    out_specs = (
        P(("groups", "tiles"), "sub"),
        P(None, ("groups", "tiles"), "sub"),
        P(None, ("groups", "tiles"), "sub"),
        P(("groups", "tiles"), "sub"),
    )
    return jax.shard_map(body, mesh=mesh, in_specs=in_specs, out_specs=out_specs, check_vma=False)
```

```python
import functools

import jax
import jax.numpy as jnp
from jax import lax
from jax.experimental import pallas as pl
from jax.experimental.pallas import tpu as pltpu
from jax.sharding import PartitionSpec as P

TILE = 16
STEPS = 2
RELAX_TIME = 0.8
SURFACE = 0.1
SEPARATION = 0.7

LANES = 128
SUBLANES = 8
FULL = 3
HALO = FULL + 1
FIELDS = 11
PLANES = FIELDS + 1
MOVED = 19
REDS = 5
RIM = 4
SLAB = HALO + 2 * RIM
END_ROWS = (1 + FULL * PLANES) * SUBLANES
OWN_TILES = SUBLANES - 2
COLOUR_BLOCK = (8, 1)
COLLIDE_BLOCK = (4, 2)
ARRIVE_BLOCK = (4, 2)
VMEM = pl.BlockSpec(memory_space=pltpu.VMEM)
SMEM = pl.BlockSpec(memory_space=pltpu.SMEM)
ANY = pl.BlockSpec(memory_space=pl.ANY)
HBM = pl.BlockSpec(memory_space=pltpu.HBM)


def roll_lanes(values, amount):
    return pltpu.roll(values, amount % LANES, 2)


class Geometry:
    def __init__(self, info, own_tiles):
        live, first, last, sub_index = info[0], info[1], info[2], info[3]
        self.live = live
        self.low_row = jnp.where(first == 1, 0, -1000)
        self.high_row = jnp.where(last == 1, live, 1000)
        shape = (1, SUBLANES, LANES)
        lane = lax.broadcasted_iota(jnp.int32, shape, 2)
        tile = lax.broadcasted_iota(jnp.int32, shape, 1)
        depth = lane & (TILE - 1)
        self.z_low = depth == 0
        self.z_high = depth == TILE - 1
        low_part = sub_index == 0
        high_part = sub_index == 1
        self.y_low = (tile == 1) & (lane < TILE) & low_part
        self.y_high = (tile == own_tiles) & (lane >= LANES - TILE) & high_part
        own = (tile >= 1) & (tile <= own_tiles)
        self.domain = own | ((tile == own_tiles + 1) & low_part) | ((tile == 0) & high_part)
        self.first_lanes = lane < TILE
        self.last_lanes = lane >= LANES - TILE

    def from_low_y(self, values, depth_shift=0):
        crossed = jnp.where(self.last_lanes, pltpu.roll(values, 1, 1), values)
        return roll_lanes(crossed, TILE + depth_shift)

    def from_high_y(self, values, depth_shift=0):
        crossed = jnp.where(self.first_lanes, pltpu.roll(values, SUBLANES - 1, 1), values)
        return roll_lanes(crossed, -TILE + depth_shift)

    def from_low_z(self, values):
        return jnp.where(self.z_low, 0.0, roll_lanes(values, 1))

    def from_high_z(self, values):
        return jnp.where(self.z_high, 0.0, roll_lanes(values, -1))


def flat_rows(row, count):
    start = row * SUBLANES
    if not isinstance(start, int):
        start = pl.multiple_of(start, SUBLANES)
    return pl.ds(start, count * SUBLANES)


class Block:
    def __init__(self, geometry, spans, inner=False):
        self.spans = spans
        rows = [row + extra for row, local, count in spans for extra in range(count)]
        if inner:
            self.x_low = self.x_high = None
            self.valid = geometry.domain
            self.kinds = [0]
            return
        shape = (1, SUBLANES, LANES)
        ids = jnp.concatenate([row + jnp.zeros(shape, jnp.int32) for row in rows], axis=0)
        self.x_low = ids == geometry.low_row
        self.x_high = ids == geometry.high_row - 1
        self.valid = geometry.domain & (ids >= geometry.low_row) & (ids < geometry.high_row)
        self.kinds = [
            jnp.where(row == geometry.low_row, 1, 0) + jnp.where(row == geometry.high_row - 1, 2, 0)
            for row in rows
        ]

    def load(self, ref, index, offset=0):
        parts = [
            ref[index, flat_rows(local + offset, count), :].reshape(count, SUBLANES, LANES)
            for row, local, count in self.spans
        ]
        return parts[0] if len(parts) == 1 else jnp.concatenate(parts, axis=0)

    def store(self, ref, index, values):
        done = 0
        for row, local, count in self.spans:
            part = values[done : done + count].reshape(count * SUBLANES, LANES)
            ref[index, flat_rows(local, count), :] = part
            done += count

    def walls(self, walls, position):
        parts = [walls[position, flat_rows(kind, 1), :][None] for kind in self.kinds]
        return jnp.concatenate(parts, axis=0)


def fill_wall_table(walls, geometry):
    one = jnp.ones((1, SUBLANES, LANES), jnp.float32)
    up_y = jnp.where(geometry.y_high, 0.0, one)
    down_y = jnp.where(geometry.y_low, 0.0, one)
    up_z = jnp.where(geometry.z_high, 0.0, one)
    down_z = jnp.where(geometry.z_low, 0.0, one)
    sum_y, sum_z = up_y + down_y, up_z + down_z
    for kind, (up_x, down_x) in enumerate(((1.0, 1.0), (1.0, 0.0), (0.0, 1.0))):
        sum_x = up_x + down_x
        around_x = 2.0 + sum_y + sum_z
        total = 12.0 + 2.0 * (sum_x + sum_y + sum_z) + sum_x * (sum_y + sum_z) + sum_y * sum_z
        rows = (
            (up_x - down_x) * around_x,
            (up_y - down_y) * (2.0 + sum_x + sum_z),
            (up_z - down_z) * (2.0 + sum_x + sum_y),
            36.0 - total,
        )
        for position, row in enumerate(rows):
            walls[position, flat_rows(kind, 1), :] = row[0]


def colour_stage(block, geometry, fields, colours):
    density = block.load(fields, 0)
    red = block.load(fields, 10)
    colour = jnp.where(block.valid, 2.0 * red - density, 0.0)
    along_y = geometry.from_low_y(colour) + geometry.from_high_y(colour)
    along_z = geometry.from_low_z(colour) + geometry.from_high_z(colour)
    block.store(colours, 0, colour)
    block.store(colours, 1, 2.0 * colour + (along_y + along_z))
    block.store(colours, 2, along_y)
    block.store(colours, 3, along_z)


def collide_stage(block, geometry, fields, solids, colours, walls, moved, reds):
    relaxing = 1.0 - 1.0 / RELAX_TIME
    third = 1.0 / 3.0
    colour = block.load(colours, 0)
    doubled = 2.0 * colour + (block.load(colours, 0, -1) + block.load(colours, 0, 1))
    term_y = doubled + block.load(colours, 3)
    term_z = doubled + block.load(colours, 2)
    grad_x = block.load(colours, 1, 1) - block.load(colours, 1, -1)
    grad_y = geometry.from_high_y(term_y) - geometry.from_low_y(term_y)
    grad_z = geometry.from_high_z(term_z) - geometry.from_low_z(term_z)
    grad_x = (grad_x - block.walls(walls, 0) * colour) * (1.0 / 12.0)
    grad_y = (grad_y - block.walls(walls, 1) * colour) * (1.0 / 12.0)
    grad_z = (grad_z - block.walls(walls, 2) * colour) * (1.0 / 12.0)

    fluid = block.load(solids, PLANES - 1) == 0.0
    density = block.load(fields, 0)
    red = block.load(fields, 10)
    flux = [block.load(fields, 1 + axis) for axis in range(3)]
    stress = [block.load(fields, 4 + part) for part in range(6)]
    square_xx, square_yy, square_zz = grad_x * grad_x, grad_y * grad_y, grad_z * grad_z
    square = square_xx + square_yy + square_zz
    inverse = jnp.where(fluid, lax.rsqrt(1.0 + square), 0.0)
    strength = SURFACE * inverse
    keep = jnp.where(fluid, relaxing, 1.0)
    sign = jnp.where(fluid, 1.0, -1.0)
    trace = third * square
    surface = (
        square_xx - trace,
        square_yy - trace,
        square_zz - trace,
        grad_x * grad_y,
        grad_x * grad_z,
        grad_y * grad_z,
    )
    pairs = ((0, 0), (1, 1), (2, 2), (0, 1), (0, 2), (1, 2))
    second = [
        flux[a] * flux[b] + (keep * before + strength * addend)
        for (a, b), before, addend in zip(pairs, stress, surface)
    ]
    flux = [sign * part for part in flux]
    mixing = (SEPARATION * red) * (density - red) * inverse
    charge = [0.5 * part + mixing * grad for part, grad in zip(flux, (grad_x, grad_y, grad_z))]

    base = (density - 1.5 * (second[0] + second[1] + second[2])) * (1.0 / 36.0)
    run = [part * (1.0 / 12.0) for part in flux]
    own = [part * 0.125 for part in second[:3]]
    cross = [part * 0.25 for part in second[3:]]
    block.store(moved, 0, 12.0 * base)
    straight = [base + part for part in own]
    for axis in range(3):
        middle = 2.0 * straight[axis]
        swing = 2.0 * run[axis]
        block.store(moved, 1 + 2 * axis, middle + swing)
        block.store(moved, 2 + 2 * axis, middle - swing)
    for plane, (a, b) in enumerate(((0, 1), (0, 2), (1, 2))):
        middle = straight[a] + own[b]
        same, other = middle + cross[plane], middle - cross[plane]
        along, against = run[a] + run[b], run[a] - run[b]
        first = 7 + 4 * plane
        block.store(moved, first, same + along)
        block.store(moved, first + 1, same - along)
        block.store(moved, first + 2, other + against)
        block.store(moved, first + 3, other - against)

    scale = jnp.where(block.valid, 1.0 / 12.0, 0.0)
    red_base = red * (scale * third)
    red_run = [part * scale for part in charge]
    block.store(reds, 0, red_base)
    block.store(reds, 1, red_base + red_run[0])
    block.store(reds, 2, red_base - red_run[0])
    block.store(reds, 3, red_run[1])
    block.store(reds, 4, red_run[2])


def arrive_stage(block, geometry, walls, moved, reds, fields):
    third = 1.0 / 3.0
    own = [None] * MOVED

    def here(direction):
        if own[direction] is None:
            own[direction] = block.load(moved, direction)
        return own[direction]

    def arrived(direction, opposite, velocity):
        vel_x, vel_y, vel_z = velocity
        values = here(direction) if vel_x == 0 else block.load(moved, direction, -vel_x)
        if vel_y == 1:
            values = geometry.from_low_y(values, vel_z)
        elif vel_y == -1:
            values = geometry.from_high_y(values, vel_z)
        elif vel_z != 0:
            values = roll_lanes(values, vel_z)
        masks = []
        if vel_x != 0 and block.x_low is not None:
            masks.append(block.x_low if vel_x == 1 else block.x_high)
        if vel_y != 0:
            masks.append(geometry.y_low if vel_y == 1 else geometry.y_high)
        if vel_z != 0:
            masks.append(geometry.z_low if vel_z == 1 else geometry.z_high)
        if not masks:
            return values
        wall = functools.reduce(lambda one, two: one | two, masks)
        return jnp.where(wall, here(opposite), values)

    rest = here(0)
    sums, diffs = [], []
    for axis in range(3):
        velocity = [0, 0, 0]
        velocity[axis] = 1
        up = arrived(1 + 2 * axis, 2 + 2 * axis, velocity)
        velocity[axis] = -1
        down = arrived(2 + 2 * axis, 1 + 2 * axis, velocity)
        sums.append(up + down)
        diffs.append(up - down)
    total = rest + sums[0] + sums[1] + sums[2]
    cross = []
    for plane, (a, b) in enumerate(((0, 1), (0, 2), (1, 2))):
        first = 7 + 4 * plane
        parts = []
        for offset, (vel_a, vel_b) in enumerate(((1, 1), (-1, -1), (1, -1), (-1, 1))):
            velocity = [0, 0, 0]
            velocity[a], velocity[b] = vel_a, vel_b
            parts.append(arrived(first + offset, first + (offset ^ 1), velocity))
        same, other = parts[0] + parts[1], parts[2] + parts[3]
        along, against = parts[0] - parts[1], parts[2] - parts[3]
        both = same + other
        cross.append(same - other)
        total = total + both
        sums[a], sums[b] = sums[a] + both, sums[b] + both
        diffs[a], diffs[b] = diffs[a] + (along + against), diffs[b] + (along - against)
    shared = third * total
    block.store(fields, 0, total)
    for axis in range(3):
        block.store(fields, 1 + axis, diffs[axis])
        block.store(fields, 4 + axis, sums[axis] - shared - diffs[axis] * diffs[axis])
    for plane, (a, b) in enumerate(((0, 1), (0, 2), (1, 2))):
        block.store(fields, 7 + plane, cross[plane] - diffs[a] * diffs[b])

    red = block.load(reds, 0)
    red_x_up = block.load(reds, 1)
    red_y = block.load(reds, 3)
    red_z = block.load(reds, 4)
    from_x = block.load(reds, 1, -1) + block.load(reds, 2, 1)
    spread = 2.0 * red + from_x
    spread_y = 2.0 * red_y + (block.load(reds, 3, -1) + block.load(reds, 3, 1))
    spread_z = 2.0 * red_z + (block.load(reds, 4, -1) + block.load(reds, 4, 1))
    up_y, down_y = red + red_y, red - red_y
    low_y = (
        (spread + spread_y)
        + geometry.from_low_z(up_y + red_z)
        + geometry.from_high_z(up_y - red_z)
    )
    high_y = (
        (spread - spread_y)
        + geometry.from_low_z(down_y + red_z)
        + geometry.from_high_z(down_y - red_z)
    )
    bounced = (
        block.walls(walls, 3) * red
        - block.walls(walls, 0) * (red_x_up - red)
        - block.walls(walls, 1) * red_y
        - block.walls(walls, 2) * red_z
    )
    red_total = (
        12.0 * red
        + 2.0 * from_x
        + geometry.from_low_z(spread + spread_z)
        + geometry.from_high_z(spread - spread_z)
        + geometry.from_low_y(low_y)
        + geometry.from_high_y(high_y)
        + bounced
    )
    block.store(fields, 10, red_total)


def over_rows(geometry, first, end, size, blocks, stage):
    trip = size * blocks

    def step(index, carry):
        start = jnp.minimum(first + index * trip, end - trip)
        for number in range(blocks):
            row = start + number * size
            stage(Block(geometry, [(row, row, size)], inner=True))
        return carry

    lax.fori_loop(0, (end - first + trip - 1) // trip, step, 0)


def load_kernel(
    tiles_count, density, momentum, stress, red, solid, widths,
    info, spread, packet, mine,
    raw, raw_solid, held_widths, sems,
):
    row_count, flat_count = raw_solid.shape
    own_tiles = flat_count // LANES
    copies = [
        pltpu.make_async_copy(widths, held_widths, sems.at[0]),
        pltpu.make_async_copy(density, raw.at[0], sems.at[1]),
        pltpu.make_async_copy(momentum, raw.at[pl.ds(1, 3)], sems.at[2]),
        pltpu.make_async_copy(stress, raw.at[pl.ds(4, 6)], sems.at[3]),
        pltpu.make_async_copy(red, raw.at[10], sems.at[4]),
        pltpu.make_async_copy(solid, raw_solid, sems.at[5]),
    ]
    for copy in copies:
        copy.start()
    tiles_index, sub_index = lax.axis_index("tiles"), lax.axis_index("sub")
    low_part = sub_index == 0
    edge_start = pl.multiple_of(jnp.where(low_part, (own_tiles - 1) * LANES, 0), LANES)

    copies[0].wait()
    live = held_widths[tiles_index] * TILE
    info[0] = live
    info[1] = (tiles_index == 0).astype(jnp.int32)
    info[2] = (tiles_index == tiles_count - 1).astype(jnp.int32)
    info[3] = sub_index

    ready = {0: copies[1], 1: copies[2], 4: copies[3], 10: copies[4], 11: copies[5]}
    for index in range(PLANES):
        if index in ready:
            ready[index].wait()
        source = raw_solid if index == FIELDS else raw.at[index]
        for row in range(0, row_count, SUBLANES):
            rows = pl.ds(row, SUBLANES)
            for tile in range(own_tiles):
                values = source[rows, pl.ds(tile * LANES, LANES)].astype(jnp.float32)
                start = row * SUBLANES + 1 + tile
                spread[index, pl.ds(start, SUBLANES, stride=SUBLANES), :] = values
            values = source[rows, pl.ds(edge_start, LANES)].astype(jnp.float32)
            packet[pl.ds(index * row_count + row, SUBLANES), :] = values

    after = PLANES * row_count
    ends = (
        (packet, after, jnp.where(low_part, 0, live - FULL), jnp.where(low_part, FULL, live - HALO)),
        (mine, 0, jnp.where(low_part, live - FULL, 0), jnp.where(low_part, live - HALO, FULL)),
    )
    for target, at, full_row, colour_row in ends:
        rows = flat_rows(colour_row, 1)
        target[pl.ds(at, SUBLANES), :] = 2.0 * spread[10, rows, :] - spread[0, rows, :]
        for index in range(PLANES):
            place = pl.ds(at + (1 + FULL * index) * SUBLANES, FULL * SUBLANES)
            target[place, :] = spread[index, flat_rows(full_row, FULL), :]


def load_inputs(arrays, widths, tiles_count):
    row_count, flat_count = arrays[0].shape
    packet_rows = PLANES * row_count + END_ROWS
    return pl.pallas_call(
        functools.partial(load_kernel, tiles_count),
        out_shape=[
            jax.ShapeDtypeStruct((4,), jnp.int32),
            jax.ShapeDtypeStruct((PLANES, row_count * SUBLANES, LANES), jnp.float32),
            jax.ShapeDtypeStruct((packet_rows, LANES), jnp.float32),
            jax.ShapeDtypeStruct((END_ROWS, LANES), jnp.float32),
        ],
        in_specs=[HBM] * 6,
        out_specs=[SMEM, VMEM, VMEM, VMEM],
        scratch_shapes=[
            pltpu.VMEM((FIELDS, row_count, flat_count), jnp.float32),
            pltpu.VMEM((row_count, flat_count), jnp.int32),
            pltpu.SMEM(widths.shape, jnp.int32),
            pltpu.SemaphoreType.DMA((6,)),
        ],
        compiler_params=pltpu.CompilerParams(vmem_limit_bytes=16 * 1024 * 1024),
        name="load",
    )(*arrays, widths)


def join_kernel(info, spread, packet, mine, whole, ends):
    low_part = info[3] == 0
    row_count = spread.shape[1] // SUBLANES
    ends[pl.ds(0, END_ROWS), :] = mine[...]
    ends[pl.ds(END_ROWS, END_ROWS), :] = packet[pl.ds(PLANES * row_count, END_ROWS), :]
    for index in range(PLANES):
        whole[index] = spread[index]
        for row in range(0, row_count, SUBLANES):
            values = packet[pl.ds(index * row_count + row, SUBLANES), :]
            start = row * SUBLANES
            below = jnp.where(low_part, 0.0, values)
            above = jnp.where(low_part, values, 0.0)
            whole[index, pl.ds(start, SUBLANES, stride=SUBLANES), :] = below
            whole[index, pl.ds(start + SUBLANES - 1, SUBLANES, stride=SUBLANES), :] = above


def join_parts(info, spread, packet, mine):
    return pl.pallas_call(
        join_kernel,
        out_shape=[
            jax.ShapeDtypeStruct(spread.shape, jnp.float32),
            jax.ShapeDtypeStruct((2 * END_ROWS, LANES), jnp.float32),
        ],
        in_specs=[SMEM, VMEM, VMEM, VMEM],
        out_specs=[VMEM] * 2,
        compiler_params=pltpu.CompilerParams(vmem_limit_bytes=16 * 1024 * 1024),
        name="join",
    )(info, spread, packet, mine)


def keep_rows(target, target_index, source, index, rows, size):
    for place, row in enumerate(rows):
        target[target_index, flat_rows(place * size, size), :] = source[
            index, flat_rows(row, size), :
        ]


def inner_step(geometry, before, whole, first, scratch, after):
    colours, walls, moved, reds = scratch
    end = geometry.live - first
    over_rows(geometry, first, end, *COLOUR_BLOCK, lambda block: colour_stage(
        block, geometry, before, colours))
    over_rows(geometry, first + 1, end - 1, *COLLIDE_BLOCK, lambda block: collide_stage(
        block, geometry, before, whole, colours, walls, moved, reds))
    over_rows(geometry, first + 2, end - 2, *ARRIVE_BLOCK, lambda block: arrive_stage(
        block, geometry, walls, moved, reds, after))


def keep_moved(target, moved, reds, rows):
    for index in range(MOVED):
        keep_rows(target, index, moved, index, rows, 2)
    for index in range(REDS):
        keep_rows(target, MOVED + index, reds, index, rows, 2)


def first_kernel(info, whole, fields, moved_rim, fields_rim, *scratch):
    geometry = Geometry(info, OWN_TILES)
    live = geometry.live
    fill_wall_table(scratch[1], geometry)
    inner_step(geometry, whole, whole, 0, scratch, fields)
    keep_moved(moved_rim, scratch[2], scratch[3], (1, live - 3))
    for index in range(FIELDS):
        keep_rows(fields_rim, index, fields, index, (2, live - 4), 2)


def second_kernel(
    info, whole, fields, arrived, density_out, momentum_out, stress_out, red_out,
    moved_rim, final_rim, final, *scratch,
):
    row_count, flat_count = density_out.shape
    geometry = Geometry(info, OWN_TILES)
    live = geometry.live
    fill_wall_table(scratch[1], geometry)
    inner_step(geometry, fields, whole, 2, scratch, final)
    keep_moved(moved_rim, scratch[2], scratch[3], (3, live - 5))
    for index in range(FIELDS):
        keep_rows(final_rim, index, final, index, (RIM, live - 2 * RIM), RIM)

    targets = [density_out] + [momentum_out.at[axis] for axis in range(3)]
    targets = targets + [stress_out.at[part] for part in range(6)] + [red_out]
    for index, target in enumerate(targets):
        for row in range(0, row_count, SUBLANES):
            alive = row < live
            for tile in range(OWN_TILES):
                start = row * SUBLANES + 1 + tile
                values = final[index, pl.ds(start, SUBLANES, stride=SUBLANES), :]
                target[pl.ds(row, SUBLANES), pl.ds(tile * LANES, LANES)] = jnp.where(
                    alive, values, 0.0
                )


def inner_scratch(flat):
    return [
        pltpu.VMEM((4, flat, LANES), jnp.float32),
        pltpu.VMEM((4, 3 * SUBLANES, LANES), jnp.float32),
        pltpu.VMEM((MOVED, flat, LANES), jnp.float32),
        pltpu.VMEM((REDS, flat, LANES), jnp.float32),
    ]


def rim_shape(count, rows):
    return jax.ShapeDtypeStruct((count, rows * SUBLANES, LANES), jnp.float32)


def run_first(info, whole):
    flat = whole.shape[1]
    shapes = [
        jax.ShapeDtypeStruct((FIELDS, flat, LANES), jnp.float32),
        rim_shape(MOVED + REDS, 4),
        rim_shape(FIELDS, 4),
    ]
    return pl.pallas_call(
        first_kernel,
        out_shape=shapes,
        in_specs=[SMEM, VMEM],
        out_specs=[VMEM] * len(shapes),
        scratch_shapes=inner_scratch(flat),
        compiler_params=pltpu.CompilerParams(vmem_limit_bytes=24 * 1024 * 1024),
        cost_estimate=pl.CostEstimate(flops=20_000_000, bytes_accessed=8_000_000, transcendentals=0),
        name="first",
    )(info, whole)


def run_second(info, whole, fields, arrived, arrays):
    flat = whole.shape[1]
    shapes = [jax.ShapeDtypeStruct(array.shape, jnp.float32) for array in arrays[:4]]
    shapes = shapes + [rim_shape(MOVED + REDS, 4), rim_shape(FIELDS, 2 * RIM)]
    return pl.pallas_call(
        second_kernel,
        out_shape=shapes,
        in_specs=[SMEM, VMEM, VMEM, ANY],
        out_specs=[VMEM] * len(shapes),
        scratch_shapes=[pltpu.VMEM((FIELDS, flat, LANES), jnp.float32)] + inner_scratch(flat),
        compiler_params=pltpu.CompilerParams(vmem_limit_bytes=24 * 1024 * 1024),
        cost_estimate=pl.CostEstimate(flops=20_000_000, bytes_accessed=8_000_000, transcendentals=0),
        name="second",
    )(info, whole, fields, arrived)


def turn_kernel(info, ends, kept, own, passing):
    low_part = info[3] == 0
    count = END_ROWS // SUBLANES
    first = ends[pl.ds(0, END_ROWS), :].reshape(count, SUBLANES, LANES)
    second = ends[pl.ds(END_ROWS, END_ROWS), :].reshape(count, SUBLANES, LANES)
    tile = lax.broadcasted_iota(jnp.int32, (1, SUBLANES, LANES), 1)
    middle = (tile >= 1) & (tile <= OWN_TILES)

    def widened(part, other, low):
        above = jnp.where(tile == 0, 0.0, pltpu.roll(other, OWN_TILES, 1))
        below = jnp.where(tile == 0, pltpu.roll(other, SUBLANES - OWN_TILES, 1), 0.0)
        full = jnp.where(middle, part, jnp.where(low, above, below))
        return full.reshape(END_ROWS, LANES)

    own[...] = widened(first, second, low_part)
    passing[...] = widened(second, first, jnp.logical_not(low_part))


def turn_ends(info, ends, kept):
    shape = jax.ShapeDtypeStruct((END_ROWS, LANES), jnp.float32)
    return pl.pallas_call(
        turn_kernel,
        out_shape=[shape, shape],
        in_specs=[SMEM, VMEM, ANY],
        out_specs=[VMEM] * 2,
        compiler_params=pltpu.CompilerParams(vmem_limit_bytes=8 * 1024 * 1024),
        name="turn",
    )(info, ends, kept)


def outer_kernel(
    info, whole, arrived, passed, moved_rim, fields_rim, moved_later_rim, final_rim, *refs,
):
    outs = refs[4:8]
    start_fields, colours, walls, moved, reds, fields, moved_later, reds_later, final = refs[8:17]
    pieces, sems = refs[17:]
    geometry = Geometry(info, OWN_TILES)
    live = geometry.live
    low_part = info[3] == 0
    fill_wall_table(walls, geometry)

    def received(place, count):
        rows = pl.ds(place, count * SUBLANES)
        straight, crossed = arrived[rows, :], passed[rows, :]
        return jnp.where(low_part, straight, crossed), jnp.where(low_part, crossed, straight)

    def spans(first, count):
        mirrored = SLAB - first - count
        return [
            (first - HALO, first, count),
            (live - 2 * RIM + mirrored, SLAB + mirrored, count),
        ]

    for index in range(PLANES):
        low, high = received((1 + FULL * index) * SUBLANES, FULL)
        start_fields[index, flat_rows(1, FULL), :] = low
        start_fields[index, flat_rows(2 * SLAB - HALO, FULL), :] = high
        start_fields[index, flat_rows(HALO, 2), :] = whole[index, flat_rows(0, 2), :]
        start_fields[index, flat_rows(2 * SLAB - HALO - 2, 2), :] = whole[
            index, flat_rows(live - 2, 2), :
        ]
    for row, colour in zip((0, 2 * SLAB - 1), received(0, 1)):
        start_fields[0, flat_rows(row, 1), :] = jnp.zeros((SUBLANES, LANES), jnp.float32)
        start_fields[10, flat_rows(row, 1), :] = 0.5 * colour

    def place(target, index, source, at, first, size):
        for place, (row, local, count) in enumerate(spans(first, size)):
            target[index, flat_rows(local, size), :] = source[at, flat_rows(place * size, size), :]

    for index in range(MOVED + REDS):
        target, later, at = moved, moved_later, index
        if index >= MOVED:
            target, later, at = reds, reds_later, index - MOVED
        place(target, at, moved_rim, index, HALO + 1, 2)
        place(later, at, moved_later_rim, index, HALO + 3, 2)
    for index in range(FIELDS):
        place(fields, index, fields_rim, index, HALO + 2, 2)
        place(final, index, final_rim, index, HALO + RIM, RIM)

    block = lambda first, count: Block(geometry, spans(first, count))
    colour_stage(block(0, 6), geometry, start_fields, colours)
    collide_stage(block(1, 4), geometry, start_fields, start_fields, colours, walls, moved, reds)
    arrive_stage(block(2, 4), geometry, walls, moved, reds, fields)
    start_fields[PLANES - 1, flat_rows(HALO + 2, 1), :] = whole[PLANES - 1, flat_rows(2, 1), :]
    start_fields[PLANES - 1, flat_rows(2 * SLAB - HALO - 3, 1), :] = whole[
        PLANES - 1, flat_rows(live - 3, 1), :
    ]
    colour_stage(block(2, 6), geometry, fields, colours)
    collide_stage(
        block(3, 4), geometry, fields, start_fields, colours, walls, moved_later, reds_later
    )
    arrive_stage(block(4, 4), geometry, walls, moved_later, reds_later, final)

    for index in range(FIELDS):
        for side, row in ((0, HALO), (1, SLAB)):
            for tile in range(OWN_TILES):
                start = row * SUBLANES + 1 + tile
                pieces[index, pl.ds(side * SUBLANES, SUBLANES), pl.ds(tile * LANES, LANES)] = final[
                    index, pl.ds(start, SUBLANES, stride=SUBLANES), :
                ]
    copies = []
    for side, row in ((0, 0), (1, pl.multiple_of(live - SUBLANES, SUBLANES))):
        rows = pl.ds(row, SUBLANES)
        held = pl.ds(side * SUBLANES, SUBLANES)
        for number, (out, source) in enumerate(
            (
                (outs[0].at[rows], pieces.at[0, held]),
                (outs[1].at[:, rows], pieces.at[pl.ds(1, 3), held]),
                (outs[2].at[:, rows], pieces.at[pl.ds(4, 6), held]),
                (outs[3].at[rows], pieces.at[10, held]),
            )
        ):
            copies.append(pltpu.make_async_copy(source, out, sems.at[side, number]))
    for copy in copies:
        copy.start()
    for copy in copies:
        copy.wait()


def run_outer(info, whole, arrived, passed, rims, outs):
    flat = 2 * SLAB * SUBLANES
    flat_count = outs[0].shape[1]
    return pl.pallas_call(
        outer_kernel,
        out_shape=[jax.ShapeDtypeStruct(out.shape, jnp.float32) for out in outs],
        in_specs=[SMEM] + [VMEM] * 7 + [ANY] * 4,
        out_specs=[ANY] * 4,
        scratch_shapes=[
            pltpu.VMEM((PLANES, flat, LANES), jnp.float32),
            pltpu.VMEM((4, flat, LANES), jnp.float32),
            pltpu.VMEM((4, 3 * SUBLANES, LANES), jnp.float32),
            pltpu.VMEM((MOVED, flat, LANES), jnp.float32),
            pltpu.VMEM((REDS, flat, LANES), jnp.float32),
            pltpu.VMEM((FIELDS, flat, LANES), jnp.float32),
            pltpu.VMEM((MOVED, flat, LANES), jnp.float32),
            pltpu.VMEM((REDS, flat, LANES), jnp.float32),
            pltpu.VMEM((FIELDS, flat, LANES), jnp.float32),
            pltpu.VMEM((FIELDS, 2 * SUBLANES, flat_count), jnp.float32),
            pltpu.SemaphoreType.DMA((2, 4)),
        ],
        input_output_aliases={8: 0, 9: 1, 10: 2, 11: 3},
        compiler_params=pltpu.CompilerParams(vmem_limit_bytes=32 * 1024 * 1024),
        name="outer",
    )(info, whole, arrived, passed, *rims, *outs)


def body(density, momentum, stress, red_density, solid, widths):
    tiles_count = lax.axis_size("tiles")
    arrays = (density, momentum, stress, red_density, solid)
    info, spread, packet, mine = load_inputs(arrays, widths, tiles_count)
    swap = [(0, 1), (1, 0)]
    packet = lax.ppermute(packet, "sub", swap)
    whole, ends = join_parts(info, spread, packet, mine)
    route = [(2 * k, 2 * k + 2) for k in range(tiles_count - 1)]
    route = route + [(2 * k + 3, 2 * k + 1) for k in range(tiles_count - 1)]
    arrived = lax.ppermute(ends, ("tiles", "sub"), route)
    fields, moved_rim, fields_rim = run_first(info, whole)
    arrived, passing = turn_ends(info, arrived, fields_rim)
    passed = lax.ppermute(passing, "sub", swap)
    results = run_second(info, whole, fields, arrived, arrays)
    rims = (moved_rim, fields_rim) + tuple(results[4:])
    return tuple(run_outer(info, whole, arrived, passed, rims, results[:4]))


def solution(mesh):
    in_specs = (
        P(("groups", "tiles"), "sub"),
        P(None, ("groups", "tiles"), "sub"),
        P(None, ("groups", "tiles"), "sub"),
        P(("groups", "tiles"), "sub"),
        P(("groups", "tiles"), "sub"),
        P("groups"),
    )
    out_specs = (
        P(("groups", "tiles"), "sub"),
        P(None, ("groups", "tiles"), "sub"),
        P(None, ("groups", "tiles"), "sub"),
        P(("groups", "tiles"), "sub"),
    )
    return jax.shard_map(body, mesh=mesh, in_specs=in_specs, out_specs=out_specs, check_vma=False)
```

```python
import functools

import jax
import jax.numpy as jnp
from jax import lax
from jax.experimental import pallas as pl
from jax.experimental.pallas import tpu as pltpu
from jax.sharding import PartitionSpec as P

TILE = 16
STEPS = 2
RELAX_TIME = 0.8
SURFACE = 0.1
SEPARATION = 0.7

LANES = 128
SUBLANES = 8
FULL = 3
HALO = FULL + 1
FIELDS = 11
PLANES = FIELDS + 1
MOVED = 19
REDS = 5
RIM = 4
SLAB = HALO + 2 * RIM
END_ROWS = (1 + FULL * PLANES) * SUBLANES
OWN_TILES = SUBLANES - 2
COLOUR_BLOCK = (8, 1)
COLLIDE_BLOCK = (4, 2)
ARRIVE_BLOCK = (4, 2)
VMEM = pl.BlockSpec(memory_space=pltpu.VMEM)
SMEM = pl.BlockSpec(memory_space=pltpu.SMEM)
ANY = pl.BlockSpec(memory_space=pl.ANY)
HBM = pl.BlockSpec(memory_space=pltpu.HBM)


def roll_lanes(values, amount):
    return pltpu.roll(values, amount % LANES, 2)


class Geometry:
    def __init__(self, info, own_tiles):
        live, first, last, sub_index = info[0], info[1], info[2], info[3]
        self.live = live
        self.low_row = jnp.where(first == 1, 0, -1000)
        self.high_row = jnp.where(last == 1, live, 1000)
        shape = (1, SUBLANES, LANES)
        lane = lax.broadcasted_iota(jnp.int32, shape, 2)
        tile = lax.broadcasted_iota(jnp.int32, shape, 1)
        depth = lane & (TILE - 1)
        self.z_low = depth == 0
        self.z_high = depth == TILE - 1
        low_part = sub_index == 0
        high_part = sub_index == 1
        self.y_low = (tile == 1) & (lane < TILE) & low_part
        self.y_high = (tile == own_tiles) & (lane >= LANES - TILE) & high_part
        own = (tile >= 1) & (tile <= own_tiles)
        self.domain = own | ((tile == own_tiles + 1) & low_part) | ((tile == 0) & high_part)
        self.first_lanes = lane < TILE
        self.last_lanes = lane >= LANES - TILE

    def from_low_y(self, values, depth_shift=0, below=None):
        if below is None:
            below = pltpu.roll(values, 1, 1)
        return roll_lanes(jnp.where(self.last_lanes, below, values), TILE + depth_shift)

    def from_high_y(self, values, depth_shift=0, above=None):
        if above is None:
            above = pltpu.roll(values, SUBLANES - 1, 1)
        return roll_lanes(jnp.where(self.first_lanes, above, values), -TILE + depth_shift)

    def from_low_z(self, values):
        return jnp.where(self.z_low, 0.0, roll_lanes(values, 1))

    def from_high_z(self, values):
        return jnp.where(self.z_high, 0.0, roll_lanes(values, -1))


def flat_rows(row, count, tile_offset=0):
    start = row * SUBLANES
    if not isinstance(start, int):
        start = pl.multiple_of(start, SUBLANES)
    return pl.ds(start + tile_offset, count * SUBLANES)


class Block:
    def __init__(self, geometry, spans, inner=False):
        self.spans = spans
        rows = [row + extra for row, local, count in spans for extra in range(count)]
        if inner:
            self.x_low = self.x_high = None
            self.valid = geometry.domain
            self.kinds = [0]
            return
        shape = (1, SUBLANES, LANES)
        ids = jnp.concatenate([row + jnp.zeros(shape, jnp.int32) for row in rows], axis=0)
        self.x_low = ids == geometry.low_row
        self.x_high = ids == geometry.high_row - 1
        self.valid = geometry.domain & (ids >= geometry.low_row) & (ids < geometry.high_row)
        self.kinds = [
            jnp.where(row == geometry.low_row, 1, 0) + jnp.where(row == geometry.high_row - 1, 2, 0)
            for row in rows
        ]

    def load(self, ref, index, offset=0, tile_offset=0):
        parts = [
            ref[index, flat_rows(local + offset, count, tile_offset), :].reshape(
                count, SUBLANES, LANES
            )
            for row, local, count in self.spans
        ]
        return parts[0] if len(parts) == 1 else jnp.concatenate(parts, axis=0)

    def store(self, ref, index, values):
        done = 0
        for row, local, count in self.spans:
            part = values[done : done + count].reshape(count * SUBLANES, LANES)
            ref[index, flat_rows(local, count), :] = part
            done += count

    def walls(self, walls, position):
        parts = [walls[position, flat_rows(kind, 1), :][None] for kind in self.kinds]
        return jnp.concatenate(parts, axis=0)


def fill_wall_table(walls, geometry):
    one = jnp.ones((1, SUBLANES, LANES), jnp.float32)
    up_y = jnp.where(geometry.y_high, 0.0, one)
    down_y = jnp.where(geometry.y_low, 0.0, one)
    up_z = jnp.where(geometry.z_high, 0.0, one)
    down_z = jnp.where(geometry.z_low, 0.0, one)
    sum_y, sum_z = up_y + down_y, up_z + down_z
    for kind, (up_x, down_x) in enumerate(((1.0, 1.0), (1.0, 0.0), (0.0, 1.0))):
        sum_x = up_x + down_x
        around_x = 2.0 + sum_y + sum_z
        total = 12.0 + 2.0 * (sum_x + sum_y + sum_z) + sum_x * (sum_y + sum_z) + sum_y * sum_z
        rows = (
            (up_x - down_x) * around_x,
            (up_y - down_y) * (2.0 + sum_x + sum_z),
            (up_z - down_z) * (2.0 + sum_x + sum_y),
            36.0 - total,
        )
        for position, row in enumerate(rows):
            walls[position, flat_rows(kind, 1), :] = row[0]


def colour_stage(block, geometry, fields, colours):
    density = block.load(fields, 0)
    red = block.load(fields, 10)
    colour = jnp.where(block.valid, 2.0 * red - density, 0.0)
    along_y = geometry.from_low_y(colour) + geometry.from_high_y(colour)
    along_z = geometry.from_low_z(colour) + geometry.from_high_z(colour)
    block.store(colours, 0, colour)
    block.store(colours, 1, 2.0 * colour + (along_y + along_z))
    block.store(colours, 2, along_y)
    block.store(colours, 3, along_z)


def collide_stage(block, geometry, fields, solids, colours, walls, moved, reds):
    relaxing = 1.0 - 1.0 / RELAX_TIME
    third = 1.0 / 3.0
    colour = block.load(colours, 0)
    doubled = 2.0 * colour + (block.load(colours, 0, -1) + block.load(colours, 0, 1))
    term_y = doubled + block.load(colours, 3)
    term_z = doubled + block.load(colours, 2)
    grad_x = block.load(colours, 1, 1) - block.load(colours, 1, -1)
    grad_y = geometry.from_high_y(term_y) - geometry.from_low_y(term_y)
    grad_z = geometry.from_high_z(term_z) - geometry.from_low_z(term_z)
    grad_x = (grad_x - block.walls(walls, 0) * colour) * (1.0 / 12.0)
    grad_y = (grad_y - block.walls(walls, 1) * colour) * (1.0 / 12.0)
    grad_z = (grad_z - block.walls(walls, 2) * colour) * (1.0 / 12.0)

    fluid = block.load(solids, PLANES - 1) == 0.0
    density = block.load(fields, 0)
    red = block.load(fields, 10)
    flux = [block.load(fields, 1 + axis) for axis in range(3)]
    stress = [block.load(fields, 4 + part) for part in range(6)]
    square_xx, square_yy, square_zz = grad_x * grad_x, grad_y * grad_y, grad_z * grad_z
    square = square_xx + square_yy + square_zz
    inverse = jnp.where(fluid, lax.rsqrt(1.0 + square), 0.0)
    strength = SURFACE * inverse
    keep = jnp.where(fluid, relaxing, 1.0)
    sign = jnp.where(fluid, 1.0, -1.0)
    trace = third * square
    surface = (
        square_xx - trace,
        square_yy - trace,
        square_zz - trace,
        grad_x * grad_y,
        grad_x * grad_z,
        grad_y * grad_z,
    )
    pairs = ((0, 0), (1, 1), (2, 2), (0, 1), (0, 2), (1, 2))
    second = [
        flux[a] * flux[b] + (keep * before + strength * addend)
        for (a, b), before, addend in zip(pairs, stress, surface)
    ]
    flux = [sign * part for part in flux]
    mixing = (SEPARATION * red) * (density - red) * inverse
    charge = [0.5 * part + mixing * grad for part, grad in zip(flux, (grad_x, grad_y, grad_z))]

    base = (density - 1.5 * (second[0] + second[1] + second[2])) * (1.0 / 36.0)
    run = [part * (1.0 / 12.0) for part in flux]
    own = [part * 0.125 for part in second[:3]]
    cross = [part * 0.25 for part in second[3:]]
    block.store(moved, 0, 12.0 * base)
    straight = [base + part for part in own]
    for axis in range(3):
        middle = 2.0 * straight[axis]
        swing = 2.0 * run[axis]
        block.store(moved, 1 + 2 * axis, middle + swing)
        block.store(moved, 2 + 2 * axis, middle - swing)
    for plane, (a, b) in enumerate(((0, 1), (0, 2), (1, 2))):
        middle = straight[a] + own[b]
        same, other = middle + cross[plane], middle - cross[plane]
        along, against = run[a] + run[b], run[a] - run[b]
        first = 7 + 4 * plane
        block.store(moved, first, same + along)
        block.store(moved, first + 1, same - along)
        block.store(moved, first + 2, other + against)
        block.store(moved, first + 3, other - against)

    scale = jnp.where(block.valid, 1.0 / 12.0, 0.0)
    red_base = red * (scale * third)
    red_run = [part * scale for part in charge]
    block.store(reds, 0, red_base)
    block.store(reds, 1, red_base + red_run[0])
    block.store(reds, 2, red_base - red_run[0])
    block.store(reds, 3, red_run[1])
    block.store(reds, 4, red_run[2])


def arrive_stage(block, geometry, walls, moved, reds, fields):
    third = 1.0 / 3.0
    own = [None] * MOVED

    def here(direction):
        if own[direction] is None:
            own[direction] = block.load(moved, direction)
        return own[direction]

    def arrived(direction, opposite, velocity):
        vel_x, vel_y, vel_z = velocity
        values = here(direction) if vel_x == 0 else block.load(moved, direction, -vel_x)
        if vel_y == 1:
            below = block.load(moved, direction, -vel_x, -1)
            values = geometry.from_low_y(values, vel_z, below)
        elif vel_y == -1:
            above = block.load(moved, direction, -vel_x, 1)
            values = geometry.from_high_y(values, vel_z, above)
        elif vel_z != 0:
            values = roll_lanes(values, vel_z)
        masks = []
        if vel_x != 0 and block.x_low is not None:
            masks.append(block.x_low if vel_x == 1 else block.x_high)
        if vel_y != 0:
            masks.append(geometry.y_low if vel_y == 1 else geometry.y_high)
        if vel_z != 0:
            masks.append(geometry.z_low if vel_z == 1 else geometry.z_high)
        if not masks:
            return values
        wall = functools.reduce(lambda one, two: one | two, masks)
        return jnp.where(wall, here(opposite), values)

    rest = here(0)
    sums, diffs = [], []
    for axis in range(3):
        velocity = [0, 0, 0]
        velocity[axis] = 1
        up = arrived(1 + 2 * axis, 2 + 2 * axis, velocity)
        velocity[axis] = -1
        down = arrived(2 + 2 * axis, 1 + 2 * axis, velocity)
        sums.append(up + down)
        diffs.append(up - down)
    total = rest + sums[0] + sums[1] + sums[2]
    cross = []
    for plane, (a, b) in enumerate(((0, 1), (0, 2), (1, 2))):
        first = 7 + 4 * plane
        parts = []
        for offset, (vel_a, vel_b) in enumerate(((1, 1), (-1, -1), (1, -1), (-1, 1))):
            velocity = [0, 0, 0]
            velocity[a], velocity[b] = vel_a, vel_b
            parts.append(arrived(first + offset, first + (offset ^ 1), velocity))
        same, other = parts[0] + parts[1], parts[2] + parts[3]
        along, against = parts[0] - parts[1], parts[2] - parts[3]
        both = same + other
        cross.append(same - other)
        total = total + both
        sums[a], sums[b] = sums[a] + both, sums[b] + both
        diffs[a], diffs[b] = diffs[a] + (along + against), diffs[b] + (along - against)
    shared = third * total
    block.store(fields, 0, total)
    for axis in range(3):
        block.store(fields, 1 + axis, diffs[axis])
        block.store(fields, 4 + axis, sums[axis] - shared - diffs[axis] * diffs[axis])
    for plane, (a, b) in enumerate(((0, 1), (0, 2), (1, 2))):
        block.store(fields, 7 + plane, cross[plane] - diffs[a] * diffs[b])

    red = block.load(reds, 0)
    red_x_up = block.load(reds, 1)
    red_y = block.load(reds, 3)
    red_z = block.load(reds, 4)
    from_x = block.load(reds, 1, -1) + block.load(reds, 2, 1)
    spread = 2.0 * red + from_x
    spread_y = 2.0 * red_y + (block.load(reds, 3, -1) + block.load(reds, 3, 1))
    spread_z = 2.0 * red_z + (block.load(reds, 4, -1) + block.load(reds, 4, 1))
    up_y, down_y = red + red_y, red - red_y
    low_y = (
        (spread + spread_y)
        + geometry.from_low_z(up_y + red_z)
        + geometry.from_high_z(up_y - red_z)
    )
    high_y = (
        (spread - spread_y)
        + geometry.from_low_z(down_y + red_z)
        + geometry.from_high_z(down_y - red_z)
    )
    bounced = (
        block.walls(walls, 3) * red
        - block.walls(walls, 0) * (red_x_up - red)
        - block.walls(walls, 1) * red_y
        - block.walls(walls, 2) * red_z
    )
    red_total = (
        12.0 * red
        + 2.0 * from_x
        + geometry.from_low_z(spread + spread_z)
        + geometry.from_high_z(spread - spread_z)
        + geometry.from_low_y(low_y)
        + geometry.from_high_y(high_y)
        + bounced
    )
    block.store(fields, 10, red_total)


def over_rows(geometry, first, end, size, blocks, stage):
    trip = size * blocks

    def step(index, carry):
        start = jnp.minimum(first + index * trip, end - trip)
        for number in range(blocks):
            row = start + number * size
            stage(Block(geometry, [(row, row, size)], inner=True))
        return carry

    lax.fori_loop(0, (end - first + trip - 1) // trip, step, 0)


def load_kernel(
    tiles_count, density, momentum, stress, red, solid, widths,
    info, spread, packet, mine,
    raw, raw_solid, held_widths, sems,
):
    row_count, flat_count = raw_solid.shape
    own_tiles = flat_count // LANES
    copies = [
        pltpu.make_async_copy(widths, held_widths, sems.at[0]),
        pltpu.make_async_copy(density, raw.at[0], sems.at[1]),
        pltpu.make_async_copy(momentum, raw.at[pl.ds(1, 3)], sems.at[2]),
        pltpu.make_async_copy(stress, raw.at[pl.ds(4, 6)], sems.at[3]),
        pltpu.make_async_copy(red, raw.at[10], sems.at[4]),
        pltpu.make_async_copy(solid, raw_solid, sems.at[5]),
    ]
    for copy in copies:
        copy.start()
    tiles_index, sub_index = lax.axis_index("tiles"), lax.axis_index("sub")
    low_part = sub_index == 0
    edge_start = pl.multiple_of(jnp.where(low_part, (own_tiles - 1) * LANES, 0), LANES)

    copies[0].wait()
    live = held_widths[tiles_index] * TILE
    info[0] = live
    info[1] = (tiles_index == 0).astype(jnp.int32)
    info[2] = (tiles_index == tiles_count - 1).astype(jnp.int32)
    info[3] = sub_index

    ready = {0: copies[1], 1: copies[2], 4: copies[3], 10: copies[4], 11: copies[5]}
    for index in range(PLANES):
        if index in ready:
            ready[index].wait()
        source = raw_solid if index == FIELDS else raw.at[index]
        for row in range(0, row_count, SUBLANES):
            rows = pl.ds(row, SUBLANES)
            for tile in range(own_tiles):
                values = source[rows, pl.ds(tile * LANES, LANES)].astype(jnp.float32)
                start = row * SUBLANES + 1 + tile
                spread[index, pl.ds(start, SUBLANES, stride=SUBLANES), :] = values
            values = source[rows, pl.ds(edge_start, LANES)].astype(jnp.float32)
            packet[pl.ds(index * row_count + row, SUBLANES), :] = values

    after = PLANES * row_count
    ends = (
        (packet, after, jnp.where(low_part, 0, live - FULL), jnp.where(low_part, FULL, live - HALO)),
        (mine, 0, jnp.where(low_part, live - FULL, 0), jnp.where(low_part, live - HALO, FULL)),
    )
    for target, at, full_row, colour_row in ends:
        rows = flat_rows(colour_row, 1)
        target[pl.ds(at, SUBLANES), :] = 2.0 * spread[10, rows, :] - spread[0, rows, :]
        for index in range(PLANES):
            place = pl.ds(at + (1 + FULL * index) * SUBLANES, FULL * SUBLANES)
            target[place, :] = spread[index, flat_rows(full_row, FULL), :]


def load_inputs(arrays, widths, tiles_count):
    row_count, flat_count = arrays[0].shape
    packet_rows = PLANES * row_count + END_ROWS
    return pl.pallas_call(
        functools.partial(load_kernel, tiles_count),
        out_shape=[
            jax.ShapeDtypeStruct((4,), jnp.int32),
            jax.ShapeDtypeStruct((PLANES, row_count * SUBLANES, LANES), jnp.float32),
            jax.ShapeDtypeStruct((packet_rows, LANES), jnp.float32),
            jax.ShapeDtypeStruct((END_ROWS, LANES), jnp.float32),
        ],
        in_specs=[HBM] * 6,
        out_specs=[SMEM, VMEM, VMEM, VMEM],
        scratch_shapes=[
            pltpu.VMEM((FIELDS, row_count, flat_count), jnp.float32),
            pltpu.VMEM((row_count, flat_count), jnp.int32),
            pltpu.SMEM(widths.shape, jnp.int32),
            pltpu.SemaphoreType.DMA((6,)),
        ],
        compiler_params=pltpu.CompilerParams(vmem_limit_bytes=16 * 1024 * 1024),
        name="load",
    )(*[pltpu.with_memory_space_constraint(array, pltpu.HBM) for array in (*arrays, widths)])


def join_kernel(info, spread, packet, mine, whole, ends):
    low_part = info[3] == 0
    row_count = spread.shape[1] // SUBLANES
    ends[pl.ds(0, END_ROWS), :] = mine[...]
    ends[pl.ds(END_ROWS, END_ROWS), :] = packet[pl.ds(PLANES * row_count, END_ROWS), :]
    for index in range(PLANES):
        whole[index] = spread[index]
        for row in range(0, row_count, SUBLANES):
            values = packet[pl.ds(index * row_count + row, SUBLANES), :]
            start = row * SUBLANES
            below = jnp.where(low_part, 0.0, values)
            above = jnp.where(low_part, values, 0.0)
            whole[index, pl.ds(start, SUBLANES, stride=SUBLANES), :] = below
            whole[index, pl.ds(start + SUBLANES - 1, SUBLANES, stride=SUBLANES), :] = above


def join_parts(info, spread, packet, mine):
    return pl.pallas_call(
        join_kernel,
        out_shape=[
            jax.ShapeDtypeStruct(spread.shape, jnp.float32),
            jax.ShapeDtypeStruct((2 * END_ROWS, LANES), jnp.float32),
        ],
        in_specs=[SMEM, VMEM, VMEM, VMEM],
        out_specs=[VMEM] * 2,
        compiler_params=pltpu.CompilerParams(vmem_limit_bytes=16 * 1024 * 1024),
        name="join",
    )(info, spread, packet, mine)


def keep_rows(target, target_index, source, index, rows, size):
    for place, row in enumerate(rows):
        target[target_index, flat_rows(place * size, size), :] = source[
            index, flat_rows(row, size), :
        ]


def collide_rows(geometry, before, whole, first, scratch, moved, reds):
    colours, walls = scratch
    end = geometry.live - first
    over_rows(geometry, first - 1, end + 1, *COLOUR_BLOCK, lambda block: colour_stage(
        block, geometry, before, colours))
    over_rows(geometry, first, end, *COLLIDE_BLOCK, lambda block: collide_stage(
        block, geometry, before, whole, colours, walls, moved, reds))


def arrive_rows(geometry, first, walls, moved, reds, after):
    over_rows(geometry, first, geometry.live - first, *ARRIVE_BLOCK, lambda block: arrive_stage(
        block, geometry, walls, moved, reds, after))


def keep_moved(target, moved, reds, rows):
    for index in range(MOVED):
        keep_rows(target, index, moved, index, rows, 2)
    for index in range(REDS):
        keep_rows(target, MOVED + index, reds, index, rows, 2)


def first_kernel(info, whole, moved_later, reds_later, moved_rim, fields_rim, *scratch):
    colours, walls, moved, reds, fields = scratch
    geometry = Geometry(info, OWN_TILES)
    live = geometry.live
    fill_wall_table(walls, geometry)
    collide_rows(geometry, whole, whole, 1, (colours, walls), moved, reds)
    arrive_rows(geometry, 2, walls, moved, reds, fields)
    keep_moved(moved_rim, moved, reds, (1, live - 3))
    for index in range(FIELDS):
        keep_rows(fields_rim, index, fields, index, (2, live - 4), 2)
    collide_rows(geometry, fields, whole, 3, (colours, walls), moved_later, reds_later)


def second_kernel(
    info, moved, reds, arrived, density_out, momentum_out, stress_out, red_out,
    moved_rim, final_rim, final, walls,
):
    row_count, flat_count = density_out.shape
    geometry = Geometry(info, OWN_TILES)
    live = geometry.live
    fill_wall_table(walls, geometry)
    arrive_rows(geometry, 4, walls, moved, reds, final)
    keep_moved(moved_rim, moved, reds, (3, live - 5))
    for index in range(FIELDS):
        keep_rows(final_rim, index, final, index, (RIM, live - 2 * RIM), RIM)

    targets = [density_out] + [momentum_out.at[axis] for axis in range(3)]
    targets = targets + [stress_out.at[part] for part in range(6)] + [red_out]
    for index, target in enumerate(targets):
        for row in range(0, row_count, SUBLANES):
            alive = row < live
            for tile in range(OWN_TILES):
                start = row * SUBLANES + 1 + tile
                values = final[index, pl.ds(start, SUBLANES, stride=SUBLANES), :]
                target[pl.ds(row, SUBLANES), pl.ds(tile * LANES, LANES)] = jnp.where(
                    alive, values, 0.0
                )


def rim_shape(count, rows):
    return jax.ShapeDtypeStruct((count, rows * SUBLANES, LANES), jnp.float32)


def run_first(info, whole):
    flat = whole.shape[1]
    shapes = [
        jax.ShapeDtypeStruct((MOVED, flat, LANES), jnp.float32),
        jax.ShapeDtypeStruct((REDS, flat, LANES), jnp.float32),
        rim_shape(MOVED + REDS, 4),
        rim_shape(FIELDS, 4),
    ]
    return pl.pallas_call(
        first_kernel,
        out_shape=shapes,
        in_specs=[SMEM, VMEM],
        out_specs=[VMEM] * len(shapes),
        scratch_shapes=[
            pltpu.VMEM((4, flat, LANES), jnp.float32),
            pltpu.VMEM((4, 3 * SUBLANES, LANES), jnp.float32),
            pltpu.VMEM((MOVED, flat, LANES), jnp.float32),
            pltpu.VMEM((REDS, flat, LANES), jnp.float32),
            pltpu.VMEM((FIELDS, flat, LANES), jnp.float32),
        ],
        compiler_params=pltpu.CompilerParams(vmem_limit_bytes=24 * 1024 * 1024),
        cost_estimate=pl.CostEstimate(flops=20_000_000, bytes_accessed=8_000_000, transcendentals=0),
        name="first",
    )(info, whole)


def run_second(info, moved, reds, arrived, arrays):
    flat = moved.shape[1]
    shapes = [jax.ShapeDtypeStruct(array.shape, jnp.float32) for array in arrays[:4]]
    shapes = shapes + [rim_shape(MOVED + REDS, 4), rim_shape(FIELDS, 2 * RIM)]
    return pl.pallas_call(
        second_kernel,
        out_shape=shapes,
        in_specs=[SMEM, VMEM, VMEM, ANY],
        out_specs=[VMEM] * len(shapes),
        scratch_shapes=[
            pltpu.VMEM((FIELDS, flat, LANES), jnp.float32),
            pltpu.VMEM((4, 3 * SUBLANES, LANES), jnp.float32),
        ],
        compiler_params=pltpu.CompilerParams(vmem_limit_bytes=24 * 1024 * 1024),
        cost_estimate=pl.CostEstimate(flops=20_000_000, bytes_accessed=8_000_000, transcendentals=0),
        name="second",
    )(info, moved, reds, arrived)


def turn_kernel(info, ends, kept, own, passing):
    low_part = info[3] == 0
    count = END_ROWS // SUBLANES
    first = ends[pl.ds(0, END_ROWS), :].reshape(count, SUBLANES, LANES)
    second = ends[pl.ds(END_ROWS, END_ROWS), :].reshape(count, SUBLANES, LANES)
    tile = lax.broadcasted_iota(jnp.int32, (1, SUBLANES, LANES), 1)
    middle = (tile >= 1) & (tile <= OWN_TILES)

    def widened(part, other, low):
        above = jnp.where(tile == 0, 0.0, pltpu.roll(other, OWN_TILES, 1))
        below = jnp.where(tile == 0, pltpu.roll(other, SUBLANES - OWN_TILES, 1), 0.0)
        full = jnp.where(middle, part, jnp.where(low, above, below))
        return full.reshape(END_ROWS, LANES)

    own[...] = widened(first, second, low_part)
    passing[...] = widened(second, first, jnp.logical_not(low_part))


def turn_ends(info, ends, kept):
    shape = jax.ShapeDtypeStruct((END_ROWS, LANES), jnp.float32)
    return pl.pallas_call(
        turn_kernel,
        out_shape=[shape, shape],
        in_specs=[SMEM, VMEM, ANY],
        out_specs=[VMEM] * 2,
        compiler_params=pltpu.CompilerParams(vmem_limit_bytes=8 * 1024 * 1024),
        name="turn",
    )(info, ends, kept)


def outer_kernel(
    info, whole, arrived, passed, moved_rim, fields_rim, moved_later_rim, final_rim, *refs,
):
    outs = refs[4:8]
    start_fields, colours, walls, moved, reds, fields, moved_later, reds_later, final = refs[8:17]
    pieces, sems = refs[17:]
    geometry = Geometry(info, OWN_TILES)
    live = geometry.live
    low_part = info[3] == 0
    fill_wall_table(walls, geometry)

    def received(place, count):
        rows = pl.ds(place, count * SUBLANES)
        straight, crossed = arrived[rows, :], passed[rows, :]
        return jnp.where(low_part, straight, crossed), jnp.where(low_part, crossed, straight)

    def spans(first, count):
        mirrored = SLAB - first - count
        return [
            (first - HALO, first, count),
            (live - 2 * RIM + mirrored, SLAB + mirrored, count),
        ]

    for index in range(PLANES):
        low, high = received((1 + FULL * index) * SUBLANES, FULL)
        start_fields[index, flat_rows(1, FULL), :] = low
        start_fields[index, flat_rows(2 * SLAB - HALO, FULL), :] = high
        start_fields[index, flat_rows(HALO, 2), :] = whole[index, flat_rows(0, 2), :]
        start_fields[index, flat_rows(2 * SLAB - HALO - 2, 2), :] = whole[
            index, flat_rows(live - 2, 2), :
        ]
    for row, colour in zip((0, 2 * SLAB - 1), received(0, 1)):
        start_fields[0, flat_rows(row, 1), :] = jnp.zeros((SUBLANES, LANES), jnp.float32)
        start_fields[10, flat_rows(row, 1), :] = 0.5 * colour

    def place(target, index, source, at, first, size):
        for place, (row, local, count) in enumerate(spans(first, size)):
            target[index, flat_rows(local, size), :] = source[at, flat_rows(place * size, size), :]

    for index in range(MOVED + REDS):
        target, later, at = moved, moved_later, index
        if index >= MOVED:
            target, later, at = reds, reds_later, index - MOVED
        place(target, at, moved_rim, index, HALO + 1, 2)
        place(later, at, moved_later_rim, index, HALO + 3, 2)
    for index in range(FIELDS):
        place(fields, index, fields_rim, index, HALO + 2, 2)
        place(final, index, final_rim, index, HALO + RIM, RIM)

    block = lambda first, count: Block(geometry, spans(first, count))
    colour_stage(block(0, 6), geometry, start_fields, colours)
    collide_stage(block(1, 4), geometry, start_fields, start_fields, colours, walls, moved, reds)
    arrive_stage(block(2, 4), geometry, walls, moved, reds, fields)
    start_fields[PLANES - 1, flat_rows(HALO + 2, 1), :] = whole[PLANES - 1, flat_rows(2, 1), :]
    start_fields[PLANES - 1, flat_rows(2 * SLAB - HALO - 3, 1), :] = whole[
        PLANES - 1, flat_rows(live - 3, 1), :
    ]
    colour_stage(block(2, 6), geometry, fields, colours)
    collide_stage(
        block(3, 4), geometry, fields, start_fields, colours, walls, moved_later, reds_later
    )
    arrive_stage(block(4, 4), geometry, walls, moved_later, reds_later, final)

    for index in range(FIELDS):
        for side, row in ((0, HALO), (1, SLAB)):
            for tile in range(OWN_TILES):
                start = row * SUBLANES + 1 + tile
                pieces[index, pl.ds(side * SUBLANES, SUBLANES), pl.ds(tile * LANES, LANES)] = final[
                    index, pl.ds(start, SUBLANES, stride=SUBLANES), :
                ]
    copies = []
    for side, row in ((0, 0), (1, pl.multiple_of(live - SUBLANES, SUBLANES))):
        rows = pl.ds(row, SUBLANES)
        held = pl.ds(side * SUBLANES, SUBLANES)
        for number, (out, source) in enumerate(
            (
                (outs[0].at[rows], pieces.at[0, held]),
                (outs[1].at[:, rows], pieces.at[pl.ds(1, 3), held]),
                (outs[2].at[:, rows], pieces.at[pl.ds(4, 6), held]),
                (outs[3].at[rows], pieces.at[10, held]),
            )
        ):
            copies.append(pltpu.make_async_copy(source, out, sems.at[side, number]))
    for copy in copies:
        copy.start()
    for copy in copies:
        copy.wait()


def run_outer(info, whole, arrived, passed, rims, outs):
    flat = 2 * SLAB * SUBLANES
    flat_count = outs[0].shape[1]
    return pl.pallas_call(
        outer_kernel,
        out_shape=[jax.ShapeDtypeStruct(out.shape, jnp.float32) for out in outs],
        in_specs=[SMEM] + [VMEM] * 7 + [ANY] * 4,
        out_specs=[ANY] * 4,
        scratch_shapes=[
            pltpu.VMEM((PLANES, flat, LANES), jnp.float32),
            pltpu.VMEM((4, flat, LANES), jnp.float32),
            pltpu.VMEM((4, 3 * SUBLANES, LANES), jnp.float32),
            pltpu.VMEM((MOVED, flat, LANES), jnp.float32),
            pltpu.VMEM((REDS, flat, LANES), jnp.float32),
            pltpu.VMEM((FIELDS, flat, LANES), jnp.float32),
            pltpu.VMEM((MOVED, flat, LANES), jnp.float32),
            pltpu.VMEM((REDS, flat, LANES), jnp.float32),
            pltpu.VMEM((FIELDS, flat, LANES), jnp.float32),
            pltpu.VMEM((FIELDS, 2 * SUBLANES, flat_count), jnp.float32),
            pltpu.SemaphoreType.DMA((2, 4)),
        ],
        input_output_aliases={8: 0, 9: 1, 10: 2, 11: 3},
        compiler_params=pltpu.CompilerParams(vmem_limit_bytes=32 * 1024 * 1024),
        name="outer",
    )(info, whole, arrived, passed, *rims, *outs)


def body(density, momentum, stress, red_density, solid, widths):
    tiles_count = lax.axis_size("tiles")
    arrays = (density, momentum, stress, red_density, solid)
    info, spread, packet, mine = load_inputs(arrays, widths, tiles_count)
    swap = [(0, 1), (1, 0)]
    packet = lax.ppermute(packet, "sub", swap)
    whole, ends = join_parts(info, spread, packet, mine)
    route = [(2 * k, 2 * k + 2) for k in range(tiles_count - 1)]
    route = route + [(2 * k + 3, 2 * k + 1) for k in range(tiles_count - 1)]
    arrived = lax.ppermute(ends, ("tiles", "sub"), route)
    moved, reds, moved_rim, fields_rim = run_first(info, whole)
    arrived, passing = turn_ends(info, arrived, fields_rim)
    passed = lax.ppermute(passing, "sub", swap)
    results = run_second(info, moved, reds, arrived, arrays)
    rims = (moved_rim, fields_rim) + tuple(results[4:])
    return tuple(run_outer(info, whole, arrived, passed, rims, results[:4]))


def solution(mesh):
    in_specs = (
        P(("groups", "tiles"), "sub"),
        P(None, ("groups", "tiles"), "sub"),
        P(None, ("groups", "tiles"), "sub"),
        P(("groups", "tiles"), "sub"),
        P(("groups", "tiles"), "sub"),
        P("groups"),
    )
    out_specs = (
        P(("groups", "tiles"), "sub"),
        P(None, ("groups", "tiles"), "sub"),
        P(None, ("groups", "tiles"), "sub"),
        P(("groups", "tiles"), "sub"),
    )
    return jax.shard_map(body, mesh=mesh, in_specs=in_specs, out_specs=out_specs, check_vma=False)
```

```python
import functools

import jax
import jax.numpy as jnp
from jax import lax
from jax.experimental import pallas as pl
from jax.experimental.pallas import tpu as pltpu
from jax.sharding import PartitionSpec as P

TILE = 16
STEPS = 2
RELAX_TIME = 0.8
SURFACE = 0.1
SEPARATION = 0.7

LANES = 128
SUBLANES = 8
FULL = 3
HALO = FULL + 1
FIELDS = 11
PLANES = FIELDS + 1
MOVED = 19
REDS = 5
RIM = 4
SLAB = HALO + 2 * RIM
COLOUR_BLOCK = 8
COLLIDE_BLOCK = 4
ARRIVE_BLOCK = 4
VMEM = pl.BlockSpec(memory_space=pltpu.VMEM)
SMEM = pl.BlockSpec(memory_space=pltpu.SMEM)
ANY = pl.BlockSpec(memory_space=pl.ANY)
HBM = pl.BlockSpec(memory_space=pltpu.HBM)


def roll_lanes(values, amount):
    return pltpu.roll(values, amount % LANES, 2)


class Geometry:
    def __init__(self, info, own_tiles):
        live, first, last, sub_index = info[0], info[1], info[2], info[3]
        self.live = live
        self.low_row = jnp.where(first == 1, 0, -1000)
        self.high_row = jnp.where(last == 1, live, 1000)
        shape = (1, SUBLANES, LANES)
        lane = lax.broadcasted_iota(jnp.int32, shape, 2)
        tile = lax.broadcasted_iota(jnp.int32, shape, 1)
        depth = lane & (TILE - 1)
        self.z_low = depth == 0
        self.z_high = depth == TILE - 1
        low_part = sub_index == 0
        high_part = sub_index == 1
        self.y_low = (tile == 1) & (lane < TILE) & low_part
        self.y_high = (tile == own_tiles) & (lane >= LANES - TILE) & high_part
        own = (tile >= 1) & (tile <= own_tiles)
        self.domain = own | ((tile == own_tiles + 1) & low_part) | ((tile == 0) & high_part)
        self.first_lanes = lane < TILE
        self.last_lanes = lane >= LANES - TILE

    def from_low_y(self, values, depth_shift=0):
        crossed = jnp.where(self.last_lanes, pltpu.roll(values, 1, 1), values)
        return roll_lanes(crossed, TILE + depth_shift)

    def from_high_y(self, values, depth_shift=0):
        crossed = jnp.where(self.first_lanes, pltpu.roll(values, SUBLANES - 1, 1), values)
        return roll_lanes(crossed, -TILE + depth_shift)

    def from_low_z(self, values):
        return jnp.where(self.z_low, 0.0, roll_lanes(values, 1))

    def from_high_z(self, values):
        return jnp.where(self.z_high, 0.0, roll_lanes(values, -1))


def flat_rows(row, count):
    start = row * SUBLANES
    if not isinstance(start, int):
        start = pl.multiple_of(start, SUBLANES)
    return pl.ds(start, count * SUBLANES)


class Block:
    def __init__(self, geometry, spans, inner=False):
        self.spans = spans
        rows = [row + extra for row, local, count in spans for extra in range(count)]
        if inner:
            self.x_low = self.x_high = None
            self.valid = geometry.domain
            self.kinds = [0]
            return
        shape = (1, SUBLANES, LANES)
        ids = jnp.concatenate([row + jnp.zeros(shape, jnp.int32) for row in rows], axis=0)
        self.x_low = ids == geometry.low_row
        self.x_high = ids == geometry.high_row - 1
        self.valid = geometry.domain & (ids >= geometry.low_row) & (ids < geometry.high_row)
        self.kinds = [
            jnp.where(row == geometry.low_row, 1, 0) + jnp.where(row == geometry.high_row - 1, 2, 0)
            for row in rows
        ]

    def load(self, ref, index, offset=0):
        parts = [
            ref[index, flat_rows(local + offset, count), :].reshape(count, SUBLANES, LANES)
            for row, local, count in self.spans
        ]
        return parts[0] if len(parts) == 1 else jnp.concatenate(parts, axis=0)

    def store(self, ref, index, values):
        done = 0
        for row, local, count in self.spans:
            part = values[done : done + count].reshape(count * SUBLANES, LANES)
            ref[index, flat_rows(local, count), :] = part
            done += count

    def walls(self, walls, position):
        parts = [walls[position, flat_rows(kind, 1), :][None] for kind in self.kinds]
        return jnp.concatenate(parts, axis=0)


def fill_wall_table(walls, geometry):
    one = jnp.ones((1, SUBLANES, LANES), jnp.float32)
    up_y = jnp.where(geometry.y_high, 0.0, one)
    down_y = jnp.where(geometry.y_low, 0.0, one)
    up_z = jnp.where(geometry.z_high, 0.0, one)
    down_z = jnp.where(geometry.z_low, 0.0, one)
    sum_y, sum_z = up_y + down_y, up_z + down_z
    for kind, (up_x, down_x) in enumerate(((1.0, 1.0), (1.0, 0.0), (0.0, 1.0))):
        sum_x = up_x + down_x
        around_x = 2.0 + sum_y + sum_z
        total = 12.0 + 2.0 * (sum_x + sum_y + sum_z) + sum_x * (sum_y + sum_z) + sum_y * sum_z
        rows = (
            (up_x - down_x) * around_x,
            (up_y - down_y) * (2.0 + sum_x + sum_z),
            (up_z - down_z) * (2.0 + sum_x + sum_y),
            36.0 - total,
        )
        for position, row in enumerate(rows):
            walls[position, flat_rows(kind, 1), :] = row[0]


def colour_stage(block, geometry, fields, colours):
    density = block.load(fields, 0)
    red = block.load(fields, 10)
    colour = jnp.where(block.valid, 2.0 * red - density, 0.0)
    along_y = geometry.from_low_y(colour) + geometry.from_high_y(colour)
    along_z = geometry.from_low_z(colour) + geometry.from_high_z(colour)
    block.store(colours, 0, colour)
    block.store(colours, 1, 2.0 * colour + (along_y + along_z))
    block.store(colours, 2, along_y)
    block.store(colours, 3, along_z)


def collide_stage(block, geometry, fields, solids, colours, walls, moved, reds):
    relaxing = 1.0 - 1.0 / RELAX_TIME
    third = 1.0 / 3.0
    colour = block.load(colours, 0)
    doubled = 2.0 * colour + (block.load(colours, 0, -1) + block.load(colours, 0, 1))
    term_y = doubled + block.load(colours, 3)
    term_z = doubled + block.load(colours, 2)
    grad_x = block.load(colours, 1, 1) - block.load(colours, 1, -1)
    grad_y = geometry.from_high_y(term_y) - geometry.from_low_y(term_y)
    grad_z = geometry.from_high_z(term_z) - geometry.from_low_z(term_z)
    grad_x = (grad_x - block.walls(walls, 0) * colour) * (1.0 / 12.0)
    grad_y = (grad_y - block.walls(walls, 1) * colour) * (1.0 / 12.0)
    grad_z = (grad_z - block.walls(walls, 2) * colour) * (1.0 / 12.0)

    fluid = block.load(solids, PLANES - 1) == 0.0
    density = block.load(fields, 0)
    red = block.load(fields, 10)
    flux = [block.load(fields, 1 + axis) for axis in range(3)]
    stress = [block.load(fields, 4 + part) for part in range(6)]
    square_xx, square_yy, square_zz = grad_x * grad_x, grad_y * grad_y, grad_z * grad_z
    square = square_xx + square_yy + square_zz
    inverse = jnp.where(fluid, lax.rsqrt(1.0 + square), 0.0)
    strength = SURFACE * inverse
    keep = jnp.where(fluid, relaxing, 1.0)
    sign = jnp.where(fluid, 1.0, -1.0)
    trace = third * square
    surface = (
        square_xx - trace,
        square_yy - trace,
        square_zz - trace,
        grad_x * grad_y,
        grad_x * grad_z,
        grad_y * grad_z,
    )
    pairs = ((0, 0), (1, 1), (2, 2), (0, 1), (0, 2), (1, 2))
    second = [
        flux[a] * flux[b] + (keep * before + strength * addend)
        for (a, b), before, addend in zip(pairs, stress, surface)
    ]
    flux = [sign * part for part in flux]
    mixing = (SEPARATION * red) * (density - red) * inverse
    charge = [0.5 * part + mixing * grad for part, grad in zip(flux, (grad_x, grad_y, grad_z))]

    base = (density - 1.5 * (second[0] + second[1] + second[2])) * (1.0 / 36.0)
    run = [part * (1.0 / 12.0) for part in flux]
    own = [part * 0.125 for part in second[:3]]
    cross = [part * 0.25 for part in second[3:]]
    block.store(moved, 0, 12.0 * base)
    straight = [base + part for part in own]
    for axis in range(3):
        middle = 2.0 * straight[axis]
        swing = 2.0 * run[axis]
        block.store(moved, 1 + 2 * axis, middle + swing)
        block.store(moved, 2 + 2 * axis, middle - swing)
    for plane, (a, b) in enumerate(((0, 1), (0, 2), (1, 2))):
        middle = straight[a] + own[b]
        same, other = middle + cross[plane], middle - cross[plane]
        along, against = run[a] + run[b], run[a] - run[b]
        first = 7 + 4 * plane
        block.store(moved, first, same + along)
        block.store(moved, first + 1, same - along)
        block.store(moved, first + 2, other + against)
        block.store(moved, first + 3, other - against)

    scale = jnp.where(block.valid, 1.0 / 12.0, 0.0)
    red_base = red * (scale * third)
    red_run = [part * scale for part in charge]
    block.store(reds, 0, red_base)
    block.store(reds, 1, red_base + red_run[0])
    block.store(reds, 2, red_base - red_run[0])
    block.store(reds, 3, red_run[1])
    block.store(reds, 4, red_run[2])


def arrive_stage(block, geometry, walls, moved, reds, fields):
    third = 1.0 / 3.0
    own = [None] * MOVED

    def here(direction):
        if own[direction] is None:
            own[direction] = block.load(moved, direction)
        return own[direction]

    def arrived(direction, opposite, velocity):
        vel_x, vel_y, vel_z = velocity
        values = here(direction) if vel_x == 0 else block.load(moved, direction, -vel_x)
        if vel_y == 1:
            values = geometry.from_low_y(values, vel_z)
        elif vel_y == -1:
            values = geometry.from_high_y(values, vel_z)
        elif vel_z != 0:
            values = roll_lanes(values, vel_z)
        masks = []
        if vel_x != 0 and block.x_low is not None:
            masks.append(block.x_low if vel_x == 1 else block.x_high)
        if vel_y != 0:
            masks.append(geometry.y_low if vel_y == 1 else geometry.y_high)
        if vel_z != 0:
            masks.append(geometry.z_low if vel_z == 1 else geometry.z_high)
        if not masks:
            return values
        wall = functools.reduce(lambda one, two: one | two, masks)
        return jnp.where(wall, here(opposite), values)

    rest = here(0)
    sums, diffs = [], []
    for axis in range(3):
        velocity = [0, 0, 0]
        velocity[axis] = 1
        up = arrived(1 + 2 * axis, 2 + 2 * axis, velocity)
        velocity[axis] = -1
        down = arrived(2 + 2 * axis, 1 + 2 * axis, velocity)
        sums.append(up + down)
        diffs.append(up - down)
    total = rest + sums[0] + sums[1] + sums[2]
    cross = []
    for plane, (a, b) in enumerate(((0, 1), (0, 2), (1, 2))):
        first = 7 + 4 * plane
        parts = []
        for offset, (vel_a, vel_b) in enumerate(((1, 1), (-1, -1), (1, -1), (-1, 1))):
            velocity = [0, 0, 0]
            velocity[a], velocity[b] = vel_a, vel_b
            parts.append(arrived(first + offset, first + (offset ^ 1), velocity))
        same, other = parts[0] + parts[1], parts[2] + parts[3]
        along, against = parts[0] - parts[1], parts[2] - parts[3]
        both = same + other
        cross.append(same - other)
        total = total + both
        sums[a], sums[b] = sums[a] + both, sums[b] + both
        diffs[a], diffs[b] = diffs[a] + (along + against), diffs[b] + (along - against)
    shared = third * total
    block.store(fields, 0, total)
    for axis in range(3):
        block.store(fields, 1 + axis, diffs[axis])
        block.store(fields, 4 + axis, sums[axis] - shared - diffs[axis] * diffs[axis])
    for plane, (a, b) in enumerate(((0, 1), (0, 2), (1, 2))):
        block.store(fields, 7 + plane, cross[plane] - diffs[a] * diffs[b])

    red = block.load(reds, 0)
    red_x_up = block.load(reds, 1)
    red_y = block.load(reds, 3)
    red_z = block.load(reds, 4)
    from_x = block.load(reds, 1, -1) + block.load(reds, 2, 1)
    spread = 2.0 * red + from_x
    spread_y = 2.0 * red_y + (block.load(reds, 3, -1) + block.load(reds, 3, 1))
    spread_z = 2.0 * red_z + (block.load(reds, 4, -1) + block.load(reds, 4, 1))
    up_y, down_y = red + red_y, red - red_y
    low_y = (
        (spread + spread_y)
        + geometry.from_low_z(up_y + red_z)
        + geometry.from_high_z(up_y - red_z)
    )
    high_y = (
        (spread - spread_y)
        + geometry.from_low_z(down_y + red_z)
        + geometry.from_high_z(down_y - red_z)
    )
    bounced = (
        block.walls(walls, 3) * red
        - block.walls(walls, 0) * (red_x_up - red)
        - block.walls(walls, 1) * red_y
        - block.walls(walls, 2) * red_z
    )
    red_total = (
        12.0 * red
        + 2.0 * from_x
        + geometry.from_low_z(spread + spread_z)
        + geometry.from_high_z(spread - spread_z)
        + geometry.from_low_y(low_y)
        + geometry.from_high_y(high_y)
        + bounced
    )
    block.store(fields, 10, red_total)


def over_rows(geometry, first, end, size, stage):
    def step(index, carry):
        row = jnp.minimum(first + index * size, end - size)
        stage(Block(geometry, [(row, row, size)], inner=True))
        return carry

    lax.fori_loop(0, (end - first + size - 1) // size, step, 0)


def edge_kernel(density, momentum, stress, red, solid, edge, solid_edge, sems):
    own_tiles = density.shape[1] // LANES
    start = jnp.where(lax.axis_index("sub") == 0, (own_tiles - 1) * LANES, 0)
    lanes = pl.ds(pl.multiple_of(start, LANES), LANES)
    copies = [
        pltpu.make_async_copy(density.at[:, lanes], edge.at[0], sems.at[0]),
        pltpu.make_async_copy(momentum.at[:, :, lanes], edge.at[pl.ds(1, 3)], sems.at[1]),
        pltpu.make_async_copy(stress.at[:, :, lanes], edge.at[pl.ds(4, 6)], sems.at[2]),
        pltpu.make_async_copy(red.at[:, lanes], edge.at[10], sems.at[3]),
        pltpu.make_async_copy(solid.at[:, lanes], solid_edge, sems.at[4]),
    ]
    for copy in copies:
        copy.start()
    for copy in copies:
        copy.wait()
    edge[PLANES - 1] = solid_edge[...].astype(jnp.float32)


def take_edge(arrays):
    row_count = arrays[0].shape[0]
    return pl.pallas_call(
        edge_kernel,
        out_shape=jax.ShapeDtypeStruct((PLANES, row_count, LANES), jnp.float32),
        in_specs=[HBM] * 5,
        out_specs=VMEM,
        scratch_shapes=[pltpu.VMEM((row_count, LANES), jnp.int32), pltpu.SemaphoreType.DMA((5,))],
        name="edge",
    )(*arrays)


def spread_kernel(density, momentum, stress, red, solid, spread):
    row_count, flat_count = density.shape
    sources = [density] + [momentum.at[axis] for axis in range(3)]
    sources = sources + [stress.at[part] for part in range(6)] + [red, solid]
    for index, source in enumerate(sources):
        for row in range(0, row_count, SUBLANES):
            for tile in range(flat_count // LANES):
                values = source[pl.ds(row, SUBLANES), pl.ds(tile * LANES, LANES)]
                start = row * SUBLANES + 1 + tile
                spread[index, pl.ds(start, SUBLANES, stride=SUBLANES), :] = values.astype(jnp.float32)


def spread_rows(arrays):
    row_count = arrays[0].shape[0]
    return pl.pallas_call(
        spread_kernel,
        out_shape=jax.ShapeDtypeStruct((PLANES, row_count * SUBLANES, LANES), jnp.float32),
        in_specs=[VMEM] * 5,
        out_specs=VMEM,
        compiler_params=pltpu.CompilerParams(vmem_limit_bytes=16 * 1024 * 1024),
        name="spread",
    )(*arrays)


def ends_kernel(info, spread, side, whole, low_end, high_end):
    live, low_part = info[0], info[3] == 0
    row_count = side.shape[1]
    for index in range(PLANES):
        whole[index] = spread[index]
        for row in range(0, row_count, SUBLANES):
            values = side[index, pl.ds(row, SUBLANES), :]
            start = row * SUBLANES
            below = jnp.where(low_part, 0.0, values)
            above = jnp.where(low_part, values, 0.0)
            whole[index, pl.ds(start, SUBLANES, stride=SUBLANES), :] = below
            whole[index, pl.ds(start + SUBLANES - 1, SUBLANES, stride=SUBLANES), :] = above
    for index in range(PLANES):
        target = pl.ds((1 + FULL * index) * SUBLANES, FULL * SUBLANES)
        low_end[target, :] = whole[index, pl.ds(0, FULL * SUBLANES), :]
        high_end[target, :] = whole[index, flat_rows(live - FULL, FULL), :]
    for end, row in ((low_end, FULL), (high_end, live - HALO)):
        rows = flat_rows(row, 1)
        end[pl.ds(0, SUBLANES), :] = 2.0 * whole[10, rows, :] - whole[0, rows, :]


def take_ends(info, spread, side):
    end = jax.ShapeDtypeStruct(((1 + FULL * PLANES) * SUBLANES, LANES), jnp.float32)
    return pl.pallas_call(
        ends_kernel,
        out_shape=[jax.ShapeDtypeStruct(spread.shape, jnp.float32), end, end],
        in_specs=[SMEM, VMEM, VMEM],
        out_specs=[VMEM] * 3,
        compiler_params=pltpu.CompilerParams(vmem_limit_bytes=16 * 1024 * 1024),
        name="ends",
    )(info, spread, side)


def inner_kernel(
    info, whole,
    density_out, momentum_out, stress_out, red_out, moved_rim, fields_rim, final_rim,
    colours, walls, moved, reds, fields, moved_later, reds_later, final,
):
    row_count, flat_count = density_out.shape
    own_tiles = flat_count // LANES
    geometry = Geometry(info, own_tiles)
    live = geometry.live
    fill_wall_table(walls, geometry)

    def colour(source, first, end):
        over_rows(geometry, first, end, COLOUR_BLOCK, lambda block: colour_stage(
            block, geometry, source, colours))

    def collide(source, target, target_reds, first, end):
        over_rows(geometry, first, end, COLLIDE_BLOCK, lambda block: collide_stage(
            block, geometry, source, whole, colours, walls, target, target_reds))

    def arrive(source, source_reds, target, first, end):
        over_rows(geometry, first, end, ARRIVE_BLOCK, lambda block: arrive_stage(
            block, geometry, walls, source, source_reds, target))

    colour(whole, 0, live)
    collide(whole, moved, reds, 1, live - 1)
    arrive(moved, reds, fields, 2, live - 2)
    colour(fields, 2, live - 2)
    collide(fields, moved_later, reds_later, 3, live - 3)
    arrive(moved_later, reds_later, final, 4, live - 4)

    def keep(target, target_index, source, index, rows, size):
        for place, row in enumerate(rows):
            target[target_index, flat_rows(place * size, size), :] = source[
                index, flat_rows(row, size), :
            ]

    for index in range(MOVED + REDS):
        first, later, at = moved, moved_later, index
        if index >= MOVED:
            first, later, at = reds, reds_later, index - MOVED
        keep(moved_rim, index, first, at, (1, live - 3), 2)
        keep(moved_rim, MOVED + REDS + index, later, at, (3, live - 5), 2)
    for index in range(FIELDS):
        keep(fields_rim, index, fields, index, (2, live - 4), 2)
        keep(final_rim, index, final, index, (RIM, live - 2 * RIM), RIM)

    targets = [density_out] + [momentum_out.at[axis] for axis in range(3)]
    targets = targets + [stress_out.at[part] for part in range(6)] + [red_out]
    for index, target in enumerate(targets):
        for row in range(0, row_count, SUBLANES):
            alive = row < live
            for tile in range(own_tiles):
                start = row * SUBLANES + 1 + tile
                values = final[index, pl.ds(start, SUBLANES, stride=SUBLANES), :]
                target[pl.ds(row, SUBLANES), pl.ds(tile * LANES, LANES)] = jnp.where(
                    alive, values, 0.0
                )


def run_inner(info, whole, arrays):
    flat = whole.shape[1]
    rim = lambda count, rows: jax.ShapeDtypeStruct((count, rows * SUBLANES, LANES), jnp.float32)
    shapes = [jax.ShapeDtypeStruct(array.shape, jnp.float32) for array in arrays[:4]]
    shapes = shapes + [rim(2 * (MOVED + REDS), 4), rim(FIELDS, 4), rim(FIELDS, 2 * RIM)]
    return pl.pallas_call(
        inner_kernel,
        out_shape=shapes,
        in_specs=[SMEM, VMEM],
        out_specs=[VMEM] * len(shapes),
        scratch_shapes=[
            pltpu.VMEM((4, flat, LANES), jnp.float32),
            pltpu.VMEM((4, 3 * SUBLANES, LANES), jnp.float32),
            pltpu.VMEM((MOVED, flat, LANES), jnp.float32),
            pltpu.VMEM((REDS, flat, LANES), jnp.float32),
            pltpu.VMEM((FIELDS, flat, LANES), jnp.float32),
            pltpu.VMEM((MOVED, flat, LANES), jnp.float32),
            pltpu.VMEM((REDS, flat, LANES), jnp.float32),
            pltpu.VMEM((FIELDS, flat, LANES), jnp.float32),
        ],
        compiler_params=pltpu.CompilerParams(vmem_limit_bytes=32 * 1024 * 1024),
        cost_estimate=pl.CostEstimate(flops=40_000_000, bytes_accessed=8_000_000, transcendentals=0),
        name="inner",
    )(info, whole)


def outer_kernel(
    info, whole, low, high, moved_rim, fields_rim, final_rim, *refs,
):
    outs = refs[4:8]
    start_fields, colours, walls, moved, reds, fields, moved_later, reds_later, final = refs[8:17]
    pieces, sems = refs[17:]
    row_count, flat_count = outs[0].shape
    own_tiles = flat_count // LANES
    geometry = Geometry(info, own_tiles)
    live = geometry.live
    fill_wall_table(walls, geometry)

    def spans(first, count):
        mirrored = SLAB - first - count
        return [
            (first - HALO, first, count),
            (live - 2 * RIM + mirrored, SLAB + mirrored, count),
        ]

    for index in range(PLANES):
        place = pl.ds((1 + FULL * index) * SUBLANES, FULL * SUBLANES)
        start_fields[index, flat_rows(1, FULL), :] = low[place, :]
        start_fields[index, flat_rows(2 * SLAB - HALO, FULL), :] = high[place, :]
        start_fields[index, flat_rows(HALO, 2), :] = whole[index, flat_rows(0, 2), :]
        start_fields[index, flat_rows(2 * SLAB - HALO - 2, 2), :] = whole[
            index, flat_rows(live - 2, 2), :
        ]
    for row, end in ((0, low), (2 * SLAB - 1, high)):
        start_fields[0, flat_rows(row, 1), :] = jnp.zeros((SUBLANES, LANES), jnp.float32)
        start_fields[10, flat_rows(row, 1), :] = 0.5 * end[pl.ds(0, SUBLANES), :]

    def place(target, index, source, at, first, size):
        for place, (row, local, count) in enumerate(spans(first, size)):
            target[index, flat_rows(local, size), :] = source[at, flat_rows(place * size, size), :]

    for index in range(MOVED + REDS):
        target, later, at = moved, moved_later, index
        if index >= MOVED:
            target, later, at = reds, reds_later, index - MOVED
        place(target, at, moved_rim, index, HALO + 1, 2)
        place(later, at, moved_rim, MOVED + REDS + index, HALO + 3, 2)
    for index in range(FIELDS):
        place(fields, index, fields_rim, index, HALO + 2, 2)
        place(final, index, final_rim, index, HALO + RIM, RIM)

    block = lambda first, count: Block(geometry, spans(first, count))
    colour_stage(block(0, 6), geometry, start_fields, colours)
    collide_stage(block(1, 4), geometry, start_fields, start_fields, colours, walls, moved, reds)
    arrive_stage(block(2, 4), geometry, walls, moved, reds, fields)
    start_fields[PLANES - 1, flat_rows(HALO + 2, 1), :] = whole[PLANES - 1, flat_rows(2, 1), :]
    start_fields[PLANES - 1, flat_rows(2 * SLAB - HALO - 3, 1), :] = whole[
        PLANES - 1, flat_rows(live - 3, 1), :
    ]
    colour_stage(block(2, 6), geometry, fields, colours)
    collide_stage(
        block(3, 4), geometry, fields, start_fields, colours, walls, moved_later, reds_later
    )
    arrive_stage(block(4, 4), geometry, walls, moved_later, reds_later, final)

    for index in range(FIELDS):
        for side, row in ((0, HALO), (1, SLAB)):
            for tile in range(own_tiles):
                start = row * SUBLANES + 1 + tile
                pieces[index, pl.ds(side * SUBLANES, SUBLANES), pl.ds(tile * LANES, LANES)] = final[
                    index, pl.ds(start, SUBLANES, stride=SUBLANES), :
                ]
    copies = []
    for side, row in ((0, 0), (1, pl.multiple_of(live - SUBLANES, SUBLANES))):
        rows = pl.ds(row, SUBLANES)
        held = pl.ds(side * SUBLANES, SUBLANES)
        for number, (out, source) in enumerate(
            (
                (outs[0].at[rows], pieces.at[0, held]),
                (outs[1].at[:, rows], pieces.at[pl.ds(1, 3), held]),
                (outs[2].at[:, rows], pieces.at[pl.ds(4, 6), held]),
                (outs[3].at[rows], pieces.at[10, held]),
            )
        ):
            copies.append(pltpu.make_async_copy(source, out, sems.at[side, number]))
    for copy in copies:
        copy.start()
    for copy in copies:
        copy.wait()


def run_outer(info, whole, low, high, rims, outs):
    flat = 2 * SLAB * SUBLANES
    flat_count = outs[0].shape[1]
    return pl.pallas_call(
        outer_kernel,
        out_shape=[jax.ShapeDtypeStruct(out.shape, jnp.float32) for out in outs],
        in_specs=[SMEM] + [VMEM] * 6 + [ANY] * 4,
        out_specs=[ANY] * 4,
        scratch_shapes=[
            pltpu.VMEM((PLANES, flat, LANES), jnp.float32),
            pltpu.VMEM((4, flat, LANES), jnp.float32),
            pltpu.VMEM((4, 3 * SUBLANES, LANES), jnp.float32),
            pltpu.VMEM((MOVED, flat, LANES), jnp.float32),
            pltpu.VMEM((REDS, flat, LANES), jnp.float32),
            pltpu.VMEM((FIELDS, flat, LANES), jnp.float32),
            pltpu.VMEM((MOVED, flat, LANES), jnp.float32),
            pltpu.VMEM((REDS, flat, LANES), jnp.float32),
            pltpu.VMEM((FIELDS, flat, LANES), jnp.float32),
            pltpu.VMEM((FIELDS, 2 * SUBLANES, flat_count), jnp.float32),
            pltpu.SemaphoreType.DMA((2, 4)),
        ],
        input_output_aliases={7: 0, 8: 1, 9: 2, 10: 3},
        compiler_params=pltpu.CompilerParams(vmem_limit_bytes=32 * 1024 * 1024),
        name="outer",
    )(info, whole, low, high, *rims, *outs)


def body(density, momentum, stress, red_density, solid, widths):
    tiles_index = lax.axis_index("tiles")
    tiles_count = lax.axis_size("tiles")
    chosen = lax.iota(jnp.int32, widths.shape[0]) == tiles_index
    live_rows = jnp.sum(jnp.where(chosen, widths, 0)) * TILE
    info = jnp.stack(
        [
            live_rows,
            (tiles_index == 0).astype(jnp.int32),
            (tiles_index == tiles_count - 1).astype(jnp.int32),
            lax.axis_index("sub").astype(jnp.int32),
        ]
    )
    arrays = (density, momentum, stress, red_density, solid)
    side = lax.ppermute(take_edge(arrays), "sub", [(0, 1), (1, 0)])
    whole, low_end, high_end = take_ends(info, spread_rows(arrays), side)
    ends = tiles_count - 1
    odd = tiles_index % 2 == 1
    even_groups = [[2 * k, 2 * k + 1] for k in range(tiles_count // 2)]
    odd_groups = [[2 * k + 1, (2 * k + 2) % tiles_count] for k in range(tiles_count // 2)]
    pair = lax.all_gather(jnp.where(odd, low_end, high_end), "tiles", axis_index_groups=even_groups)
    other = lax.all_gather(jnp.where(odd, high_end, low_end), "tiles", axis_index_groups=odd_groups)
    low = jnp.where(odd, pair[0], other[0])
    high = jnp.where(odd, other[1], pair[1])
    low = jnp.where(tiles_index == 0, 0.0, low)
    high = jnp.where(tiles_index == tiles_count - 1, 0.0, high)
    results = run_inner(info, whole, arrays)
    return tuple(run_outer(info, whole, low, high, results[4:], results[:4]))


def solution(mesh):
    in_specs = (
        P(("groups", "tiles"), "sub"),
        P(None, ("groups", "tiles"), "sub"),
        P(None, ("groups", "tiles"), "sub"),
        P(("groups", "tiles"), "sub"),
        P(("groups", "tiles"), "sub"),
        P("groups"),
    )
    out_specs = (
        P(("groups", "tiles"), "sub"),
        P(None, ("groups", "tiles"), "sub"),
        P(None, ("groups", "tiles"), "sub"),
        P(("groups", "tiles"), "sub"),
    )
    return jax.shard_map(body, mesh=mesh, in_specs=in_specs, out_specs=out_specs, check_vma=False)
```

```python
import functools

import jax
import jax.numpy as jnp
from jax import lax
from jax.experimental import pallas as pl
from jax.experimental.pallas import tpu as pltpu
from jax.sharding import PartitionSpec as P

TILE = 16
STEPS = 2
RELAX_TIME = 0.8
SURFACE = 0.1
SEPARATION = 0.7

LANES = 128
SUBLANES = 8
FULL = 3
HALO = FULL + 1
FIELDS = 11
PLANES = FIELDS + 1
MOVED = 19
REDS = 5
RIM = 4
SLAB = HALO + 2 * RIM
OWN_TILES = SUBLANES - 2
END_COUNT = 1 + FULL * PLANES
END_ROWS = -(-END_COUNT * OWN_TILES // SUBLANES) * SUBLANES
HALF = LANES // 2
PAIRS = PLANES // 2
COLOUR_BLOCK = (8, 1)
COLLIDE_BLOCK = (2, 4)
ARRIVE_BLOCK = (8, 1)
VMEM = pl.BlockSpec(memory_space=pltpu.VMEM)
SMEM = pl.BlockSpec(memory_space=pltpu.SMEM)
ANY = pl.BlockSpec(memory_space=pl.ANY)
HBM = pl.BlockSpec(memory_space=pltpu.HBM)


def roll_lanes(values, amount):
    return pltpu.roll(values, amount % LANES, 2)


class Geometry:
    def __init__(self, info, own_tiles):
        live, first, last, sub_index = info[0], info[1], info[2], info[3]
        self.live = live
        self.low_row = jnp.where(first == 1, 0, -1000)
        self.high_row = jnp.where(last == 1, live, 1000)
        shape = (1, SUBLANES, LANES)
        lane = lax.broadcasted_iota(jnp.int32, shape, 2)
        tile = lax.broadcasted_iota(jnp.int32, shape, 1)
        depth = lane & (TILE - 1)
        self.z_low = depth == 0
        self.z_high = depth == TILE - 1
        low_part = sub_index == 0
        high_part = sub_index == 1
        self.y_low = (tile == 1) & (lane < TILE) & low_part
        self.y_high = (tile == own_tiles) & (lane >= LANES - TILE) & high_part
        own = (tile >= 1) & (tile <= own_tiles)
        self.domain = own | ((tile == own_tiles + 1) & low_part) | ((tile == 0) & high_part)
        self.first_lanes = lane < TILE
        self.last_lanes = lane >= LANES - TILE

    def from_low_y(self, values, depth_shift=0, below=None):
        if below is None:
            below = pltpu.roll(values, 1, 1)
        return roll_lanes(jnp.where(self.last_lanes, below, values), TILE + depth_shift)

    def from_high_y(self, values, depth_shift=0, above=None):
        if above is None:
            above = pltpu.roll(values, SUBLANES - 1, 1)
        return roll_lanes(jnp.where(self.first_lanes, above, values), -TILE + depth_shift)

    def from_low_z(self, values):
        return jnp.where(self.z_low, 0.0, roll_lanes(values, 1))

    def from_high_z(self, values):
        return jnp.where(self.z_high, 0.0, roll_lanes(values, -1))


def flat_rows(row, count, tile_offset=0):
    start = row * SUBLANES
    if not isinstance(start, int):
        start = pl.multiple_of(start, SUBLANES)
    return pl.ds(start + tile_offset, count * SUBLANES)


class Block:
    def __init__(self, geometry, spans, inner=False, store_rows=None):
        self.spans = spans
        self.store_rows = store_rows or [local for row, local, count in spans]
        rows = [row + extra for row, local, count in spans for extra in range(count)]
        if inner:
            self.x_low = self.x_high = None
            self.valid = geometry.domain
            self.kinds = [0]
            return
        shape = (1, SUBLANES, LANES)
        ids = jnp.concatenate([row + jnp.zeros(shape, jnp.int32) for row in rows], axis=0)
        self.x_low = ids == geometry.low_row
        self.x_high = ids == geometry.high_row - 1
        self.valid = geometry.domain & (ids >= geometry.low_row) & (ids < geometry.high_row)
        self.kinds = [
            jnp.where(row == geometry.low_row, 1, 0) + jnp.where(row == geometry.high_row - 1, 2, 0)
            for row in rows
        ]

    def load(self, ref, index, offset=0, tile_offset=0):
        parts = [
            ref[index, flat_rows(local + offset, count, tile_offset), :].reshape(
                count, SUBLANES, LANES
            )
            for row, local, count in self.spans
        ]
        return parts[0] if len(parts) == 1 else jnp.concatenate(parts, axis=0)

    def store(self, ref, index, values):
        done = 0
        for (row, local, count), target in zip(self.spans, self.store_rows):
            part = values[done : done + count].reshape(count * SUBLANES, LANES)
            ref[index, flat_rows(target, count), :] = part
            done += count

    def walls(self, walls, position):
        parts = [walls[position, flat_rows(kind, 1), :][None] for kind in self.kinds]
        return jnp.concatenate(parts, axis=0)


def fill_wall_table(walls, geometry):
    one = jnp.ones((1, SUBLANES, LANES), jnp.float32)
    up_y = jnp.where(geometry.y_high, 0.0, one)
    down_y = jnp.where(geometry.y_low, 0.0, one)
    up_z = jnp.where(geometry.z_high, 0.0, one)
    down_z = jnp.where(geometry.z_low, 0.0, one)
    sum_y, sum_z = up_y + down_y, up_z + down_z
    for kind, (up_x, down_x) in enumerate(((1.0, 1.0), (1.0, 0.0), (0.0, 1.0))):
        sum_x = up_x + down_x
        around_x = 2.0 + sum_y + sum_z
        total = 12.0 + 2.0 * (sum_x + sum_y + sum_z) + sum_x * (sum_y + sum_z) + sum_y * sum_z
        rows = (
            (up_x - down_x) * around_x,
            (up_y - down_y) * (2.0 + sum_x + sum_z),
            (up_z - down_z) * (2.0 + sum_x + sum_y),
            36.0 - total,
        )
        for position, row in enumerate(rows):
            walls[position, flat_rows(kind, 1), :] = row[0]


def colour_stage(block, geometry, fields, colours):
    density = block.load(fields, 0)
    red = block.load(fields, 10)
    colour = jnp.where(block.valid, 2.0 * red - density, 0.0)
    along_y = geometry.from_low_y(colour) + geometry.from_high_y(colour)
    along_z = geometry.from_low_z(colour) + geometry.from_high_z(colour)
    block.store(colours, 0, colour)
    block.store(colours, 1, 2.0 * colour + (along_y + along_z))
    block.store(colours, 2, along_y)
    block.store(colours, 3, along_z)


def collide_stage(block, geometry, fields, solids, colours, walls, moved, reds):
    relaxing = 1.0 - 1.0 / RELAX_TIME
    third = 1.0 / 3.0
    colour = block.load(colours, 0)
    doubled = 2.0 * colour + (block.load(colours, 0, -1) + block.load(colours, 0, 1))
    term_y = doubled + block.load(colours, 3)
    term_z = doubled + block.load(colours, 2)
    grad_x = block.load(colours, 1, 1) - block.load(colours, 1, -1)
    grad_y = geometry.from_high_y(term_y) - geometry.from_low_y(term_y)
    grad_z = geometry.from_high_z(term_z) - geometry.from_low_z(term_z)
    grad_x = (grad_x - block.walls(walls, 0) * colour) * (1.0 / 12.0)
    grad_y = (grad_y - block.walls(walls, 1) * colour) * (1.0 / 12.0)
    grad_z = (grad_z - block.walls(walls, 2) * colour) * (1.0 / 12.0)

    fluid = block.load(solids, PLANES - 1) == 0.0
    density = block.load(fields, 0)
    red = block.load(fields, 10)
    flux = [block.load(fields, 1 + axis) for axis in range(3)]
    stress = [block.load(fields, 4 + part) for part in range(6)]
    square_xx, square_yy, square_zz = grad_x * grad_x, grad_y * grad_y, grad_z * grad_z
    square = square_xx + square_yy + square_zz
    inverse = jnp.where(fluid, lax.rsqrt(1.0 + square), 0.0)
    strength = SURFACE * inverse
    keep = jnp.where(fluid, relaxing, 1.0)
    sign = jnp.where(fluid, 1.0, -1.0)
    trace = third * square
    surface = (
        square_xx - trace,
        square_yy - trace,
        square_zz - trace,
        grad_x * grad_y,
        grad_x * grad_z,
        grad_y * grad_z,
    )
    pairs = ((0, 0), (1, 1), (2, 2), (0, 1), (0, 2), (1, 2))
    second = [
        flux[a] * flux[b] + (keep * before + strength * addend)
        for (a, b), before, addend in zip(pairs, stress, surface)
    ]
    flux = [sign * part for part in flux]
    mixing = (SEPARATION * red) * (density - red) * inverse
    charge = [0.5 * part + mixing * grad for part, grad in zip(flux, (grad_x, grad_y, grad_z))]

    base = (density - 1.5 * (second[0] + second[1] + second[2])) * (1.0 / 36.0)
    run = [part * (1.0 / 12.0) for part in flux]
    own = [part * 0.125 for part in second[:3]]
    cross = [part * 0.25 for part in second[3:]]
    block.store(moved, 0, 12.0 * base)
    straight = [base + part for part in own]
    for axis in range(3):
        middle = 2.0 * straight[axis]
        swing = 2.0 * run[axis]
        block.store(moved, 1 + 2 * axis, middle + swing)
        block.store(moved, 2 + 2 * axis, middle - swing)
    for plane, (a, b) in enumerate(((0, 1), (0, 2), (1, 2))):
        middle = straight[a] + own[b]
        same, other = middle + cross[plane], middle - cross[plane]
        along, against = run[a] + run[b], run[a] - run[b]
        first = 7 + 4 * plane
        block.store(moved, first, same + along)
        block.store(moved, first + 1, same - along)
        block.store(moved, first + 2, other + against)
        block.store(moved, first + 3, other - against)

    scale = jnp.where(block.valid, 1.0 / 12.0, 0.0)
    red_base = red * (scale * third)
    red_run = [part * scale for part in charge]
    block.store(reds, 0, red_base)
    block.store(reds, 1, red_base + red_run[0])
    block.store(reds, 2, red_base - red_run[0])
    block.store(reds, 3, red_run[1])
    block.store(reds, 4, red_run[2])


def arrive_stage(block, geometry, walls, moved, reds, fields):
    third = 1.0 / 3.0
    own = [None] * MOVED

    def here(direction):
        if own[direction] is None:
            own[direction] = block.load(moved, direction)
        return own[direction]

    def arrived(direction, opposite, velocity):
        vel_x, vel_y, vel_z = velocity
        values = here(direction) if vel_x == 0 else block.load(moved, direction, -vel_x)
        if vel_y == 1:
            below = block.load(moved, direction, -vel_x, -1)
            values = geometry.from_low_y(values, vel_z, below)
        elif vel_y == -1:
            above = block.load(moved, direction, -vel_x, 1)
            values = geometry.from_high_y(values, vel_z, above)
        elif vel_z != 0:
            values = roll_lanes(values, vel_z)
        masks = []
        if vel_x != 0 and block.x_low is not None:
            masks.append(block.x_low if vel_x == 1 else block.x_high)
        if vel_y != 0:
            masks.append(geometry.y_low if vel_y == 1 else geometry.y_high)
        if vel_z != 0:
            masks.append(geometry.z_low if vel_z == 1 else geometry.z_high)
        if not masks:
            return values
        wall = functools.reduce(lambda one, two: one | two, masks)
        return jnp.where(wall, here(opposite), values)

    rest = here(0)
    sums, diffs = [], []
    for axis in range(3):
        velocity = [0, 0, 0]
        velocity[axis] = 1
        up = arrived(1 + 2 * axis, 2 + 2 * axis, velocity)
        velocity[axis] = -1
        down = arrived(2 + 2 * axis, 1 + 2 * axis, velocity)
        sums.append(up + down)
        diffs.append(up - down)
    total = rest + sums[0] + sums[1] + sums[2]
    cross = []
    for plane, (a, b) in enumerate(((0, 1), (0, 2), (1, 2))):
        first = 7 + 4 * plane
        parts = []
        for offset, (vel_a, vel_b) in enumerate(((1, 1), (-1, -1), (1, -1), (-1, 1))):
            velocity = [0, 0, 0]
            velocity[a], velocity[b] = vel_a, vel_b
            parts.append(arrived(first + offset, first + (offset ^ 1), velocity))
        same, other = parts[0] + parts[1], parts[2] + parts[3]
        along, against = parts[0] - parts[1], parts[2] - parts[3]
        both = same + other
        cross.append(same - other)
        total = total + both
        sums[a], sums[b] = sums[a] + both, sums[b] + both
        diffs[a], diffs[b] = diffs[a] + (along + against), diffs[b] + (along - against)
    shared = third * total
    block.store(fields, 0, total)
    for axis in range(3):
        block.store(fields, 1 + axis, diffs[axis])
        block.store(fields, 4 + axis, sums[axis] - shared - diffs[axis] * diffs[axis])
    for plane, (a, b) in enumerate(((0, 1), (0, 2), (1, 2))):
        block.store(fields, 7 + plane, cross[plane] - diffs[a] * diffs[b])

    red = block.load(reds, 0)
    red_x_up = block.load(reds, 1)
    red_y = block.load(reds, 3)
    red_z = block.load(reds, 4)
    from_x = block.load(reds, 1, -1) + block.load(reds, 2, 1)
    spread = 2.0 * red + from_x
    spread_y = 2.0 * red_y + (block.load(reds, 3, -1) + block.load(reds, 3, 1))
    spread_z = 2.0 * red_z + (block.load(reds, 4, -1) + block.load(reds, 4, 1))
    up_y, down_y = red + red_y, red - red_y
    low_y = (
        (spread + spread_y)
        + geometry.from_low_z(up_y + red_z)
        + geometry.from_high_z(up_y - red_z)
    )
    high_y = (
        (spread - spread_y)
        + geometry.from_low_z(down_y + red_z)
        + geometry.from_high_z(down_y - red_z)
    )
    bounced = (
        block.walls(walls, 3) * red
        - block.walls(walls, 0) * (red_x_up - red)
        - block.walls(walls, 1) * red_y
        - block.walls(walls, 2) * red_z
    )
    red_total = (
        12.0 * red
        + 2.0 * from_x
        + geometry.from_low_z(spread + spread_z)
        + geometry.from_high_z(spread - spread_z)
        + geometry.from_low_y(low_y)
        + geometry.from_high_y(high_y)
        + bounced
    )
    block.store(fields, 10, red_total)


def over_rows(geometry, first, end, size, blocks, stage):
    trip = size * blocks

    def step(index, carry):
        start = jnp.minimum(first + index * trip, end - trip)
        for number in range(blocks):
            row = start + number * size
            stage(Block(geometry, [(row, row, size)], inner=True))
        return carry

    lax.fori_loop(0, (end - first + trip - 1) // trip, step, 0)


def load_kernel(
    tiles_count, density, momentum, stress, red, solid, widths,
    info, spread, packet, mine,
    raw, raw_solid, held_widths, sems,
):
    row_count, flat_count = raw_solid.shape
    own_tiles = flat_count // LANES
    planes = [density] + [momentum.at[axis] for axis in range(3)]
    planes = planes + [stress.at[part] for part in range(6)] + [red]
    copies = [pltpu.make_async_copy(widths, held_widths, sems.at[PLANES])]
    copies.append(pltpu.make_async_copy(solid, raw_solid, sems.at[FIELDS]))
    for index, plane in enumerate(planes):
        copies.append(pltpu.make_async_copy(plane, raw.at[index], sems.at[index]))
    for copy in copies:
        copy.start()
    tiles_index, sub_index = lax.axis_index("tiles"), lax.axis_index("sub")
    low_part = sub_index == 0
    edge_start = pl.multiple_of(jnp.where(low_part, (own_tiles - 1) * LANES, 0), LANES)

    copies[0].wait()
    live = held_widths[tiles_index] * TILE
    info[0] = live
    info[1] = (tiles_index == 0).astype(jnp.int32)
    info[2] = (tiles_index == tiles_count - 1).astype(jnp.int32)
    info[3] = sub_index

    near_cut = lax.broadcasted_iota(jnp.int32, (SUBLANES, LANES), 1) < HALF
    near_cut = near_cut == jnp.logical_not(low_part)
    for index in range(PLANES):
        source = raw_solid if index == FIELDS else raw.at[index]
        copies[1 if index == FIELDS else 2 + index].wait()
        for row in range(0, row_count, SUBLANES):
            rows = pl.ds(row, SUBLANES)
            for tile in range(own_tiles):
                values = source[rows, pl.ds(tile * LANES, LANES)].astype(jnp.float32)
                start = row * SUBLANES + 1 + tile
                spread[index, pl.ds(start, SUBLANES, stride=SUBLANES), :] = values
            if index >= PAIRS:
                values = source[rows, pl.ds(edge_start, LANES)].astype(jnp.float32)
                first = raw[index - PAIRS, rows, pl.ds(edge_start, LANES)]
                both = jnp.where(near_cut, first, pltpu.roll(values, HALF, 1))
                packet[pl.ds((index - PAIRS) * row_count + row, SUBLANES), :] = both

    after = PAIRS * row_count
    ends = (
        (packet, after, jnp.where(low_part, 0, live - FULL), jnp.where(low_part, FULL, live - HALO)),
        (mine, 0, jnp.where(low_part, live - FULL, 0), jnp.where(low_part, live - HALO, FULL)),
    )
    for target, at, full_row, colour_row in ends:
        rows = pl.ds(colour_row * SUBLANES + 1, OWN_TILES)
        target[pl.ds(at, OWN_TILES), :] = 2.0 * spread[10, rows, :] - spread[0, rows, :]
        for index in range(PLANES):
            for extra in range(FULL):
                place = at + (1 + FULL * index + extra) * OWN_TILES
                rows = pl.ds((full_row + extra) * SUBLANES + 1, OWN_TILES)
                target[pl.ds(place, OWN_TILES), :] = spread[index, rows, :]


def load_inputs(arrays, widths, tiles_count):
    row_count, flat_count = arrays[0].shape
    packet_rows = PAIRS * row_count + END_ROWS
    return pl.pallas_call(
        functools.partial(load_kernel, tiles_count),
        out_shape=[
            jax.ShapeDtypeStruct((4,), jnp.int32),
            jax.ShapeDtypeStruct((PLANES, row_count * SUBLANES, LANES), jnp.float32),
            jax.ShapeDtypeStruct((packet_rows, LANES), jnp.float32),
            jax.ShapeDtypeStruct((END_ROWS, LANES), jnp.float32),
        ],
        in_specs=[HBM] * 6,
        out_specs=[SMEM, VMEM, VMEM, VMEM],
        scratch_shapes=[
            pltpu.VMEM((FIELDS, row_count, flat_count), jnp.float32),
            pltpu.VMEM((row_count, flat_count), jnp.int32),
            pltpu.SMEM(widths.shape, jnp.int32),
            pltpu.SemaphoreType.DMA((PLANES + 1,)),
        ],
        compiler_params=pltpu.CompilerParams(vmem_limit_bytes=16 * 1024 * 1024),
        name="load",
    )(*[pltpu.with_memory_space_constraint(array, pltpu.HBM) for array in (*arrays, widths)])


def join_kernel(info, spread, packet, mine, whole, ends):
    low_part = info[3] == 0
    row_count = spread.shape[1] // SUBLANES
    ends[pl.ds(0, END_ROWS), :] = mine[...]
    ends[pl.ds(END_ROWS, END_ROWS), :] = packet[pl.ds(PAIRS * row_count, END_ROWS), :]
    for pair in range(PAIRS):
        for row in range(0, row_count, SUBLANES):
            both = packet[pl.ds(pair * row_count + row, SUBLANES), :]
            start = row * SUBLANES
            for index, values in ((pair, both), (pair + PAIRS, pltpu.roll(both, HALF, 1))):
                below = jnp.where(low_part, 0.0, values)
                above = jnp.where(low_part, values, 0.0)
                whole[index, pl.ds(start, SUBLANES, stride=SUBLANES), :] = below
                whole[index, pl.ds(start + SUBLANES - 1, SUBLANES, stride=SUBLANES), :] = above


def join_parts(info, spread, packet, mine):
    return pl.pallas_call(
        join_kernel,
        out_shape=[
            jax.ShapeDtypeStruct(spread.shape, jnp.float32),
            jax.ShapeDtypeStruct((2 * END_ROWS, LANES), jnp.float32),
        ],
        in_specs=[SMEM, VMEM, VMEM, VMEM],
        out_specs=[VMEM] * 2,
        input_output_aliases={1: 0},
        compiler_params=pltpu.CompilerParams(vmem_limit_bytes=16 * 1024 * 1024),
        name="join",
    )(info, pltpu.with_memory_space_constraint(spread, pltpu.VMEM), packet, mine)


def keep_rows(target, target_index, source, index, rows, size):
    for place, row in enumerate(rows):
        target[target_index, flat_rows(place * size, size), :] = source[
            index, flat_rows(row, size), :
        ]


def collide_rows(geometry, before, whole, first, scratch, moved, reds):
    colours, walls = scratch
    end = geometry.live - first
    over_rows(geometry, first - 1, end + 1, *COLOUR_BLOCK, lambda block: colour_stage(
        block, geometry, before, colours))
    over_rows(geometry, first, end, *COLLIDE_BLOCK, lambda block: collide_stage(
        block, geometry, before, whole, colours, walls, moved, reds))


def arrive_rows(geometry, first, walls, moved, reds, after):
    over_rows(geometry, first, geometry.live - first, *ARRIVE_BLOCK, lambda block: arrive_stage(
        block, geometry, walls, moved, reds, after))


def keep_moved(target, moved, reds, rows):
    for index in range(MOVED):
        keep_rows(target, index, moved, index, rows, 2)
    for index in range(REDS):
        keep_rows(target, MOVED + index, reds, index, rows, 2)


def first_kernel(info, whole, moved_later, reds_later, moved_rim, fields_rim, *scratch):
    colours, walls, moved, reds, fields = scratch
    geometry = Geometry(info, OWN_TILES)
    live = geometry.live
    fill_wall_table(walls, geometry)
    collide_rows(geometry, whole, whole, 1, (colours, walls), moved, reds)
    arrive_rows(geometry, 2, walls, moved, reds, fields)
    keep_moved(moved_rim, moved, reds, (1, live - 3))
    for index in range(FIELDS):
        keep_rows(fields_rim, index, fields, index, (2, live - 4), 2)
    collide_rows(geometry, fields, whole, 3, (colours, walls), moved_later, reds_later)


def tile_copies(pieces, outs, held_row, out_row, sems):
    held, rows = pl.ds(held_row, SUBLANES), pl.ds(out_row, SUBLANES)
    parts = (
        (pieces.at[0, held], outs[0].at[rows]),
        (pieces.at[pl.ds(1, 3), held], outs[1].at[:, rows]),
        (pieces.at[pl.ds(4, 6), held], outs[2].at[:, rows]),
        (pieces.at[10, held], outs[3].at[rows]),
    )
    return [
        pltpu.make_async_copy(source, target, sems.at[number])
        for number, (source, target) in enumerate(parts)
    ]


def gather_tiles(final, row, pieces, held_row):
    for index in range(FIELDS):
        for tile in range(OWN_TILES):
            start = pl.multiple_of(row * SUBLANES, SUBLANES) + 1 + tile
            pieces[index, pl.ds(held_row, SUBLANES), pl.ds(tile * LANES, LANES)] = final[
                index, pl.ds(start, SUBLANES, stride=SUBLANES), :
            ]


def second_kernel(
    info, moved, reds, arrived, density_out, momentum_out, stress_out, red_out,
    moved_rim, final_rim, final, walls, pieces, zeros, sems,
):
    outs = (density_out, momentum_out, stress_out, red_out)
    row_tiles = density_out.shape[0] // SUBLANES
    geometry = Geometry(info, OWN_TILES)
    live = geometry.live
    fill_wall_table(walls, geometry)

    zeros[...] = jnp.zeros(zeros.shape, zeros.dtype)
    dead = {}
    for tile in range(row_tiles):
        dead[tile] = tile_copies(zeros, outs, 0, tile * SUBLANES, sems.at[tile])

        @pl.when(tile * SUBLANES >= live)
        def _():
            for copy in dead[tile]:
                copy.start()

    edge = Block(geometry, [(RIM, RIM, RIM), (live - 2 * RIM, live - 2 * RIM, RIM)], True, [0, RIM])
    arrive_stage(edge, geometry, walls, moved, reds, final_rim)
    keep_moved(moved_rim, moved, reds, (3, live - 5))

    def copies_of(tile):
        row = pl.multiple_of(tile * SUBLANES, SUBLANES)
        return tile_copies(pieces, outs, row, row, sems.at[tile])

    def finish(tile, carry):
        row = pl.multiple_of(tile * SUBLANES, SUBLANES)
        arrive_stage(
            Block(geometry, [(row, row, SUBLANES)], inner=True), geometry, walls, moved, reds, final
        )
        gather_tiles(final, row, pieces, row)
        for copy in copies_of(tile):
            copy.start()
        return carry

    def settle(tile, carry):
        for copy in copies_of(tile):
            copy.wait()
        return carry

    last = live // SUBLANES - 1
    lax.fori_loop(1, last, finish, 0)
    lax.fori_loop(1, last, settle, 0)
    for tile in range(row_tiles):

        @pl.when(tile * SUBLANES >= live)
        def _():
            for copy in dead[tile]:
                copy.wait()


def rim_shape(count, rows):
    return jax.ShapeDtypeStruct((count, rows * SUBLANES, LANES), jnp.float32)


def run_first(info, whole):
    flat = whole.shape[1]
    shapes = [
        jax.ShapeDtypeStruct((MOVED, flat, LANES), jnp.float32),
        jax.ShapeDtypeStruct((REDS, flat, LANES), jnp.float32),
        rim_shape(MOVED + REDS, 4),
        rim_shape(FIELDS, 4),
    ]
    return pl.pallas_call(
        first_kernel,
        out_shape=shapes,
        in_specs=[SMEM, VMEM],
        out_specs=[VMEM] * len(shapes),
        scratch_shapes=[
            pltpu.VMEM((4, flat, LANES), jnp.float32),
            pltpu.VMEM((4, 3 * SUBLANES, LANES), jnp.float32),
            pltpu.VMEM((MOVED, flat, LANES), jnp.float32),
            pltpu.VMEM((REDS, flat, LANES), jnp.float32),
            pltpu.VMEM((FIELDS, flat, LANES), jnp.float32),
        ],
        compiler_params=pltpu.CompilerParams(vmem_limit_bytes=24 * 1024 * 1024),
        cost_estimate=pl.CostEstimate(flops=20_000_000, bytes_accessed=8_000_000, transcendentals=0),
        name="first",
    )(info, whole)


def run_second(info, moved, reds, arrived, arrays):
    flat = moved.shape[1]
    row_count, flat_count = arrays[0].shape
    shapes = [jax.ShapeDtypeStruct(array.shape, jnp.float32) for array in arrays[:4]]
    shapes = shapes + [rim_shape(MOVED + REDS, 4), rim_shape(FIELDS, 2 * RIM)]
    return pl.pallas_call(
        second_kernel,
        out_shape=shapes,
        in_specs=[SMEM, VMEM, VMEM, ANY],
        out_specs=[ANY] * 4 + [VMEM] * 2,
        scratch_shapes=[
            pltpu.VMEM((FIELDS, flat, LANES), jnp.float32),
            pltpu.VMEM((4, 3 * SUBLANES, LANES), jnp.float32),
            pltpu.VMEM((FIELDS, row_count, flat_count), jnp.float32),
            pltpu.VMEM((FIELDS, SUBLANES, flat_count), jnp.float32),
            pltpu.SemaphoreType.DMA((row_count // SUBLANES, 4)),
        ],
        compiler_params=pltpu.CompilerParams(vmem_limit_bytes=24 * 1024 * 1024),
        cost_estimate=pl.CostEstimate(flops=20_000_000, bytes_accessed=8_000_000, transcendentals=0),
        name="second",
    )(info, moved, reds, arrived)


def outer_kernel(
    info, whole, arrived, passed, moved_rim, fields_rim, moved_later_rim, final_rim, *refs,
):
    outs = refs[4:8]
    start_fields, colours, walls, moved, reds, fields, moved_later, reds_later, final = refs[8:17]
    pieces, sems = refs[17:]
    geometry = Geometry(info, OWN_TILES)
    live = geometry.live
    low_part = info[3] == 0
    fill_wall_table(walls, geometry)

    def receive(piece, index, low_row, high_row):
        here = pl.ds(piece * OWN_TILES, OWN_TILES)
        there = pl.ds(END_ROWS + piece * OWN_TILES, OWN_TILES)
        straight, crossed = (arrived[here, :], arrived[there, :]), (passed[there, :], passed[here, :])
        for row, first, second in ((low_row, straight, crossed), (high_row, crossed, straight)):
            own, other = [jnp.where(low_part, one, two) for one, two in zip(first, second)]
            start = row * SUBLANES
            below = jnp.where(low_part, 0.0, other[OWN_TILES - 1 :])
            above = jnp.where(low_part, other[:1], 0.0)
            start_fields[index, pl.ds(start, 1), :] = below
            start_fields[index, pl.ds(start + 1, OWN_TILES), :] = own
            start_fields[index, pl.ds(start + SUBLANES - 1, 1), :] = above

    def spans(first, count):
        mirrored = SLAB - first - count
        return [
            (first - HALO, first, count),
            (live - 2 * RIM + mirrored, SLAB + mirrored, count),
        ]

    for index in range(PLANES):
        for extra in range(FULL):
            receive(1 + FULL * index + extra, index, 1 + extra, 2 * SLAB - HALO + extra)
        start_fields[index, flat_rows(HALO, 2), :] = whole[index, flat_rows(0, 2), :]
        start_fields[index, flat_rows(2 * SLAB - HALO - 2, 2), :] = whole[
            index, flat_rows(live - 2, 2), :
        ]
    receive(0, 10, 0, 2 * SLAB - 1)
    for row in (0, 2 * SLAB - 1):
        start_fields[0, flat_rows(row, 1), :] = jnp.zeros((SUBLANES, LANES), jnp.float32)
        start_fields[10, flat_rows(row, 1), :] = 0.5 * start_fields[10, flat_rows(row, 1), :]

    def place(target, index, source, at, first, size):
        for place, (row, local, count) in enumerate(spans(first, size)):
            target[index, flat_rows(local, size), :] = source[at, flat_rows(place * size, size), :]

    for index in range(MOVED + REDS):
        target, later, at = moved, moved_later, index
        if index >= MOVED:
            target, later, at = reds, reds_later, index - MOVED
        place(target, at, moved_rim, index, HALO + 1, 2)
        place(later, at, moved_later_rim, index, HALO + 3, 2)
    for index in range(FIELDS):
        place(fields, index, fields_rim, index, HALO + 2, 2)
        place(final, index, final_rim, index, HALO + RIM, RIM)

    block = lambda first, count: Block(geometry, spans(first, count))
    colour_stage(block(0, 6), geometry, start_fields, colours)
    collide_stage(block(1, 4), geometry, start_fields, start_fields, colours, walls, moved, reds)
    arrive_stage(block(2, 4), geometry, walls, moved, reds, fields)
    start_fields[PLANES - 1, flat_rows(HALO + 2, 1), :] = whole[PLANES - 1, flat_rows(2, 1), :]
    start_fields[PLANES - 1, flat_rows(2 * SLAB - HALO - 3, 1), :] = whole[
        PLANES - 1, flat_rows(live - 3, 1), :
    ]
    colour_stage(block(2, 6), geometry, fields, colours)
    collide_stage(
        block(3, 4), geometry, fields, start_fields, colours, walls, moved_later, reds_later
    )
    arrive_stage(block(4, 4), geometry, walls, moved_later, reds_later, final)

    copies = []
    for side, row, out_row in ((0, HALO, 0), (1, SLAB, live - SUBLANES)):
        gather_tiles(final, row, pieces, side * SUBLANES)
        out_row = pl.multiple_of(out_row, SUBLANES)
        copies = copies + tile_copies(pieces, outs, side * SUBLANES, out_row, sems.at[side])
    for copy in copies:
        copy.start()
    for copy in copies:
        copy.wait()


def run_outer(info, whole, arrived, passed, rims, outs):
    flat = 2 * SLAB * SUBLANES
    flat_count = outs[0].shape[1]
    return pl.pallas_call(
        outer_kernel,
        out_shape=[jax.ShapeDtypeStruct(out.shape, jnp.float32) for out in outs],
        in_specs=[SMEM] + [VMEM] * 7 + [ANY] * 4,
        out_specs=[ANY] * 4,
        scratch_shapes=[
            pltpu.VMEM((PLANES, flat, LANES), jnp.float32),
            pltpu.VMEM((4, flat, LANES), jnp.float32),
            pltpu.VMEM((4, 3 * SUBLANES, LANES), jnp.float32),
            pltpu.VMEM((MOVED, flat, LANES), jnp.float32),
            pltpu.VMEM((REDS, flat, LANES), jnp.float32),
            pltpu.VMEM((FIELDS, flat, LANES), jnp.float32),
            pltpu.VMEM((MOVED, flat, LANES), jnp.float32),
            pltpu.VMEM((REDS, flat, LANES), jnp.float32),
            pltpu.VMEM((FIELDS, flat, LANES), jnp.float32),
            pltpu.VMEM((FIELDS, 2 * SUBLANES, flat_count), jnp.float32),
            pltpu.SemaphoreType.DMA((2, 4)),
        ],
        input_output_aliases={8: 0, 9: 1, 10: 2, 11: 3},
        compiler_params=pltpu.CompilerParams(vmem_limit_bytes=32 * 1024 * 1024),
        name="outer",
    )(info, whole, arrived, passed, *rims, *outs)


def body(density, momentum, stress, red_density, solid, widths):
    tiles_count = lax.axis_size("tiles")
    arrays = (density, momentum, stress, red_density, solid)
    info, spread, packet, mine = load_inputs(arrays, widths, tiles_count)
    swap = [(0, 1), (1, 0)]
    packet = lax.ppermute(packet, "sub", swap)
    whole, ends = join_parts(info, spread, packet, mine)
    route = [(2 * k, 2 * k + 2) for k in range(tiles_count - 1)]
    route = route + [(2 * k + 3, 2 * k + 1) for k in range(tiles_count - 1)]
    arrived = lax.ppermute(ends, ("tiles", "sub"), route)
    moved, reds, moved_rim, fields_rim = run_first(info, whole)
    arrived = lax.dynamic_update_slice(arrived, fields_rim[0, :1, :1], (END_ROWS - 1, 0))
    passed = lax.ppermute(arrived, "sub", swap)
    results = run_second(info, moved, reds, arrived, arrays)
    rims = (moved_rim, fields_rim) + tuple(results[4:])
    return tuple(run_outer(info, whole, arrived, passed, rims, results[:4]))


def solution(mesh):
    in_specs = (
        P(("groups", "tiles"), "sub"),
        P(None, ("groups", "tiles"), "sub"),
        P(None, ("groups", "tiles"), "sub"),
        P(("groups", "tiles"), "sub"),
        P(("groups", "tiles"), "sub"),
        P("groups"),
    )
    out_specs = (
        P(("groups", "tiles"), "sub"),
        P(None, ("groups", "tiles"), "sub"),
        P(None, ("groups", "tiles"), "sub"),
        P(("groups", "tiles"), "sub"),
    )
    return jax.shard_map(body, mesh=mesh, in_specs=in_specs, out_specs=out_specs, check_vma=False)
```

```python
import functools

import jax
import jax.numpy as jnp
from jax import lax
from jax.experimental import pallas as pl
from jax.experimental.pallas import tpu as pltpu
from jax.sharding import PartitionSpec as P

TILE = 16
STEPS = 2
RELAX_TIME = 0.8
SURFACE = 0.1
SEPARATION = 0.7

LANES = 128
SUBLANES = 8
FULL = 3
HALO = FULL + 1
FIELDS = 11
PLANES = FIELDS + 1
MOVED = 19
REDS = 5
RIM = 4
SLAB = HALO + 2 * RIM
OWN_TILES = SUBLANES - 2
GROUP = 4
PACKED = FULL * PLANES // GROUP * (GROUP - 1)
END_ROWS = (PACKED + 1) * SUBLANES
HALF = LANES // 2
PAIRS = PLANES // 2
COLOUR_BLOCK = (8, 1)
COLLIDE_BLOCK = (2, 4)
ARRIVE_BLOCK = (8, 1)
VMEM = pl.BlockSpec(memory_space=pltpu.VMEM)
SMEM = pl.BlockSpec(memory_space=pltpu.SMEM)
ANY = pl.BlockSpec(memory_space=pl.ANY)
HBM = pl.BlockSpec(memory_space=pltpu.HBM)


def roll_lanes(values, amount):
    return pltpu.roll(values, amount % LANES, 2)


class Geometry:
    def __init__(self, info, own_tiles):
        live, first, last, sub_index = info[0], info[1], info[2], info[3]
        self.live = live
        self.low_row = jnp.where(first == 1, 0, -1000)
        self.high_row = jnp.where(last == 1, live, 1000)
        shape = (1, SUBLANES, LANES)
        lane = lax.broadcasted_iota(jnp.int32, shape, 2)
        tile = lax.broadcasted_iota(jnp.int32, shape, 1)
        depth = lane & (TILE - 1)
        self.z_low = depth == 0
        self.z_high = depth == TILE - 1
        low_part = sub_index == 0
        high_part = sub_index == 1
        self.y_low = (tile == 1) & (lane < TILE) & low_part
        self.y_high = (tile == own_tiles) & (lane >= LANES - TILE) & high_part
        own = (tile >= 1) & (tile <= own_tiles)
        self.domain = own | ((tile == own_tiles + 1) & low_part) | ((tile == 0) & high_part)
        self.first_lanes = lane < TILE
        self.last_lanes = lane >= LANES - TILE

    def from_low_y(self, values, depth_shift=0, below=None):
        if below is None:
            below = pltpu.roll(values, 1, 1)
        return roll_lanes(jnp.where(self.last_lanes, below, values), TILE + depth_shift)

    def from_high_y(self, values, depth_shift=0, above=None):
        if above is None:
            above = pltpu.roll(values, SUBLANES - 1, 1)
        return roll_lanes(jnp.where(self.first_lanes, above, values), -TILE + depth_shift)

    def from_low_z(self, values):
        return jnp.where(self.z_low, 0.0, roll_lanes(values, 1))

    def from_high_z(self, values):
        return jnp.where(self.z_high, 0.0, roll_lanes(values, -1))


def flat_rows(row, count, tile_offset=0):
    start = row * SUBLANES
    if not isinstance(start, int):
        start = pl.multiple_of(start, SUBLANES)
    return pl.ds(start + tile_offset, count * SUBLANES)


class Block:
    def __init__(self, geometry, spans, inner=False, store_rows=None):
        self.spans = spans
        self.store_rows = store_rows or [local for row, local, count in spans]
        rows = [row + extra for row, local, count in spans for extra in range(count)]
        self.inner = inner
        if inner:
            self.x_low = self.x_high = None
            self.valid = geometry.domain
            self.kinds = [0]
            return
        shape = (1, SUBLANES, LANES)
        ids = jnp.concatenate([row + jnp.zeros(shape, jnp.int32) for row in rows], axis=0)
        self.x_low = ids == geometry.low_row
        self.x_high = ids == geometry.high_row - 1
        self.valid = geometry.domain & (ids >= geometry.low_row) & (ids < geometry.high_row)
        self.kinds = [
            jnp.where(row == geometry.low_row, 1, 0) + jnp.where(row == geometry.high_row - 1, 2, 0)
            for row in rows
        ]

    def load(self, ref, index, offset=0, tile_offset=0):
        parts = [
            ref[index, flat_rows(local + offset, count, tile_offset), :].reshape(
                count, SUBLANES, LANES
            )
            for row, local, count in self.spans
        ]
        return parts[0] if len(parts) == 1 else jnp.concatenate(parts, axis=0)

    def store(self, ref, index, values):
        done = 0
        for (row, local, count), target in zip(self.spans, self.store_rows):
            part = values[done : done + count].reshape(count * SUBLANES, LANES)
            ref[index, flat_rows(target, count), :] = part
            done += count

    def walls(self, walls, position):
        parts = [walls[position, flat_rows(kind, 1), :][None] for kind in self.kinds]
        return jnp.concatenate(parts, axis=0)


def fill_wall_table(walls, geometry):
    one = jnp.ones((1, SUBLANES, LANES), jnp.float32)
    up_y = jnp.where(geometry.y_high, 0.0, one)
    down_y = jnp.where(geometry.y_low, 0.0, one)
    up_z = jnp.where(geometry.z_high, 0.0, one)
    down_z = jnp.where(geometry.z_low, 0.0, one)
    sum_y, sum_z = up_y + down_y, up_z + down_z
    for kind, (up_x, down_x) in enumerate(((1.0, 1.0), (1.0, 0.0), (0.0, 1.0))):
        sum_x = up_x + down_x
        around_x = 2.0 + sum_y + sum_z
        total = 12.0 + 2.0 * (sum_x + sum_y + sum_z) + sum_x * (sum_y + sum_z) + sum_y * sum_z
        rows = (
            (up_x - down_x) * around_x,
            (up_y - down_y) * (2.0 + sum_x + sum_z),
            (up_z - down_z) * (2.0 + sum_x + sum_y),
            36.0 - total,
        )
        for position, row in enumerate(rows):
            walls[position, flat_rows(kind, 1), :] = row[0]


def colour_stage(block, geometry, fields, colours):
    density = block.load(fields, 0)
    red = block.load(fields, 10)
    colour = jnp.where(block.valid, 2.0 * red - density, 0.0)
    along_y = geometry.from_low_y(colour) + geometry.from_high_y(colour)
    along_z = geometry.from_low_z(colour) + geometry.from_high_z(colour)
    block.store(colours, 0, colour)
    block.store(colours, 1, 2.0 * colour + (along_y + along_z))
    block.store(colours, 2, along_y)
    block.store(colours, 3, along_z)


def collide_stage(block, geometry, fields, solids, colours, walls, moved, reds):
    relaxing = 1.0 - 1.0 / RELAX_TIME
    third = 1.0 / 3.0
    colour = block.load(colours, 0)
    doubled = 2.0 * colour + (block.load(colours, 0, -1) + block.load(colours, 0, 1))
    term_y = doubled + block.load(colours, 3)
    term_z = doubled + block.load(colours, 2)
    grad_x = block.load(colours, 1, 1) - block.load(colours, 1, -1)
    grad_y = geometry.from_high_y(term_y) - geometry.from_low_y(term_y)
    grad_z = geometry.from_high_z(term_z) - geometry.from_low_z(term_z)
    if not block.inner:
        grad_x = grad_x - block.walls(walls, 0) * colour
    grad_y = grad_y - block.walls(walls, 1) * colour
    grad_z = grad_z - block.walls(walls, 2) * colour

    fluid = block.load(solids, PLANES - 1) == 0.0
    density = block.load(fields, 0)
    red = block.load(fields, 10)
    flux = [block.load(fields, 1 + axis) for axis in range(3)]
    stress = [block.load(fields, 4 + part) for part in range(6)]
    square_xx, square_yy, square_zz = grad_x * grad_x, grad_y * grad_y, grad_z * grad_z
    square = square_xx + square_yy + square_zz
    inverse = jnp.where(fluid, lax.rsqrt(1.0 + square * (1.0 / 144.0)), 0.0)
    trace = third * square
    strength = (SURFACE / (8.0 * 144.0)) * inverse
    keep = jnp.where(fluid, relaxing / 8.0, 1.0 / 8.0)
    eighths = [0.125 * part for part in flux]
    own = [
        eighths[axis] * flux[axis] + (keep * stress[axis] + strength * (squared - trace))
        for axis, squared in enumerate((square_xx, square_yy, square_zz))
    ]
    strength, keep = 2.0 * strength, 2.0 * keep
    quarters = [2.0 * part for part in eighths[:2]]
    grads = (grad_x, grad_y, grad_z)
    cross = [
        quarters[a] * flux[b] + (keep * stress[3 + plane] + strength * (grads[a] * grads[b]))
        for plane, (a, b) in enumerate(((0, 1), (0, 2), (1, 2)))
    ]
    base = density * (1.0 / 36.0) - third * (own[0] + own[1] + own[2])
    sign = jnp.where(fluid, 1.0 / 12.0, -1.0 / 12.0)
    run = [sign * part for part in flux]
    mixing = ((SEPARATION / 144.0) * red) * ((density - red) * inverse)
    red_run = [0.5 * part + mixing * grad for part, grad in zip(run, grads)]
    block.store(moved, 0, 12.0 * base)
    straight = [base + part for part in own]
    for axis in range(3):
        middle = 2.0 * straight[axis]
        swing = 2.0 * run[axis]
        block.store(moved, 1 + 2 * axis, middle + swing)
        block.store(moved, 2 + 2 * axis, middle - swing)
    for plane, (a, b) in enumerate(((0, 1), (0, 2), (1, 2))):
        middle = straight[a] + own[b]
        same, other = middle + cross[plane], middle - cross[plane]
        along, against = run[a] + run[b], run[a] - run[b]
        first = 7 + 4 * plane
        block.store(moved, first, same + along)
        block.store(moved, first + 1, same - along)
        block.store(moved, first + 2, other + against)
        block.store(moved, first + 3, other - against)

    red_base = red * jnp.where(block.valid, 1.0 / 36.0, 0.0)
    red_run = [jnp.where(block.valid, part, 0.0) for part in red_run]
    block.store(reds, 0, red_base)
    block.store(reds, 1, red_base + red_run[0])
    block.store(reds, 2, red_base - red_run[0])
    block.store(reds, 3, red_run[1])
    block.store(reds, 4, red_run[2])


def arrive_stage(block, geometry, walls, moved, reds, fields):
    third = 1.0 / 3.0
    own = [None] * MOVED

    def here(direction):
        if own[direction] is None:
            own[direction] = block.load(moved, direction)
        return own[direction]

    def arrived(direction, opposite, velocity):
        vel_x, vel_y, vel_z = velocity
        values = here(direction) if vel_x == 0 else block.load(moved, direction, -vel_x)
        if vel_y == 1:
            below = block.load(moved, direction, -vel_x, -1)
            values = geometry.from_low_y(values, vel_z, below)
        elif vel_y == -1:
            above = block.load(moved, direction, -vel_x, 1)
            values = geometry.from_high_y(values, vel_z, above)
        elif vel_z != 0:
            values = roll_lanes(values, vel_z)
        masks = []
        if vel_x != 0 and block.x_low is not None:
            masks.append(block.x_low if vel_x == 1 else block.x_high)
        if vel_y != 0:
            masks.append(geometry.y_low if vel_y == 1 else geometry.y_high)
        if vel_z != 0:
            masks.append(geometry.z_low if vel_z == 1 else geometry.z_high)
        if not masks:
            return values
        wall = functools.reduce(lambda one, two: one | two, masks)
        return jnp.where(wall, here(opposite), values)

    red = block.load(reds, 0)
    red_y = block.load(reds, 3)
    red_z = block.load(reds, 4)
    from_x = block.load(reds, 1, -1) + block.load(reds, 2, 1)
    spread = 2.0 * red + from_x
    spread_y = 2.0 * red_y + (block.load(reds, 3, -1) + block.load(reds, 3, 1))
    spread_z = 2.0 * red_z + (block.load(reds, 4, -1) + block.load(reds, 4, 1))
    up_y, down_y = red + red_y, red - red_y
    low_y = (
        (spread + spread_y)
        + geometry.from_low_z(up_y + red_z)
        + geometry.from_high_z(up_y - red_z)
    )
    high_y = (
        (spread - spread_y)
        + geometry.from_low_z(down_y + red_z)
        + geometry.from_high_z(down_y - red_z)
    )
    bounced = (
        block.walls(walls, 3) * red
        - block.walls(walls, 1) * red_y
        - block.walls(walls, 2) * red_z
    )
    if not block.inner:
        bounced = bounced - block.walls(walls, 0) * (block.load(reds, 1) - red)
    red_total = (
        12.0 * red
        + 2.0 * from_x
        + geometry.from_low_z(spread + spread_z)
        + geometry.from_high_z(spread - spread_z)
        + geometry.from_low_y(low_y)
        + geometry.from_high_y(high_y)
        + bounced
    )
    rest = here(0)
    sums, diffs = [], []
    for axis in range(3):
        velocity = [0, 0, 0]
        velocity[axis] = 1
        up = arrived(1 + 2 * axis, 2 + 2 * axis, velocity)
        velocity[axis] = -1
        down = arrived(2 + 2 * axis, 1 + 2 * axis, velocity)
        sums.append(up + down)
        diffs.append(up - down)
    total = rest + sums[0] + sums[1] + sums[2]
    cross = []
    for plane, (a, b) in enumerate(((0, 1), (0, 2), (1, 2))):
        first = 7 + 4 * plane
        parts = []
        for offset, (vel_a, vel_b) in enumerate(((1, 1), (-1, -1), (1, -1), (-1, 1))):
            velocity = [0, 0, 0]
            velocity[a], velocity[b] = vel_a, vel_b
            parts.append(arrived(first + offset, first + (offset ^ 1), velocity))
        same, other = parts[0] + parts[1], parts[2] + parts[3]
        along, against = parts[0] - parts[1], parts[2] - parts[3]
        both = same + other
        cross.append(same - other)
        total = total + both
        sums[a], sums[b] = sums[a] + both, sums[b] + both
        diffs[a], diffs[b] = diffs[a] + (along + against), diffs[b] + (along - against)
    shared = third * total
    block.store(fields, 0, total)
    for axis in range(3):
        block.store(fields, 1 + axis, diffs[axis])
        block.store(fields, 4 + axis, sums[axis] - shared - diffs[axis] * diffs[axis])
    for plane, (a, b) in enumerate(((0, 1), (0, 2), (1, 2))):
        block.store(fields, 7 + plane, cross[plane] - diffs[a] * diffs[b])
    block.store(fields, 10, red_total)


def over_rows(geometry, first, end, size, blocks, stage):
    trip = size * blocks

    def step(index, carry):
        start = jnp.minimum(first + index * trip, end - trip)
        for number in range(blocks):
            row = start + number * size
            stage(Block(geometry, [(row, row, size)], inner=True))
        return carry

    lax.fori_loop(0, (end - first + trip - 1) // trip, step, 0)


def block_tiles():
    return lax.broadcasted_iota(jnp.int32, (SUBLANES, LANES), 0)


def roll_tiles(block, amount):
    return pltpu.roll(block, amount % SUBLANES, 0)


def pack_blocks(blocks):
    tiles, rest = block_tiles(), blocks[GROUP - 1]
    packed = []
    for number, block in enumerate(blocks[: GROUP - 1]):
        low, high = 2 * number + 1, 2 * number + 2
        block = jnp.where(tiles == 0, roll_tiles(rest, -low), block)
        packed.append(jnp.where(tiles == SUBLANES - 1, roll_tiles(rest, SUBLANES - 1 - high), block))
    return packed


def unpack_blocks(packed):
    tiles, rest = block_tiles(), None
    for number, block in enumerate(packed):
        low, high = 2 * number + 1, 2 * number + 2
        part = jnp.where(tiles == low, roll_tiles(block, low), roll_tiles(block, high - SUBLANES + 1))
        rest = part if rest is None else jnp.where(tiles >= low, part, rest)
    return list(packed) + [rest]


def load_kernel(
    tiles_count, density, momentum, stress, red, solid, widths,
    info, spread, packet, mine,
    raw, raw_solid, held_widths, sems,
):
    row_count, flat_count = raw_solid.shape
    own_tiles = flat_count // LANES
    copies = [
        pltpu.make_async_copy(widths, held_widths, sems.at[0]),
        pltpu.make_async_copy(density, raw.at[0], sems.at[1]),
        pltpu.make_async_copy(momentum, raw.at[pl.ds(1, 3)], sems.at[2]),
        pltpu.make_async_copy(red, raw.at[10], sems.at[3]),
        pltpu.make_async_copy(solid, raw_solid, sems.at[4]),
        pltpu.make_async_copy(stress.at[pl.ds(0, 3)], raw.at[pl.ds(4, 3)], sems.at[5]),
        pltpu.make_async_copy(stress.at[pl.ds(3, 3)], raw.at[pl.ds(7, 3)], sems.at[6]),
    ]
    for copy in copies:
        copy.start()
    tiles_index, sub_index = lax.axis_index("tiles"), lax.axis_index("sub")
    low_part = sub_index == 0
    edge_start = pl.multiple_of(jnp.where(low_part, (own_tiles - 1) * LANES, 0), LANES)

    copies[0].wait()
    live = held_widths[tiles_index] * TILE
    info[0] = live
    info[1] = (tiles_index == 0).astype(jnp.int32)
    info[2] = (tiles_index == tiles_count - 1).astype(jnp.int32)
    info[3] = sub_index

    near_cut = lax.broadcasted_iota(jnp.int32, (SUBLANES, LANES), 1) < HALF
    near_cut = near_cut == jnp.logical_not(low_part)
    ready = {0: copies[1], 1: copies[2], 10: copies[3], 11: copies[4], 4: copies[5], 7: copies[6]}
    for index in (0, 1, 2, 3, 10, 11, 4, 5, 6, 7, 8, 9):
        source = raw_solid if index == FIELDS else raw.at[index]
        if index in ready:
            ready[index].wait()
        for row in range(0, row_count, SUBLANES):
            rows = pl.ds(row, SUBLANES)
            for tile in range(own_tiles):
                values = source[rows, pl.ds(tile * LANES, LANES)].astype(jnp.float32)
                start = row * SUBLANES + 1 + tile
                spread[index, pl.ds(start, SUBLANES, stride=SUBLANES), :] = values

    edges = pl.ds(edge_start, LANES)
    for pair in range(PAIRS):
        later = raw_solid if pair + PAIRS == FIELDS else raw.at[pair + PAIRS]
        for row in range(0, row_count, SUBLANES):
            rows = pl.ds(row, SUBLANES)
            beside = pltpu.roll(later[rows, edges].astype(jnp.float32), HALF, 1)
            both = jnp.where(near_cut, raw[pair, rows, edges], beside)
            packet[pl.ds(pair * row_count + row, SUBLANES), :] = both

    after = PAIRS * row_count
    ends = (
        (packet, after, jnp.where(low_part, 0, live - FULL), jnp.where(low_part, FULL, live - HALO)),
        (mine, 0, jnp.where(low_part, live - FULL, 0), jnp.where(low_part, live - HALO, FULL)),
    )
    for target, at, full_row, colour_row in ends:
        rows = flat_rows(colour_row, 1)
        place = pl.ds(at + PACKED * SUBLANES, SUBLANES)
        target[place, :] = 2.0 * spread[10, rows, :] - spread[0, rows, :]
        for group in range(FULL * PLANES // GROUP):
            blocks = []
            for number in range(group * GROUP, (group + 1) * GROUP):
                index, extra = divmod(number, FULL)
                blocks.append(spread[index, flat_rows(full_row + extra, 1), :])
            for number, block in enumerate(pack_blocks(blocks)):
                place = at + (group * (GROUP - 1) + number) * SUBLANES
                target[pl.ds(place, SUBLANES), :] = block


def load_inputs(arrays, widths, tiles_count):
    row_count, flat_count = arrays[0].shape
    packet_rows = PAIRS * row_count + END_ROWS
    return pl.pallas_call(
        functools.partial(load_kernel, tiles_count),
        out_shape=[
            jax.ShapeDtypeStruct((4,), jnp.int32),
            jax.ShapeDtypeStruct((PLANES, row_count * SUBLANES, LANES), jnp.float32),
            jax.ShapeDtypeStruct((packet_rows, LANES), jnp.float32),
            jax.ShapeDtypeStruct((END_ROWS, LANES), jnp.float32),
        ],
        in_specs=[HBM] * 6,
        out_specs=[SMEM, VMEM, VMEM, VMEM],
        scratch_shapes=[
            pltpu.VMEM((FIELDS, row_count, flat_count), jnp.float32),
            pltpu.VMEM((row_count, flat_count), jnp.int32),
            pltpu.SMEM(widths.shape, jnp.int32),
            pltpu.SemaphoreType.DMA((7,)),
        ],
        compiler_params=pltpu.CompilerParams(vmem_limit_bytes=16 * 1024 * 1024),
        name="load",
    )(*[pltpu.with_memory_space_constraint(array, pltpu.HBM) for array in (*arrays, widths)])


def join_kernel(info, spread, packet, mine, whole, ends):
    low_part = info[3] == 0
    row_count = spread.shape[1] // SUBLANES
    ends[pl.ds(0, END_ROWS), :] = mine[...]
    ends[pl.ds(END_ROWS, END_ROWS), :] = packet[pl.ds(PAIRS * row_count, END_ROWS), :]
    for pair in range(PAIRS):
        for row in range(0, row_count, SUBLANES):
            both = packet[pl.ds(pair * row_count + row, SUBLANES), :]
            start = row * SUBLANES
            for index, values in ((pair, both), (pair + PAIRS, pltpu.roll(both, HALF, 1))):
                below = jnp.where(low_part, 0.0, values)
                above = jnp.where(low_part, values, 0.0)
                whole[index, pl.ds(start, SUBLANES, stride=SUBLANES), :] = below
                whole[index, pl.ds(start + SUBLANES - 1, SUBLANES, stride=SUBLANES), :] = above


def join_parts(info, spread, packet, mine):
    return pl.pallas_call(
        join_kernel,
        out_shape=[
            jax.ShapeDtypeStruct(spread.shape, jnp.float32),
            jax.ShapeDtypeStruct((2 * END_ROWS, LANES), jnp.float32),
        ],
        in_specs=[SMEM, VMEM, VMEM, VMEM],
        out_specs=[VMEM] * 2,
        input_output_aliases={1: 0},
        compiler_params=pltpu.CompilerParams(vmem_limit_bytes=16 * 1024 * 1024),
        name="join",
    )(info, pltpu.with_memory_space_constraint(spread, pltpu.VMEM), packet, mine)


def keep_rows(target, target_index, source, index, rows, size):
    for place, row in enumerate(rows):
        target[target_index, flat_rows(place * size, size), :] = source[
            index, flat_rows(row, size), :
        ]


def collide_rows(geometry, before, whole, first, scratch, moved, reds):
    colours, walls = scratch
    end = geometry.live - first
    over_rows(geometry, first - 1, end + 1, *COLOUR_BLOCK, lambda block: colour_stage(
        block, geometry, before, colours))
    over_rows(geometry, first, end, *COLLIDE_BLOCK, lambda block: collide_stage(
        block, geometry, before, whole, colours, walls, moved, reds))


def arrive_rows(geometry, first, walls, moved, reds, after):
    over_rows(geometry, first, geometry.live - first, *ARRIVE_BLOCK, lambda block: arrive_stage(
        block, geometry, walls, moved, reds, after))


def keep_moved(target, moved, reds, rows):
    for index in range(MOVED):
        keep_rows(target, index, moved, index, rows, 2)
    for index in range(REDS):
        keep_rows(target, MOVED + index, reds, index, rows, 2)


def first_kernel(info, whole, moved_later, reds_later, moved_rim, fields_rim, *scratch):
    colours, walls, moved, reds, fields = scratch
    geometry = Geometry(info, OWN_TILES)
    live = geometry.live
    fill_wall_table(walls, geometry)
    collide_rows(geometry, whole, whole, 1, (colours, walls), moved, reds)
    arrive_rows(geometry, 2, walls, moved, reds, fields)
    keep_moved(moved_rim, moved, reds, (1, live - 3))
    for index in range(FIELDS):
        keep_rows(fields_rim, index, fields, index, (2, live - 4), 2)
    collide_rows(geometry, fields, whole, 3, (colours, walls), moved_later, reds_later)


def tile_copies(pieces, outs, held_row, out_row, sems):
    held, rows = pl.ds(held_row, SUBLANES), pl.ds(out_row, SUBLANES)
    parts = (
        (pieces.at[0, held], outs[0].at[rows]),
        (pieces.at[pl.ds(1, 3), held], outs[1].at[:, rows]),
        (pieces.at[pl.ds(4, 6), held], outs[2].at[:, rows]),
        (pieces.at[10, held], outs[3].at[rows]),
    )
    return [
        pltpu.make_async_copy(source, target, sems.at[number])
        for number, (source, target) in enumerate(parts)
    ]


def gather_tiles(final, row, pieces, held_row):
    for index in range(FIELDS):
        for tile in range(OWN_TILES):
            start = pl.multiple_of(row * SUBLANES, SUBLANES) + 1 + tile
            pieces[index, pl.ds(held_row, SUBLANES), pl.ds(tile * LANES, LANES)] = final[
                index, pl.ds(start, SUBLANES, stride=SUBLANES), :
            ]


def second_kernel(
    info, moved, reds, arrived, density_out, momentum_out, stress_out, red_out,
    moved_rim, final_rim, final, walls, pieces, zeros, sems,
):
    outs = (density_out, momentum_out, stress_out, red_out)
    row_tiles = density_out.shape[0] // SUBLANES
    geometry = Geometry(info, OWN_TILES)
    live = geometry.live
    fill_wall_table(walls, geometry)

    zeros[...] = jnp.zeros(zeros.shape, zeros.dtype)
    dead = {}
    for tile in range(row_tiles):
        dead[tile] = tile_copies(zeros, outs, 0, tile * SUBLANES, sems.at[tile])

        @pl.when(tile * SUBLANES >= live)
        def _():
            for copy in dead[tile]:
                copy.start()

    edge = Block(geometry, [(RIM, RIM, RIM), (live - 2 * RIM, live - 2 * RIM, RIM)], True, [0, RIM])
    arrive_stage(edge, geometry, walls, moved, reds, final_rim)
    keep_moved(moved_rim, moved, reds, (3, live - 5))

    def copies_of(tile):
        row = pl.multiple_of(tile * SUBLANES, SUBLANES)
        return tile_copies(pieces, outs, row, row, sems.at[tile])

    def finish(tile, carry):
        row = pl.multiple_of(tile * SUBLANES, SUBLANES)
        arrive_stage(
            Block(geometry, [(row, row, SUBLANES)], inner=True), geometry, walls, moved, reds, final
        )
        gather_tiles(final, row, pieces, row)
        for copy in copies_of(tile):
            copy.start()
        return carry

    def settle(tile, carry):
        for copy in copies_of(tile):
            copy.wait()
        return carry

    last = live // SUBLANES - 1
    lax.fori_loop(1, last, finish, 0)
    lax.fori_loop(1, last, settle, 0)
    for tile in range(row_tiles):

        @pl.when(tile * SUBLANES >= live)
        def _():
            for copy in dead[tile]:
                copy.wait()


def rim_shape(count, rows):
    return jax.ShapeDtypeStruct((count, rows * SUBLANES, LANES), jnp.float32)


def run_first(info, whole):
    flat = whole.shape[1]
    shapes = [
        jax.ShapeDtypeStruct((MOVED, flat, LANES), jnp.float32),
        jax.ShapeDtypeStruct((REDS, flat, LANES), jnp.float32),
        rim_shape(MOVED + REDS, 4),
        rim_shape(FIELDS, 4),
    ]
    return pl.pallas_call(
        first_kernel,
        out_shape=shapes,
        in_specs=[SMEM, VMEM],
        out_specs=[VMEM] * len(shapes),
        scratch_shapes=[
            pltpu.VMEM((4, flat, LANES), jnp.float32),
            pltpu.VMEM((4, 3 * SUBLANES, LANES), jnp.float32),
            pltpu.VMEM((MOVED, flat, LANES), jnp.float32),
            pltpu.VMEM((REDS, flat, LANES), jnp.float32),
            pltpu.VMEM((FIELDS, flat, LANES), jnp.float32),
        ],
        compiler_params=pltpu.CompilerParams(vmem_limit_bytes=24 * 1024 * 1024),
        cost_estimate=pl.CostEstimate(flops=20_000_000, bytes_accessed=8_000_000, transcendentals=0),
        name="first",
    )(info, whole)


def run_second(info, moved, reds, arrived, arrays):
    flat = moved.shape[1]
    row_count, flat_count = arrays[0].shape
    shapes = [jax.ShapeDtypeStruct(array.shape, jnp.float32) for array in arrays[:4]]
    shapes = shapes + [rim_shape(MOVED + REDS, 4), rim_shape(FIELDS, 2 * RIM)]
    return pl.pallas_call(
        second_kernel,
        out_shape=shapes,
        in_specs=[SMEM, VMEM, VMEM, ANY],
        out_specs=[ANY] * 4 + [VMEM] * 2,
        scratch_shapes=[
            pltpu.VMEM((FIELDS, flat, LANES), jnp.float32),
            pltpu.VMEM((4, 3 * SUBLANES, LANES), jnp.float32),
            pltpu.VMEM((FIELDS, row_count, flat_count), jnp.float32),
            pltpu.VMEM((FIELDS, SUBLANES, flat_count), jnp.float32),
            pltpu.SemaphoreType.DMA((row_count // SUBLANES, 4)),
        ],
        compiler_params=pltpu.CompilerParams(vmem_limit_bytes=24 * 1024 * 1024),
        cost_estimate=pl.CostEstimate(flops=20_000_000, bytes_accessed=8_000_000, transcendentals=0),
        name="second",
    )(info, moved, reds, arrived)


def follow_kernel(ends, kept, out):
    out[pl.ds(PACKED * SUBLANES, 1), :] = jnp.zeros((1, LANES), jnp.float32)


def follow(ends, kept):
    return pl.pallas_call(
        follow_kernel,
        out_shape=jax.ShapeDtypeStruct(ends.shape, jnp.float32),
        in_specs=[VMEM, ANY],
        out_specs=VMEM,
        input_output_aliases={0: 0},
        compiler_params=pltpu.CompilerParams(vmem_limit_bytes=8 * 1024 * 1024),
        name="follow",
    )(pltpu.with_memory_space_constraint(ends, pltpu.VMEM), kept)


def outer_kernel(
    info, whole, arrived, passed, moved_rim, fields_rim, moved_later_rim, final_rim, *refs,
):
    outs = refs[4:8]
    start_fields, colours, walls, moved, reds, fields, moved_later, reds_later, final = refs[8:17]
    pieces, sems = refs[17:]
    geometry = Geometry(info, OWN_TILES)
    live = geometry.live
    low_part = info[3] == 0
    fill_wall_table(walls, geometry)

    def ends_of(ref, half):
        blocks = []
        for group in range(FULL * PLANES // GROUP):
            first = half * (PACKED + 1) + group * (GROUP - 1)
            packed = [ref[pl.ds((first + k) * SUBLANES, SUBLANES), :] for k in range(GROUP - 1)]
            blocks = blocks + unpack_blocks(packed)
        last = half * (PACKED + 1) + PACKED
        return blocks + [ref[pl.ds(last * SUBLANES, SUBLANES), :]]

    tiles = block_tiles()
    middle = (tiles >= 1) & (tiles <= OWN_TILES)
    inside = geometry.domain[0]

    def widened(own, other):
        beside = jnp.where(tiles == 0, roll_tiles(other, -OWN_TILES), roll_tiles(other, OWN_TILES))
        return jnp.where(inside, jnp.where(middle, own, beside), 0.0)

    straight = [widened(*pair) for pair in zip(ends_of(arrived, 0), ends_of(arrived, 1))]
    crossed = [widened(*pair) for pair in zip(ends_of(passed, 1), ends_of(passed, 0))]
    below = [jnp.where(low_part, *pair) for pair in zip(straight, crossed)]
    above = [jnp.where(low_part, *pair) for pair in zip(crossed, straight)]

    def spans(first, count):
        mirrored = SLAB - first - count
        return [
            (first - HALO, first, count),
            (live - 2 * RIM + mirrored, SLAB + mirrored, count),
        ]

    for index in range(PLANES):
        for extra in range(FULL):
            number = FULL * index + extra
            start_fields[index, flat_rows(1 + extra, 1), :] = below[number]
            start_fields[index, flat_rows(2 * SLAB - HALO + extra, 1), :] = above[number]
        start_fields[index, flat_rows(HALO, 2), :] = whole[index, flat_rows(0, 2), :]
        start_fields[index, flat_rows(2 * SLAB - HALO - 2, 2), :] = whole[
            index, flat_rows(live - 2, 2), :
        ]
    for row, colour in ((0, below[-1]), (2 * SLAB - 1, above[-1])):
        start_fields[0, flat_rows(row, 1), :] = jnp.zeros((SUBLANES, LANES), jnp.float32)
        start_fields[10, flat_rows(row, 1), :] = 0.5 * colour

    def place(target, index, source, at, first, size):
        for place, (row, local, count) in enumerate(spans(first, size)):
            target[index, flat_rows(local, size), :] = source[at, flat_rows(place * size, size), :]

    for index in range(MOVED + REDS):
        target, later, at = moved, moved_later, index
        if index >= MOVED:
            target, later, at = reds, reds_later, index - MOVED
        place(target, at, moved_rim, index, HALO + 1, 2)
        place(later, at, moved_later_rim, index, HALO + 3, 2)
    for index in range(FIELDS):
        place(fields, index, fields_rim, index, HALO + 2, 2)
        place(final, index, final_rim, index, HALO + RIM, RIM)

    block = lambda first, count: Block(geometry, spans(first, count))
    colour_stage(block(0, 6), geometry, start_fields, colours)
    collide_stage(block(1, 4), geometry, start_fields, start_fields, colours, walls, moved, reds)
    arrive_stage(block(2, 4), geometry, walls, moved, reds, fields)
    start_fields[PLANES - 1, flat_rows(HALO + 2, 1), :] = whole[PLANES - 1, flat_rows(2, 1), :]
    start_fields[PLANES - 1, flat_rows(2 * SLAB - HALO - 3, 1), :] = whole[
        PLANES - 1, flat_rows(live - 3, 1), :
    ]
    colour_stage(block(2, 6), geometry, fields, colours)
    collide_stage(
        block(3, 4), geometry, fields, start_fields, colours, walls, moved_later, reds_later
    )
    arrive_stage(block(4, 4), geometry, walls, moved_later, reds_later, final)

    copies = []
    for side, row, out_row in ((0, HALO, 0), (1, SLAB, live - SUBLANES)):
        gather_tiles(final, row, pieces, side * SUBLANES)
        out_row = pl.multiple_of(out_row, SUBLANES)
        copies = copies + tile_copies(pieces, outs, side * SUBLANES, out_row, sems.at[side])
    for copy in copies:
        copy.start()
    for copy in copies:
        copy.wait()


def run_outer(info, whole, arrived, passed, rims, outs):
    flat = 2 * SLAB * SUBLANES
    flat_count = outs[0].shape[1]
    return pl.pallas_call(
        outer_kernel,
        out_shape=[jax.ShapeDtypeStruct(out.shape, jnp.float32) for out in outs],
        in_specs=[SMEM] + [VMEM] * 7 + [ANY] * 4,
        out_specs=[ANY] * 4,
        scratch_shapes=[
            pltpu.VMEM((PLANES, flat, LANES), jnp.float32),
            pltpu.VMEM((4, flat, LANES), jnp.float32),
            pltpu.VMEM((4, 3 * SUBLANES, LANES), jnp.float32),
            pltpu.VMEM((MOVED, flat, LANES), jnp.float32),
            pltpu.VMEM((REDS, flat, LANES), jnp.float32),
            pltpu.VMEM((FIELDS, flat, LANES), jnp.float32),
            pltpu.VMEM((MOVED, flat, LANES), jnp.float32),
            pltpu.VMEM((REDS, flat, LANES), jnp.float32),
            pltpu.VMEM((FIELDS, flat, LANES), jnp.float32),
            pltpu.VMEM((FIELDS, 2 * SUBLANES, flat_count), jnp.float32),
            pltpu.SemaphoreType.DMA((2, 4)),
        ],
        input_output_aliases={8: 0, 9: 1, 10: 2, 11: 3},
        compiler_params=pltpu.CompilerParams(vmem_limit_bytes=32 * 1024 * 1024),
        name="outer",
    )(info, whole, arrived, passed, *rims, *outs)


def body(density, momentum, stress, red_density, solid, widths):
    tiles_count = lax.axis_size("tiles")
    arrays = (density, momentum, stress, red_density, solid)
    info, spread, packet, mine = load_inputs(arrays, widths, tiles_count)
    swap = [(0, 1), (1, 0)]
    packet = lax.ppermute(packet, "sub", swap)
    whole, ends = join_parts(info, spread, packet, mine)
    route = [(2 * k, 2 * k + 2) for k in range(tiles_count - 1)]
    route = route + [(2 * k + 3, 2 * k + 1) for k in range(tiles_count - 1)]
    arrived = lax.ppermute(ends, ("tiles", "sub"), route)
    moved, reds, moved_rim, fields_rim = run_first(info, whole)
    arrived = follow(arrived, fields_rim)
    passed = lax.ppermute(arrived, "sub", swap)
    results = run_second(info, moved, reds, arrived, arrays)
    rims = (moved_rim, fields_rim) + tuple(results[4:])
    return tuple(run_outer(info, whole, arrived, passed, rims, results[:4]))


def solution(mesh):
    in_specs = (
        P(("groups", "tiles"), "sub"),
        P(None, ("groups", "tiles"), "sub"),
        P(None, ("groups", "tiles"), "sub"),
        P(("groups", "tiles"), "sub"),
        P(("groups", "tiles"), "sub"),
        P("groups"),
    )
    out_specs = (
        P(("groups", "tiles"), "sub"),
        P(None, ("groups", "tiles"), "sub"),
        P(None, ("groups", "tiles"), "sub"),
        P(("groups", "tiles"), "sub"),
    )
    return jax.shard_map(body, mesh=mesh, in_specs=in_specs, out_specs=out_specs, check_vma=False)
```

```python
import functools

import jax
import jax.numpy as jnp
from jax import lax
from jax.experimental import pallas as pl
from jax.experimental.pallas import tpu as pltpu
from jax.sharding import PartitionSpec as P

TILE = 16
STEPS = 2
RELAX_TIME = 0.8
SURFACE = 0.1
SEPARATION = 0.7

LANES = 128
SUBLANES = 8
FULL = 3
HALO = FULL + 1
FIELDS = 11
PLANES = FIELDS + 1
MOVED = 19
REDS = 5
RIM = 4
SLAB = HALO + 2 * RIM
OWN_TILES = SUBLANES - 2
GROUP = 4
PACKED = FULL * PLANES // GROUP * (GROUP - 1)
END_ROWS = (PACKED + 1) * SUBLANES
HALF = LANES // 2
PAIRS = PLANES // 2
COLOUR_BLOCK = (8, 1)
COLLIDE_BLOCK = (2, 4)
ARRIVE_BLOCK = (8, 1)
VMEM = pl.BlockSpec(memory_space=pltpu.VMEM)
SMEM = pl.BlockSpec(memory_space=pltpu.SMEM)
ANY = pl.BlockSpec(memory_space=pl.ANY)
HBM = pl.BlockSpec(memory_space=pltpu.HBM)


class Rows:
    def __init__(self, parts):
        self.parts = parts

    def _with(self, other, operation):
        others = other.parts if isinstance(other, Rows) else [other] * len(self.parts)
        return Rows([operation(one, two) for one, two in zip(self.parts, others)])

    def __add__(self, other):
        return self._with(other, lambda one, two: one + two)

    def __sub__(self, other):
        return self._with(other, lambda one, two: one - two)

    def __rsub__(self, other):
        return self._with(other, lambda one, two: two - one)

    def __mul__(self, other):
        return self._with(other, lambda one, two: one * two)

    def __or__(self, other):
        return self._with(other, lambda one, two: one | two)

    def __eq__(self, other):
        return self._with(other, lambda one, two: one == two)

    __radd__, __rmul__, __ror__ = __add__, __mul__, __or__

    def each(self, operation):
        return Rows([operation(part) for part in self.parts])


def select(mask, yes, no):
    count = max(len(item.parts) for item in (mask, yes, no) if isinstance(item, Rows))
    columns = [
        item.parts if isinstance(item, Rows) else [item] * count for item in (mask, yes, no)
    ]
    return Rows([jnp.where(*row) for row in zip(*columns)])


def roll_lanes(values, amount):
    return values.each(lambda part: pltpu.roll(part, amount % LANES, 1))


def roll_sublanes(values, amount):
    return values.each(lambda part: pltpu.roll(part, amount % SUBLANES, 0))


class Geometry:
    def __init__(self, info, own_tiles):
        live, first, last, sub_index = info[0], info[1], info[2], info[3]
        self.live = live
        self.low_row = jnp.where(first == 1, 0, -1000)
        self.high_row = jnp.where(last == 1, live, 1000)
        shape = (SUBLANES, LANES)
        lane = lax.broadcasted_iota(jnp.int32, shape, 1)
        tile = lax.broadcasted_iota(jnp.int32, shape, 0)
        depth = lane & (TILE - 1)
        low_part = sub_index == 0
        high_part = sub_index == 1
        z_walls = {1: depth == 0, -1: depth == TILE - 1}
        y_walls = {
            1: (tile == 1) & (lane < TILE) & low_part,
            -1: (tile == own_tiles) & (lane >= LANES - TILE) & high_part,
        }
        self.walls = {(0, vel_z): wall for vel_z, wall in z_walls.items()}
        for vel_y, y_wall in y_walls.items():
            self.walls[vel_y, 0] = y_wall
            for vel_z, z_wall in z_walls.items():
                self.walls[vel_y, vel_z] = y_wall | z_wall
        own = (tile >= 1) & (tile <= own_tiles)
        self.domain = own | ((tile == own_tiles + 1) & low_part) | ((tile == 0) & high_part)
        self.first_lanes = lane < TILE
        self.last_lanes = lane >= LANES - TILE

    def from_low_y(self, values, depth_shift=0, below=None):
        if below is None:
            below = roll_sublanes(values, 1)
        return roll_lanes(select(self.last_lanes, below, values), TILE + depth_shift)

    def from_high_y(self, values, depth_shift=0, above=None):
        if above is None:
            above = roll_sublanes(values, -1)
        return roll_lanes(select(self.first_lanes, above, values), -TILE + depth_shift)

    def from_low_z(self, values):
        return select(self.walls[0, 1], 0.0, roll_lanes(values, 1))

    def from_high_z(self, values):
        return select(self.walls[0, -1], 0.0, roll_lanes(values, -1))


def flat_rows(row, count, tile_offset=0):
    start = row * SUBLANES
    if not isinstance(start, int):
        start = pl.multiple_of(start, SUBLANES)
    return pl.ds(start + tile_offset, count * SUBLANES)


class Block:
    def __init__(self, geometry, spans, inner=False, store_rows=None):
        self.spans = spans
        self.store_rows = store_rows or [local for row, local, count in spans]
        rows = [row + extra for row, local, count in spans for extra in range(count)]
        self.inner = inner
        rows = [row + extra for row, local, count in spans for extra in range(count)]
        if inner:
            self.x_walls = {}
            self.valid = geometry.domain
            self.kinds = [0]
            return
        ids = Rows([row + jnp.zeros((SUBLANES, LANES), jnp.int32) for row in rows])
        self.x_walls = {1: ids == geometry.low_row, -1: ids == geometry.high_row - 1}
        self.valid = ids.each(
            lambda part: geometry.domain & (part >= geometry.low_row) & (part < geometry.high_row)
        )
        self.kinds = [
            jnp.where(row == geometry.low_row, 1, 0) + jnp.where(row == geometry.high_row - 1, 2, 0)
            for row in rows
        ]

    def load(self, ref, index, offset=0, tile_offset=0):
        return Rows([
            ref[index, flat_rows(local + offset + extra, 1, tile_offset), :]
            for row, local, count in self.spans
            for extra in range(count)
        ])

    def store(self, ref, index, values):
        targets = [
            target + extra
            for (row, local, count), target in zip(self.spans, self.store_rows)
            for extra in range(count)
        ]
        for target, part in zip(targets, values.parts):
            ref[index, flat_rows(target, 1), :] = part

    def wall_terms(self, walls, position):
        terms = [walls[position, flat_rows(kind, 1), :] for kind in self.kinds]
        return terms[0] if self.inner else Rows(terms)


def fill_wall_table(walls, geometry):
    one = jnp.ones((SUBLANES, LANES), jnp.float32)
    up_y, down_y, up_z, down_z = [
        jnp.where(geometry.walls[key], 0.0, one) for key in ((-1, 0), (1, 0), (0, -1), (0, 1))
    ]
    sum_y, sum_z = up_y + down_y, up_z + down_z
    for kind, (up_x, down_x) in enumerate(((1.0, 1.0), (1.0, 0.0), (0.0, 1.0))):
        sum_x = up_x + down_x
        around_x = 2.0 + sum_y + sum_z
        total = 12.0 + 2.0 * (sum_x + sum_y + sum_z) + sum_x * (sum_y + sum_z) + sum_y * sum_z
        rows = (
            (up_x - down_x) * around_x,
            (up_y - down_y) * (2.0 + sum_x + sum_z),
            (up_z - down_z) * (2.0 + sum_x + sum_y),
            36.0 - total,
        )
        for position, row in enumerate(rows):
            walls[position, flat_rows(kind, 1), :] = row


def colour_stage(block, geometry, fields, colours):
    density = block.load(fields, 0)
    red = block.load(fields, 10)
    colour = select(block.valid, 2.0 * red - density, 0.0)
    along_y = geometry.from_low_y(colour) + geometry.from_high_y(colour)
    along_z = geometry.from_low_z(colour) + geometry.from_high_z(colour)
    block.store(colours, 0, colour)
    block.store(colours, 1, 2.0 * colour + (along_y + along_z))
    block.store(colours, 2, along_y)
    block.store(colours, 3, along_z)


def collide_stage(block, geometry, fields, solids, colours, walls, moved, reds):
    relaxing = 1.0 - 1.0 / RELAX_TIME
    third = 1.0 / 3.0
    colour = block.load(colours, 0)
    doubled = 2.0 * colour + (block.load(colours, 0, -1) + block.load(colours, 0, 1))
    term_y = doubled + block.load(colours, 3)
    term_z = doubled + block.load(colours, 2)
    grad_x = block.load(colours, 1, 1) - block.load(colours, 1, -1)
    grad_y = geometry.from_high_y(term_y) - geometry.from_low_y(term_y)
    grad_z = geometry.from_high_z(term_z) - geometry.from_low_z(term_z)
    if not block.inner:
        grad_x = grad_x - block.wall_terms(walls, 0) * colour
    grad_y = grad_y - block.wall_terms(walls, 1) * colour
    grad_z = grad_z - block.wall_terms(walls, 2) * colour

    fluid = block.load(solids, PLANES - 1) == 0.0
    density = block.load(fields, 0)
    red = block.load(fields, 10)
    flux = [block.load(fields, 1 + axis) for axis in range(3)]
    stress = [block.load(fields, 4 + part) for part in range(6)]
    square_xx, square_yy, square_zz = grad_x * grad_x, grad_y * grad_y, grad_z * grad_z
    square = square_xx + square_yy + square_zz
    inverse = select(fluid, (1.0 + square * (1.0 / 144.0)).each(lax.rsqrt), 0.0)
    trace = third * square
    strength = (SURFACE / (8.0 * 144.0)) * inverse
    keep = select(fluid, relaxing / 8.0, 1.0 / 8.0)
    eighths = [0.125 * part for part in flux]
    own = [
        eighths[axis] * flux[axis] + (keep * stress[axis] + strength * (squared - trace))
        for axis, squared in enumerate((square_xx, square_yy, square_zz))
    ]
    strength, keep = 2.0 * strength, 2.0 * keep
    quarters = [2.0 * part for part in eighths[:2]]
    grads = (grad_x, grad_y, grad_z)
    cross = [
        quarters[a] * flux[b] + (keep * stress[3 + plane] + strength * (grads[a] * grads[b]))
        for plane, (a, b) in enumerate(((0, 1), (0, 2), (1, 2)))
    ]
    base = density * (1.0 / 36.0) - third * (own[0] + own[1] + own[2])
    sign = select(fluid, 1.0 / 12.0, -1.0 / 12.0)
    run = [sign * part for part in flux]
    mixing = ((SEPARATION / 144.0) * red) * ((density - red) * inverse)
    red_run = [0.5 * part + mixing * grad for part, grad in zip(run, grads)]
    block.store(moved, 0, 12.0 * base)
    straight = [base + part for part in own]
    for axis in range(3):
        middle = 2.0 * straight[axis]
        swing = 2.0 * run[axis]
        block.store(moved, 1 + 2 * axis, middle + swing)
        block.store(moved, 2 + 2 * axis, middle - swing)
    for plane, (a, b) in enumerate(((0, 1), (0, 2), (1, 2))):
        middle = straight[a] + own[b]
        same, other = middle + cross[plane], middle - cross[plane]
        along, against = run[a] + run[b], run[a] - run[b]
        first = 7 + 4 * plane
        block.store(moved, first, same + along)
        block.store(moved, first + 1, same - along)
        block.store(moved, first + 2, other + against)
        block.store(moved, first + 3, other - against)

    red_base = select(block.valid, red * (1.0 / 36.0), 0.0)
    red_run = [select(block.valid, part, 0.0) for part in red_run]
    block.store(reds, 0, red_base)
    block.store(reds, 1, red_base + red_run[0])
    block.store(reds, 2, red_base - red_run[0])
    block.store(reds, 3, red_run[1])
    block.store(reds, 4, red_run[2])


def arrive_stage(block, geometry, walls, moved, reds, fields):
    third = 1.0 / 3.0
    own = [None] * MOVED

    def here(direction):
        if own[direction] is None:
            own[direction] = block.load(moved, direction)
        return own[direction]

    def arrived(direction, opposite, velocity):
        vel_x, vel_y, vel_z = velocity
        values = here(direction) if vel_x == 0 else block.load(moved, direction, -vel_x)
        if vel_y == 1:
            below = block.load(moved, direction, -vel_x, -1)
            values = geometry.from_low_y(values, vel_z, below)
        elif vel_y == -1:
            above = block.load(moved, direction, -vel_x, 1)
            values = geometry.from_high_y(values, vel_z, above)
        elif vel_z != 0:
            values = roll_lanes(values, vel_z)
        masks = []
        if vel_x in block.x_walls:
            masks.append(block.x_walls[vel_x])
        if (vel_y, vel_z) in geometry.walls:
            masks.append(geometry.walls[vel_y, vel_z])
        if not masks:
            return values
        wall = functools.reduce(lambda one, two: one | two, masks)
        return select(wall, here(opposite), values)

    red = block.load(reds, 0)
    red_y = block.load(reds, 3)
    red_z = block.load(reds, 4)
    from_x = block.load(reds, 1, -1) + block.load(reds, 2, 1)
    spread = 2.0 * red + from_x
    spread_y = 2.0 * red_y + (block.load(reds, 3, -1) + block.load(reds, 3, 1))
    spread_z = 2.0 * red_z + (block.load(reds, 4, -1) + block.load(reds, 4, 1))
    up_y, down_y = red + red_y, red - red_y
    low_y = (
        (spread + spread_y)
        + geometry.from_low_z(up_y + red_z)
        + geometry.from_high_z(up_y - red_z)
    )
    high_y = (
        (spread - spread_y)
        + geometry.from_low_z(down_y + red_z)
        + geometry.from_high_z(down_y - red_z)
    )
    bounced = (
        block.wall_terms(walls, 3) * red
        - block.wall_terms(walls, 1) * red_y
        - block.wall_terms(walls, 2) * red_z
    )
    if not block.inner:
        bounced = bounced - block.wall_terms(walls, 0) * (block.load(reds, 1) - red)
    red_total = (
        12.0 * red
        + 2.0 * from_x
        + geometry.from_low_z(spread + spread_z)
        + geometry.from_high_z(spread - spread_z)
        + geometry.from_low_y(low_y)
        + geometry.from_high_y(high_y)
        + bounced
    )
    rest = here(0)
    sums, diffs = [], []
    for axis in range(3):
        velocity = [0, 0, 0]
        velocity[axis] = 1
        up = arrived(1 + 2 * axis, 2 + 2 * axis, velocity)
        velocity[axis] = -1
        down = arrived(2 + 2 * axis, 1 + 2 * axis, velocity)
        sums.append(up + down)
        diffs.append(up - down)
    total = rest + sums[0] + sums[1] + sums[2]
    cross = []
    for plane, (a, b) in enumerate(((0, 1), (0, 2), (1, 2))):
        first = 7 + 4 * plane
        parts = []
        for offset, (vel_a, vel_b) in enumerate(((1, 1), (-1, -1), (1, -1), (-1, 1))):
            velocity = [0, 0, 0]
            velocity[a], velocity[b] = vel_a, vel_b
            parts.append(arrived(first + offset, first + (offset ^ 1), velocity))
        same, other = parts[0] + parts[1], parts[2] + parts[3]
        along, against = parts[0] - parts[1], parts[2] - parts[3]
        both = same + other
        cross.append(same - other)
        total = total + both
        sums[a], sums[b] = sums[a] + both, sums[b] + both
        diffs[a], diffs[b] = diffs[a] + (along + against), diffs[b] + (along - against)
    shared = third * total
    block.store(fields, 0, total)
    for axis in range(3):
        block.store(fields, 1 + axis, diffs[axis])
        block.store(fields, 4 + axis, sums[axis] - shared - diffs[axis] * diffs[axis])
    for plane, (a, b) in enumerate(((0, 1), (0, 2), (1, 2))):
        block.store(fields, 7 + plane, cross[plane] - diffs[a] * diffs[b])
    block.store(fields, 10, red_total)


def over_rows(geometry, first, end, size, blocks, stage):
    trip = size * blocks

    def step(index, carry):
        start = jnp.minimum(first + index * trip, end - trip)
        for number in range(blocks):
            row = start + number * size
            stage(Block(geometry, [(row, row, size)], inner=True))
        return carry

    lax.fori_loop(0, (end - first + trip - 1) // trip, step, 0)


def block_tiles():
    return lax.broadcasted_iota(jnp.int32, (SUBLANES, LANES), 0)


def roll_tiles(block, amount):
    return pltpu.roll(block, amount % SUBLANES, 0)


def pack_blocks(blocks):
    tiles, rest = block_tiles(), blocks[GROUP - 1]
    packed = []
    for number, block in enumerate(blocks[: GROUP - 1]):
        low, high = 2 * number + 1, 2 * number + 2
        block = jnp.where(tiles == 0, roll_tiles(rest, -low), block)
        packed.append(jnp.where(tiles == SUBLANES - 1, roll_tiles(rest, SUBLANES - 1 - high), block))
    return packed


def unpack_blocks(packed):
    tiles, rest = block_tiles(), None
    for number, block in enumerate(packed):
        low, high = 2 * number + 1, 2 * number + 2
        part = jnp.where(tiles == low, roll_tiles(block, low), roll_tiles(block, high - SUBLANES + 1))
        rest = part if rest is None else jnp.where(tiles >= low, part, rest)
    return list(packed) + [rest]


def spread_tile(raw, raw_solid, index, row, target, target_row):
    source = raw_solid if index == FIELDS else raw.at[index]
    for tile in range(OWN_TILES):
        values = source[pl.ds(row, SUBLANES), pl.ds(tile * LANES, LANES)].astype(jnp.float32)
        start = target_row * SUBLANES + 1 + tile
        target[index, pl.ds(start, SUBLANES, stride=SUBLANES), :] = values


def load_kernel(
    tiles_count, density, momentum, stress, red, solid, widths,
    info, raw, raw_solid, packet, mine,
    first_tile, last_tile, held_widths, sems,
):
    row_count, flat_count = raw_solid.shape
    own_tiles = flat_count // LANES
    copies = [
        pltpu.make_async_copy(widths, held_widths, sems.at[0]),
        pltpu.make_async_copy(density, raw.at[0], sems.at[1]),
        pltpu.make_async_copy(momentum, raw.at[pl.ds(1, 3)], sems.at[2]),
        pltpu.make_async_copy(red, raw.at[10], sems.at[3]),
        pltpu.make_async_copy(solid, raw_solid, sems.at[4]),
        pltpu.make_async_copy(stress.at[pl.ds(0, 3)], raw.at[pl.ds(4, 3)], sems.at[5]),
        pltpu.make_async_copy(stress.at[pl.ds(3, 3)], raw.at[pl.ds(7, 3)], sems.at[6]),
    ]
    for copy in copies:
        copy.start()
    tiles_index, sub_index = lax.axis_index("tiles"), lax.axis_index("sub")
    low_part = sub_index == 0
    edge_start = pl.multiple_of(jnp.where(low_part, (own_tiles - 1) * LANES, 0), LANES)

    copies[0].wait()
    live = held_widths[tiles_index] * TILE
    info[0] = live
    info[1] = (tiles_index == 0).astype(jnp.int32)
    info[2] = (tiles_index == tiles_count - 1).astype(jnp.int32)
    info[3] = sub_index

    near_cut = lax.broadcasted_iota(jnp.int32, (SUBLANES, LANES), 1) < HALF
    near_cut = near_cut == jnp.logical_not(low_part)
    near_last = pl.multiple_of(live - SUBLANES, SUBLANES)
    ready = {0: copies[1], 1: copies[2], 10: copies[3], 11: copies[4], 4: copies[5], 7: copies[6]}
    for index in (0, 1, 2, 3, 10, 11, 4, 5, 6, 7, 8, 9):
        if index in ready:
            ready[index].wait()
        for target, row in ((first_tile, 0), (last_tile, near_last)):
            spread_tile(raw, raw_solid, index, row, target, 0)

    edges = pl.ds(edge_start, LANES)
    for pair in range(PAIRS):
        later = raw_solid if pair + PAIRS == FIELDS else raw.at[pair + PAIRS]
        for row in range(0, row_count, SUBLANES):
            rows = pl.ds(row, SUBLANES)
            beside = pltpu.roll(later[rows, edges].astype(jnp.float32), HALF, 1)
            both = jnp.where(near_cut, raw[pair, rows, edges], beside)
            packet[pl.ds(pair * row_count + row, SUBLANES), :] = both

    after = PAIRS * row_count
    ends = ((packet, after, jnp.logical_not(low_part)), (mine, 0, low_part))
    for target, at, use_last in ends:
        def row_of(index, number_first, number_last):
            first = first_tile[index, flat_rows(number_first, 1), :]
            last = last_tile[index, flat_rows(number_last, 1), :]
            return jnp.where(use_last, last, first)

        place = pl.ds(at + PACKED * SUBLANES, SUBLANES)
        ends_row = (FULL, SUBLANES - HALO)
        target[place, :] = 2.0 * row_of(10, *ends_row) - row_of(0, *ends_row)
        for group in range(FULL * PLANES // GROUP):
            blocks = []
            for number in range(group * GROUP, (group + 1) * GROUP):
                index, extra = divmod(number, FULL)
                blocks.append(row_of(index, extra, SUBLANES - FULL + extra))
            for number, block in enumerate(pack_blocks(blocks)):
                place = at + (group * (GROUP - 1) + number) * SUBLANES
                target[pl.ds(place, SUBLANES), :] = block


def load_inputs(arrays, widths, tiles_count):
    row_count, flat_count = arrays[0].shape
    packet_rows = PAIRS * row_count + END_ROWS
    return pl.pallas_call(
        functools.partial(load_kernel, tiles_count),
        out_shape=[
            pltpu.SMEM((4,), jnp.int32),
            jax.ShapeDtypeStruct((FIELDS, row_count, flat_count), jnp.float32),
            jax.ShapeDtypeStruct((row_count, flat_count), jnp.int32),
            jax.ShapeDtypeStruct((packet_rows, LANES), jnp.float32),
            jax.ShapeDtypeStruct((END_ROWS, LANES), jnp.float32),
        ],
        in_specs=[HBM] * 6,
        out_specs=[SMEM, VMEM, VMEM, VMEM, VMEM],
        scratch_shapes=[
            pltpu.VMEM((PLANES, SUBLANES * SUBLANES, LANES), jnp.float32),
            pltpu.VMEM((PLANES, SUBLANES * SUBLANES, LANES), jnp.float32),
            pltpu.SMEM(widths.shape, jnp.int32),
            pltpu.SemaphoreType.DMA((7,)),
        ],
        compiler_params=pltpu.CompilerParams(vmem_limit_bytes=16 * 1024 * 1024),
        name="load",
    )(*[pltpu.with_memory_space_constraint(array, pltpu.HBM) for array in (*arrays, widths)])


def spread_kernel(raw, raw_solid, spread):
    for index in range(PLANES):
        for row in range(0, raw_solid.shape[0], SUBLANES):
            spread_tile(raw, raw_solid, index, row, spread, row)


def spread_rows(raw, raw_solid):
    row_count = raw_solid.shape[0]
    return pl.pallas_call(
        spread_kernel,
        out_shape=jax.ShapeDtypeStruct((PLANES, row_count * SUBLANES, LANES), jnp.float32),
        in_specs=[VMEM, VMEM],
        out_specs=VMEM,
        compiler_params=pltpu.CompilerParams(vmem_limit_bytes=16 * 1024 * 1024),
        cost_estimate=pl.CostEstimate(flops=1_000_000, bytes_accessed=4_000_000, transcendentals=0),
        name="spread",
    )(raw, raw_solid)


def join_kernel(info, spread, packet, mine, whole, ends):
    low_part = info[3] == 0
    row_count = spread.shape[1] // SUBLANES
    ends[pl.ds(0, END_ROWS), :] = mine[...]
    ends[pl.ds(END_ROWS, END_ROWS), :] = packet[pl.ds(PAIRS * row_count, END_ROWS), :]
    for pair in range(PAIRS):
        for row in range(0, row_count, SUBLANES):
            both = packet[pl.ds(pair * row_count + row, SUBLANES), :]
            start = row * SUBLANES
            for index, values in ((pair, both), (pair + PAIRS, pltpu.roll(both, HALF, 1))):
                below = jnp.where(low_part, 0.0, values)
                above = jnp.where(low_part, values, 0.0)
                whole[index, pl.ds(start, SUBLANES, stride=SUBLANES), :] = below
                whole[index, pl.ds(start + SUBLANES - 1, SUBLANES, stride=SUBLANES), :] = above


def join_parts(info, spread, packet, mine):
    return pl.pallas_call(
        join_kernel,
        out_shape=[
            jax.ShapeDtypeStruct(spread.shape, jnp.float32),
            jax.ShapeDtypeStruct((2 * END_ROWS, LANES), jnp.float32),
        ],
        in_specs=[SMEM, VMEM, VMEM, VMEM],
        out_specs=[VMEM] * 2,
        input_output_aliases={1: 0},
        compiler_params=pltpu.CompilerParams(vmem_limit_bytes=16 * 1024 * 1024),
        name="join",
    )(info, pltpu.with_memory_space_constraint(spread, pltpu.VMEM), packet, mine)


def keep_rows(target, target_index, source, index, rows, size):
    for place, row in enumerate(rows):
        target[target_index, flat_rows(place * size, size), :] = source[
            index, flat_rows(row, size), :
        ]


def collide_rows(geometry, before, whole, first, scratch, moved, reds):
    colours, walls = scratch
    end = geometry.live - first
    over_rows(geometry, first - 1, end + 1, *COLOUR_BLOCK, lambda block: colour_stage(
        block, geometry, before, colours))
    over_rows(geometry, first, end, *COLLIDE_BLOCK, lambda block: collide_stage(
        block, geometry, before, whole, colours, walls, moved, reds))


def arrive_rows(geometry, first, walls, moved, reds, after):
    over_rows(geometry, first, geometry.live - first, *ARRIVE_BLOCK, lambda block: arrive_stage(
        block, geometry, walls, moved, reds, after))


def keep_moved(target, moved, reds, rows):
    for index in range(MOVED):
        keep_rows(target, index, moved, index, rows, 2)
    for index in range(REDS):
        keep_rows(target, MOVED + index, reds, index, rows, 2)


def first_kernel(info, whole, moved_later, reds_later, moved_rim, fields_rim, *scratch):
    colours, walls, moved, reds, fields = scratch
    geometry = Geometry(info, OWN_TILES)
    live = geometry.live
    fill_wall_table(walls, geometry)
    collide_rows(geometry, whole, whole, 1, (colours, walls), moved, reds)
    arrive_rows(geometry, 2, walls, moved, reds, fields)
    keep_moved(moved_rim, moved, reds, (1, live - 3))
    for index in range(FIELDS):
        keep_rows(fields_rim, index, fields, index, (2, live - 4), 2)
    collide_rows(geometry, fields, whole, 3, (colours, walls), moved_later, reds_later)


def tile_copies(pieces, outs, held_row, out_row, sems):
    held, rows = pl.ds(held_row, SUBLANES), pl.ds(out_row, SUBLANES)
    parts = (
        (pieces.at[0, held], outs[0].at[rows]),
        (pieces.at[pl.ds(1, 3), held], outs[1].at[:, rows]),
        (pieces.at[pl.ds(4, 6), held], outs[2].at[:, rows]),
        (pieces.at[10, held], outs[3].at[rows]),
    )
    return [
        pltpu.make_async_copy(source, target, sems.at[number])
        for number, (source, target) in enumerate(parts)
    ]


def gather_tiles(final, row, pieces, held_row):
    for index in range(FIELDS):
        for tile in range(OWN_TILES):
            start = pl.multiple_of(row * SUBLANES, SUBLANES) + 1 + tile
            pieces[index, pl.ds(held_row, SUBLANES), pl.ds(tile * LANES, LANES)] = final[
                index, pl.ds(start, SUBLANES, stride=SUBLANES), :
            ]


def second_kernel(
    info, moved, reds, arrived, density_out, momentum_out, stress_out, red_out,
    moved_rim, final_rim, final, walls, pieces, zeros, sems,
):
    outs = (density_out, momentum_out, stress_out, red_out)
    row_tiles = density_out.shape[0] // SUBLANES
    geometry = Geometry(info, OWN_TILES)
    live = geometry.live
    fill_wall_table(walls, geometry)

    zeros[...] = jnp.zeros(zeros.shape, zeros.dtype)
    dead = {}
    for tile in range(row_tiles):
        dead[tile] = tile_copies(zeros, outs, 0, tile * SUBLANES, sems.at[tile])

        @pl.when(tile * SUBLANES >= live)
        def _():
            for copy in dead[tile]:
                copy.start()

    edge = Block(geometry, [(RIM, RIM, RIM), (live - 2 * RIM, live - 2 * RIM, RIM)], True, [0, RIM])
    arrive_stage(edge, geometry, walls, moved, reds, final_rim)
    keep_moved(moved_rim, moved, reds, (3, live - 5))

    def copies_of(tile):
        row = pl.multiple_of(tile * SUBLANES, SUBLANES)
        return tile_copies(pieces, outs, row, row, sems.at[tile])

    def finish(tile, carry):
        row = pl.multiple_of(tile * SUBLANES, SUBLANES)
        arrive_stage(
            Block(geometry, [(row, row, SUBLANES)], inner=True), geometry, walls, moved, reds, final
        )
        gather_tiles(final, row, pieces, row)
        for copy in copies_of(tile):
            copy.start()
        return carry

    def settle(tile, carry):
        for copy in copies_of(tile):
            copy.wait()
        return carry

    last = live // SUBLANES - 1
    lax.fori_loop(1, last, finish, 0)
    lax.fori_loop(1, last, settle, 0)
    for tile in range(row_tiles):

        @pl.when(tile * SUBLANES >= live)
        def _():
            for copy in dead[tile]:
                copy.wait()


def rim_shape(count, rows):
    return jax.ShapeDtypeStruct((count, rows * SUBLANES, LANES), jnp.float32)


def run_first(info, whole):
    flat = whole.shape[1]
    shapes = [
        jax.ShapeDtypeStruct((MOVED, flat, LANES), jnp.float32),
        jax.ShapeDtypeStruct((REDS, flat, LANES), jnp.float32),
        rim_shape(MOVED + REDS, 4),
        rim_shape(FIELDS, 4),
    ]
    return pl.pallas_call(
        first_kernel,
        out_shape=shapes,
        in_specs=[SMEM, VMEM],
        out_specs=[VMEM] * len(shapes),
        scratch_shapes=[
            pltpu.VMEM((4, flat, LANES), jnp.float32),
            pltpu.VMEM((4, 3 * SUBLANES, LANES), jnp.float32),
            pltpu.VMEM((MOVED, flat, LANES), jnp.float32),
            pltpu.VMEM((REDS, flat, LANES), jnp.float32),
            pltpu.VMEM((FIELDS, flat, LANES), jnp.float32),
        ],
        compiler_params=pltpu.CompilerParams(vmem_limit_bytes=24 * 1024 * 1024),
        cost_estimate=pl.CostEstimate(flops=20_000_000, bytes_accessed=8_000_000, transcendentals=0),
        name="first",
    )(info, whole)


def run_second(info, moved, reds, arrived, arrays):
    flat = moved.shape[1]
    row_count, flat_count = arrays[0].shape
    shapes = [jax.ShapeDtypeStruct(array.shape, jnp.float32) for array in arrays[:4]]
    shapes = shapes + [rim_shape(MOVED + REDS, 4), rim_shape(FIELDS, 2 * RIM)]
    return pl.pallas_call(
        second_kernel,
        out_shape=shapes,
        in_specs=[SMEM, VMEM, VMEM, ANY],
        out_specs=[ANY] * 4 + [VMEM] * 2,
        scratch_shapes=[
            pltpu.VMEM((FIELDS, flat, LANES), jnp.float32),
            pltpu.VMEM((4, 3 * SUBLANES, LANES), jnp.float32),
            pltpu.VMEM((FIELDS, row_count, flat_count), jnp.float32),
            pltpu.VMEM((FIELDS, SUBLANES, flat_count), jnp.float32),
            pltpu.SemaphoreType.DMA((row_count // SUBLANES, 4)),
        ],
        compiler_params=pltpu.CompilerParams(vmem_limit_bytes=24 * 1024 * 1024),
        cost_estimate=pl.CostEstimate(flops=20_000_000, bytes_accessed=8_000_000, transcendentals=0),
        name="second",
    )(info, moved, reds, arrived)


def follow_kernel(ends, kept, out):
    out[pl.ds(PACKED * SUBLANES, 1), :] = jnp.zeros((1, LANES), jnp.float32)


def follow(ends, kept):
    return pl.pallas_call(
        follow_kernel,
        out_shape=jax.ShapeDtypeStruct(ends.shape, jnp.float32),
        in_specs=[VMEM, ANY],
        out_specs=VMEM,
        input_output_aliases={0: 0},
        compiler_params=pltpu.CompilerParams(vmem_limit_bytes=8 * 1024 * 1024),
        name="follow",
    )(pltpu.with_memory_space_constraint(ends, pltpu.VMEM), kept)


def outer_kernel(
    info, whole, arrived, passed, moved_rim, fields_rim, moved_later_rim, final_rim, *refs,
):
    outs = refs[4:8]
    start_fields, colours, walls, moved, reds, fields, moved_later, reds_later, final = refs[8:17]
    pieces, sems = refs[17:]
    geometry = Geometry(info, OWN_TILES)
    live = geometry.live
    low_part = info[3] == 0
    fill_wall_table(walls, geometry)

    def ends_of(ref, half):
        blocks = []
        for group in range(FULL * PLANES // GROUP):
            first = half * (PACKED + 1) + group * (GROUP - 1)
            packed = [ref[pl.ds((first + k) * SUBLANES, SUBLANES), :] for k in range(GROUP - 1)]
            blocks = blocks + unpack_blocks(packed)
        last = half * (PACKED + 1) + PACKED
        return blocks + [ref[pl.ds(last * SUBLANES, SUBLANES), :]]

    tiles = block_tiles()
    middle = (tiles >= 1) & (tiles <= OWN_TILES)

    def widened(own, other):
        beside = jnp.where(tiles == 0, roll_tiles(other, -OWN_TILES), roll_tiles(other, OWN_TILES))
        return jnp.where(geometry.domain, jnp.where(middle, own, beside), 0.0)

    straight = [widened(*pair) for pair in zip(ends_of(arrived, 0), ends_of(arrived, 1))]
    crossed = [widened(*pair) for pair in zip(ends_of(passed, 1), ends_of(passed, 0))]
    below = [jnp.where(low_part, *pair) for pair in zip(straight, crossed)]
    above = [jnp.where(low_part, *pair) for pair in zip(crossed, straight)]

    def spans(first, count):
        mirrored = SLAB - first - count
        return [
            (first - HALO, first, count),
            (live - 2 * RIM + mirrored, SLAB + mirrored, count),
        ]

    for index in range(PLANES):
        for extra in range(FULL):
            number = FULL * index + extra
            start_fields[index, flat_rows(1 + extra, 1), :] = below[number]
            start_fields[index, flat_rows(2 * SLAB - HALO + extra, 1), :] = above[number]
        start_fields[index, flat_rows(HALO, 2), :] = whole[index, flat_rows(0, 2), :]
        start_fields[index, flat_rows(2 * SLAB - HALO - 2, 2), :] = whole[
            index, flat_rows(live - 2, 2), :
        ]
    for row, colour in ((0, below[-1]), (2 * SLAB - 1, above[-1])):
        start_fields[0, flat_rows(row, 1), :] = jnp.zeros((SUBLANES, LANES), jnp.float32)
        start_fields[10, flat_rows(row, 1), :] = 0.5 * colour

    def place(target, index, source, at, first, size):
        for place, (row, local, count) in enumerate(spans(first, size)):
            target[index, flat_rows(local, size), :] = source[at, flat_rows(place * size, size), :]

    for index in range(MOVED + REDS):
        target, later, at = moved, moved_later, index
        if index >= MOVED:
            target, later, at = reds, reds_later, index - MOVED
        place(target, at, moved_rim, index, HALO + 1, 2)
        place(later, at, moved_later_rim, index, HALO + 3, 2)
    for index in range(FIELDS):
        place(fields, index, fields_rim, index, HALO + 2, 2)
        place(final, index, final_rim, index, HALO + RIM, RIM)

    block = lambda first, count: Block(geometry, spans(first, count))
    colour_stage(block(0, 6), geometry, start_fields, colours)
    collide_stage(block(1, 4), geometry, start_fields, start_fields, colours, walls, moved, reds)
    arrive_stage(block(2, 4), geometry, walls, moved, reds, fields)
    start_fields[PLANES - 1, flat_rows(HALO + 2, 1), :] = whole[PLANES - 1, flat_rows(2, 1), :]
    start_fields[PLANES - 1, flat_rows(2 * SLAB - HALO - 3, 1), :] = whole[
        PLANES - 1, flat_rows(live - 3, 1), :
    ]
    colour_stage(block(2, 6), geometry, fields, colours)
    collide_stage(
        block(3, 4), geometry, fields, start_fields, colours, walls, moved_later, reds_later
    )
    arrive_stage(block(4, 4), geometry, walls, moved_later, reds_later, final)

    copies = []
    for side, row, out_row in ((0, HALO, 0), (1, SLAB, live - SUBLANES)):
        gather_tiles(final, row, pieces, side * SUBLANES)
        out_row = pl.multiple_of(out_row, SUBLANES)
        copies = copies + tile_copies(pieces, outs, side * SUBLANES, out_row, sems.at[side])
    for copy in copies:
        copy.start()
    for copy in copies:
        copy.wait()


def run_outer(info, whole, arrived, passed, rims, outs):
    flat = 2 * SLAB * SUBLANES
    flat_count = outs[0].shape[1]
    return pl.pallas_call(
        outer_kernel,
        out_shape=[jax.ShapeDtypeStruct(out.shape, jnp.float32) for out in outs],
        in_specs=[SMEM] + [VMEM] * 7 + [ANY] * 4,
        out_specs=[ANY] * 4,
        scratch_shapes=[
            pltpu.VMEM((PLANES, flat, LANES), jnp.float32),
            pltpu.VMEM((4, flat, LANES), jnp.float32),
            pltpu.VMEM((4, 3 * SUBLANES, LANES), jnp.float32),
            pltpu.VMEM((MOVED, flat, LANES), jnp.float32),
            pltpu.VMEM((REDS, flat, LANES), jnp.float32),
            pltpu.VMEM((FIELDS, flat, LANES), jnp.float32),
            pltpu.VMEM((MOVED, flat, LANES), jnp.float32),
            pltpu.VMEM((REDS, flat, LANES), jnp.float32),
            pltpu.VMEM((FIELDS, flat, LANES), jnp.float32),
            pltpu.VMEM((FIELDS, 2 * SUBLANES, flat_count), jnp.float32),
            pltpu.SemaphoreType.DMA((2, 4)),
        ],
        input_output_aliases={8: 0, 9: 1, 10: 2, 11: 3},
        compiler_params=pltpu.CompilerParams(vmem_limit_bytes=32 * 1024 * 1024),
        name="outer",
    )(info, whole, arrived, passed, *rims, *outs)


def body(density, momentum, stress, red_density, solid, widths):
    tiles_count = lax.axis_size("tiles")
    arrays = (density, momentum, stress, red_density, solid)
    info, raw, raw_solid, packet, mine = load_inputs(arrays, widths, tiles_count)
    info = pltpu.with_memory_space_constraint(info, pltpu.SMEM)
    swap = [(0, 1), (1, 0)]
    packet = lax.ppermute(packet, "sub", swap)
    spread = spread_rows(raw, raw_solid)
    whole, ends = join_parts(info, spread, packet, mine)
    route = [(2 * k, 2 * k + 2) for k in range(tiles_count - 1)]
    route = route + [(2 * k + 3, 2 * k + 1) for k in range(tiles_count - 1)]
    arrived = lax.ppermute(ends, ("tiles", "sub"), route)
    moved, reds, moved_rim, fields_rim = run_first(info, whole)
    arrived = follow(arrived, fields_rim)
    passed = lax.ppermute(arrived, "sub", swap)
    results = run_second(info, moved, reds, arrived, arrays)
    rims = (moved_rim, fields_rim) + tuple(results[4:])
    return tuple(run_outer(info, whole, arrived, passed, rims, results[:4]))


def solution(mesh):
    in_specs = (
        P(("groups", "tiles"), "sub"),
        P(None, ("groups", "tiles"), "sub"),
        P(None, ("groups", "tiles"), "sub"),
        P(("groups", "tiles"), "sub"),
        P(("groups", "tiles"), "sub"),
        P("groups"),
    )
    out_specs = (
        P(("groups", "tiles"), "sub"),
        P(None, ("groups", "tiles"), "sub"),
        P(None, ("groups", "tiles"), "sub"),
        P(("groups", "tiles"), "sub"),
    )
    return jax.shard_map(body, mesh=mesh, in_specs=in_specs, out_specs=out_specs, check_vma=False)
```

```python
import functools

import jax
import jax.numpy as jnp
from jax import lax
from jax.experimental import pallas as pl
from jax.experimental.pallas import tpu as pltpu
from jax.sharding import PartitionSpec as P

TILE = 16
STEPS = 2
RELAX_TIME = 0.8
SURFACE = 0.1
SEPARATION = 0.7

LANES = 128
SUBLANES = 8
FULL = 3
HALO = FULL + 1
FIELDS = 11
PLANES = FIELDS + 1
MOVED = 19
REDS = 5
RIM = 4
SLAB = HALO + 2 * RIM
OWN_TILES = SUBLANES - 2
GROUP = 4
PACKED = FULL * PLANES // GROUP * (GROUP - 1)
END_ROWS = (PACKED + 1) * SUBLANES
HALF = LANES // 2
PAIRS = PLANES // 2
KEPT = 2
COLOUR_BLOCK = (8, 1)
COLLIDE_BLOCK = (2, 4)
ARRIVE_BLOCK = (8, 1)
VMEM = pl.BlockSpec(memory_space=pltpu.VMEM)
SMEM = pl.BlockSpec(memory_space=pltpu.SMEM)
ANY = pl.BlockSpec(memory_space=pl.ANY)
HBM = pl.BlockSpec(memory_space=pltpu.HBM)


class Rows:
    def __init__(self, parts):
        self.parts = parts

    def _with(self, other, operation):
        others = other.parts if isinstance(other, Rows) else [other] * len(self.parts)
        return Rows([operation(one, two) for one, two in zip(self.parts, others)])

    def __add__(self, other):
        return self._with(other, lambda one, two: one + two)

    def __sub__(self, other):
        return self._with(other, lambda one, two: one - two)

    def __rsub__(self, other):
        return self._with(other, lambda one, two: two - one)

    def __mul__(self, other):
        return self._with(other, lambda one, two: one * two)

    def __or__(self, other):
        return self._with(other, lambda one, two: one | two)

    def __eq__(self, other):
        return self._with(other, lambda one, two: one == two)

    __radd__, __rmul__, __ror__ = __add__, __mul__, __or__

    def each(self, operation):
        return Rows([operation(part) for part in self.parts])


def select(mask, yes, no):
    count = max(len(item.parts) for item in (mask, yes, no) if isinstance(item, Rows))
    columns = [
        item.parts if isinstance(item, Rows) else [item] * count for item in (mask, yes, no)
    ]
    return Rows([jnp.where(*row) for row in zip(*columns)])


def roll_lanes(values, amount):
    return values.each(lambda part: pltpu.roll(part, amount % LANES, 1))


def roll_sublanes(values, amount):
    return values.each(lambda part: pltpu.roll(part, amount % SUBLANES, 0))


class Geometry:
    def __init__(self, info, own_tiles):
        live, first, last, sub_index = info[0], info[1], info[2], info[3]
        self.live = live
        self.low_row = jnp.where(first == 1, 0, -1000)
        self.high_row = jnp.where(last == 1, live, 1000)
        shape = (SUBLANES, LANES)
        lane = lax.broadcasted_iota(jnp.int32, shape, 1)
        tile = lax.broadcasted_iota(jnp.int32, shape, 0)
        depth = lane & (TILE - 1)
        low_part = sub_index == 0
        high_part = sub_index == 1
        z_walls = {1: depth == 0, -1: depth == TILE - 1}
        y_walls = {
            1: (tile == 1) & (lane < TILE) & low_part,
            -1: (tile == own_tiles) & (lane >= LANES - TILE) & high_part,
        }
        self.walls = {(0, vel_z): wall for vel_z, wall in z_walls.items()}
        for vel_y, y_wall in y_walls.items():
            self.walls[vel_y, 0] = y_wall
            for vel_z, z_wall in z_walls.items():
                self.walls[vel_y, vel_z] = y_wall | z_wall
        own = (tile >= 1) & (tile <= own_tiles)
        self.domain = own | ((tile == own_tiles + 1) & low_part) | ((tile == 0) & high_part)
        self.first_lanes = lane < TILE
        self.last_lanes = lane >= LANES - TILE

    def from_low_y(self, values):
        return roll_lanes(select(self.last_lanes, roll_sublanes(values, 1), values), TILE)

    def from_high_y(self, values):
        return roll_lanes(select(self.first_lanes, roll_sublanes(values, -1), values), -TILE)

    def from_low_z(self, values):
        return select(self.walls[0, 1], 0.0, roll_lanes(values, 1))

    def from_high_z(self, values):
        return select(self.walls[0, -1], 0.0, roll_lanes(values, -1))


def flat_rows(row, count, tile_offset=0):
    start = row * SUBLANES
    if not isinstance(start, int):
        start = pl.multiple_of(start, SUBLANES)
    return pl.ds(start + tile_offset, count * SUBLANES)


class Block:
    def __init__(self, geometry, spans, inner=False, store_rows=None):
        self.spans = spans
        self.store_rows = store_rows or [local for row, local, count in spans]
        rows = [row + extra for row, local, count in spans for extra in range(count)]
        self.inner = inner
        rows = [row + extra for row, local, count in spans for extra in range(count)]
        if inner:
            self.x_walls = {}
            self.valid = geometry.domain
            self.kinds = [0]
            return
        ids = Rows([row + jnp.zeros((SUBLANES, LANES), jnp.int32) for row in rows])
        self.x_walls = {1: ids == geometry.low_row, -1: ids == geometry.high_row - 1}
        self.valid = ids.each(
            lambda part: geometry.domain & (part >= geometry.low_row) & (part < geometry.high_row)
        )
        self.kinds = [
            jnp.where(row == geometry.low_row, 1, 0) + jnp.where(row == geometry.high_row - 1, 2, 0)
            for row in rows
        ]

    def load(self, ref, index, offset=0):
        return Rows([
            ref[index, flat_rows(local + offset + extra, 1), :]
            for row, local, count in self.spans
            for extra in range(count)
        ])

    def store(self, ref, index, values):
        targets = [
            target + extra
            for (row, local, count), target in zip(self.spans, self.store_rows)
            for extra in range(count)
        ]
        for target, part in zip(targets, values.parts):
            ref[index, flat_rows(target, 1), :] = part

    def store_crossed(self, geometry, ref, index, vel_y, values):
        mask = geometry.last_lanes if vel_y == 1 else geometry.first_lanes
        rows = [local + extra for row, local, count in self.spans for extra in range(count)]
        for row, part in zip(rows, values.parts):
            ref[index, flat_rows(row, 1), :] = part
            pltpu.store(ref.at[index, flat_rows(row, 1, vel_y), :], part, mask=mask)

    def wall_terms(self, walls, position):
        terms = [walls[position, flat_rows(kind, 1), :] for kind in self.kinds]
        return terms[0] if self.inner else Rows(terms)


def fill_wall_table(walls, geometry):
    one = jnp.ones((SUBLANES, LANES), jnp.float32)
    up_y, down_y, up_z, down_z = [
        jnp.where(geometry.walls[key], 0.0, one) for key in ((-1, 0), (1, 0), (0, -1), (0, 1))
    ]
    sum_y, sum_z = up_y + down_y, up_z + down_z
    for kind, (up_x, down_x) in enumerate(((1.0, 1.0), (1.0, 0.0), (0.0, 1.0))):
        sum_x = up_x + down_x
        around_x = 2.0 + sum_y + sum_z
        total = 12.0 + 2.0 * (sum_x + sum_y + sum_z) + sum_x * (sum_y + sum_z) + sum_y * sum_z
        rows = (
            (up_x - down_x) * around_x,
            (up_y - down_y) * (2.0 + sum_x + sum_z),
            (up_z - down_z) * (2.0 + sum_x + sum_y),
            36.0 - total,
        )
        for position, row in enumerate(rows):
            walls[position, flat_rows(kind, 1), :] = row


VELOCITIES = tuple(
    tuple(sign if axis == place else 0 for place in range(3)) for axis in range(3) for sign in (1, -1)
) + tuple(
    tuple({a: one, b: two}.get(place, 0) for place in range(3))
    for a, b in ((0, 1), (0, 2), (1, 2))
    for one, two in ((1, 1), (-1, -1), (1, -1), (-1, 1))
)
VELOCITIES = ((0, 0, 0),) + VELOCITIES
SIDEWAYS = tuple(place for place, velocity in enumerate(VELOCITIES) if velocity[1] != 0)
CROSSED = len(SIDEWAYS)


def colour_stage(block, geometry, fields, colours):
    density = block.load(fields, 0)
    red = block.load(fields, 10)
    colour = select(block.valid, 2.0 * red - density, 0.0)
    along_y = geometry.from_low_y(colour) + geometry.from_high_y(colour)
    along_z = geometry.from_low_z(colour) + geometry.from_high_z(colour)
    block.store(colours, 0, colour)
    block.store(colours, 1, 2.0 * colour + (along_y + along_z))
    block.store(colours, 2, along_y)
    block.store(colours, 3, along_z)


def collide_stage(block, geometry, fields, solids, colours, walls, state):
    relaxing = 1.0 - 1.0 / RELAX_TIME
    third = 1.0 / 3.0
    colour = block.load(colours, 0)
    doubled = 2.0 * colour + (block.load(colours, 0, -1) + block.load(colours, 0, 1))
    term_y = doubled + block.load(colours, 3)
    term_z = doubled + block.load(colours, 2)
    grad_x = block.load(colours, 1, 1) - block.load(colours, 1, -1)
    grad_y = geometry.from_high_y(term_y) - geometry.from_low_y(term_y)
    grad_z = geometry.from_high_z(term_z) - geometry.from_low_z(term_z)
    if not block.inner:
        grad_x = grad_x - block.wall_terms(walls, 0) * colour
    grad_y = grad_y - block.wall_terms(walls, 1) * colour
    grad_z = grad_z - block.wall_terms(walls, 2) * colour

    fluid = block.load(solids, PLANES - 1) == 0.0
    density = block.load(fields, 0)
    red = block.load(fields, 10)
    flux = [block.load(fields, 1 + axis) for axis in range(3)]
    stress = [block.load(fields, 4 + part) for part in range(6)]
    square_xx, square_yy, square_zz = grad_x * grad_x, grad_y * grad_y, grad_z * grad_z
    square = square_xx + square_yy + square_zz
    inverse = select(fluid, (1.0 + square * (1.0 / 144.0)).each(lax.rsqrt), 0.0)
    trace = third * square
    strength = (SURFACE / (8.0 * 144.0)) * inverse
    keep = select(fluid, relaxing / 8.0, 1.0 / 8.0)
    eighths = [0.125 * part for part in flux]
    own = [
        eighths[axis] * flux[axis] + (keep * stress[axis] + strength * (squared - trace))
        for axis, squared in enumerate((square_xx, square_yy, square_zz))
    ]
    strength, keep = 2.0 * strength, 2.0 * keep
    quarters = [2.0 * part for part in eighths[:2]]
    grads = (grad_x, grad_y, grad_z)
    cross = [
        quarters[a] * flux[b] + (keep * stress[3 + plane] + strength * (grads[a] * grads[b]))
        for plane, (a, b) in enumerate(((0, 1), (0, 2), (1, 2)))
    ]
    base = density * (1.0 / 36.0) - third * (own[0] + own[1] + own[2])
    sign = select(fluid, 1.0 / 12.0, -1.0 / 12.0)
    run = [sign * part for part in flux]
    mixing = ((SEPARATION / 144.0) * red) * ((density - red) * inverse)
    red_run = [0.5 * part + mixing * grad for part, grad in zip(run, grads)]
    moved, reds, crossed = state

    def leave(direction, values):
        block.store(moved, direction, values)
        if direction in SIDEWAYS:
            place = SIDEWAYS.index(direction)
            block.store_crossed(geometry, crossed, place, VELOCITIES[direction][1], values)

    leave(0, 12.0 * base)
    straight = [base + part for part in own]
    for axis in range(3):
        middle = 2.0 * straight[axis]
        swing = 2.0 * run[axis]
        leave(1 + 2 * axis, middle + swing)
        leave(2 + 2 * axis, middle - swing)
    for plane, (a, b) in enumerate(((0, 1), (0, 2), (1, 2))):
        middle = straight[a] + own[b]
        same, other = middle + cross[plane], middle - cross[plane]
        along, against = run[a] + run[b], run[a] - run[b]
        first = 7 + 4 * plane
        leave(first, same + along)
        leave(first + 1, same - along)
        leave(first + 2, other + against)
        leave(first + 3, other - against)

    red_base = select(block.valid, red * (1.0 / 36.0), 0.0)
    red_run = [select(block.valid, part, 0.0) for part in red_run]
    block.store(reds, 0, red_base)
    block.store(reds, 1, red_base + red_run[0])
    block.store(reds, 2, red_base - red_run[0])
    block.store(reds, 3, red_run[1])
    block.store(reds, 4, red_run[2])


def arrive_stage(block, geometry, walls, state, fields):
    third = 1.0 / 3.0
    moved, reds, crossed = state
    own = [None] * MOVED

    def here(direction):
        if own[direction] is None:
            own[direction] = block.load(moved, direction)
        return own[direction]

    def arrived(direction, opposite):
        vel_x, vel_y, vel_z = VELOCITIES[direction]
        if vel_y != 0:
            values = block.load(crossed, SIDEWAYS.index(direction), -vel_x)
        else:
            values = here(direction) if vel_x == 0 else block.load(moved, direction, -vel_x)
        if vel_y != 0 or vel_z != 0:
            values = roll_lanes(values, TILE * vel_y + vel_z)
        masks = []
        if vel_x in block.x_walls:
            masks.append(block.x_walls[vel_x])
        if (vel_y, vel_z) in geometry.walls:
            masks.append(geometry.walls[vel_y, vel_z])
        if not masks:
            return values
        wall = functools.reduce(lambda one, two: one | two, masks)
        return select(wall, here(opposite), values)

    red = block.load(reds, 0)
    red_y = block.load(reds, 3)
    red_z = block.load(reds, 4)
    from_x = block.load(reds, 1, -1) + block.load(reds, 2, 1)
    spread = 2.0 * red + from_x
    spread_y = 2.0 * red_y + (block.load(reds, 3, -1) + block.load(reds, 3, 1))
    spread_z = 2.0 * red_z + (block.load(reds, 4, -1) + block.load(reds, 4, 1))
    up_y, down_y = red + red_y, red - red_y
    low_y = (
        (spread + spread_y)
        + geometry.from_low_z(up_y + red_z)
        + geometry.from_high_z(up_y - red_z)
    )
    high_y = (
        (spread - spread_y)
        + geometry.from_low_z(down_y + red_z)
        + geometry.from_high_z(down_y - red_z)
    )
    bounced = (
        block.wall_terms(walls, 3) * red
        - block.wall_terms(walls, 1) * red_y
        - block.wall_terms(walls, 2) * red_z
    )
    if not block.inner:
        bounced = bounced - block.wall_terms(walls, 0) * (block.load(reds, 1) - red)
    red_total = (
        12.0 * red
        + 2.0 * from_x
        + geometry.from_low_z(spread + spread_z)
        + geometry.from_high_z(spread - spread_z)
        + geometry.from_low_y(low_y)
        + geometry.from_high_y(high_y)
        + bounced
    )
    rest = here(0)
    sums, diffs = [], []
    for axis in range(3):
        up = arrived(1 + 2 * axis, 2 + 2 * axis)
        down = arrived(2 + 2 * axis, 1 + 2 * axis)
        sums.append(up + down)
        diffs.append(up - down)
    total = rest + sums[0] + sums[1] + sums[2]
    cross = []
    for plane, (a, b) in enumerate(((0, 1), (0, 2), (1, 2))):
        first = 7 + 4 * plane
        parts = [arrived(first + offset, first + (offset ^ 1)) for offset in range(4)]
        same, other = parts[0] + parts[1], parts[2] + parts[3]
        along, against = parts[0] - parts[1], parts[2] - parts[3]
        both = same + other
        cross.append(same - other)
        total = total + both
        sums[a], sums[b] = sums[a] + both, sums[b] + both
        diffs[a], diffs[b] = diffs[a] + (along + against), diffs[b] + (along - against)
    shared = third * total
    block.store(fields, 0, total)
    for axis in range(3):
        block.store(fields, 1 + axis, diffs[axis])
        block.store(fields, 4 + axis, sums[axis] - shared - diffs[axis] * diffs[axis])
    for plane, (a, b) in enumerate(((0, 1), (0, 2), (1, 2))):
        block.store(fields, 7 + plane, cross[plane] - diffs[a] * diffs[b])
    block.store(fields, 10, red_total)


def over_rows(geometry, first, size, blocks, stage):
    trip = size * blocks
    rest = -2 * first % trip
    assert TILE % trip == 0 and rest % min(size, rest or size) == 0

    def run(start, count, step_size):
        for offset in range(0, count, step_size):
            row = start + offset
            stage(Block(geometry, [(row, row, step_size)], inner=True))

    def step(index, carry):
        run(first + index * trip, trip, size)
        return carry

    trips = (geometry.live - 2 * first - rest) // trip
    lax.fori_loop(0, trips, step, 0)
    if rest:
        run(geometry.live - first - rest, rest, min(size, rest))


def block_tiles():
    return lax.broadcasted_iota(jnp.int32, (SUBLANES, LANES), 0)


def roll_tiles(block, amount):
    return pltpu.roll(block, amount % SUBLANES, 0)


def pack_blocks(blocks):
    tiles, rest = block_tiles(), blocks[GROUP - 1]
    packed = []
    for number, block in enumerate(blocks[: GROUP - 1]):
        low, high = 2 * number + 1, 2 * number + 2
        block = jnp.where(tiles == 0, roll_tiles(rest, -low), block)
        packed.append(jnp.where(tiles == SUBLANES - 1, roll_tiles(rest, SUBLANES - 1 - high), block))
    return packed


def unpack_blocks(packed):
    tiles, rest = block_tiles(), None
    for number, block in enumerate(packed):
        low, high = 2 * number + 1, 2 * number + 2
        part = jnp.where(tiles == low, roll_tiles(block, low), roll_tiles(block, high - SUBLANES + 1))
        rest = part if rest is None else jnp.where(tiles >= low, part, rest)
    return list(packed) + [rest]


def spread_tile(raw, raw_solid, index, row, target, target_row):
    source = raw_solid if index == FIELDS else raw.at[index]
    for tile in range(OWN_TILES):
        values = source[pl.ds(row, SUBLANES), pl.ds(tile * LANES, LANES)].astype(jnp.float32)
        start = target_row * SUBLANES + 1 + tile
        target[index, pl.ds(start, SUBLANES, stride=SUBLANES), :] = values


def load_kernel(
    tiles_count, density, momentum, stress, red, solid, widths,
    info, raw, raw_solid, packet, mine,
    first_tile, last_tile, held_widths, sems,
):
    row_count, flat_count = raw_solid.shape
    own_tiles = flat_count // LANES
    copies = [
        pltpu.make_async_copy(widths, held_widths, sems.at[0]),
        pltpu.make_async_copy(density, raw.at[0], sems.at[1]),
        pltpu.make_async_copy(momentum, raw.at[pl.ds(1, 3)], sems.at[2]),
        pltpu.make_async_copy(red, raw.at[10], sems.at[3]),
        pltpu.make_async_copy(solid, raw_solid, sems.at[4]),
        pltpu.make_async_copy(stress.at[pl.ds(0, 3)], raw.at[pl.ds(4, 3)], sems.at[5]),
        pltpu.make_async_copy(stress.at[pl.ds(3, 3)], raw.at[pl.ds(7, 3)], sems.at[6]),
    ]
    for copy in copies:
        copy.start()
    tiles_index, sub_index = lax.axis_index("tiles"), lax.axis_index("sub")
    low_part = sub_index == 0
    edge_start = pl.multiple_of(jnp.where(low_part, (own_tiles - 1) * LANES, 0), LANES)

    copies[0].wait()
    live = held_widths[tiles_index] * TILE
    info[0] = live
    info[1] = (tiles_index == 0).astype(jnp.int32)
    info[2] = (tiles_index == tiles_count - 1).astype(jnp.int32)
    info[3] = sub_index

    near_cut = lax.broadcasted_iota(jnp.int32, (SUBLANES, LANES), 1) < HALF
    near_cut = near_cut == jnp.logical_not(low_part)
    near_last = pl.multiple_of(live - SUBLANES, SUBLANES)
    ready = {0: copies[1], 1: copies[2], 10: copies[3], 11: copies[4], 4: copies[5], 7: copies[6]}
    for index in (0, 1, 2, 3, 10, 11, 4, 5, 6, 7, 8, 9):
        if index in ready:
            ready[index].wait()
        for target, row in ((first_tile, 0), (last_tile, near_last)):
            spread_tile(raw, raw_solid, index, row, target, 0)

    edges = pl.ds(edge_start, LANES)
    for pair in range(PAIRS):
        later = raw_solid if pair + PAIRS == FIELDS else raw.at[pair + PAIRS]
        for row in range(0, row_count, SUBLANES):
            rows = pl.ds(row, SUBLANES)
            beside = pltpu.roll(later[rows, edges].astype(jnp.float32), HALF, 1)
            both = jnp.where(near_cut, raw[pair, rows, edges], beside)
            packet[pl.ds(pair * row_count + row, SUBLANES), :] = both

    after = PAIRS * row_count
    ends = ((packet, after, jnp.logical_not(low_part)), (mine, 0, low_part))
    for target, at, use_last in ends:
        def row_of(index, number_first, number_last):
            first = first_tile[index, flat_rows(number_first, 1), :]
            last = last_tile[index, flat_rows(number_last, 1), :]
            return jnp.where(use_last, last, first)

        place = pl.ds(at + PACKED * SUBLANES, SUBLANES)
        ends_row = (FULL, SUBLANES - HALO)
        target[place, :] = 2.0 * row_of(10, *ends_row) - row_of(0, *ends_row)
        for group in range(FULL * PLANES // GROUP):
            blocks = []
            for number in range(group * GROUP, (group + 1) * GROUP):
                index, extra = divmod(number, FULL)
                blocks.append(row_of(index, extra, SUBLANES - FULL + extra))
            for number, block in enumerate(pack_blocks(blocks)):
                place = at + (group * (GROUP - 1) + number) * SUBLANES
                target[pl.ds(place, SUBLANES), :] = block


def load_inputs(arrays, widths, tiles_count):
    row_count, flat_count = arrays[0].shape
    packet_rows = PAIRS * row_count + END_ROWS
    return pl.pallas_call(
        functools.partial(load_kernel, tiles_count),
        out_shape=[
            pltpu.SMEM((4,), jnp.int32),
            jax.ShapeDtypeStruct((FIELDS, row_count, flat_count), jnp.float32),
            jax.ShapeDtypeStruct((row_count, flat_count), jnp.int32),
            jax.ShapeDtypeStruct((packet_rows, LANES), jnp.float32),
            jax.ShapeDtypeStruct((END_ROWS, LANES), jnp.float32),
        ],
        in_specs=[HBM] * 6,
        out_specs=[SMEM, VMEM, VMEM, VMEM, VMEM],
        scratch_shapes=[
            pltpu.VMEM((PLANES, SUBLANES * SUBLANES, LANES), jnp.float32),
            pltpu.VMEM((PLANES, SUBLANES * SUBLANES, LANES), jnp.float32),
            pltpu.SMEM(widths.shape, jnp.int32),
            pltpu.SemaphoreType.DMA((7,)),
        ],
        compiler_params=pltpu.CompilerParams(vmem_limit_bytes=16 * 1024 * 1024),
        name="load",
    )(*[pltpu.with_memory_space_constraint(array, pltpu.HBM) for array in (*arrays, widths)])


def spread_kernel(raw, raw_solid, spread):
    for index in range(PLANES):
        for row in range(0, raw_solid.shape[0], SUBLANES):
            spread_tile(raw, raw_solid, index, row, spread, row)


def spread_rows(raw, raw_solid):
    row_count = raw_solid.shape[0]
    return pl.pallas_call(
        spread_kernel,
        out_shape=jax.ShapeDtypeStruct((PLANES, row_count * SUBLANES, LANES), jnp.float32),
        in_specs=[VMEM, VMEM],
        out_specs=VMEM,
        compiler_params=pltpu.CompilerParams(vmem_limit_bytes=16 * 1024 * 1024),
        cost_estimate=pl.CostEstimate(flops=1_000_000, bytes_accessed=4_000_000, transcendentals=0),
        name="spread",
    )(raw, raw_solid)


def join_kernel(info, spread, packet, mine, whole, ends):
    low_part = info[3] == 0
    row_count = spread.shape[1] // SUBLANES
    ends[pl.ds(0, END_ROWS), :] = mine[...]
    ends[pl.ds(END_ROWS, END_ROWS), :] = packet[pl.ds(PAIRS * row_count, END_ROWS), :]
    for pair in range(PAIRS):
        for row in range(0, row_count, SUBLANES):
            both = packet[pl.ds(pair * row_count + row, SUBLANES), :]
            start = row * SUBLANES
            for index, values in ((pair, both), (pair + PAIRS, pltpu.roll(both, HALF, 1))):
                below = jnp.where(low_part, 0.0, values)
                above = jnp.where(low_part, values, 0.0)
                whole[index, pl.ds(start, SUBLANES, stride=SUBLANES), :] = below
                whole[index, pl.ds(start + SUBLANES - 1, SUBLANES, stride=SUBLANES), :] = above


def join_parts(info, spread, packet, mine):
    return pl.pallas_call(
        join_kernel,
        out_shape=[
            jax.ShapeDtypeStruct(spread.shape, jnp.float32),
            jax.ShapeDtypeStruct((2 * END_ROWS, LANES), jnp.float32),
        ],
        in_specs=[SMEM, VMEM, VMEM, VMEM],
        out_specs=[VMEM] * 2,
        input_output_aliases={1: 0},
        compiler_params=pltpu.CompilerParams(vmem_limit_bytes=16 * 1024 * 1024),
        name="join",
    )(info, pltpu.with_memory_space_constraint(spread, pltpu.VMEM), packet, mine)


def keep_rows(target, target_index, source, index, rows, size):
    for place, row in enumerate(rows):
        target[target_index, flat_rows(place * size, size), :] = source[
            index, flat_rows(row, size), :
        ]


def collide_rows(geometry, before, whole, first, colours, walls, state):
    over_rows(geometry, first - 1, *COLOUR_BLOCK, lambda block: colour_stage(
        block, geometry, before, colours))
    over_rows(geometry, first, *COLLIDE_BLOCK, lambda block: collide_stage(
        block, geometry, before, whole, colours, walls, state))


def keep_state(target, state, rows):
    place = 0
    for part in state:
        for index in range(part.shape[0]):
            keep_rows(target, place, part, index, rows, KEPT)
            place += 1


def first_kernel(
    info, whole, moved_later, reds_later, crossed_later,
    state_rim, fields_rim, state_later_rim, final_rim,
    colours, walls, moved, reds, crossed, fields,
):
    state, later = (moved, reds, crossed), (moved_later, reds_later, crossed_later)
    geometry = Geometry(info, OWN_TILES)
    live = geometry.live
    fill_wall_table(walls, geometry)
    collide_rows(geometry, whole, whole, 1, colours, walls, state)
    over_rows(geometry, 2, *ARRIVE_BLOCK, lambda block: arrive_stage(
        block, geometry, walls, state, fields))
    keep_state(state_rim, state, (1, live - 3))
    for index in range(FIELDS):
        keep_rows(fields_rim, index, fields, index, (2, live - 4), KEPT)
    collide_rows(geometry, fields, whole, 3, colours, walls, later)
    edge = Block(geometry, [(RIM, RIM, RIM), (live - 2 * RIM, live - 2 * RIM, RIM)], True, [0, RIM])
    arrive_stage(edge, geometry, walls, later, final_rim)
    keep_state(state_later_rim, later, (3, live - 5))


def tile_copies(pieces, outs, held_row, out_row, sems):
    held, rows = pl.ds(held_row, SUBLANES), pl.ds(out_row, SUBLANES)
    parts = (
        (pieces.at[0, held], outs[0].at[rows]),
        (pieces.at[pl.ds(1, 3), held], outs[1].at[:, rows]),
        (pieces.at[pl.ds(4, 6), held], outs[2].at[:, rows]),
        (pieces.at[10, held], outs[3].at[rows]),
    )
    return [
        pltpu.make_async_copy(source, target, sems.at[number])
        for number, (source, target) in enumerate(parts)
    ]


def gather_tiles(final, row, pieces, held_row):
    for index in range(FIELDS):
        for tile in range(OWN_TILES):
            start = pl.multiple_of(row * SUBLANES, SUBLANES) + 1 + tile
            pieces[index, pl.ds(held_row, SUBLANES), pl.ds(tile * LANES, LANES)] = final[
                index, pl.ds(start, SUBLANES, stride=SUBLANES), :
            ]


def second_kernel(
    info, moved, reds, crossed, arrived, density_out, momentum_out, stress_out, red_out,
    final, walls, pieces, zeros, sems,
):
    outs = (density_out, momentum_out, stress_out, red_out)
    row_tiles = density_out.shape[0] // SUBLANES
    geometry = Geometry(info, OWN_TILES)
    live = geometry.live
    fill_wall_table(walls, geometry)

    zeros[...] = jnp.zeros(zeros.shape, zeros.dtype)
    dead = {}
    for tile in range(row_tiles):
        dead[tile] = tile_copies(zeros, outs, 0, tile * SUBLANES, sems.at[tile])

        @pl.when(tile * SUBLANES >= live)
        def _():
            for copy in dead[tile]:
                copy.start()

    def copies_of(tile):
        row = pl.multiple_of(tile * SUBLANES, SUBLANES)
        return tile_copies(pieces, outs, row, row, sems.at[tile])

    def finish(tile, carry):
        row = pl.multiple_of(tile * SUBLANES, SUBLANES)
        block = Block(geometry, [(row, row, SUBLANES)], inner=True)
        arrive_stage(block, geometry, walls, (moved, reds, crossed), final)
        gather_tiles(final, row, pieces, row)
        for copy in copies_of(tile):
            copy.start()
        return carry

    def settle(tile, carry):
        for copy in copies_of(tile):
            copy.wait()
        return carry

    last = live // SUBLANES - 1
    lax.fori_loop(1, last, finish, 0)
    lax.fori_loop(1, last, settle, 0)
    for tile in range(row_tiles):

        @pl.when(tile * SUBLANES >= live)
        def _():
            for copy in dead[tile]:
                copy.wait()


def rim_shape(count, rows):
    return jax.ShapeDtypeStruct((count, rows * SUBLANES, LANES), jnp.float32)


def state_shapes(flat):
    return [jax.ShapeDtypeStruct((count, flat, LANES), jnp.float32) for count in (MOVED, REDS, CROSSED)]


def run_first(info, whole):
    flat = whole.shape[1]
    state_rim = rim_shape(MOVED + REDS + CROSSED, 2 * KEPT)
    shapes = state_shapes(flat)
    shapes = shapes + [state_rim, rim_shape(FIELDS, 2 * KEPT), state_rim, rim_shape(FIELDS, 2 * RIM)]
    return pl.pallas_call(
        first_kernel,
        out_shape=shapes,
        in_specs=[SMEM, VMEM],
        out_specs=[VMEM] * len(shapes),
        scratch_shapes=[
            pltpu.VMEM((4, flat, LANES), jnp.float32),
            pltpu.VMEM((4, 3 * SUBLANES, LANES), jnp.float32),
        ]
        + [pltpu.VMEM(shape.shape, shape.dtype) for shape in state_shapes(flat)]
        + [pltpu.VMEM((FIELDS, flat, LANES), jnp.float32)],
        compiler_params=pltpu.CompilerParams(vmem_limit_bytes=24 * 1024 * 1024),
        cost_estimate=pl.CostEstimate(flops=20_000_000, bytes_accessed=8_000_000, transcendentals=0),
        name="first",
    )(info, whole)


def run_second(info, state, arrived, arrays):
    flat = state[0].shape[1]
    row_count, flat_count = arrays[0].shape
    shapes = [jax.ShapeDtypeStruct(array.shape, jnp.float32) for array in arrays[:4]]
    return pl.pallas_call(
        second_kernel,
        out_shape=shapes,
        in_specs=[SMEM, VMEM, VMEM, VMEM, ANY],
        out_specs=[ANY] * 4,
        scratch_shapes=[
            pltpu.VMEM((FIELDS, flat, LANES), jnp.float32),
            pltpu.VMEM((4, 3 * SUBLANES, LANES), jnp.float32),
            pltpu.VMEM((FIELDS, row_count, flat_count), jnp.float32),
            pltpu.VMEM((FIELDS, SUBLANES, flat_count), jnp.float32),
            pltpu.SemaphoreType.DMA((row_count // SUBLANES, 4)),
        ],
        compiler_params=pltpu.CompilerParams(vmem_limit_bytes=24 * 1024 * 1024),
        cost_estimate=pl.CostEstimate(flops=20_000_000, bytes_accessed=8_000_000, transcendentals=0),
        name="second",
    )(info, *state, arrived)


def follow_kernel(ends, kept, out):
    out[pl.ds(PACKED * SUBLANES, 1), :] = jnp.zeros((1, LANES), jnp.float32)


def follow(ends, kept):
    return pl.pallas_call(
        follow_kernel,
        out_shape=jax.ShapeDtypeStruct(ends.shape, jnp.float32),
        in_specs=[VMEM, ANY],
        out_specs=VMEM,
        input_output_aliases={0: 0},
        compiler_params=pltpu.CompilerParams(vmem_limit_bytes=8 * 1024 * 1024),
        name="follow",
    )(pltpu.with_memory_space_constraint(ends, pltpu.VMEM), kept)


def outer_kernel(
    info, whole, arrived, passed, state_rim, fields_rim, state_later_rim, final_rim, *refs,
):
    outs = refs[4:8]
    start_fields, colours, walls, fields, final = refs[8:13]
    state, later = refs[13:16], refs[16:19]
    pieces, sems = refs[19:]
    geometry = Geometry(info, OWN_TILES)
    live = geometry.live
    low_part = info[3] == 0
    fill_wall_table(walls, geometry)

    def ends_of(ref, half):
        blocks = []
        for group in range(FULL * PLANES // GROUP):
            first = half * (PACKED + 1) + group * (GROUP - 1)
            packed = [ref[pl.ds((first + k) * SUBLANES, SUBLANES), :] for k in range(GROUP - 1)]
            blocks = blocks + unpack_blocks(packed)
        last = half * (PACKED + 1) + PACKED
        return blocks + [ref[pl.ds(last * SUBLANES, SUBLANES), :]]

    tiles = block_tiles()
    middle = (tiles >= 1) & (tiles <= OWN_TILES)

    def widened(own, other):
        beside = jnp.where(tiles == 0, roll_tiles(other, -OWN_TILES), roll_tiles(other, OWN_TILES))
        return jnp.where(geometry.domain, jnp.where(middle, own, beside), 0.0)

    straight = [widened(*pair) for pair in zip(ends_of(arrived, 0), ends_of(arrived, 1))]
    crossed = [widened(*pair) for pair in zip(ends_of(passed, 1), ends_of(passed, 0))]
    below = [jnp.where(low_part, *pair) for pair in zip(straight, crossed)]
    above = [jnp.where(low_part, *pair) for pair in zip(crossed, straight)]

    def spans(first, count):
        mirrored = SLAB - first - count
        return [
            (first - HALO, first, count),
            (live - 2 * RIM + mirrored, SLAB + mirrored, count),
        ]

    for index in range(PLANES):
        for extra in range(FULL):
            number = FULL * index + extra
            start_fields[index, flat_rows(1 + extra, 1), :] = below[number]
            start_fields[index, flat_rows(2 * SLAB - HALO + extra, 1), :] = above[number]
        start_fields[index, flat_rows(HALO, 2), :] = whole[index, flat_rows(0, 2), :]
        start_fields[index, flat_rows(2 * SLAB - HALO - 2, 2), :] = whole[
            index, flat_rows(live - 2, 2), :
        ]
    for row, colour in ((0, below[-1]), (2 * SLAB - 1, above[-1])):
        start_fields[0, flat_rows(row, 1), :] = jnp.zeros((SUBLANES, LANES), jnp.float32)
        start_fields[10, flat_rows(row, 1), :] = 0.5 * colour

    def place(target, index, source, at, first, size):
        for place, (row, local, count) in enumerate(spans(first, size)):
            target[index, flat_rows(local, size), :] = source[at, flat_rows(place * size, size), :]

    for parts, rim, first in ((state, state_rim, HALO + 1), (later, state_later_rim, HALO + 3)):
        at = 0
        for part in parts:
            for index in range(part.shape[0]):
                place(part, index, rim, at, first, KEPT)
                at += 1
    for index in range(FIELDS):
        place(fields, index, fields_rim, index, HALO + 2, 2)
        place(final, index, final_rim, index, HALO + RIM, RIM)

    block = lambda first, count: Block(geometry, spans(first, count))
    colour_stage(block(0, 6), geometry, start_fields, colours)
    collide_stage(block(1, 4), geometry, start_fields, start_fields, colours, walls, state)
    arrive_stage(block(2, 4), geometry, walls, state, fields)
    start_fields[PLANES - 1, flat_rows(HALO + 2, 1), :] = whole[PLANES - 1, flat_rows(2, 1), :]
    start_fields[PLANES - 1, flat_rows(2 * SLAB - HALO - 3, 1), :] = whole[
        PLANES - 1, flat_rows(live - 3, 1), :
    ]
    colour_stage(block(2, 6), geometry, fields, colours)
    collide_stage(block(3, 4), geometry, fields, start_fields, colours, walls, later)
    arrive_stage(block(4, 4), geometry, walls, later, final)

    copies = []
    for side, row, out_row in ((0, HALO, 0), (1, SLAB, live - SUBLANES)):
        gather_tiles(final, row, pieces, side * SUBLANES)
        out_row = pl.multiple_of(out_row, SUBLANES)
        copies = copies + tile_copies(pieces, outs, side * SUBLANES, out_row, sems.at[side])
    for copy in copies:
        copy.start()
    for copy in copies:
        copy.wait()


def run_outer(info, whole, arrived, passed, rims, outs):
    flat = 2 * SLAB * SUBLANES
    flat_count = outs[0].shape[1]
    return pl.pallas_call(
        outer_kernel,
        out_shape=[jax.ShapeDtypeStruct(out.shape, jnp.float32) for out in outs],
        in_specs=[SMEM] + [VMEM] * 7 + [ANY] * 4,
        out_specs=[ANY] * 4,
        scratch_shapes=[
            pltpu.VMEM((PLANES, flat, LANES), jnp.float32),
            pltpu.VMEM((4, flat, LANES), jnp.float32),
            pltpu.VMEM((4, 3 * SUBLANES, LANES), jnp.float32),
            pltpu.VMEM((FIELDS, flat, LANES), jnp.float32),
            pltpu.VMEM((FIELDS, flat, LANES), jnp.float32),
        ]
        + [pltpu.VMEM(shape.shape, shape.dtype) for shape in 2 * state_shapes(flat)]
        + [
            pltpu.VMEM((FIELDS, 2 * SUBLANES, flat_count), jnp.float32),
            pltpu.SemaphoreType.DMA((2, 4)),
        ],
        input_output_aliases={8: 0, 9: 1, 10: 2, 11: 3},
        compiler_params=pltpu.CompilerParams(vmem_limit_bytes=32 * 1024 * 1024),
        name="outer",
    )(info, whole, arrived, passed, *rims, *outs)


def body(density, momentum, stress, red_density, solid, widths):
    tiles_count = lax.axis_size("tiles")
    arrays = (density, momentum, stress, red_density, solid)
    info, raw, raw_solid, packet, mine = load_inputs(arrays, widths, tiles_count)
    info = pltpu.with_memory_space_constraint(info, pltpu.SMEM)
    swap = [(0, 1), (1, 0)]
    packet = lax.ppermute(packet, "sub", swap)
    spread = spread_rows(raw, raw_solid)
    whole, ends = join_parts(info, spread, packet, mine)
    route = [(2 * k, 2 * k + 2) for k in range(tiles_count - 1)]
    route = route + [(2 * k + 3, 2 * k + 1) for k in range(tiles_count - 1)]
    arrived = lax.ppermute(ends, ("tiles", "sub"), route)
    *state, state_rim, fields_rim, state_later_rim, final_rim = run_first(info, whole)
    arrived = follow(arrived, fields_rim)
    passed = lax.ppermute(arrived, "sub", swap)
    outs = run_second(info, state, arrived, arrays)
    rims = (state_rim, fields_rim, state_later_rim, final_rim)
    return tuple(run_outer(info, whole, arrived, passed, rims, outs))


def solution(mesh):
    in_specs = (
        P(("groups", "tiles"), "sub"),
        P(None, ("groups", "tiles"), "sub"),
        P(None, ("groups", "tiles"), "sub"),
        P(("groups", "tiles"), "sub"),
        P(("groups", "tiles"), "sub"),
        P("groups"),
    )
    out_specs = (
        P(("groups", "tiles"), "sub"),
        P(None, ("groups", "tiles"), "sub"),
        P(None, ("groups", "tiles"), "sub"),
        P(("groups", "tiles"), "sub"),
    )
    return jax.shard_map(body, mesh=mesh, in_specs=in_specs, out_specs=out_specs, check_vma=False)
```

```python
import functools

import jax
import jax.numpy as jnp
from jax import lax
from jax.experimental import pallas as pl
from jax.experimental.pallas import tpu as pltpu
from jax.sharding import PartitionSpec as P

TILE = 16
STEPS = 2
RELAX_TIME = 0.8
SURFACE = 0.1
SEPARATION = 0.7

LANES = 128
SUBLANES = 8
FULL = 3
HALO = FULL + 1
FIELDS = 11
PLANES = FIELDS + 1
MOVED = 19
REDS = 5
HELD = MOVED + 1
RIM = 4
SLAB = HALO + 2 * RIM
OWN_TILES = SUBLANES - 2
GROUP = 4
PACKED = FULL * PLANES // GROUP * (GROUP - 1)
END_ROWS = (PACKED + 1) * SUBLANES
HALF = LANES // 2
PAIRS = PLANES // 2
KEPT = 2
COLOUR_BLOCK = (8, 1)
COLLIDE_BLOCK = (2, 4)
ARRIVE_BLOCK = (8, 1)
VMEM = pl.BlockSpec(memory_space=pltpu.VMEM)
SMEM = pl.BlockSpec(memory_space=pltpu.SMEM)
ANY = pl.BlockSpec(memory_space=pl.ANY)
HBM = pl.BlockSpec(memory_space=pltpu.HBM)


class Rows:
    def __init__(self, parts):
        self.parts = parts

    def _with(self, other, operation):
        others = other.parts if isinstance(other, Rows) else [other] * len(self.parts)
        return Rows([operation(one, two) for one, two in zip(self.parts, others)])

    def __add__(self, other):
        return self._with(other, lambda one, two: one + two)

    def __sub__(self, other):
        return self._with(other, lambda one, two: one - two)

    def __rsub__(self, other):
        return self._with(other, lambda one, two: two - one)

    def __mul__(self, other):
        return self._with(other, lambda one, two: one * two)

    def __or__(self, other):
        return self._with(other, lambda one, two: one | two)

    def __eq__(self, other):
        return self._with(other, lambda one, two: one == two)

    __radd__, __rmul__, __ror__ = __add__, __mul__, __or__

    def each(self, operation):
        return Rows([operation(part) for part in self.parts])


def select(mask, yes, no):
    count = max(len(item.parts) for item in (mask, yes, no) if isinstance(item, Rows))
    columns = [
        item.parts if isinstance(item, Rows) else [item] * count for item in (mask, yes, no)
    ]
    return Rows([jnp.where(*row) for row in zip(*columns)])


def roll_lanes(values, amount):
    return values.each(lambda part: pltpu.roll(part, amount % LANES, 1))


def roll_sublanes(values, amount):
    return values.each(lambda part: pltpu.roll(part, amount % SUBLANES, 0))


class Geometry:
    def __init__(self, info, own_tiles):
        live, first, last, sub_index = info[0], info[1], info[2], info[3]
        self.live = live
        self.low_row = jnp.where(first == 1, 0, -1000)
        self.high_row = jnp.where(last == 1, live, 1000)
        shape = (SUBLANES, LANES)
        lane = lax.broadcasted_iota(jnp.int32, shape, 1)
        tile = lax.broadcasted_iota(jnp.int32, shape, 0)
        depth = lane & (TILE - 1)
        low_part = sub_index == 0
        high_part = sub_index == 1
        z_walls = {1: depth == 0, -1: depth == TILE - 1}
        y_walls = {
            1: (tile == 1) & (lane < TILE) & low_part,
            -1: (tile == own_tiles) & (lane >= LANES - TILE) & high_part,
        }
        self.walls = {(0, vel_z): wall for vel_z, wall in z_walls.items()}
        for vel_y, y_wall in y_walls.items():
            self.walls[vel_y, 0] = y_wall
            for vel_z, z_wall in z_walls.items():
                self.walls[vel_y, vel_z] = y_wall | z_wall
        own = (tile >= 1) & (tile <= own_tiles)
        self.domain = own | ((tile == own_tiles + 1) & low_part) | ((tile == 0) & high_part)
        self.first_lanes = lane < TILE
        self.last_lanes = lane >= LANES - TILE

    def from_low_y(self, values):
        return roll_lanes(select(self.last_lanes, roll_sublanes(values, 1), values), TILE)

    def from_high_y(self, values):
        return roll_lanes(select(self.first_lanes, roll_sublanes(values, -1), values), -TILE)

    def from_low_z(self, values):
        return select(self.walls[0, 1], 0.0, roll_lanes(values, 1))

    def from_high_z(self, values):
        return select(self.walls[0, -1], 0.0, roll_lanes(values, -1))


def flat_rows(row, count, tile_offset=0):
    start = row * SUBLANES
    if not isinstance(start, int):
        start = pl.multiple_of(start, SUBLANES)
    return pl.ds(start + tile_offset, count * SUBLANES)


class ByRow:
    def __init__(self, ref):
        self.ref = ref


def place_of(ref, index, row, tile_offset=0):
    if isinstance(ref, ByRow):
        return ref.ref, row, pl.ds(index * SUBLANES + tile_offset, SUBLANES)
    return ref, index, flat_rows(row, 1, tile_offset)


def read_row(ref, index, row, tile_offset=0):
    ref, first, second = place_of(ref, index, row, tile_offset)
    return ref[first, second, :]


def write_row(ref, index, row, values):
    ref, first, second = place_of(ref, index, row)
    ref[first, second, :] = values


class Block:
    def __init__(self, geometry, spans, inner=False, store_rows=None):
        self.spans = spans
        self.store_rows = store_rows or [local for row, local, count in spans]
        rows = [row + extra for row, local, count in spans for extra in range(count)]
        self.inner = inner
        rows = [row + extra for row, local, count in spans for extra in range(count)]
        if inner:
            self.x_walls = {}
            self.valid = geometry.domain
            self.kinds = [0]
            return
        ids = Rows([row + jnp.zeros((SUBLANES, LANES), jnp.int32) for row in rows])
        self.x_walls = {1: ids == geometry.low_row, -1: ids == geometry.high_row - 1}
        self.valid = ids.each(
            lambda part: geometry.domain & (part >= geometry.low_row) & (part < geometry.high_row)
        )
        self.kinds = [
            jnp.where(row == geometry.low_row, 1, 0) + jnp.where(row == geometry.high_row - 1, 2, 0)
            for row in rows
        ]

    def load(self, ref, index, offset=0, tile_offset=0):
        return Rows([
            read_row(ref, index, local + offset + extra, tile_offset)
            for row, local, count in self.spans
            for extra in range(count)
        ])

    def store(self, ref, index, values):
        targets = [
            target + extra
            for (row, local, count), target in zip(self.spans, self.store_rows)
            for extra in range(count)
        ]
        for target, part in zip(targets, values.parts):
            write_row(ref, index, target, part)

    def wall_terms(self, walls, position):
        terms = [walls[position, flat_rows(kind, 1), :] for kind in self.kinds]
        return terms[0] if self.inner else Rows(terms)


def fill_wall_table(walls, geometry):
    one = jnp.ones((SUBLANES, LANES), jnp.float32)
    up_y, down_y, up_z, down_z = [
        jnp.where(geometry.walls[key], 0.0, one) for key in ((-1, 0), (1, 0), (0, -1), (0, 1))
    ]
    sum_y, sum_z = up_y + down_y, up_z + down_z
    for kind, (up_x, down_x) in enumerate(((1.0, 1.0), (1.0, 0.0), (0.0, 1.0))):
        sum_x = up_x + down_x
        around_x = 2.0 + sum_y + sum_z
        total = 12.0 + 2.0 * (sum_x + sum_y + sum_z) + sum_x * (sum_y + sum_z) + sum_y * sum_z
        rows = (
            (up_x - down_x) * around_x,
            (up_y - down_y) * (2.0 + sum_x + sum_z),
            (up_z - down_z) * (2.0 + sum_x + sum_y),
            36.0 - total,
        )
        for position, row in enumerate(rows):
            walls[position, flat_rows(kind, 1), :] = row


VELOCITIES = tuple(
    tuple(sign if axis == place else 0 for place in range(3)) for axis in range(3) for sign in (1, -1)
) + tuple(
    tuple({a: one, b: two}.get(place, 0) for place in range(3))
    for a, b in ((0, 1), (0, 2), (1, 2))
    for one, two in ((1, 1), (-1, -1), (1, -1), (-1, 1))
)
VELOCITIES = ((0, 0, 0),) + VELOCITIES


def colour_stage(block, geometry, fields, colours):
    density = block.load(fields, 0)
    red = block.load(fields, 10)
    colour = select(block.valid, 2.0 * red - density, 0.0)
    along_y = geometry.from_low_y(colour) + geometry.from_high_y(colour)
    along_z = geometry.from_low_z(colour) + geometry.from_high_z(colour)
    block.store(colours, 0, colour)
    block.store(colours, 1, 2.0 * colour + (along_y + along_z))
    block.store(colours, 2, along_y)
    block.store(colours, 3, along_z)


def collide_stage(block, geometry, fields, solids, colours, walls, state):
    relaxing = 1.0 - 1.0 / RELAX_TIME
    third = 1.0 / 3.0
    colour = block.load(colours, 0)
    doubled = 2.0 * colour + (block.load(colours, 0, -1) + block.load(colours, 0, 1))
    term_y = doubled + block.load(colours, 3)
    term_z = doubled + block.load(colours, 2)
    grad_x = block.load(colours, 1, 1) - block.load(colours, 1, -1)
    grad_y = geometry.from_high_y(term_y) - geometry.from_low_y(term_y)
    grad_z = geometry.from_high_z(term_z) - geometry.from_low_z(term_z)
    if not block.inner:
        grad_x = grad_x - block.wall_terms(walls, 0) * colour
    grad_y = grad_y - block.wall_terms(walls, 1) * colour
    grad_z = grad_z - block.wall_terms(walls, 2) * colour

    fluid = block.load(solids, PLANES - 1) == 0.0
    density = block.load(fields, 0)
    red = block.load(fields, 10)
    flux = [block.load(fields, 1 + axis) for axis in range(3)]
    stress = [block.load(fields, 4 + part) for part in range(6)]
    square_xx, square_yy, square_zz = grad_x * grad_x, grad_y * grad_y, grad_z * grad_z
    square = square_xx + square_yy + square_zz
    inverse = select(fluid, (1.0 + square * (1.0 / 144.0)).each(lax.rsqrt), 0.0)
    trace = third * square
    strength = (SURFACE / (8.0 * 144.0)) * inverse
    keep = select(fluid, relaxing / 8.0, 1.0 / 8.0)
    eighths = [0.125 * part for part in flux]
    own = [
        eighths[axis] * flux[axis] + (keep * stress[axis] + strength * (squared - trace))
        for axis, squared in enumerate((square_xx, square_yy, square_zz))
    ]
    strength, keep = 2.0 * strength, 2.0 * keep
    quarters = [2.0 * part for part in eighths[:2]]
    grads = (grad_x, grad_y, grad_z)
    cross = [
        quarters[a] * flux[b] + (keep * stress[3 + plane] + strength * (grads[a] * grads[b]))
        for plane, (a, b) in enumerate(((0, 1), (0, 2), (1, 2)))
    ]
    base = density * (1.0 / 36.0) - third * (own[0] + own[1] + own[2])
    sign = select(fluid, 1.0 / 12.0, -1.0 / 12.0)
    run = [sign * part for part in flux]
    mixing = ((SEPARATION / 144.0) * red) * ((density - red) * inverse)
    red_run = [0.5 * part + mixing * grad for part, grad in zip(run, grads)]
    moved, reds = state
    block.store(moved, 0, 12.0 * base)
    straight = [base + part for part in own]
    for axis in range(3):
        middle = 2.0 * straight[axis]
        swing = 2.0 * run[axis]
        block.store(moved, 1 + 2 * axis, middle + swing)
        block.store(moved, 2 + 2 * axis, middle - swing)
    for plane, (a, b) in enumerate(((0, 1), (0, 2), (1, 2))):
        middle = straight[a] + own[b]
        same, other = middle + cross[plane], middle - cross[plane]
        along, against = run[a] + run[b], run[a] - run[b]
        first = 7 + 4 * plane
        block.store(moved, first, same + along)
        block.store(moved, first + 1, same - along)
        block.store(moved, first + 2, other + against)
        block.store(moved, first + 3, other - against)

    red_base = select(block.valid, red * (1.0 / 36.0), 0.0)
    red_run = [select(block.valid, part, 0.0) for part in red_run]
    block.store(reds, 0, red_base)
    block.store(reds, 1, red_base + red_run[0])
    block.store(reds, 2, red_base - red_run[0])
    block.store(reds, 3, red_run[1])
    block.store(reds, 4, red_run[2])


def arrive_stage(block, geometry, walls, state, fields):
    third = 1.0 / 3.0
    moved, reds = state
    own = [None] * MOVED

    def here(direction):
        if own[direction] is None:
            own[direction] = block.load(moved, direction)
        return own[direction]

    def arrived(direction, opposite):
        vel_x, vel_y, vel_z = VELOCITIES[direction]
        values = here(direction) if vel_x == 0 else block.load(moved, direction, -vel_x)
        if vel_y != 0:
            beside = block.load(moved, direction, -vel_x, -vel_y)
            leaving = geometry.last_lanes if vel_y == 1 else geometry.first_lanes
            values = select(leaving, beside, values)
        if vel_y != 0 or vel_z != 0:
            values = roll_lanes(values, TILE * vel_y + vel_z)
        masks = []
        if vel_x in block.x_walls:
            masks.append(block.x_walls[vel_x])
        if (vel_y, vel_z) in geometry.walls:
            masks.append(geometry.walls[vel_y, vel_z])
        if not masks:
            return values
        wall = functools.reduce(lambda one, two: one | two, masks)
        return select(wall, here(opposite), values)

    red = block.load(reds, 0)
    red_y = block.load(reds, 3)
    red_z = block.load(reds, 4)
    from_x = block.load(reds, 1, -1) + block.load(reds, 2, 1)
    spread = 2.0 * red + from_x
    spread_y = 2.0 * red_y + (block.load(reds, 3, -1) + block.load(reds, 3, 1))
    spread_z = 2.0 * red_z + (block.load(reds, 4, -1) + block.load(reds, 4, 1))
    up_y, down_y = red + red_y, red - red_y
    low_y = (
        (spread + spread_y)
        + geometry.from_low_z(up_y + red_z)
        + geometry.from_high_z(up_y - red_z)
    )
    high_y = (
        (spread - spread_y)
        + geometry.from_low_z(down_y + red_z)
        + geometry.from_high_z(down_y - red_z)
    )
    bounced = (
        block.wall_terms(walls, 3) * red
        - block.wall_terms(walls, 1) * red_y
        - block.wall_terms(walls, 2) * red_z
    )
    if not block.inner:
        bounced = bounced - block.wall_terms(walls, 0) * (block.load(reds, 1) - red)
    red_total = (
        12.0 * red
        + 2.0 * from_x
        + geometry.from_low_z(spread + spread_z)
        + geometry.from_high_z(spread - spread_z)
        + geometry.from_low_y(low_y)
        + geometry.from_high_y(high_y)
        + bounced
    )
    rest = here(0)
    sums, diffs = [], []
    for axis in range(3):
        up = arrived(1 + 2 * axis, 2 + 2 * axis)
        down = arrived(2 + 2 * axis, 1 + 2 * axis)
        sums.append(up + down)
        diffs.append(up - down)
    total = rest + sums[0] + sums[1] + sums[2]
    cross = []
    for plane, (a, b) in enumerate(((0, 1), (0, 2), (1, 2))):
        first = 7 + 4 * plane
        parts = [arrived(first + offset, first + (offset ^ 1)) for offset in range(4)]
        same, other = parts[0] + parts[1], parts[2] + parts[3]
        along, against = parts[0] - parts[1], parts[2] - parts[3]
        both = same + other
        cross.append(same - other)
        total = total + both
        sums[a], sums[b] = sums[a] + both, sums[b] + both
        diffs[a], diffs[b] = diffs[a] + (along + against), diffs[b] + (along - against)
    shared = third * total
    block.store(fields, 0, total)
    for axis in range(3):
        block.store(fields, 1 + axis, diffs[axis])
        block.store(fields, 4 + axis, sums[axis] - shared - diffs[axis] * diffs[axis])
    for plane, (a, b) in enumerate(((0, 1), (0, 2), (1, 2))):
        block.store(fields, 7 + plane, cross[plane] - diffs[a] * diffs[b])
    block.store(fields, 10, red_total)


def over_rows(geometry, first, size, blocks, stage):
    trip = size * blocks
    rest = -2 * first % trip
    assert TILE % trip == 0 and rest % min(size, rest or size) == 0

    def run(start, count, step_size):
        for offset in range(0, count, step_size):
            row = start + offset
            stage(Block(geometry, [(row, row, step_size)], inner=True))

    def step(index, carry):
        run(first + index * trip, trip, size)
        return carry

    trips = (geometry.live - 2 * first - rest) // trip
    lax.fori_loop(0, trips, step, 0)
    if rest:
        run(geometry.live - first - rest, rest, min(size, rest))


def block_tiles():
    return lax.broadcasted_iota(jnp.int32, (SUBLANES, LANES), 0)


def roll_tiles(block, amount):
    return pltpu.roll(block, amount % SUBLANES, 0)


def pack_blocks(blocks):
    tiles, rest = block_tiles(), blocks[GROUP - 1]
    packed = []
    for number, block in enumerate(blocks[: GROUP - 1]):
        low, high = 2 * number + 1, 2 * number + 2
        block = jnp.where(tiles == 0, roll_tiles(rest, -low), block)
        packed.append(jnp.where(tiles == SUBLANES - 1, roll_tiles(rest, SUBLANES - 1 - high), block))
    return packed


def unpack_blocks(packed):
    tiles, rest = block_tiles(), None
    for number, block in enumerate(packed):
        low, high = 2 * number + 1, 2 * number + 2
        part = jnp.where(tiles == low, roll_tiles(block, low), roll_tiles(block, high - SUBLANES + 1))
        rest = part if rest is None else jnp.where(tiles >= low, part, rest)
    return list(packed) + [rest]


def spread_tile(raw, raw_solid, index, row, target, target_row):
    source = raw_solid if index == FIELDS else raw.at[index]
    for tile in range(OWN_TILES):
        values = source[pl.ds(row, SUBLANES), pl.ds(tile * LANES, LANES)].astype(jnp.float32)
        start = target_row * SUBLANES + 1 + tile
        target[index, pl.ds(start, SUBLANES, stride=SUBLANES), :] = values


def load_kernel(
    tiles_count, density, momentum, stress, red, solid, widths,
    info, raw, raw_solid, packet, mine,
    first_tile, last_tile, held_widths, sems,
):
    row_count, flat_count = raw_solid.shape
    own_tiles = flat_count // LANES
    copies = [
        pltpu.make_async_copy(widths, held_widths, sems.at[0]),
        pltpu.make_async_copy(density, raw.at[0], sems.at[1]),
        pltpu.make_async_copy(momentum, raw.at[pl.ds(1, 3)], sems.at[2]),
        pltpu.make_async_copy(red, raw.at[10], sems.at[3]),
        pltpu.make_async_copy(solid, raw_solid, sems.at[4]),
        pltpu.make_async_copy(stress.at[pl.ds(0, 3)], raw.at[pl.ds(4, 3)], sems.at[5]),
        pltpu.make_async_copy(stress.at[pl.ds(3, 3)], raw.at[pl.ds(7, 3)], sems.at[6]),
    ]
    for copy in copies:
        copy.start()
    tiles_index, sub_index = lax.axis_index("tiles"), lax.axis_index("sub")
    low_part = sub_index == 0
    edge_start = pl.multiple_of(jnp.where(low_part, (own_tiles - 1) * LANES, 0), LANES)

    copies[0].wait()
    live = held_widths[tiles_index] * TILE
    info[0] = live
    info[1] = (tiles_index == 0).astype(jnp.int32)
    info[2] = (tiles_index == tiles_count - 1).astype(jnp.int32)
    info[3] = sub_index

    near_cut = lax.broadcasted_iota(jnp.int32, (SUBLANES, LANES), 1) < HALF
    near_cut = near_cut == jnp.logical_not(low_part)
    near_last = pl.multiple_of(live - SUBLANES, SUBLANES)
    ready = {0: copies[1], 1: copies[2], 10: copies[3], 11: copies[4], 4: copies[5], 7: copies[6]}
    for index in (0, 1, 2, 3, 10, 11, 4, 5, 6, 7, 8, 9):
        if index in ready:
            ready[index].wait()
        for target, row in ((first_tile, 0), (last_tile, near_last)):
            spread_tile(raw, raw_solid, index, row, target, 0)

    edges = pl.ds(edge_start, LANES)
    for pair in range(PAIRS):
        later = raw_solid if pair + PAIRS == FIELDS else raw.at[pair + PAIRS]
        for row in range(0, row_count, SUBLANES):
            rows = pl.ds(row, SUBLANES)
            beside = pltpu.roll(later[rows, edges].astype(jnp.float32), HALF, 1)
            both = jnp.where(near_cut, raw[pair, rows, edges], beside)
            packet[pl.ds(pair * row_count + row, SUBLANES), :] = both

    after = PAIRS * row_count
    ends = ((packet, after, jnp.logical_not(low_part)), (mine, 0, low_part))
    for target, at, use_last in ends:
        def row_of(index, number_first, number_last):
            first = first_tile[index, flat_rows(number_first, 1), :]
            last = last_tile[index, flat_rows(number_last, 1), :]
            return jnp.where(use_last, last, first)

        place = pl.ds(at + PACKED * SUBLANES, SUBLANES)
        ends_row = (FULL, SUBLANES - HALO)
        target[place, :] = 2.0 * row_of(10, *ends_row) - row_of(0, *ends_row)
        for group in range(FULL * PLANES // GROUP):
            blocks = []
            for number in range(group * GROUP, (group + 1) * GROUP):
                index, extra = divmod(number, FULL)
                blocks.append(row_of(index, extra, SUBLANES - FULL + extra))
            for number, block in enumerate(pack_blocks(blocks)):
                place = at + (group * (GROUP - 1) + number) * SUBLANES
                target[pl.ds(place, SUBLANES), :] = block


def load_inputs(arrays, widths, tiles_count):
    row_count, flat_count = arrays[0].shape
    packet_rows = PAIRS * row_count + END_ROWS
    return pl.pallas_call(
        functools.partial(load_kernel, tiles_count),
        out_shape=[
            pltpu.SMEM((4,), jnp.int32),
            jax.ShapeDtypeStruct((FIELDS, row_count, flat_count), jnp.float32),
            jax.ShapeDtypeStruct((row_count, flat_count), jnp.int32),
            jax.ShapeDtypeStruct((packet_rows, LANES), jnp.float32),
            jax.ShapeDtypeStruct((END_ROWS, LANES), jnp.float32),
        ],
        in_specs=[HBM] * 6,
        out_specs=[SMEM, VMEM, VMEM, VMEM, VMEM],
        scratch_shapes=[
            pltpu.VMEM((PLANES, SUBLANES * SUBLANES, LANES), jnp.float32),
            pltpu.VMEM((PLANES, SUBLANES * SUBLANES, LANES), jnp.float32),
            pltpu.SMEM(widths.shape, jnp.int32),
            pltpu.SemaphoreType.DMA((7,)),
        ],
        compiler_params=pltpu.CompilerParams(vmem_limit_bytes=16 * 1024 * 1024),
        name="load",
    )(*[pltpu.with_memory_space_constraint(array, pltpu.HBM) for array in (*arrays, widths)])


def spread_kernel(raw, raw_solid, spread):
    for index in range(PLANES):
        for row in range(0, raw_solid.shape[0], SUBLANES):
            spread_tile(raw, raw_solid, index, row, spread, row)


def spread_rows(raw, raw_solid):
    row_count = raw_solid.shape[0]
    return pl.pallas_call(
        spread_kernel,
        out_shape=jax.ShapeDtypeStruct((PLANES, row_count * SUBLANES, LANES), jnp.float32),
        in_specs=[VMEM, VMEM],
        out_specs=VMEM,
        compiler_params=pltpu.CompilerParams(vmem_limit_bytes=16 * 1024 * 1024),
        cost_estimate=pl.CostEstimate(flops=1_000_000, bytes_accessed=4_000_000, transcendentals=0),
        name="spread",
    )(raw, raw_solid)


def join_kernel(info, spread, packet, mine, whole, ends):
    low_part = info[3] == 0
    row_count = spread.shape[1] // SUBLANES
    ends[pl.ds(0, END_ROWS), :] = mine[...]
    ends[pl.ds(END_ROWS, END_ROWS), :] = packet[pl.ds(PAIRS * row_count, END_ROWS), :]
    for pair in range(PAIRS):
        for row in range(0, row_count, SUBLANES):
            both = packet[pl.ds(pair * row_count + row, SUBLANES), :]
            start = row * SUBLANES
            for index, values in ((pair, both), (pair + PAIRS, pltpu.roll(both, HALF, 1))):
                below = jnp.where(low_part, 0.0, values)
                above = jnp.where(low_part, values, 0.0)
                whole[index, pl.ds(start, SUBLANES, stride=SUBLANES), :] = below
                whole[index, pl.ds(start + SUBLANES - 1, SUBLANES, stride=SUBLANES), :] = above


def join_parts(info, spread, packet, mine):
    return pl.pallas_call(
        join_kernel,
        out_shape=[
            jax.ShapeDtypeStruct(spread.shape, jnp.float32),
            jax.ShapeDtypeStruct((2 * END_ROWS, LANES), jnp.float32),
        ],
        in_specs=[SMEM, VMEM, VMEM, VMEM],
        out_specs=[VMEM] * 2,
        input_output_aliases={1: 0},
        compiler_params=pltpu.CompilerParams(vmem_limit_bytes=16 * 1024 * 1024),
        name="join",
    )(info, pltpu.with_memory_space_constraint(spread, pltpu.VMEM), packet, mine)


def keep_rows(target, source, rows, size):
    for place, row in enumerate(rows):
        for extra in range(size):
            target[place * size + extra] = source[row + extra]


def collide_rows(geometry, before, whole, first, colours, walls, state):
    over_rows(geometry, first - 1, *COLOUR_BLOCK, lambda block: colour_stage(
        block, geometry, before, colours))
    over_rows(geometry, first, *COLLIDE_BLOCK, lambda block: collide_stage(
        block, geometry, before, whole, colours, walls, state))


def first_kernel(
    info, whole, moved_later, reds_later,
    moved_rim, reds_rim, fields_rim, moved_later_rim, reds_later_rim, final_rim,
    colours, walls, moved, reds, fields,
):
    state, later = (ByRow(moved), ByRow(reds)), (ByRow(moved_later), ByRow(reds_later))
    geometry = Geometry(info, OWN_TILES)
    live = geometry.live
    fill_wall_table(walls, geometry)
    collide_rows(geometry, whole, whole, 1, ByRow(colours), walls, state)
    over_rows(geometry, 2, *ARRIVE_BLOCK, lambda block: arrive_stage(
        block, geometry, walls, state, ByRow(fields)))
    keep_rows(moved_rim, moved, (1, live - 3), KEPT)
    keep_rows(reds_rim, reds, (1, live - 3), KEPT)
    keep_rows(fields_rim, fields, (2, live - 4), KEPT)
    collide_rows(geometry, ByRow(fields), whole, 3, ByRow(colours), walls, later)
    edge = Block(geometry, [(RIM, RIM, RIM), (live - 2 * RIM, live - 2 * RIM, RIM)], True, [0, RIM])
    arrive_stage(edge, geometry, walls, later, final_rim)
    keep_rows(moved_later_rim, moved_later, (3, live - 5), KEPT)
    keep_rows(reds_later_rim, reds_later, (3, live - 5), KEPT)


def tile_copies(pieces, outs, held_row, out_row, sems):
    held, rows = pl.ds(held_row, SUBLANES), pl.ds(out_row, SUBLANES)
    parts = (
        (pieces.at[0, held], outs[0].at[rows]),
        (pieces.at[pl.ds(1, 3), held], outs[1].at[:, rows]),
        (pieces.at[pl.ds(4, 6), held], outs[2].at[:, rows]),
        (pieces.at[10, held], outs[3].at[rows]),
    )
    return [
        pltpu.make_async_copy(source, target, sems.at[number])
        for number, (source, target) in enumerate(parts)
    ]


def gather_tiles(final, row, pieces, held_row):
    for index in range(FIELDS):
        for tile in range(OWN_TILES):
            start = pl.multiple_of(row * SUBLANES, SUBLANES) + 1 + tile
            pieces[index, pl.ds(held_row, SUBLANES), pl.ds(tile * LANES, LANES)] = final[
                index, pl.ds(start, SUBLANES, stride=SUBLANES), :
            ]


def second_kernel(
    info, moved, reds, arrived, density_out, momentum_out, stress_out, red_out,
    final, walls, pieces, zeros, sems,
):
    outs = (density_out, momentum_out, stress_out, red_out)
    row_tiles = density_out.shape[0] // SUBLANES
    geometry = Geometry(info, OWN_TILES)
    live = geometry.live
    fill_wall_table(walls, geometry)

    zeros[...] = jnp.zeros(zeros.shape, zeros.dtype)
    dead = {}
    for tile in range(row_tiles):
        dead[tile] = tile_copies(zeros, outs, 0, tile * SUBLANES, sems.at[tile])

        @pl.when(tile * SUBLANES >= live)
        def _():
            for copy in dead[tile]:
                copy.start()

    def copies_of(tile):
        row = pl.multiple_of(tile * SUBLANES, SUBLANES)
        return tile_copies(pieces, outs, row, row, sems.at[tile])

    def finish(tile, carry):
        row = pl.multiple_of(tile * SUBLANES, SUBLANES)
        block = Block(geometry, [(row, row, SUBLANES)], inner=True)
        arrive_stage(block, geometry, walls, (ByRow(moved), ByRow(reds)), final)
        gather_tiles(final, row, pieces, row)
        for copy in copies_of(tile):
            copy.start()
        return carry

    def settle(tile, carry):
        for copy in copies_of(tile):
            copy.wait()
        return carry

    last = live // SUBLANES - 1
    lax.fori_loop(1, last, finish, 0)
    lax.fori_loop(1, last, settle, 0)
    for tile in range(row_tiles):

        @pl.when(tile * SUBLANES >= live)
        def _():
            for copy in dead[tile]:
                copy.wait()


def by_row(rows, count):
    return jax.ShapeDtypeStruct((rows, count * SUBLANES, LANES), jnp.float32)


def run_first(info, whole):
    rows = whole.shape[1] // SUBLANES
    shapes = [
        by_row(rows, HELD),
        by_row(rows, REDS),
        by_row(2 * KEPT, HELD),
        by_row(2 * KEPT, REDS),
        by_row(2 * KEPT, FIELDS),
        by_row(2 * KEPT, HELD),
        by_row(2 * KEPT, REDS),
        jax.ShapeDtypeStruct((FIELDS, 2 * RIM * SUBLANES, LANES), jnp.float32),
    ]
    scratch = [by_row(rows, 4), by_row(4, 3), by_row(rows, HELD), by_row(rows, REDS), by_row(rows, FIELDS)]
    return pl.pallas_call(
        first_kernel,
        out_shape=shapes,
        in_specs=[SMEM, VMEM],
        out_specs=[VMEM] * len(shapes),
        scratch_shapes=[pltpu.VMEM(shape.shape, shape.dtype) for shape in scratch],
        compiler_params=pltpu.CompilerParams(vmem_limit_bytes=24 * 1024 * 1024),
        cost_estimate=pl.CostEstimate(flops=20_000_000, bytes_accessed=8_000_000, transcendentals=0),
        name="first",
    )(info, whole)


def run_second(info, state, arrived, arrays):
    row_count, flat_count = arrays[0].shape
    flat = row_count * SUBLANES
    shapes = [jax.ShapeDtypeStruct(array.shape, jnp.float32) for array in arrays[:4]]
    return pl.pallas_call(
        second_kernel,
        out_shape=shapes,
        in_specs=[SMEM, VMEM, VMEM, ANY],
        out_specs=[ANY] * 4,
        scratch_shapes=[
            pltpu.VMEM((FIELDS, flat, LANES), jnp.float32),
            pltpu.VMEM((4, 3 * SUBLANES, LANES), jnp.float32),
            pltpu.VMEM((FIELDS, row_count, flat_count), jnp.float32),
            pltpu.VMEM((FIELDS, SUBLANES, flat_count), jnp.float32),
            pltpu.SemaphoreType.DMA((row_count // SUBLANES, 4)),
        ],
        compiler_params=pltpu.CompilerParams(vmem_limit_bytes=24 * 1024 * 1024),
        cost_estimate=pl.CostEstimate(flops=20_000_000, bytes_accessed=8_000_000, transcendentals=0),
        name="second",
    )(info, *state, arrived)


def follow_kernel(ends, kept, out):
    out[pl.ds(PACKED * SUBLANES, 1), :] = jnp.zeros((1, LANES), jnp.float32)


def follow(ends, kept):
    return pl.pallas_call(
        follow_kernel,
        out_shape=jax.ShapeDtypeStruct(ends.shape, jnp.float32),
        in_specs=[VMEM, ANY],
        out_specs=VMEM,
        input_output_aliases={0: 0},
        compiler_params=pltpu.CompilerParams(vmem_limit_bytes=8 * 1024 * 1024),
        name="follow",
    )(pltpu.with_memory_space_constraint(ends, pltpu.VMEM), kept)


def outer_kernel(
    info, whole, arrived, passed,
    moved_rim, reds_rim, fields_rim, moved_later_rim, reds_later_rim, final_rim, *refs,
):
    outs = refs[4:8]
    start_fields, colours, walls, fields, final = refs[8:13]
    moved, reds, moved_later, reds_later, pieces, sems = refs[13:]
    state, later = (ByRow(moved), ByRow(reds)), (ByRow(moved_later), ByRow(reds_later))
    geometry = Geometry(info, OWN_TILES)
    live = geometry.live
    low_part = info[3] == 0
    fill_wall_table(walls, geometry)

    def ends_of(ref, half):
        blocks = []
        for group in range(FULL * PLANES // GROUP):
            first = half * (PACKED + 1) + group * (GROUP - 1)
            packed = [ref[pl.ds((first + k) * SUBLANES, SUBLANES), :] for k in range(GROUP - 1)]
            blocks = blocks + unpack_blocks(packed)
        last = half * (PACKED + 1) + PACKED
        return blocks + [ref[pl.ds(last * SUBLANES, SUBLANES), :]]

    tiles = block_tiles()
    middle = (tiles >= 1) & (tiles <= OWN_TILES)

    def widened(own, other):
        beside = jnp.where(tiles == 0, roll_tiles(other, -OWN_TILES), roll_tiles(other, OWN_TILES))
        return jnp.where(geometry.domain, jnp.where(middle, own, beside), 0.0)

    straight = [widened(*pair) for pair in zip(ends_of(arrived, 0), ends_of(arrived, 1))]
    crossed = [widened(*pair) for pair in zip(ends_of(passed, 1), ends_of(passed, 0))]
    below = [jnp.where(low_part, *pair) for pair in zip(straight, crossed)]
    above = [jnp.where(low_part, *pair) for pair in zip(crossed, straight)]

    def spans(first, count):
        mirrored = SLAB - first - count
        return [
            (first - HALO, first, count),
            (live - 2 * RIM + mirrored, SLAB + mirrored, count),
        ]

    for index in range(PLANES):
        for extra in range(FULL):
            number = FULL * index + extra
            start_fields[index, flat_rows(1 + extra, 1), :] = below[number]
            start_fields[index, flat_rows(2 * SLAB - HALO + extra, 1), :] = above[number]
        start_fields[index, flat_rows(HALO, 2), :] = whole[index, flat_rows(0, 2), :]
        start_fields[index, flat_rows(2 * SLAB - HALO - 2, 2), :] = whole[
            index, flat_rows(live - 2, 2), :
        ]
    for row, colour in ((0, below[-1]), (2 * SLAB - 1, above[-1])):
        start_fields[0, flat_rows(row, 1), :] = jnp.zeros((SUBLANES, LANES), jnp.float32)
        start_fields[10, flat_rows(row, 1), :] = 0.5 * colour

    def place(target, source, first, size):
        for number, (row, local, count) in enumerate(spans(first, size)):
            for extra in range(size):
                target[local + extra] = source[number * size + extra]

    place(moved, moved_rim, HALO + 1, KEPT)
    place(reds, reds_rim, HALO + 1, KEPT)
    place(fields, fields_rim, HALO + 2, KEPT)
    place(moved_later, moved_later_rim, HALO + 3, KEPT)
    place(reds_later, reds_later_rim, HALO + 3, KEPT)
    for index in range(FIELDS):
        for number, (row, local, count) in enumerate(spans(HALO + RIM, RIM)):
            final[index, flat_rows(local, RIM), :] = final_rim[index, flat_rows(number * RIM, RIM), :]

    block = lambda first, count: Block(geometry, spans(first, count))
    colour_stage(block(0, 6), geometry, start_fields, ByRow(colours))
    collide_stage(block(1, 4), geometry, start_fields, start_fields, ByRow(colours), walls, state)
    arrive_stage(block(2, 4), geometry, walls, state, ByRow(fields))
    start_fields[PLANES - 1, flat_rows(HALO + 2, 1), :] = whole[PLANES - 1, flat_rows(2, 1), :]
    start_fields[PLANES - 1, flat_rows(2 * SLAB - HALO - 3, 1), :] = whole[
        PLANES - 1, flat_rows(live - 3, 1), :
    ]
    colour_stage(block(2, 6), geometry, ByRow(fields), ByRow(colours))
    collide_stage(block(3, 4), geometry, ByRow(fields), start_fields, ByRow(colours), walls, later)
    arrive_stage(block(4, 4), geometry, walls, later, final)

    copies = []
    for side, row, out_row in ((0, HALO, 0), (1, SLAB, live - SUBLANES)):
        gather_tiles(final, row, pieces, side * SUBLANES)
        out_row = pl.multiple_of(out_row, SUBLANES)
        copies = copies + tile_copies(pieces, outs, side * SUBLANES, out_row, sems.at[side])
    for copy in copies:
        copy.start()
    for copy in copies:
        copy.wait()


def run_outer(info, whole, arrived, passed, rims, outs):
    flat = 2 * SLAB * SUBLANES
    scratch = lambda count: pltpu.VMEM((2 * SLAB, count * SUBLANES, LANES), jnp.float32)
    flat_count = outs[0].shape[1]
    return pl.pallas_call(
        outer_kernel,
        out_shape=[jax.ShapeDtypeStruct(out.shape, jnp.float32) for out in outs],
        in_specs=[SMEM] + [VMEM] * 9 + [ANY] * 4,
        out_specs=[ANY] * 4,
        scratch_shapes=[
            pltpu.VMEM((PLANES, flat, LANES), jnp.float32),
            scratch(4),
            pltpu.VMEM((4, 3 * SUBLANES, LANES), jnp.float32),
            scratch(FIELDS),
            pltpu.VMEM((FIELDS, flat, LANES), jnp.float32),
        ]
        + [scratch(count) for count in (HELD, REDS, HELD, REDS)]
        + [
            pltpu.VMEM((FIELDS, 2 * SUBLANES, flat_count), jnp.float32),
            pltpu.SemaphoreType.DMA((2, 4)),
        ],
        input_output_aliases={10: 0, 11: 1, 12: 2, 13: 3},
        compiler_params=pltpu.CompilerParams(vmem_limit_bytes=32 * 1024 * 1024),
        name="outer",
    )(info, whole, arrived, passed, *rims, *outs)


def body(density, momentum, stress, red_density, solid, widths):
    tiles_count = lax.axis_size("tiles")
    arrays = (density, momentum, stress, red_density, solid)
    info, raw, raw_solid, packet, mine = load_inputs(arrays, widths, tiles_count)
    info = pltpu.with_memory_space_constraint(info, pltpu.SMEM)
    swap = [(0, 1), (1, 0)]
    packet = lax.ppermute(packet, "sub", swap)
    spread = spread_rows(raw, raw_solid)
    whole, ends = join_parts(info, spread, packet, mine)
    route = [(2 * k, 2 * k + 2) for k in range(tiles_count - 1)]
    route = route + [(2 * k + 3, 2 * k + 1) for k in range(tiles_count - 1)]
    arrived = lax.ppermute(ends, ("tiles", "sub"), route)
    moved, reds, *rims = run_first(info, whole)
    arrived = follow(arrived, rims[-1])
    passed = lax.ppermute(arrived, "sub", swap)
    outs = run_second(info, (moved, reds), arrived, arrays)
    return tuple(run_outer(info, whole, arrived, passed, rims, outs))


def solution(mesh):
    in_specs = (
        P(("groups", "tiles"), "sub"),
        P(None, ("groups", "tiles"), "sub"),
        P(None, ("groups", "tiles"), "sub"),
        P(("groups", "tiles"), "sub"),
        P(("groups", "tiles"), "sub"),
        P("groups"),
    )
    out_specs = (
        P(("groups", "tiles"), "sub"),
        P(None, ("groups", "tiles"), "sub"),
        P(None, ("groups", "tiles"), "sub"),
        P(("groups", "tiles"), "sub"),
    )
    return jax.shard_map(body, mesh=mesh, in_specs=in_specs, out_specs=out_specs, check_vma=False)
```

```python
import functools

import jax
import jax.numpy as jnp
from jax import lax
from jax.experimental import pallas as pl
from jax.experimental.pallas import tpu as pltpu
from jax.sharding import PartitionSpec as P

TILE = 16
STEPS = 2
RELAX_TIME = 0.8
SURFACE = 0.1
SEPARATION = 0.7

LANES = 128
SUBLANES = 8
FULL = 3
HALO = FULL + 1
FIELDS = 11
PLANES = FIELDS + 1
MOVED = 19
REDS = 5
HELD = MOVED + 1
RIM = 4
SLAB = HALO + 2 * RIM
OWN_TILES = SUBLANES - 2
GROUP = 4
PACKED = FULL * PLANES // GROUP * (GROUP - 1)
END_ROWS = (PACKED + 1) * SUBLANES
HALF = LANES // 2
PAIRS = PLANES // 2
SPLIT = 3
KEPT = 2
COLOUR_BLOCK = (8, 1)
COLLIDE_BLOCK = (2, 4)
ARRIVE_BLOCK = (8, 1)
VMEM = pl.BlockSpec(memory_space=pltpu.VMEM)
SMEM = pl.BlockSpec(memory_space=pltpu.SMEM)
ANY = pl.BlockSpec(memory_space=pl.ANY)
HBM = pl.BlockSpec(memory_space=pltpu.HBM)


class Rows:
    def __init__(self, parts):
        self.parts = parts

    def _with(self, other, operation):
        others = other.parts if isinstance(other, Rows) else [other] * len(self.parts)
        return Rows([operation(one, two) for one, two in zip(self.parts, others)])

    def __add__(self, other):
        return self._with(other, lambda one, two: one + two)

    def __sub__(self, other):
        return self._with(other, lambda one, two: one - two)

    def __rsub__(self, other):
        return self._with(other, lambda one, two: two - one)

    def __mul__(self, other):
        return self._with(other, lambda one, two: one * two)

    def __or__(self, other):
        return self._with(other, lambda one, two: one | two)

    def __eq__(self, other):
        return self._with(other, lambda one, two: one == two)

    __radd__, __rmul__, __ror__ = __add__, __mul__, __or__

    def each(self, operation):
        return Rows([operation(part) for part in self.parts])


def select(mask, yes, no):
    count = max(len(item.parts) for item in (mask, yes, no) if isinstance(item, Rows))
    columns = [
        item.parts if isinstance(item, Rows) else [item] * count for item in (mask, yes, no)
    ]
    return Rows([jnp.where(*row) for row in zip(*columns)])


def roll_lanes(values, amount):
    return values.each(lambda part: pltpu.roll(part, amount % LANES, 1))


def roll_sublanes(values, amount):
    return values.each(lambda part: pltpu.roll(part, amount % SUBLANES, 0))


class Geometry:
    def __init__(self, info, own_tiles):
        live, first, last, sub_index = info[0], info[1], info[2], info[3]
        self.live = live
        self.low_row = jnp.where(first == 1, 0, -1000)
        self.high_row = jnp.where(last == 1, live, 1000)
        shape = (SUBLANES, LANES)
        lane = lax.broadcasted_iota(jnp.int32, shape, 1)
        tile = lax.broadcasted_iota(jnp.int32, shape, 0)
        depth = lane & (TILE - 1)
        low_part = sub_index == 0
        high_part = sub_index == 1
        z_walls = {1: depth == 0, -1: depth == TILE - 1}
        y_walls = {
            1: (tile == 1) & (lane < TILE) & low_part,
            -1: (tile == own_tiles) & (lane >= LANES - TILE) & high_part,
        }
        self.walls = {(0, vel_z): wall for vel_z, wall in z_walls.items()}
        for vel_y, y_wall in y_walls.items():
            self.walls[vel_y, 0] = y_wall
            for vel_z, z_wall in z_walls.items():
                self.walls[vel_y, vel_z] = y_wall | z_wall
        own = (tile >= 1) & (tile <= own_tiles)
        self.domain = own | ((tile == own_tiles + 1) & low_part) | ((tile == 0) & high_part)
        self.first_lanes = lane < TILE
        self.last_lanes = lane >= LANES - TILE

    def from_low_y(self, values):
        return roll_lanes(select(self.last_lanes, roll_sublanes(values, 1), values), TILE)

    def from_high_y(self, values):
        return roll_lanes(select(self.first_lanes, roll_sublanes(values, -1), values), -TILE)

    def from_low_z(self, values):
        return select(self.walls[0, 1], 0.0, roll_lanes(values, 1))

    def from_high_z(self, values):
        return select(self.walls[0, -1], 0.0, roll_lanes(values, -1))


def flat_rows(row, count, tile_offset=0):
    start = row * SUBLANES
    if not isinstance(start, int):
        start = pl.multiple_of(start, SUBLANES)
    return pl.ds(start + tile_offset, count * SUBLANES)


class ByRow:
    def __init__(self, ref):
        self.ref = ref


def by_row(rows, count):
    return jax.ShapeDtypeStruct((rows, count * SUBLANES, LANES), jnp.float32)


def place_of(ref, index, row, tile_offset=0):
    if isinstance(ref, ByRow):
        return ref.ref, row, pl.ds(index * SUBLANES + tile_offset, SUBLANES)
    return ref, index, flat_rows(row, 1, tile_offset)


def read_row(ref, index, row, tile_offset=0):
    ref, first, second = place_of(ref, index, row, tile_offset)
    return ref[first, second, :]


def write_row(ref, index, row, values):
    ref, first, second = place_of(ref, index, row)
    ref[first, second, :] = values


class Block:
    def __init__(self, geometry, spans, inner=False, store_rows=None):
        self.spans = spans
        self.store_rows = store_rows or [local for row, local, count in spans]
        rows = [row + extra for row, local, count in spans for extra in range(count)]
        self.inner = inner
        rows = [row + extra for row, local, count in spans for extra in range(count)]
        if inner:
            self.x_walls = {}
            self.valid = geometry.domain
            self.kinds = [0]
            return
        ids = Rows([row + jnp.zeros((SUBLANES, LANES), jnp.int32) for row in rows])
        self.x_walls = {1: ids == geometry.low_row, -1: ids == geometry.high_row - 1}
        self.valid = ids.each(
            lambda part: geometry.domain & (part >= geometry.low_row) & (part < geometry.high_row)
        )
        self.kinds = [
            jnp.where(row == geometry.low_row, 1, 0) + jnp.where(row == geometry.high_row - 1, 2, 0)
            for row in rows
        ]

    def load(self, ref, index, offset=0, tile_offset=0):
        return Rows([
            read_row(ref, index, local + offset + extra, tile_offset)
            for row, local, count in self.spans
            for extra in range(count)
        ])

    def store(self, ref, index, values):
        targets = [
            target + extra
            for (row, local, count), target in zip(self.spans, self.store_rows)
            for extra in range(count)
        ]
        for target, part in zip(targets, values.parts):
            write_row(ref, index, target, part)

    def wall_terms(self, walls, position):
        terms = [walls[position, flat_rows(kind, 1), :] for kind in self.kinds]
        return terms[0] if self.inner else Rows(terms)


def fill_wall_table(walls, geometry):
    one = jnp.ones((SUBLANES, LANES), jnp.float32)
    up_y, down_y, up_z, down_z = [
        jnp.where(geometry.walls[key], 0.0, one) for key in ((-1, 0), (1, 0), (0, -1), (0, 1))
    ]
    sum_y, sum_z = up_y + down_y, up_z + down_z
    for kind, (up_x, down_x) in enumerate(((1.0, 1.0), (1.0, 0.0), (0.0, 1.0))):
        sum_x = up_x + down_x
        around_x = 2.0 + sum_y + sum_z
        total = 12.0 + 2.0 * (sum_x + sum_y + sum_z) + sum_x * (sum_y + sum_z) + sum_y * sum_z
        rows = (
            (up_x - down_x) * around_x,
            (up_y - down_y) * (2.0 + sum_x + sum_z),
            (up_z - down_z) * (2.0 + sum_x + sum_y),
            36.0 - total,
        )
        for position, row in enumerate(rows):
            walls[position, flat_rows(kind, 1), :] = row


VELOCITIES = tuple(
    tuple(sign if axis == place else 0 for place in range(3)) for axis in range(3) for sign in (1, -1)
) + tuple(
    tuple({a: one, b: two}.get(place, 0) for place in range(3))
    for a, b in ((0, 1), (0, 2), (1, 2))
    for one, two in ((1, 1), (-1, -1), (1, -1), (-1, 1))
)
VELOCITIES = ((0, 0, 0),) + VELOCITIES


def colour_stage(block, geometry, fields, colours):
    density = block.load(fields, 0)
    red = block.load(fields, 10)
    colour = select(block.valid, 2.0 * red - density, 0.0)
    along_y = geometry.from_low_y(colour) + geometry.from_high_y(colour)
    along_z = geometry.from_low_z(colour) + geometry.from_high_z(colour)
    block.store(colours, 0, colour)
    block.store(colours, 1, 2.0 * colour + (along_y + along_z))
    block.store(colours, 2, along_y)
    block.store(colours, 3, along_z)


def collide_stage(block, geometry, fields, solids, colours, walls, state):
    relaxing = 1.0 - 1.0 / RELAX_TIME
    third = 1.0 / 3.0
    colour = block.load(colours, 0)
    doubled = 2.0 * colour + (block.load(colours, 0, -1) + block.load(colours, 0, 1))
    term_y = doubled + block.load(colours, 3)
    term_z = doubled + block.load(colours, 2)
    grad_x = block.load(colours, 1, 1) - block.load(colours, 1, -1)
    grad_y = geometry.from_high_y(term_y) - geometry.from_low_y(term_y)
    grad_z = geometry.from_high_z(term_z) - geometry.from_low_z(term_z)
    if not block.inner:
        grad_x = grad_x - block.wall_terms(walls, 0) * colour
    grad_y = grad_y - block.wall_terms(walls, 1) * colour
    grad_z = grad_z - block.wall_terms(walls, 2) * colour

    fluid = block.load(solids, PLANES - 1) == 0.0
    density = block.load(fields, 0)
    red = block.load(fields, 10)
    flux = [block.load(fields, 1 + axis) for axis in range(3)]
    stress = [block.load(fields, 4 + part) for part in range(6)]
    square_xx, square_yy, square_zz = grad_x * grad_x, grad_y * grad_y, grad_z * grad_z
    square = square_xx + square_yy + square_zz
    inverse = select(fluid, (1.0 + square * (1.0 / 144.0)).each(lax.rsqrt), 0.0)
    trace = third * square
    strength = (SURFACE / (8.0 * 144.0)) * inverse
    keep = select(fluid, relaxing / 8.0, 1.0 / 8.0)
    eighths = [0.125 * part for part in flux]
    own = [
        eighths[axis] * flux[axis] + (keep * stress[axis] + strength * (squared - trace))
        for axis, squared in enumerate((square_xx, square_yy, square_zz))
    ]
    strength, keep = 2.0 * strength, 2.0 * keep
    quarters = [2.0 * part for part in eighths[:2]]
    grads = (grad_x, grad_y, grad_z)
    cross = [
        quarters[a] * flux[b] + (keep * stress[3 + plane] + strength * (grads[a] * grads[b]))
        for plane, (a, b) in enumerate(((0, 1), (0, 2), (1, 2)))
    ]
    base = density * (1.0 / 36.0) - third * (own[0] + own[1] + own[2])
    sign = select(fluid, 1.0 / 12.0, -1.0 / 12.0)
    run = [sign * part for part in flux]
    mixing = ((SEPARATION / 144.0) * red) * ((density - red) * inverse)
    red_run = [0.5 * part + mixing * grad for part, grad in zip(run, grads)]
    moved, reds = state
    block.store(moved, 0, 12.0 * base)
    straight = [base + part for part in own]
    for axis in range(3):
        middle = 2.0 * straight[axis]
        swing = 2.0 * run[axis]
        block.store(moved, 1 + 2 * axis, middle + swing)
        block.store(moved, 2 + 2 * axis, middle - swing)
    for plane, (a, b) in enumerate(((0, 1), (0, 2), (1, 2))):
        middle = straight[a] + own[b]
        same, other = middle + cross[plane], middle - cross[plane]
        along, against = run[a] + run[b], run[a] - run[b]
        first = 7 + 4 * plane
        block.store(moved, first, same + along)
        block.store(moved, first + 1, same - along)
        block.store(moved, first + 2, other + against)
        block.store(moved, first + 3, other - against)

    red_base = select(block.valid, red * (1.0 / 36.0), 0.0)
    red_run = [select(block.valid, part, 0.0) for part in red_run]
    block.store(reds, 0, red_base)
    block.store(reds, 1, red_base + red_run[0])
    block.store(reds, 2, red_base - red_run[0])
    block.store(reds, 3, red_run[1])
    block.store(reds, 4, red_run[2])


def arrive_stage(block, geometry, walls, state, fields):
    third = 1.0 / 3.0
    moved, reds = state
    own = [None] * MOVED

    def here(direction):
        if own[direction] is None:
            own[direction] = block.load(moved, direction)
        return own[direction]

    def arrived(direction, opposite):
        vel_x, vel_y, vel_z = VELOCITIES[direction]
        values = here(direction) if vel_x == 0 else block.load(moved, direction, -vel_x)
        if vel_y != 0:
            beside = block.load(moved, direction, -vel_x, -vel_y)
            leaving = geometry.last_lanes if vel_y == 1 else geometry.first_lanes
            values = select(leaving, beside, values)
        if vel_y != 0 or vel_z != 0:
            values = roll_lanes(values, TILE * vel_y + vel_z)
        masks = []
        if vel_x in block.x_walls:
            masks.append(block.x_walls[vel_x])
        if (vel_y, vel_z) in geometry.walls:
            masks.append(geometry.walls[vel_y, vel_z])
        if not masks:
            return values
        wall = functools.reduce(lambda one, two: one | two, masks)
        return select(wall, here(opposite), values)

    red = block.load(reds, 0)
    red_y = block.load(reds, 3)
    red_z = block.load(reds, 4)
    from_x = block.load(reds, 1, -1) + block.load(reds, 2, 1)
    spread = 2.0 * red + from_x
    spread_y = 2.0 * red_y + (block.load(reds, 3, -1) + block.load(reds, 3, 1))
    spread_z = 2.0 * red_z + (block.load(reds, 4, -1) + block.load(reds, 4, 1))
    up_y, down_y = red + red_y, red - red_y
    low_y = (
        (spread + spread_y)
        + geometry.from_low_z(up_y + red_z)
        + geometry.from_high_z(up_y - red_z)
    )
    high_y = (
        (spread - spread_y)
        + geometry.from_low_z(down_y + red_z)
        + geometry.from_high_z(down_y - red_z)
    )
    bounced = (
        block.wall_terms(walls, 3) * red
        - block.wall_terms(walls, 1) * red_y
        - block.wall_terms(walls, 2) * red_z
    )
    if not block.inner:
        bounced = bounced - block.wall_terms(walls, 0) * (block.load(reds, 1) - red)
    red_total = (
        12.0 * red
        + 2.0 * from_x
        + geometry.from_low_z(spread + spread_z)
        + geometry.from_high_z(spread - spread_z)
        + geometry.from_low_y(low_y)
        + geometry.from_high_y(high_y)
        + bounced
    )
    rest = here(0)
    sums, diffs = [], []
    for axis in range(3):
        up = arrived(1 + 2 * axis, 2 + 2 * axis)
        down = arrived(2 + 2 * axis, 1 + 2 * axis)
        sums.append(up + down)
        diffs.append(up - down)
    total = rest + sums[0] + sums[1] + sums[2]
    cross = []
    for plane, (a, b) in enumerate(((0, 1), (0, 2), (1, 2))):
        first = 7 + 4 * plane
        parts = [arrived(first + offset, first + (offset ^ 1)) for offset in range(4)]
        same, other = parts[0] + parts[1], parts[2] + parts[3]
        along, against = parts[0] - parts[1], parts[2] - parts[3]
        both = same + other
        cross.append(same - other)
        total = total + both
        sums[a], sums[b] = sums[a] + both, sums[b] + both
        diffs[a], diffs[b] = diffs[a] + (along + against), diffs[b] + (along - against)
    shared = third * total
    block.store(fields, 0, total)
    for axis in range(3):
        block.store(fields, 1 + axis, diffs[axis])
        block.store(fields, 4 + axis, sums[axis] - shared - diffs[axis] * diffs[axis])
    for plane, (a, b) in enumerate(((0, 1), (0, 2), (1, 2))):
        block.store(fields, 7 + plane, cross[plane] - diffs[a] * diffs[b])
    block.store(fields, 10, red_total)


def over_rows(geometry, first, size, blocks, stage):
    trip = size * blocks
    rest = -2 * first % trip
    assert TILE % trip == 0 and rest % min(size, rest or size) == 0

    def run(start, count, step_size):
        for offset in range(0, count, step_size):
            row = start + offset
            stage(Block(geometry, [(row, row, step_size)], inner=True))

    def step(index, carry):
        run(first + index * trip, trip, size)
        return carry

    trips = (geometry.live - 2 * first - rest) // trip
    lax.fori_loop(0, trips, step, 0)
    if rest:
        run(geometry.live - first - rest, rest, min(size, rest))


def block_tiles():
    return lax.broadcasted_iota(jnp.int32, (SUBLANES, LANES), 0)


def roll_tiles(block, amount):
    return pltpu.roll(block, amount % SUBLANES, 0)


def pack_blocks(blocks):
    tiles, rest = block_tiles(), blocks[GROUP - 1]
    packed = []
    for number, block in enumerate(blocks[: GROUP - 1]):
        low, high = 2 * number + 1, 2 * number + 2
        block = jnp.where(tiles == 0, roll_tiles(rest, -low), block)
        packed.append(jnp.where(tiles == SUBLANES - 1, roll_tiles(rest, SUBLANES - 1 - high), block))
    return packed


def unpack_blocks(packed):
    tiles, rest = block_tiles(), None
    for number, block in enumerate(packed):
        low, high = 2 * number + 1, 2 * number + 2
        part = jnp.where(tiles == low, roll_tiles(block, low), roll_tiles(block, high - SUBLANES + 1))
        rest = part if rest is None else jnp.where(tiles >= low, part, rest)
    return list(packed) + [rest]


def flat_view(ref):
    rows, width, lanes = ref.shape
    return ref.reshape(rows * width, lanes)


def spread_tile(raw, raw_solid, index, row, target, target_row):
    source = raw_solid if index == FIELDS else raw.at[index]
    width = target.shape[1]
    for tile in range(OWN_TILES):
        values = source[pl.ds(row, SUBLANES), pl.ds(tile * LANES, LANES)].astype(jnp.float32)
        start = target_row * width + index * SUBLANES + 1 + tile
        flat_view(target)[pl.ds(start, SUBLANES, stride=width), :] = values


def load_kernel(
    tiles_count, density, momentum, stress, red, solid, widths,
    info, raw, raw_solid, packet, mine,
    first_tile, last_tile, held_widths, sems,
):
    row_count, flat_count = raw_solid.shape
    own_tiles = flat_count // LANES
    copies = [
        pltpu.make_async_copy(widths, held_widths, sems.at[0]),
        pltpu.make_async_copy(density, raw.at[0], sems.at[1]),
        pltpu.make_async_copy(momentum, raw.at[pl.ds(1, 3)], sems.at[2]),
        pltpu.make_async_copy(red, raw.at[10], sems.at[3]),
        pltpu.make_async_copy(solid, raw_solid, sems.at[4]),
        pltpu.make_async_copy(stress.at[pl.ds(0, 3)], raw.at[pl.ds(4, 3)], sems.at[5]),
        pltpu.make_async_copy(stress.at[pl.ds(3, 3)], raw.at[pl.ds(7, 3)], sems.at[6]),
    ]
    for copy in copies:
        copy.start()
    tiles_index, sub_index = lax.axis_index("tiles"), lax.axis_index("sub")
    low_part = sub_index == 0
    edge_start = pl.multiple_of(jnp.where(low_part, (own_tiles - 1) * LANES, 0), LANES)

    copies[0].wait()
    live = held_widths[tiles_index] * TILE
    info[0] = live
    info[1] = (tiles_index == 0).astype(jnp.int32)
    info[2] = (tiles_index == tiles_count - 1).astype(jnp.int32)
    info[3] = sub_index

    near_cut = lax.broadcasted_iota(jnp.int32, (SUBLANES, LANES), 1) < HALF
    near_cut = near_cut == jnp.logical_not(low_part)
    near_last = pl.multiple_of(live - SUBLANES, SUBLANES)
    ready = {0: copies[1], 1: copies[2], 10: copies[3], 11: copies[4], 4: copies[5], 7: copies[6]}
    for index in (0, 1, 2, 3, 10, 11, 4, 5, 6, 7, 8, 9):
        if index in ready:
            ready[index].wait()
        for target, row in ((first_tile, 0), (last_tile, near_last)):
            spread_tile(raw, raw_solid, index, row, target, 0)

    edges = pl.ds(edge_start, LANES)
    for pair in range(PAIRS):
        later = raw_solid if pair + PAIRS == FIELDS else raw.at[pair + PAIRS]
        for row in range(0, row_count, SUBLANES):
            rows = pl.ds(row, SUBLANES)
            beside = pltpu.roll(later[rows, edges].astype(jnp.float32), HALF, 1)
            both = jnp.where(near_cut, raw[pair, rows, edges], beside)
            packet[pl.ds(pair * row_count + row, SUBLANES), :] = both

    after = PAIRS * row_count
    ends = ((packet, after, jnp.logical_not(low_part)), (mine, 0, low_part))
    for target, at, use_last in ends:
        def row_of(index, number_first, number_last):
            first = read_row(ByRow(first_tile), index, number_first)
            last = read_row(ByRow(last_tile), index, number_last)
            return jnp.where(use_last, last, first)

        place = pl.ds(at + PACKED * SUBLANES, SUBLANES)
        ends_row = (FULL, SUBLANES - HALO)
        target[place, :] = 2.0 * row_of(10, *ends_row) - row_of(0, *ends_row)
        for group in range(FULL * PLANES // GROUP):
            blocks = []
            for number in range(group * GROUP, (group + 1) * GROUP):
                index, extra = divmod(number, FULL)
                blocks.append(row_of(index, extra, SUBLANES - FULL + extra))
            for number, block in enumerate(pack_blocks(blocks)):
                place = at + (group * (GROUP - 1) + number) * SUBLANES
                target[pl.ds(place, SUBLANES), :] = block


def load_inputs(arrays, widths, tiles_count):
    row_count, flat_count = arrays[0].shape
    packet_rows = PAIRS * row_count + END_ROWS
    return pl.pallas_call(
        functools.partial(load_kernel, tiles_count),
        out_shape=[
            pltpu.SMEM((4,), jnp.int32),
            jax.ShapeDtypeStruct((FIELDS, row_count, flat_count), jnp.float32),
            jax.ShapeDtypeStruct((row_count, flat_count), jnp.int32),
            jax.ShapeDtypeStruct((packet_rows, LANES), jnp.float32),
            jax.ShapeDtypeStruct((END_ROWS, LANES), jnp.float32),
        ],
        in_specs=[HBM] * 6,
        out_specs=[SMEM, VMEM, VMEM, VMEM, VMEM],
        scratch_shapes=[
            pltpu.VMEM((SUBLANES, PLANES * SUBLANES, LANES), jnp.float32),
            pltpu.VMEM((SUBLANES, PLANES * SUBLANES, LANES), jnp.float32),
            pltpu.SMEM(widths.shape, jnp.int32),
            pltpu.SemaphoreType.DMA((7,)),
        ],
        compiler_params=pltpu.CompilerParams(vmem_limit_bytes=16 * 1024 * 1024),
        name="load",
    )(*[pltpu.with_memory_space_constraint(array, pltpu.HBM) for array in (*arrays, widths)])


def spread_kernel(raw, raw_solid, spread):
    for index in range(PLANES):
        for row in range(0, raw_solid.shape[0], SUBLANES):
            spread_tile(raw, raw_solid, index, row, spread, row)


def spread_rows(raw, raw_solid):
    row_count = raw_solid.shape[0]
    return pl.pallas_call(
        spread_kernel,
        out_shape=by_row(row_count, PLANES),
        in_specs=[VMEM, VMEM],
        out_specs=VMEM,
        compiler_params=pltpu.CompilerParams(vmem_limit_bytes=16 * 1024 * 1024),
        cost_estimate=pl.CostEstimate(flops=1_000_000, bytes_accessed=4_000_000, transcendentals=0),
        name="spread",
    )(raw, raw_solid)


def join_kernel(info, spread, packet, mine, whole, ends):
    low_part = info[3] == 0
    row_count, width = spread.shape[:2]
    flat = flat_view(whole)
    ends[pl.ds(0, END_ROWS), :] = mine[...]
    ends[pl.ds(END_ROWS, END_ROWS), :] = packet[pl.ds(PAIRS * row_count, END_ROWS), :]
    for pair in range(PAIRS):
        for row in range(0, row_count, SUBLANES):
            both = packet[pl.ds(pair * row_count + row, SUBLANES), :]
            for index, values in ((pair, both), (pair + PAIRS, pltpu.roll(both, HALF, 1))):
                start = row * width + index * SUBLANES
                below = jnp.where(low_part, 0.0, values)
                above = jnp.where(low_part, values, 0.0)
                flat[pl.ds(start, SUBLANES, stride=width), :] = below
                flat[pl.ds(start + SUBLANES - 1, SUBLANES, stride=width), :] = above


def join_parts(info, spread, packet, mine):
    return pl.pallas_call(
        join_kernel,
        out_shape=[
            jax.ShapeDtypeStruct(spread.shape, jnp.float32),
            jax.ShapeDtypeStruct((2 * END_ROWS, LANES), jnp.float32),
        ],
        in_specs=[SMEM, VMEM, VMEM, VMEM],
        out_specs=[VMEM] * 2,
        input_output_aliases={1: 0},
        compiler_params=pltpu.CompilerParams(vmem_limit_bytes=16 * 1024 * 1024),
        name="join",
    )(info, pltpu.with_memory_space_constraint(spread, pltpu.VMEM), packet, mine)


def keep_rows(slab, source, first, size, live):
    for slab_row, row in slab_rows(live, first, size):
        for extra in range(size):
            slab[slab_row + extra] = source[row + extra]


def slab_rows(live, first, size):
    mirrored = SLAB - first - size
    return [(first, first - HALO), (SLAB + mirrored, live - 2 * RIM + mirrored)]


def collide_rows(geometry, before, whole, first, colours, walls, state):
    over_rows(geometry, first - 1, *COLOUR_BLOCK, lambda block: colour_stage(
        block, geometry, before, colours))
    over_rows(geometry, first, *COLLIDE_BLOCK, lambda block: collide_stage(
        block, geometry, before, whole, colours, walls, state))


def tile_copies(pieces, outs, held_row, out_row, sems):
    held, rows = pl.ds(held_row, SUBLANES), pl.ds(out_row, SUBLANES)
    parts = (
        (pieces.at[0, held], outs[0].at[rows]),
        (pieces.at[pl.ds(1, 3), held], outs[1].at[:, rows]),
        (pieces.at[pl.ds(4, 6), held], outs[2].at[:, rows]),
        (pieces.at[10, held], outs[3].at[rows]),
    )
    return [
        pltpu.make_async_copy(source, target, sems.at[number])
        for number, (source, target) in enumerate(parts)
    ]


def gather_tiles(final, row, pieces, held_row):
    width = final.shape[1]
    start = row * width
    if not isinstance(start, int):
        start = pl.multiple_of(start, SUBLANES)
    for index in range(FIELDS):
        for tile in range(OWN_TILES):
            place = start + index * SUBLANES + 1 + tile
            pieces[index, pl.ds(held_row, SUBLANES), pl.ds(tile * LANES, LANES)] = flat_view(final)[
                pl.ds(place, SUBLANES, stride=width), :
            ]


def finish_tiles(geometry, walls, state, final, pieces, outs, sems, first, end):
    def copies_of(tile):
        held_row = pl.multiple_of((tile - first) * SUBLANES, SUBLANES)
        out_row = pl.multiple_of(tile * SUBLANES, SUBLANES)
        return tile_copies(pieces, outs, held_row, out_row, sems.at[tile])

    def finish(tile, carry):
        row = pl.multiple_of(tile * SUBLANES, SUBLANES)
        block = Block(geometry, [(row, row, SUBLANES)], inner=True)
        arrive_stage(block, geometry, walls, state, ByRow(final))
        gather_tiles(final, row, pieces, pl.multiple_of((tile - first) * SUBLANES, SUBLANES))
        for copy in copies_of(tile):
            copy.start()
        return carry

    def settle(tile, carry):
        for copy in copies_of(tile):
            copy.wait()
        return carry

    lax.fori_loop(first, end, finish, 0)
    return lambda: lax.fori_loop(first, end, settle, 0)


def first_kernel(
    info, whole, density_out, momentum_out, stress_out, red_out, moved_later, reds_later,
    moved_slab, reds_slab, fields_slab, moved_later_slab, reds_later_slab, final_slab,
    colours, walls, moved, reds, fields, final, pieces, zeros, sems,
):
    outs = (density_out, momentum_out, stress_out, red_out)
    row_tiles = density_out.shape[0] // SUBLANES
    state, later = (ByRow(moved), ByRow(reds)), (ByRow(moved_later), ByRow(reds_later))
    geometry = Geometry(info, OWN_TILES)
    live = geometry.live
    fill_wall_table(walls, geometry)

    zeros[...] = jnp.zeros(zeros.shape, zeros.dtype)
    dead = {}
    for tile in range(row_tiles):
        dead[tile] = tile_copies(zeros, outs, 0, tile * SUBLANES, sems.at[tile])

        @pl.when(tile * SUBLANES >= live)
        def _():
            for copy in dead[tile]:
                copy.start()

    collide_rows(geometry, ByRow(whole), ByRow(whole), 1, ByRow(colours), walls, state)
    over_rows(geometry, 2, *ARRIVE_BLOCK, lambda block: arrive_stage(
        block, geometry, walls, state, ByRow(fields)))
    keep_rows(moved_slab, moved, HALO + 1, KEPT, live)
    keep_rows(reds_slab, reds, HALO + 1, KEPT, live)
    keep_rows(fields_slab, fields, HALO + 2, KEPT, live)
    collide_rows(geometry, ByRow(fields), ByRow(whole), 3, ByRow(colours), walls, later)
    keep_rows(moved_later_slab, moved_later, HALO + 3, KEPT, live)
    keep_rows(reds_later_slab, reds_later, HALO + 3, KEPT, live)
    last = live // SUBLANES - 1
    settle = finish_tiles(
        geometry, walls, later, final, pieces, outs, sems, 1, jnp.minimum(SPLIT, last)
    )
    edges = slab_rows(live, HALO + RIM, RIM)
    rim = Block(geometry, [(row, row, RIM) for _, row in edges], True, [at for at, _ in edges])
    arrive_stage(rim, geometry, walls, later, ByRow(final_slab))
    settle()
    for tile in range(row_tiles):

        @pl.when(tile * SUBLANES >= live)
        def _():
            for copy in dead[tile]:
                copy.wait()


def second_kernel(info, moved, reds, arrived, *refs):
    outs = refs[4:8]
    final, walls, pieces, sems = refs[8:]
    geometry = Geometry(info, OWN_TILES)
    fill_wall_table(walls, geometry)
    last = geometry.live // SUBLANES - 1
    state = (ByRow(moved), ByRow(reds))
    finish_tiles(geometry, walls, state, final, pieces, outs, sems, SPLIT, last)()


def scratch_of(shape):
    return pltpu.VMEM(shape.shape, shape.dtype)


def pieces_of(rows, flat_count):
    return pltpu.VMEM((FIELDS, rows, flat_count), jnp.float32)


def run_first(info, whole, arrays):
    row_count, flat_count = arrays[0].shape
    outs = [jax.ShapeDtypeStruct(array.shape, jnp.float32) for array in arrays[:4]]
    shapes = outs + [by_row(row_count, HELD), by_row(row_count, REDS)]
    slabs = [by_row(2 * SLAB, count) for count in (HELD, REDS, FIELDS, HELD, REDS, FIELDS)]
    scratch = [by_row(row_count, 4), by_row(4, 3)]
    scratch = scratch + [by_row(row_count, count) for count in (HELD, REDS, FIELDS, FIELDS)]
    return pl.pallas_call(
        first_kernel,
        out_shape=shapes + slabs,
        in_specs=[SMEM, VMEM],
        out_specs=[ANY] * 4 + [VMEM] * 8,
        scratch_shapes=[scratch_of(shape) for shape in scratch]
        + [
            pieces_of((SPLIT - 1) * SUBLANES, flat_count),
            pieces_of(SUBLANES, flat_count),
            pltpu.SemaphoreType.DMA((row_count // SUBLANES, 4)),
        ],
        compiler_params=pltpu.CompilerParams(vmem_limit_bytes=24 * 1024 * 1024),
        cost_estimate=pl.CostEstimate(flops=20_000_000, bytes_accessed=8_000_000, transcendentals=0),
        name="first",
    )(info, whole)


def run_second(info, state, arrived, outs):
    row_count, flat_count = outs[0].shape
    return pl.pallas_call(
        second_kernel,
        out_shape=[jax.ShapeDtypeStruct(out.shape, jnp.float32) for out in outs],
        in_specs=[SMEM, VMEM, VMEM, ANY] + [ANY] * 4,
        out_specs=[ANY] * 4,
        scratch_shapes=[
            scratch_of(by_row(row_count, FIELDS)),
            scratch_of(by_row(4, 3)),
            pieces_of(row_count - (SPLIT + 1) * SUBLANES, flat_count),
            pltpu.SemaphoreType.DMA((row_count // SUBLANES, 4)),
        ],
        input_output_aliases={4: 0, 5: 1, 6: 2, 7: 3},
        compiler_params=pltpu.CompilerParams(vmem_limit_bytes=24 * 1024 * 1024),
        cost_estimate=pl.CostEstimate(flops=20_000_000, bytes_accessed=8_000_000, transcendentals=0),
        name="second",
    )(info, *state, arrived, *outs)


def follow_kernel(ends, kept, out):
    out[pl.ds(PACKED * SUBLANES, 1), :] = jnp.zeros((1, LANES), jnp.float32)


def follow(ends, kept):
    return pl.pallas_call(
        follow_kernel,
        out_shape=jax.ShapeDtypeStruct(ends.shape, jnp.float32),
        in_specs=[VMEM, ANY],
        out_specs=VMEM,
        input_output_aliases={0: 0},
        compiler_params=pltpu.CompilerParams(vmem_limit_bytes=8 * 1024 * 1024),
        name="follow",
    )(pltpu.with_memory_space_constraint(ends, pltpu.VMEM), kept)


def outer_kernel(info, whole, arrived, passed, *refs):
    outs = refs[10:14]
    moved, reds, fields, moved_later, reds_later, final = refs[14:20]
    start_fields, colours, walls, pieces, sems = refs[20:]
    state, later = (ByRow(moved), ByRow(reds)), (ByRow(moved_later), ByRow(reds_later))
    geometry = Geometry(info, OWN_TILES)
    live = geometry.live
    low_part = info[3] == 0
    fill_wall_table(walls, geometry)

    def ends_of(ref, half):
        blocks = []
        for group in range(FULL * PLANES // GROUP):
            first = half * (PACKED + 1) + group * (GROUP - 1)
            packed = [ref[pl.ds((first + k) * SUBLANES, SUBLANES), :] for k in range(GROUP - 1)]
            blocks = blocks + unpack_blocks(packed)
        last = half * (PACKED + 1) + PACKED
        return blocks + [ref[pl.ds(last * SUBLANES, SUBLANES), :]]

    tiles = block_tiles()
    middle = (tiles >= 1) & (tiles <= OWN_TILES)

    def widened(own, other):
        beside = jnp.where(tiles == 0, roll_tiles(other, -OWN_TILES), roll_tiles(other, OWN_TILES))
        return jnp.where(geometry.domain, jnp.where(middle, own, beside), 0.0)

    straight = [widened(*pair) for pair in zip(ends_of(arrived, 0), ends_of(arrived, 1))]
    crossed = [widened(*pair) for pair in zip(ends_of(passed, 1), ends_of(passed, 0))]
    below = [jnp.where(low_part, *pair) for pair in zip(straight, crossed)]
    above = [jnp.where(low_part, *pair) for pair in zip(crossed, straight)]

    for number in range(FULL * PLANES):
        index, extra = divmod(number, FULL)
        write_row(ByRow(start_fields), index, 1 + extra, below[number])
        write_row(ByRow(start_fields), index, 2 * SLAB - HALO + extra, above[number])
    for row, colour in ((0, below[-1]), (2 * SLAB - 1, above[-1])):
        write_row(ByRow(start_fields), 0, row, jnp.zeros((SUBLANES, LANES), jnp.float32))
        write_row(ByRow(start_fields), 10, row, 0.5 * colour)
    for slab_row, row in slab_rows(live, HALO, FULL):
        for extra in range(FULL):
            start_fields[slab_row + extra] = whole[row + extra]

    def block(first, count):
        return Block(geometry, [(row, at, count) for at, row in slab_rows(live, first, count)])

    held, solids, marks = ByRow(fields), ByRow(start_fields), ByRow(colours)
    colour_stage(block(0, 6), geometry, solids, marks)
    collide_stage(block(1, 4), geometry, solids, solids, marks, walls, state)
    arrive_stage(block(2, 4), geometry, walls, state, held)
    colour_stage(block(2, 6), geometry, held, marks)
    collide_stage(block(3, 4), geometry, held, solids, marks, walls, later)
    arrive_stage(block(4, 4), geometry, walls, later, ByRow(final))

    copies = []
    for side, row, out_row in ((0, HALO, 0), (1, SLAB, live - SUBLANES)):
        gather_tiles(final, row, pieces, side * SUBLANES)
        out_row = pl.multiple_of(out_row, SUBLANES)
        copies = copies + tile_copies(pieces, outs, side * SUBLANES, out_row, sems.at[side])
    for copy in copies:
        copy.start()
    for copy in copies:
        copy.wait()


def run_outer(info, whole, arrived, passed, slabs, outs):
    flat_count = outs[0].shape[1]
    shapes = [jax.ShapeDtypeStruct(array.shape, jnp.float32) for array in (*outs, *slabs)]
    slabs = [pltpu.with_memory_space_constraint(slab, pltpu.VMEM) for slab in slabs]
    aliases = {4 + number: 4 + number for number in range(6)}
    aliases.update({10 + number: number for number in range(4)})
    return pl.pallas_call(
        outer_kernel,
        out_shape=shapes,
        in_specs=[SMEM] + [VMEM] * 9 + [ANY] * 4,
        out_specs=[ANY] * 4 + [VMEM] * 6,
        scratch_shapes=[
            scratch_of(by_row(2 * SLAB, PLANES)),
            scratch_of(by_row(2 * SLAB, 4)),
            scratch_of(by_row(4, 3)),
            pieces_of(2 * SUBLANES, flat_count),
            pltpu.SemaphoreType.DMA((2, 4)),
        ],
        input_output_aliases=aliases,
        compiler_params=pltpu.CompilerParams(vmem_limit_bytes=24 * 1024 * 1024),
        name="outer",
    )(info, whole, arrived, passed, *slabs, *outs)


def body(density, momentum, stress, red_density, solid, widths):
    tiles_count = lax.axis_size("tiles")
    arrays = (density, momentum, stress, red_density, solid)
    info, raw, raw_solid, packet, mine = load_inputs(arrays, widths, tiles_count)
    info = pltpu.with_memory_space_constraint(info, pltpu.SMEM)
    swap = [(0, 1), (1, 0)]
    packet = lax.ppermute(packet, "sub", swap)
    spread = spread_rows(raw, raw_solid)
    whole, ends = join_parts(info, spread, packet, mine)
    route = [(2 * k, 2 * k + 2) for k in range(tiles_count - 1)]
    route = route + [(2 * k + 3, 2 * k + 1) for k in range(tiles_count - 1)]
    arrived = lax.ppermute(ends, ("tiles", "sub"), route)
    results = run_first(info, whole, arrays)
    outs, state, slabs = results[:4], results[4:6], results[6:]
    arrived = follow(arrived, slabs[-1])
    passed = lax.ppermute(arrived, "sub", swap)
    outs = run_second(info, state, arrived, outs)
    return tuple(run_outer(info, whole, arrived, passed, slabs, outs)[:4])


def solution(mesh):
    in_specs = (
        P(("groups", "tiles"), "sub"),
        P(None, ("groups", "tiles"), "sub"),
        P(None, ("groups", "tiles"), "sub"),
        P(("groups", "tiles"), "sub"),
        P(("groups", "tiles"), "sub"),
        P("groups"),
    )
    out_specs = (
        P(("groups", "tiles"), "sub"),
        P(None, ("groups", "tiles"), "sub"),
        P(None, ("groups", "tiles"), "sub"),
        P(("groups", "tiles"), "sub"),
    )
    return jax.shard_map(body, mesh=mesh, in_specs=in_specs, out_specs=out_specs, check_vma=False)
```

```python
import functools

import jax
import jax.numpy as jnp
from jax import lax
from jax.experimental import pallas as pl
from jax.experimental.pallas import tpu as pltpu
from jax.sharding import PartitionSpec as P

TILE = 16
STEPS = 2
RELAX_TIME = 0.8
SURFACE = 0.1
SEPARATION = 0.7

LANES = 128
SUBLANES = 8
FULL = 3
HALO = FULL + 1
FIELDS = 11
PLANES = FIELDS + 1
MOVED = 19
REDS = 5
HELD = MOVED + 1
RIM = 4
SLAB = HALO + 2 * RIM
OWN_TILES = SUBLANES - 2
GROUP = 4
PACKED = FULL * PLANES // GROUP * (GROUP - 1)
END_ROWS = (PACKED + 1) * SUBLANES
HALF = LANES // 2
PAIRS = PLANES // 2
PLACES = PLANES + 1
SPLIT = 3
KEPT = 2
COLOUR_BLOCK = (8, 1)
COLLIDE_BLOCK = (2, 4)
ARRIVE_BLOCK = (8, 1)
VMEM = pl.BlockSpec(memory_space=pltpu.VMEM)
SMEM = pl.BlockSpec(memory_space=pltpu.SMEM)
ANY = pl.BlockSpec(memory_space=pl.ANY)
HBM = pl.BlockSpec(memory_space=pltpu.HBM)


class Rows:
    def __init__(self, parts):
        self.parts = parts

    def _with(self, other, operation):
        others = other.parts if isinstance(other, Rows) else [other] * len(self.parts)
        return Rows([operation(one, two) for one, two in zip(self.parts, others)])

    def __add__(self, other):
        return self._with(other, lambda one, two: one + two)

    def __sub__(self, other):
        return self._with(other, lambda one, two: one - two)

    def __rsub__(self, other):
        return self._with(other, lambda one, two: two - one)

    def __mul__(self, other):
        return self._with(other, lambda one, two: one * two)

    def __or__(self, other):
        return self._with(other, lambda one, two: one | two)

    def __eq__(self, other):
        return self._with(other, lambda one, two: one == two)

    __radd__, __rmul__, __ror__ = __add__, __mul__, __or__

    def each(self, operation):
        return Rows([operation(part) for part in self.parts])


def select(mask, yes, no):
    count = max(len(item.parts) for item in (mask, yes, no) if isinstance(item, Rows))
    columns = [
        item.parts if isinstance(item, Rows) else [item] * count for item in (mask, yes, no)
    ]
    return Rows([jnp.where(*row) for row in zip(*columns)])


def roll_lanes(values, amount):
    return values.each(lambda part: pltpu.roll(part, amount % LANES, 1))


def roll_sublanes(values, amount):
    return values.each(lambda part: pltpu.roll(part, amount % SUBLANES, 0))


class Geometry:
    def __init__(self, info, own_tiles):
        live, first, last, sub_index = info[0], info[1], info[2], info[3]
        self.live = live
        self.low_row = jnp.where(first == 1, 0, -1000)
        self.high_row = jnp.where(last == 1, live, 1000)
        shape = (SUBLANES, LANES)
        lane = lax.broadcasted_iota(jnp.int32, shape, 1)
        tile = lax.broadcasted_iota(jnp.int32, shape, 0)
        depth = lane & (TILE - 1)
        low_part = sub_index == 0
        high_part = sub_index == 1
        z_walls = {1: depth == 0, -1: depth == TILE - 1}
        y_walls = {
            1: (tile == 1) & (lane < TILE) & low_part,
            -1: (tile == own_tiles) & (lane >= LANES - TILE) & high_part,
        }
        self.walls = {(0, vel_z): wall for vel_z, wall in z_walls.items()}
        for vel_y, y_wall in y_walls.items():
            self.walls[vel_y, 0] = y_wall
            for vel_z, z_wall in z_walls.items():
                self.walls[vel_y, vel_z] = y_wall | z_wall
        own = (tile >= 1) & (tile <= own_tiles)
        self.domain = own | ((tile == own_tiles + 1) & low_part) | ((tile == 0) & high_part)
        self.first_lanes = lane < TILE
        self.last_lanes = lane >= LANES - TILE

    def from_low_y(self, values):
        return roll_lanes(select(self.last_lanes, roll_sublanes(values, 1), values), TILE)

    def from_high_y(self, values):
        return roll_lanes(select(self.first_lanes, roll_sublanes(values, -1), values), -TILE)

    def from_low_z(self, values):
        return select(self.walls[0, 1], 0.0, roll_lanes(values, 1))

    def from_high_z(self, values):
        return select(self.walls[0, -1], 0.0, roll_lanes(values, -1))


def flat_rows(row, count, tile_offset=0):
    start = row * SUBLANES
    if not isinstance(start, int):
        start = pl.multiple_of(start, SUBLANES)
    return pl.ds(start + tile_offset, count * SUBLANES)


class ByRow:
    def __init__(self, ref):
        self.ref = ref


def by_row(rows, count):
    return jax.ShapeDtypeStruct((rows, count * SUBLANES, LANES), jnp.float32)


def place_of(ref, index, row, tile_offset=0):
    if isinstance(ref, ByRow):
        return ref.ref, row, pl.ds(index * SUBLANES + tile_offset, SUBLANES)
    return ref, index, flat_rows(row, 1, tile_offset)


def read_row(ref, index, row, tile_offset=0):
    ref, first, second = place_of(ref, index, row, tile_offset)
    return ref[first, second, :]


def write_row(ref, index, row, values):
    ref, first, second = place_of(ref, index, row)
    ref[first, second, :] = values


class Block:
    def __init__(self, geometry, spans, inner=False, store_rows=None):
        self.spans = spans
        self.store_rows = store_rows or [local for row, local, count in spans]
        rows = [row + extra for row, local, count in spans for extra in range(count)]
        self.inner = inner
        rows = [row + extra for row, local, count in spans for extra in range(count)]
        if inner:
            self.x_walls = {}
            self.valid = geometry.domain
            self.kinds = [0]
            return
        ids = Rows([row + jnp.zeros((SUBLANES, LANES), jnp.int32) for row in rows])
        self.x_walls = {1: ids == geometry.low_row, -1: ids == geometry.high_row - 1}
        self.valid = ids.each(
            lambda part: geometry.domain & (part >= geometry.low_row) & (part < geometry.high_row)
        )
        self.kinds = [
            jnp.where(row == geometry.low_row, 1, 0) + jnp.where(row == geometry.high_row - 1, 2, 0)
            for row in rows
        ]

    def load(self, ref, index, offset=0, tile_offset=0):
        return Rows([
            read_row(ref, index, local + offset + extra, tile_offset)
            for row, local, count in self.spans
            for extra in range(count)
        ])

    def store(self, ref, index, values):
        targets = [
            target + extra
            for (row, local, count), target in zip(self.spans, self.store_rows)
            for extra in range(count)
        ]
        for target, part in zip(targets, values.parts):
            write_row(ref, index, target, part)

    def wall_terms(self, walls, position):
        terms = [walls[position, flat_rows(kind, 1), :] for kind in self.kinds]
        return terms[0] if self.inner else Rows(terms)


def fill_wall_table(walls, geometry):
    one = jnp.ones((SUBLANES, LANES), jnp.float32)
    up_y, down_y, up_z, down_z = [
        jnp.where(geometry.walls[key], 0.0, one) for key in ((-1, 0), (1, 0), (0, -1), (0, 1))
    ]
    sum_y, sum_z = up_y + down_y, up_z + down_z
    for kind, (up_x, down_x) in enumerate(((1.0, 1.0), (1.0, 0.0), (0.0, 1.0))):
        sum_x = up_x + down_x
        around_x = 2.0 + sum_y + sum_z
        total = 12.0 + 2.0 * (sum_x + sum_y + sum_z) + sum_x * (sum_y + sum_z) + sum_y * sum_z
        rows = (
            (up_x - down_x) * around_x,
            (up_y - down_y) * (2.0 + sum_x + sum_z),
            (up_z - down_z) * (2.0 + sum_x + sum_y),
            36.0 - total,
        )
        for position, row in enumerate(rows):
            walls[position, flat_rows(kind, 1), :] = row


VELOCITIES = tuple(
    tuple(sign if axis == place else 0 for place in range(3)) for axis in range(3) for sign in (1, -1)
) + tuple(
    tuple({a: one, b: two}.get(place, 0) for place in range(3))
    for a, b in ((0, 1), (0, 2), (1, 2))
    for one, two in ((1, 1), (-1, -1), (1, -1), (-1, 1))
)
VELOCITIES = ((0, 0, 0),) + VELOCITIES


def colour_stage(block, geometry, fields, colours):
    density = block.load(fields, 0)
    red = block.load(fields, 10)
    colour = select(block.valid, 2.0 * red - density, 0.0)
    along_y = geometry.from_low_y(colour) + geometry.from_high_y(colour)
    along_z = geometry.from_low_z(colour) + geometry.from_high_z(colour)
    block.store(colours, 0, colour)
    block.store(colours, 1, 2.0 * colour + (along_y + along_z))
    block.store(colours, 2, along_y)
    block.store(colours, 3, along_z)


def collide_stage(block, geometry, fields, solids, colours, walls, state):
    relaxing = 1.0 - 1.0 / RELAX_TIME
    third = 1.0 / 3.0
    colour = block.load(colours, 0)
    doubled = 2.0 * colour + (block.load(colours, 0, -1) + block.load(colours, 0, 1))
    term_y = doubled + block.load(colours, 3)
    term_z = doubled + block.load(colours, 2)
    grad_x = block.load(colours, 1, 1) - block.load(colours, 1, -1)
    grad_y = geometry.from_high_y(term_y) - geometry.from_low_y(term_y)
    grad_z = geometry.from_high_z(term_z) - geometry.from_low_z(term_z)
    if not block.inner:
        grad_x = grad_x - block.wall_terms(walls, 0) * colour
    grad_y = grad_y - block.wall_terms(walls, 1) * colour
    grad_z = grad_z - block.wall_terms(walls, 2) * colour

    fluid = block.load(solids, PLANES - 1) == 0.0
    density = block.load(fields, 0)
    red = block.load(fields, 10)
    flux = [block.load(fields, 1 + axis) for axis in range(3)]
    stress = [block.load(fields, 4 + part) for part in range(6)]
    square_xx, square_yy, square_zz = grad_x * grad_x, grad_y * grad_y, grad_z * grad_z
    square = square_xx + square_yy + square_zz
    inverse = select(fluid, (1.0 + square * (1.0 / 144.0)).each(lax.rsqrt), 0.0)
    trace = third * square
    strength = (SURFACE / (8.0 * 144.0)) * inverse
    keep = select(fluid, relaxing / 8.0, 1.0 / 8.0)
    eighths = [0.125 * part for part in flux]
    own = [
        eighths[axis] * flux[axis] + (keep * stress[axis] + strength * (squared - trace))
        for axis, squared in enumerate((square_xx, square_yy, square_zz))
    ]
    strength, keep = 2.0 * strength, 2.0 * keep
    quarters = [2.0 * part for part in eighths[:2]]
    grads = (grad_x, grad_y, grad_z)
    cross = [
        quarters[a] * flux[b] + (keep * stress[3 + plane] + strength * (grads[a] * grads[b]))
        for plane, (a, b) in enumerate(((0, 1), (0, 2), (1, 2)))
    ]
    base = density * (1.0 / 36.0) - third * (own[0] + own[1] + own[2])
    sign = select(fluid, 1.0 / 12.0, -1.0 / 12.0)
    run = [sign * part for part in flux]
    mixing = ((SEPARATION / 144.0) * red) * ((density - red) * inverse)
    red_run = [0.5 * part + mixing * grad for part, grad in zip(run, grads)]
    moved, reds = state
    block.store(moved, 0, 12.0 * base)
    straight = [base + part for part in own]
    for axis in range(3):
        middle = 2.0 * straight[axis]
        swing = 2.0 * run[axis]
        block.store(moved, 1 + 2 * axis, middle + swing)
        block.store(moved, 2 + 2 * axis, middle - swing)
    for plane, (a, b) in enumerate(((0, 1), (0, 2), (1, 2))):
        middle = straight[a] + own[b]
        same, other = middle + cross[plane], middle - cross[plane]
        along, against = run[a] + run[b], run[a] - run[b]
        first = 7 + 4 * plane
        block.store(moved, first, same + along)
        block.store(moved, first + 1, same - along)
        block.store(moved, first + 2, other + against)
        block.store(moved, first + 3, other - against)

    red_base = select(block.valid, red * (1.0 / 36.0), 0.0)
    red_run = [select(block.valid, part, 0.0) for part in red_run]
    block.store(reds, 0, red_base)
    block.store(reds, 1, red_base + red_run[0])
    block.store(reds, 2, red_base - red_run[0])
    block.store(reds, 3, red_run[1])
    block.store(reds, 4, red_run[2])


def arrive_stage(block, geometry, walls, state, fields):
    third = 1.0 / 3.0
    moved, reds = state
    own = [None] * MOVED

    def here(direction):
        if own[direction] is None:
            own[direction] = block.load(moved, direction)
        return own[direction]

    def arrived(direction, opposite):
        vel_x, vel_y, vel_z = VELOCITIES[direction]
        values = here(direction) if vel_x == 0 else block.load(moved, direction, -vel_x)
        if vel_y != 0:
            beside = block.load(moved, direction, -vel_x, -vel_y)
            leaving = geometry.last_lanes if vel_y == 1 else geometry.first_lanes
            values = select(leaving, beside, values)
        if vel_y != 0 or vel_z != 0:
            values = roll_lanes(values, TILE * vel_y + vel_z)
        masks = []
        if vel_x in block.x_walls:
            masks.append(block.x_walls[vel_x])
        if (vel_y, vel_z) in geometry.walls:
            masks.append(geometry.walls[vel_y, vel_z])
        if not masks:
            return values
        wall = functools.reduce(lambda one, two: one | two, masks)
        return select(wall, here(opposite), values)

    red = block.load(reds, 0)
    red_y = block.load(reds, 3)
    red_z = block.load(reds, 4)
    from_x = block.load(reds, 1, -1) + block.load(reds, 2, 1)
    spread = 2.0 * red + from_x
    spread_y = 2.0 * red_y + (block.load(reds, 3, -1) + block.load(reds, 3, 1))
    spread_z = 2.0 * red_z + (block.load(reds, 4, -1) + block.load(reds, 4, 1))
    up_y, down_y = red + red_y, red - red_y
    low_y = (
        (spread + spread_y)
        + geometry.from_low_z(up_y + red_z)
        + geometry.from_high_z(up_y - red_z)
    )
    high_y = (
        (spread - spread_y)
        + geometry.from_low_z(down_y + red_z)
        + geometry.from_high_z(down_y - red_z)
    )
    bounced = (
        block.wall_terms(walls, 3) * red
        - block.wall_terms(walls, 1) * red_y
        - block.wall_terms(walls, 2) * red_z
    )
    if not block.inner:
        bounced = bounced - block.wall_terms(walls, 0) * (block.load(reds, 1) - red)
    red_total = (
        12.0 * red
        + 2.0 * from_x
        + geometry.from_low_z(spread + spread_z)
        + geometry.from_high_z(spread - spread_z)
        + geometry.from_low_y(low_y)
        + geometry.from_high_y(high_y)
        + bounced
    )
    rest = here(0)
    sums, diffs = [], []
    for axis in range(3):
        up = arrived(1 + 2 * axis, 2 + 2 * axis)
        down = arrived(2 + 2 * axis, 1 + 2 * axis)
        sums.append(up + down)
        diffs.append(up - down)
    total = rest + sums[0] + sums[1] + sums[2]
    cross = []
    for plane, (a, b) in enumerate(((0, 1), (0, 2), (1, 2))):
        first = 7 + 4 * plane
        parts = [arrived(first + offset, first + (offset ^ 1)) for offset in range(4)]
        same, other = parts[0] + parts[1], parts[2] + parts[3]
        along, against = parts[0] - parts[1], parts[2] - parts[3]
        both = same + other
        cross.append(same - other)
        total = total + both
        sums[a], sums[b] = sums[a] + both, sums[b] + both
        diffs[a], diffs[b] = diffs[a] + (along + against), diffs[b] + (along - against)
    shared = third * total
    block.store(fields, 0, total)
    for axis in range(3):
        block.store(fields, 1 + axis, diffs[axis])
        block.store(fields, 4 + axis, sums[axis] - shared - diffs[axis] * diffs[axis])
    for plane, (a, b) in enumerate(((0, 1), (0, 2), (1, 2))):
        block.store(fields, 7 + plane, cross[plane] - diffs[a] * diffs[b])
    block.store(fields, 10, red_total)


def over_rows(geometry, first, size, blocks, stage):
    trip = size * blocks
    rest = -2 * first % trip
    assert TILE % trip == 0 and rest % min(size, rest or size) == 0

    def run(start, count, step_size):
        for offset in range(0, count, step_size):
            row = start + offset
            stage(Block(geometry, [(row, row, step_size)], inner=True))

    def step(index, carry):
        run(first + index * trip, trip, size)
        return carry

    trips = (geometry.live - 2 * first - rest) // trip
    lax.fori_loop(0, trips, step, 0)
    if rest:
        run(geometry.live - first - rest, rest, min(size, rest))


def block_tiles():
    return lax.broadcasted_iota(jnp.int32, (SUBLANES, LANES), 0)


def roll_tiles(block, amount):
    return pltpu.roll(block, amount % SUBLANES, 0)


def pack_blocks(blocks):
    tiles, rest = block_tiles(), blocks[GROUP - 1]
    packed = []
    for number, block in enumerate(blocks[: GROUP - 1]):
        low, high = 2 * number + 1, 2 * number + 2
        block = jnp.where(tiles == 0, roll_tiles(rest, -low), block)
        packed.append(jnp.where(tiles == SUBLANES - 1, roll_tiles(rest, SUBLANES - 1 - high), block))
    return packed


def unpack_blocks(packed):
    tiles, rest = block_tiles(), None
    for number, block in enumerate(packed):
        low, high = 2 * number + 1, 2 * number + 2
        part = jnp.where(tiles == low, roll_tiles(block, low), roll_tiles(block, high - SUBLANES + 1))
        rest = part if rest is None else jnp.where(tiles >= low, part, rest)
    return list(packed) + [rest]


def flat_view(ref):
    rows, width, lanes = ref.shape
    return ref.reshape(rows * width, lanes)


def spread_tile(raw, raw_solid, index, row, target, target_row):
    source = raw_solid if index == FIELDS else raw.at[index]
    width = target.shape[1]
    for tile in range(OWN_TILES):
        values = source[pl.ds(row, SUBLANES), pl.ds(tile * LANES, LANES)].astype(jnp.float32)
        start = target_row * width + index * SUBLANES + 1 + tile
        flat_view(target)[pl.ds(start, SUBLANES, stride=width), :] = values


def load_kernel(
    tiles_count, density, momentum, stress, red, solid, widths,
    info, raw, raw_solid, packet, mine,
    first_tile, last_tile, held_widths, sems,
):
    row_count, flat_count = raw_solid.shape
    own_tiles = flat_count // LANES
    copies = [
        pltpu.make_async_copy(widths, held_widths, sems.at[0]),
        pltpu.make_async_copy(density, raw.at[0], sems.at[1]),
        pltpu.make_async_copy(momentum, raw.at[pl.ds(1, 3)], sems.at[2]),
        pltpu.make_async_copy(red, raw.at[10], sems.at[3]),
        pltpu.make_async_copy(solid, raw_solid, sems.at[4]),
        pltpu.make_async_copy(stress.at[pl.ds(0, 3)], raw.at[pl.ds(4, 3)], sems.at[5]),
        pltpu.make_async_copy(stress.at[pl.ds(3, 3)], raw.at[pl.ds(7, 3)], sems.at[6]),
    ]
    for copy in copies:
        copy.start()
    tiles_index, sub_index = lax.axis_index("tiles"), lax.axis_index("sub")
    low_part = sub_index == 0
    edge_start = pl.multiple_of(jnp.where(low_part, (own_tiles - 1) * LANES, 0), LANES)

    copies[0].wait()
    live = held_widths[tiles_index] * TILE
    info[0] = live
    info[1] = (tiles_index == 0).astype(jnp.int32)
    info[2] = (tiles_index == tiles_count - 1).astype(jnp.int32)
    info[3] = sub_index

    near_cut = lax.broadcasted_iota(jnp.int32, (SUBLANES, LANES), 1) < HALF
    near_cut = near_cut == jnp.logical_not(low_part)
    near_last = pl.multiple_of(live - SUBLANES, SUBLANES)
    ready = {0: copies[1], 1: copies[2], 10: copies[3], 11: copies[4], 4: copies[5], 7: copies[6]}
    for index in (0, 1, 2, 3, 10, 11, 4, 5, 6, 7, 8, 9):
        if index in ready:
            ready[index].wait()
        for target, row in ((first_tile, 0), (last_tile, near_last)):
            spread_tile(raw, raw_solid, index, row, target, 0)

    edges = pl.ds(edge_start, LANES)
    for pair in range(PAIRS):
        later = raw_solid if pair + PAIRS == FIELDS else raw.at[pair + PAIRS]
        for row in range(0, row_count, SUBLANES):
            rows = pl.ds(row, SUBLANES)
            beside = pltpu.roll(later[rows, edges].astype(jnp.float32), HALF, 1)
            both = jnp.where(near_cut, raw[pair, rows, edges], beside)
            packet[pl.ds(END_ROWS + pair * row_count + row, SUBLANES), :] = both

    for target, use_last in ((packet, jnp.logical_not(low_part)), (mine, low_part)):
        def row_of(index, number_first, number_last):
            first = read_row(ByRow(first_tile), index, number_first)
            last = read_row(ByRow(last_tile), index, number_last)
            return jnp.where(use_last, last, first)

        place = pl.ds(PACKED * SUBLANES, SUBLANES)
        ends_row = (FULL, SUBLANES - HALO)
        target[place, :] = 2.0 * row_of(10, *ends_row) - row_of(0, *ends_row)
        for group in range(FULL * PLANES // GROUP):
            blocks = []
            for number in range(group * GROUP, (group + 1) * GROUP):
                index, extra = divmod(number, FULL)
                blocks.append(row_of(index, extra, SUBLANES - FULL + extra))
            for number, block in enumerate(pack_blocks(blocks)):
                place = (group * (GROUP - 1) + number) * SUBLANES
                target[pl.ds(place, SUBLANES), :] = block


def load_inputs(arrays, widths, tiles_count):
    row_count, flat_count = arrays[0].shape
    return pl.pallas_call(
        functools.partial(load_kernel, tiles_count),
        out_shape=[
            pltpu.SMEM((4,), jnp.int32),
            jax.ShapeDtypeStruct((FIELDS, row_count, flat_count), jnp.float32),
            jax.ShapeDtypeStruct((row_count, flat_count), jnp.int32),
            jax.ShapeDtypeStruct((END_ROWS + PAIRS * row_count, LANES), jnp.float32),
            jax.ShapeDtypeStruct((END_ROWS, LANES), jnp.float32),
        ],
        in_specs=[HBM] * 6,
        out_specs=[SMEM] + [VMEM] * 4,
        scratch_shapes=[
            pltpu.VMEM((SUBLANES, PLACES * SUBLANES, LANES), jnp.float32),
            pltpu.VMEM((SUBLANES, PLACES * SUBLANES, LANES), jnp.float32),
            pltpu.SMEM(widths.shape, jnp.int32),
            pltpu.SemaphoreType.DMA((7,)),
        ],
        compiler_params=pltpu.CompilerParams(vmem_limit_bytes=16 * 1024 * 1024),
        name="load",
    )(*[pltpu.with_memory_space_constraint(array, pltpu.HBM) for array in (*arrays, widths)])


def spread_kernel(raw, raw_solid, spread):
    for index in range(PLANES):
        for row in range(0, raw_solid.shape[0], SUBLANES):
            spread_tile(raw, raw_solid, index, row, spread, row)


def spread_rows(raw, raw_solid):
    row_count = raw_solid.shape[0]
    return pl.pallas_call(
        spread_kernel,
        out_shape=by_row(row_count, PLACES),
        in_specs=[VMEM, VMEM],
        out_specs=VMEM,
        compiler_params=pltpu.CompilerParams(vmem_limit_bytes=16 * 1024 * 1024),
        cost_estimate=pl.CostEstimate(flops=1_000_000, bytes_accessed=4_000_000, transcendentals=0),
        name="spread",
    )(raw, raw_solid)


def join_kernel(mine, packet, spread, ends):
    ends[pl.ds(0, END_ROWS), :] = mine[...]
    ends[pl.ds(END_ROWS, END_ROWS), :] = packet[pl.ds(0, END_ROWS), :]


def join_ends(mine, packet, spread):
    return pl.pallas_call(
        join_kernel,
        out_shape=jax.ShapeDtypeStruct((2 * END_ROWS, LANES), jnp.float32),
        in_specs=[VMEM, VMEM, ANY],
        out_specs=VMEM,
        compiler_params=pltpu.CompilerParams(vmem_limit_bytes=8 * 1024 * 1024),
        name="join",
    )(mine, packet, spread)


def beside_kernel(info, spread, packet, whole):
    low_part = info[3] == 0
    row_count, width = spread.shape[:2]
    flat = flat_view(whole)
    for pair in range(PAIRS):
        for row in range(0, row_count, SUBLANES):
            both = packet[pl.ds(END_ROWS + pair * row_count + row, SUBLANES), :]
            for index, values in ((pair, both), (pair + PAIRS, pltpu.roll(both, HALF, 1))):
                start = row * width + index * SUBLANES
                below = jnp.where(low_part, 0.0, values)
                above = jnp.where(low_part, values, 0.0)
                flat[pl.ds(start, SUBLANES, stride=width), :] = below
                flat[pl.ds(start + SUBLANES - 1, SUBLANES, stride=width), :] = above


def put_beside(info, spread, packet):
    return pl.pallas_call(
        beside_kernel,
        out_shape=jax.ShapeDtypeStruct(spread.shape, jnp.float32),
        in_specs=[SMEM, VMEM, VMEM],
        out_specs=VMEM,
        input_output_aliases={1: 0},
        compiler_params=pltpu.CompilerParams(vmem_limit_bytes=16 * 1024 * 1024),
        name="beside",
    )(info, pltpu.with_memory_space_constraint(spread, pltpu.VMEM), packet)


def keep_rows(slab, source, first, size, live):
    for slab_row, row in slab_rows(live, first, size):
        for extra in range(size):
            slab[slab_row + extra] = source[row + extra]


def slab_rows(live, first, size):
    mirrored = SLAB - first - size
    return [(first, first - HALO), (SLAB + mirrored, live - 2 * RIM + mirrored)]


def collide_rows(geometry, before, whole, first, colours, walls, state):
    over_rows(geometry, first - 1, *COLOUR_BLOCK, lambda block: colour_stage(
        block, geometry, before, colours))
    over_rows(geometry, first, *COLLIDE_BLOCK, lambda block: collide_stage(
        block, geometry, before, whole, colours, walls, state))


def tile_copies(pieces, outs, held_row, out_row, sems):
    held, rows = pl.ds(held_row, SUBLANES), pl.ds(out_row, SUBLANES)
    parts = (
        (pieces.at[0, held], outs[0].at[rows]),
        (pieces.at[pl.ds(1, 3), held], outs[1].at[:, rows]),
        (pieces.at[pl.ds(4, 6), held], outs[2].at[:, rows]),
        (pieces.at[10, held], outs[3].at[rows]),
    )
    return [
        pltpu.make_async_copy(source, target, sems.at[number])
        for number, (source, target) in enumerate(parts)
    ]


def gather_tiles(final, row, pieces, held_row):
    width = final.shape[1]
    start = row * width
    if not isinstance(start, int):
        start = pl.multiple_of(start, SUBLANES)
    for index in range(FIELDS):
        for tile in range(OWN_TILES):
            place = start + index * SUBLANES + 1 + tile
            pieces[index, pl.ds(held_row, SUBLANES), pl.ds(tile * LANES, LANES)] = flat_view(final)[
                pl.ds(place, SUBLANES, stride=width), :
            ]


def first_kernel(
    info, whole, moved_later, reds_later, final,
    moved_slab, reds_slab, fields_slab, moved_later_slab, reds_later_slab, final_slab,
    colours, walls, moved, reds, fields,
):
    state, later = (ByRow(moved), ByRow(reds)), (ByRow(moved_later), ByRow(reds_later))
    geometry = Geometry(info, OWN_TILES)
    live = geometry.live
    fill_wall_table(walls, geometry)
    collide_rows(geometry, ByRow(whole), ByRow(whole), 1, ByRow(colours), walls, state)
    over_rows(geometry, 2, *ARRIVE_BLOCK, lambda block: arrive_stage(
        block, geometry, walls, state, ByRow(fields)))
    keep_rows(moved_slab, moved, HALO + 1, KEPT, live)
    keep_rows(reds_slab, reds, HALO + 1, KEPT, live)
    keep_rows(fields_slab, fields, HALO + 2, KEPT, live)
    collide_rows(geometry, ByRow(fields), ByRow(whole), 3, ByRow(colours), walls, later)
    keep_rows(moved_later_slab, moved_later, HALO + 3, KEPT, live)
    keep_rows(reds_later_slab, reds_later, HALO + 3, KEPT, live)
    edges = slab_rows(live, HALO + RIM, RIM)
    rim = Block(geometry, [(row, row, RIM) for _, row in edges], True, [at for at, _ in edges])
    arrive_stage(rim, geometry, walls, later, ByRow(final_slab))

    def arrive_tile(tile, carry):
        row = tile * SUBLANES
        block = Block(geometry, [(row, row, SUBLANES)], inner=True)
        arrive_stage(block, geometry, walls, later, ByRow(final))
        return carry

    lax.fori_loop(1, jnp.minimum(SPLIT, live // SUBLANES - 1), arrive_tile, 0)


def second_kernel(
    info, moved, reds, earlier, arrived, density_out, momentum_out, stress_out, red_out,
    final, walls, pieces, zeros, sems,
):
    outs = (density_out, momentum_out, stress_out, red_out)
    row_tiles = density_out.shape[0] // SUBLANES
    state = (ByRow(moved), ByRow(reds))
    geometry = Geometry(info, OWN_TILES)
    live = geometry.live
    last = live // SUBLANES - 1
    fill_wall_table(walls, geometry)

    def copies_of(tile):
        row = pl.multiple_of(tile * SUBLANES, SUBLANES)
        return tile_copies(pieces, outs, row, row, sems.at[tile])

    def send_out(tile, source):
        row = pl.multiple_of(tile * SUBLANES, SUBLANES)
        gather_tiles(source, row, pieces, row)
        for copy in copies_of(tile):
            copy.start()

    def pass_on(tile, carry):
        send_out(tile, earlier)
        return carry

    def finish(tile, carry):
        row = tile * SUBLANES
        block = Block(geometry, [(row, row, SUBLANES)], inner=True)
        arrive_stage(block, geometry, walls, state, ByRow(final))
        send_out(tile, final)
        return carry

    def settle(tile, carry):
        for copy in copies_of(tile):
            copy.wait()
        return carry

    lax.fori_loop(1, jnp.minimum(SPLIT, last), pass_on, 0)
    zeros[...] = jnp.zeros(zeros.shape, zeros.dtype)
    dead = {}
    for tile in range(row_tiles):
        dead[tile] = tile_copies(zeros, outs, 0, tile * SUBLANES, sems.at[tile])

        @pl.when(tile * SUBLANES >= live)
        def _():
            for copy in dead[tile]:
                copy.start()

    lax.fori_loop(SPLIT, last, finish, 0)
    lax.fori_loop(1, last, settle, 0)
    for tile in range(row_tiles):

        @pl.when(tile * SUBLANES >= live)
        def _():
            for copy in dead[tile]:
                copy.wait()


def scratch_of(shape):
    return pltpu.VMEM(shape.shape, shape.dtype)


def pieces_of(rows, flat_count):
    return pltpu.VMEM((FIELDS, rows, flat_count), jnp.float32)


def run_first(info, whole):
    rows = whole.shape[0]
    shapes = [by_row(rows, count) for count in (HELD, REDS, FIELDS)]
    slabs = [by_row(2 * SLAB, count) for count in (HELD, REDS, FIELDS, HELD, REDS, FIELDS)]
    scratch = [by_row(rows, 4), by_row(4, 3)]
    scratch = scratch + [by_row(rows, count) for count in (HELD, REDS, FIELDS)]
    return pl.pallas_call(
        first_kernel,
        out_shape=shapes + slabs,
        in_specs=[SMEM, VMEM],
        out_specs=[VMEM] * 9,
        scratch_shapes=[scratch_of(shape) for shape in scratch],
        compiler_params=pltpu.CompilerParams(vmem_limit_bytes=24 * 1024 * 1024),
        cost_estimate=pl.CostEstimate(flops=20_000_000, bytes_accessed=8_000_000, transcendentals=0),
        name="first",
    )(info, whole)


def run_second(info, state, earlier, arrived, arrays):
    row_count, flat_count = arrays[0].shape
    return pl.pallas_call(
        second_kernel,
        out_shape=[jax.ShapeDtypeStruct(array.shape, jnp.float32) for array in arrays[:4]],
        in_specs=[SMEM] + [VMEM] * 3 + [ANY],
        out_specs=[ANY] * 4,
        scratch_shapes=[
            scratch_of(by_row(row_count, FIELDS)),
            scratch_of(by_row(4, 3)),
            pieces_of(row_count, flat_count),
            pieces_of(SUBLANES, flat_count),
            pltpu.SemaphoreType.DMA((row_count // SUBLANES, 4)),
        ],
        compiler_params=pltpu.CompilerParams(vmem_limit_bytes=24 * 1024 * 1024),
        cost_estimate=pl.CostEstimate(flops=20_000_000, bytes_accessed=8_000_000, transcendentals=0),
        name="second",
    )(info, *state, earlier, arrived)


def follow_kernel(ends, kept, out):
    out[pl.ds(PACKED * SUBLANES, 1), :] = jnp.zeros((1, LANES), jnp.float32)


def follow(ends, kept):
    return pl.pallas_call(
        follow_kernel,
        out_shape=jax.ShapeDtypeStruct(ends.shape, jnp.float32),
        in_specs=[VMEM, ANY],
        out_specs=VMEM,
        input_output_aliases={0: 0},
        compiler_params=pltpu.CompilerParams(vmem_limit_bytes=8 * 1024 * 1024),
        name="follow",
    )(pltpu.with_memory_space_constraint(ends, pltpu.VMEM), kept)


def outer_kernel(info, whole, arrived, passed, *refs):
    outs = refs[10:14]
    moved, reds, fields, moved_later, reds_later, final = refs[14:20]
    start_fields, colours, walls, pieces, sems = refs[20:]
    state, later = (ByRow(moved), ByRow(reds)), (ByRow(moved_later), ByRow(reds_later))
    geometry = Geometry(info, OWN_TILES)
    live = geometry.live
    low_part = info[3] == 0
    fill_wall_table(walls, geometry)

    def ends_of(ref, half):
        blocks = []
        for group in range(FULL * PLANES // GROUP):
            first = half * (PACKED + 1) + group * (GROUP - 1)
            packed = [ref[pl.ds((first + k) * SUBLANES, SUBLANES), :] for k in range(GROUP - 1)]
            blocks = blocks + unpack_blocks(packed)
        last = half * (PACKED + 1) + PACKED
        return blocks + [ref[pl.ds(last * SUBLANES, SUBLANES), :]]

    tiles = block_tiles()
    middle = (tiles >= 1) & (tiles <= OWN_TILES)

    def widened(own, other):
        beside = jnp.where(tiles == 0, roll_tiles(other, -OWN_TILES), roll_tiles(other, OWN_TILES))
        return jnp.where(geometry.domain, jnp.where(middle, own, beside), 0.0)

    straight = [widened(*pair) for pair in zip(ends_of(arrived, 0), ends_of(arrived, 1))]
    crossed = [widened(*pair) for pair in zip(ends_of(passed, 1), ends_of(passed, 0))]
    below = [jnp.where(low_part, *pair) for pair in zip(straight, crossed)]
    above = [jnp.where(low_part, *pair) for pair in zip(crossed, straight)]

    for number in range(FULL * PLANES):
        index, extra = divmod(number, FULL)
        write_row(ByRow(start_fields), index, 1 + extra, below[number])
        write_row(ByRow(start_fields), index, 2 * SLAB - HALO + extra, above[number])
    for row, colour in ((0, below[-1]), (2 * SLAB - 1, above[-1])):
        write_row(ByRow(start_fields), 0, row, jnp.zeros((SUBLANES, LANES), jnp.float32))
        write_row(ByRow(start_fields), 10, row, 0.5 * colour)
    for slab_row, row in slab_rows(live, HALO, FULL):
        for extra in range(FULL):
            start_fields[slab_row + extra] = whole[row + extra]

    def block(first, count):
        return Block(geometry, [(row, at, count) for at, row in slab_rows(live, first, count)])

    held, solids, marks = ByRow(fields), ByRow(start_fields), ByRow(colours)
    colour_stage(block(0, 6), geometry, solids, marks)
    collide_stage(block(1, 4), geometry, solids, solids, marks, walls, state)
    arrive_stage(block(2, 4), geometry, walls, state, held)
    colour_stage(block(2, 6), geometry, held, marks)
    collide_stage(block(3, 4), geometry, held, solids, marks, walls, later)
    arrive_stage(block(4, 4), geometry, walls, later, ByRow(final))

    copies = []
    for side, row, out_row in ((0, HALO, 0), (1, SLAB, live - SUBLANES)):
        gather_tiles(final, row, pieces, side * SUBLANES)
        out_row = pl.multiple_of(out_row, SUBLANES)
        copies = copies + tile_copies(pieces, outs, side * SUBLANES, out_row, sems.at[side])
    for copy in copies:
        copy.start()
    for copy in copies:
        copy.wait()


def run_outer(info, whole, arrived, passed, slabs, outs):
    flat_count = outs[0].shape[1]
    shapes = [jax.ShapeDtypeStruct(array.shape, jnp.float32) for array in (*outs, *slabs)]
    slabs = [pltpu.with_memory_space_constraint(slab, pltpu.VMEM) for slab in slabs]
    aliases = {4 + number: 4 + number for number in range(6)}
    aliases.update({10 + number: number for number in range(4)})
    return pl.pallas_call(
        outer_kernel,
        out_shape=shapes,
        in_specs=[SMEM] + [VMEM] * 9 + [ANY] * 4,
        out_specs=[ANY] * 4 + [VMEM] * 6,
        scratch_shapes=[
            scratch_of(by_row(2 * SLAB, PLACES)),
            scratch_of(by_row(2 * SLAB, 4)),
            scratch_of(by_row(4, 3)),
            pieces_of(2 * SUBLANES, flat_count),
            pltpu.SemaphoreType.DMA((2, 4)),
        ],
        input_output_aliases=aliases,
        compiler_params=pltpu.CompilerParams(vmem_limit_bytes=24 * 1024 * 1024),
        name="outer",
    )(info, whole, arrived, passed, *slabs, *outs)


def body(density, momentum, stress, red_density, solid, widths):
    tiles_count = lax.axis_size("tiles")
    arrays = (density, momentum, stress, red_density, solid)
    info, raw, raw_solid, packet, mine = load_inputs(arrays, widths, tiles_count)
    info = pltpu.with_memory_space_constraint(info, pltpu.SMEM)
    swap = [(0, 1), (1, 0)]
    packet = lax.ppermute(packet, "sub", swap)
    spread = spread_rows(raw, raw_solid)
    ends = join_ends(mine, packet, spread)
    route = [(2 * k, 2 * k + 2) for k in range(tiles_count - 1)]
    route = route + [(2 * k + 3, 2 * k + 1) for k in range(tiles_count - 1)]
    arrived = lax.ppermute(ends, ("tiles", "sub"), route)
    whole = put_beside(info, spread, packet)
    moved, reds, earlier, *slabs = run_first(info, whole)
    arrived = follow(arrived, slabs[-1])
    passed = lax.ppermute(arrived, "sub", swap)
    outs = run_second(info, (moved, reds), earlier, arrived, arrays)
    return tuple(run_outer(info, whole, arrived, passed, slabs, outs)[:4])


def solution(mesh):
    in_specs = (
        P(("groups", "tiles"), "sub"),
        P(None, ("groups", "tiles"), "sub"),
        P(None, ("groups", "tiles"), "sub"),
        P(("groups", "tiles"), "sub"),
        P(("groups", "tiles"), "sub"),
        P("groups"),
    )
    out_specs = (
        P(("groups", "tiles"), "sub"),
        P(None, ("groups", "tiles"), "sub"),
        P(None, ("groups", "tiles"), "sub"),
        P(("groups", "tiles"), "sub"),
    )
    return jax.shard_map(body, mesh=mesh, in_specs=in_specs, out_specs=out_specs, check_vma=False)
```

```python
import functools

import jax
import jax.numpy as jnp
from jax import lax
from jax.experimental import pallas as pl
from jax.experimental.pallas import tpu as pltpu
from jax.sharding import PartitionSpec as P

TILE = 16
STEPS = 2
RELAX_TIME = 0.8
SURFACE = 0.1
SEPARATION = 0.7

LANES = 128
SUBLANES = 8
FULL = 3
HALO = FULL + 1
FIELDS = 11
PLANES = FIELDS + 1
MOVED = 19
REDS = 5
HELD = MOVED + 1
RIM = 4
SLAB = HALO + 2 * RIM
OWN_TILES = SUBLANES - 2
GROUP = 4
PACKED = FULL * PLANES // GROUP * (GROUP - 1)
END_ROWS = (PACKED + 1) * SUBLANES
HALF = LANES // 2
ORDER = (0, 1, 2, 3, 10, 11, 4, 5, 6, 7, 8, 9)
PAIRS = PLANES // 2
PLACES = PLANES + 1
SPLIT = 3
KEPT = 2
COLOUR_BLOCK = (8, 1)
COLLIDE_BLOCK = (2, 4)
ARRIVE_BLOCK = (8, 1)
VMEM = pl.BlockSpec(memory_space=pltpu.VMEM)
SMEM = pl.BlockSpec(memory_space=pltpu.SMEM)
ANY = pl.BlockSpec(memory_space=pl.ANY)
HBM = pl.BlockSpec(memory_space=pltpu.HBM)


class Rows:
    def __init__(self, parts):
        self.parts = parts

    def _with(self, other, operation):
        others = other.parts if isinstance(other, Rows) else [other] * len(self.parts)
        return Rows([operation(one, two) for one, two in zip(self.parts, others)])

    def __add__(self, other):
        return self._with(other, lambda one, two: one + two)

    def __sub__(self, other):
        return self._with(other, lambda one, two: one - two)

    def __rsub__(self, other):
        return self._with(other, lambda one, two: two - one)

    def __mul__(self, other):
        return self._with(other, lambda one, two: one * two)

    def __or__(self, other):
        return self._with(other, lambda one, two: one | two)

    def __eq__(self, other):
        return self._with(other, lambda one, two: one == two)

    __radd__, __rmul__, __ror__ = __add__, __mul__, __or__

    def each(self, operation):
        return Rows([operation(part) for part in self.parts])


def select(mask, yes, no):
    count = max(len(item.parts) for item in (mask, yes, no) if isinstance(item, Rows))
    columns = [
        item.parts if isinstance(item, Rows) else [item] * count for item in (mask, yes, no)
    ]
    return Rows([jnp.where(*row) for row in zip(*columns)])


def roll_lanes(values, amount):
    return values.each(lambda part: pltpu.roll(part, amount % LANES, 1))


def roll_sublanes(values, amount):
    return values.each(lambda part: pltpu.roll(part, amount % SUBLANES, 0))


class Geometry:
    def __init__(self, info, own_tiles):
        live, first, last, sub_index = info[0], info[1], info[2], info[3]
        self.live = live
        self.low_row = jnp.where(first == 1, 0, -1000)
        self.high_row = jnp.where(last == 1, live, 1000)
        shape = (SUBLANES, LANES)
        lane = lax.broadcasted_iota(jnp.int32, shape, 1)
        tile = lax.broadcasted_iota(jnp.int32, shape, 0)
        depth = lane & (TILE - 1)
        low_part = sub_index == 0
        high_part = sub_index == 1
        z_walls = {1: depth == 0, -1: depth == TILE - 1}
        y_walls = {
            1: (tile == 1) & (lane < TILE) & low_part,
            -1: (tile == own_tiles) & (lane >= LANES - TILE) & high_part,
        }
        self.walls = {(0, vel_z): wall for vel_z, wall in z_walls.items()}
        for vel_y, y_wall in y_walls.items():
            self.walls[vel_y, 0] = y_wall
            for vel_z, z_wall in z_walls.items():
                self.walls[vel_y, vel_z] = y_wall | z_wall
        own = (tile >= 1) & (tile <= own_tiles)
        self.domain = own | ((tile == own_tiles + 1) & low_part) | ((tile == 0) & high_part)
        self.first_lanes = lane < TILE
        self.last_lanes = lane >= LANES - TILE

    def from_low_y(self, values):
        return roll_lanes(select(self.last_lanes, roll_sublanes(values, 1), values), TILE)

    def from_high_y(self, values):
        return roll_lanes(select(self.first_lanes, roll_sublanes(values, -1), values), -TILE)

    def from_low_z(self, values):
        return select(self.walls[0, 1], 0.0, roll_lanes(values, 1))

    def from_high_z(self, values):
        return select(self.walls[0, -1], 0.0, roll_lanes(values, -1))


def flat_rows(row, count, tile_offset=0):
    start = row * SUBLANES
    if not isinstance(start, int):
        start = pl.multiple_of(start, SUBLANES)
    return pl.ds(start + tile_offset, count * SUBLANES)


class ByRow:
    def __init__(self, ref):
        self.ref = ref


def by_row(rows, count):
    return jax.ShapeDtypeStruct((rows, count * SUBLANES, LANES), jnp.float32)


def place_of(ref, index, row, tile_offset=0):
    if isinstance(ref, ByRow):
        return ref.ref, row, pl.ds(index * SUBLANES + tile_offset, SUBLANES)
    return ref, index, flat_rows(row, 1, tile_offset)


def read_row(ref, index, row, tile_offset=0):
    ref, first, second = place_of(ref, index, row, tile_offset)
    return ref[first, second, :]


def write_row(ref, index, row, values):
    ref, first, second = place_of(ref, index, row)
    ref[first, second, :] = values


class Block:
    def __init__(self, geometry, spans, inner=False, store_rows=None):
        self.spans = spans
        self.store_rows = store_rows or [local for row, local, count in spans]
        rows = [row + extra for row, local, count in spans for extra in range(count)]
        self.inner = inner
        rows = [row + extra for row, local, count in spans for extra in range(count)]
        if inner:
            self.x_walls = {}
            self.valid = geometry.domain
            self.kinds = [0]
            return
        ids = Rows([row + jnp.zeros((SUBLANES, LANES), jnp.int32) for row in rows])
        self.x_walls = {1: ids == geometry.low_row, -1: ids == geometry.high_row - 1}
        self.valid = ids.each(
            lambda part: geometry.domain & (part >= geometry.low_row) & (part < geometry.high_row)
        )
        self.kinds = [
            jnp.where(row == geometry.low_row, 1, 0) + jnp.where(row == geometry.high_row - 1, 2, 0)
            for row in rows
        ]

    def load(self, ref, index, offset=0, tile_offset=0):
        return Rows([
            read_row(ref, index, local + offset + extra, tile_offset)
            for row, local, count in self.spans
            for extra in range(count)
        ])

    def store(self, ref, index, values):
        targets = [
            target + extra
            for (row, local, count), target in zip(self.spans, self.store_rows)
            for extra in range(count)
        ]
        for target, part in zip(targets, values.parts):
            write_row(ref, index, target, part)

    def wall_terms(self, walls, position):
        terms = [walls[position, flat_rows(kind, 1), :] for kind in self.kinds]
        return terms[0] if self.inner else Rows(terms)


def fill_wall_table(walls, geometry):
    one = jnp.ones((SUBLANES, LANES), jnp.float32)
    up_y, down_y, up_z, down_z = [
        jnp.where(geometry.walls[key], 0.0, one) for key in ((-1, 0), (1, 0), (0, -1), (0, 1))
    ]
    sum_y, sum_z = up_y + down_y, up_z + down_z
    for kind, (up_x, down_x) in enumerate(((1.0, 1.0), (1.0, 0.0), (0.0, 1.0))):
        sum_x = up_x + down_x
        around_x = 2.0 + sum_y + sum_z
        total = 12.0 + 2.0 * (sum_x + sum_y + sum_z) + sum_x * (sum_y + sum_z) + sum_y * sum_z
        rows = (
            (up_x - down_x) * around_x,
            (up_y - down_y) * (2.0 + sum_x + sum_z),
            (up_z - down_z) * (2.0 + sum_x + sum_y),
            36.0 - total,
        )
        for position, row in enumerate(rows):
            walls[position, flat_rows(kind, 1), :] = row


VELOCITIES = tuple(
    tuple(sign if axis == place else 0 for place in range(3)) for axis in range(3) for sign in (1, -1)
) + tuple(
    tuple({a: one, b: two}.get(place, 0) for place in range(3))
    for a, b in ((0, 1), (0, 2), (1, 2))
    for one, two in ((1, 1), (-1, -1), (1, -1), (-1, 1))
)
VELOCITIES = ((0, 0, 0),) + VELOCITIES


def colour_stage(block, geometry, fields, colours):
    density = block.load(fields, 0)
    red = block.load(fields, 10)
    colour = select(block.valid, 2.0 * red - density, 0.0)
    along_y = geometry.from_low_y(colour) + geometry.from_high_y(colour)
    along_z = geometry.from_low_z(colour) + geometry.from_high_z(colour)
    block.store(colours, 0, colour)
    block.store(colours, 1, 2.0 * colour + (along_y + along_z))
    block.store(colours, 2, along_y)
    block.store(colours, 3, along_z)


def collide_stage(block, geometry, fields, solids, colours, walls, state):
    relaxing = 1.0 - 1.0 / RELAX_TIME
    third = 1.0 / 3.0
    colour = block.load(colours, 0)
    doubled = 2.0 * colour + (block.load(colours, 0, -1) + block.load(colours, 0, 1))
    term_y = doubled + block.load(colours, 3)
    term_z = doubled + block.load(colours, 2)
    grad_x = block.load(colours, 1, 1) - block.load(colours, 1, -1)
    grad_y = geometry.from_high_y(term_y) - geometry.from_low_y(term_y)
    grad_z = geometry.from_high_z(term_z) - geometry.from_low_z(term_z)
    if not block.inner:
        grad_x = grad_x - block.wall_terms(walls, 0) * colour
    grad_y = grad_y - block.wall_terms(walls, 1) * colour
    grad_z = grad_z - block.wall_terms(walls, 2) * colour

    fluid = block.load(solids, PLANES - 1) == 0.0
    density = block.load(fields, 0)
    red = block.load(fields, 10)
    flux = [block.load(fields, 1 + axis) for axis in range(3)]
    stress = [block.load(fields, 4 + part) for part in range(6)]
    square_xx, square_yy, square_zz = grad_x * grad_x, grad_y * grad_y, grad_z * grad_z
    square = square_xx + square_yy + square_zz
    inverse = select(fluid, (1.0 + square * (1.0 / 144.0)).each(lax.rsqrt), 0.0)
    trace = third * square
    strength = (SURFACE / (8.0 * 144.0)) * inverse
    keep = select(fluid, relaxing / 8.0, 1.0 / 8.0)
    eighths = [0.125 * part for part in flux]
    own = [
        eighths[axis] * flux[axis] + (keep * stress[axis] + strength * (squared - trace))
        for axis, squared in enumerate((square_xx, square_yy, square_zz))
    ]
    strength, keep = 2.0 * strength, 2.0 * keep
    quarters = [2.0 * part for part in eighths[:2]]
    grads = (grad_x, grad_y, grad_z)
    cross = [
        quarters[a] * flux[b] + (keep * stress[3 + plane] + strength * (grads[a] * grads[b]))
        for plane, (a, b) in enumerate(((0, 1), (0, 2), (1, 2)))
    ]
    base = density * (1.0 / 36.0) - third * (own[0] + own[1] + own[2])
    sign = select(fluid, 1.0 / 12.0, -1.0 / 12.0)
    run = [sign * part for part in flux]
    mixing = ((SEPARATION / 144.0) * red) * ((density - red) * inverse)
    red_run = [0.5 * part + mixing * grad for part, grad in zip(run, grads)]
    moved, reds = state
    block.store(moved, 0, 12.0 * base)
    straight = [base + part for part in own]
    for axis in range(3):
        middle = 2.0 * straight[axis]
        swing = 2.0 * run[axis]
        block.store(moved, 1 + 2 * axis, middle + swing)
        block.store(moved, 2 + 2 * axis, middle - swing)
    for plane, (a, b) in enumerate(((0, 1), (0, 2), (1, 2))):
        middle = straight[a] + own[b]
        same, other = middle + cross[plane], middle - cross[plane]
        along, against = run[a] + run[b], run[a] - run[b]
        first = 7 + 4 * plane
        block.store(moved, first, same + along)
        block.store(moved, first + 1, same - along)
        block.store(moved, first + 2, other + against)
        block.store(moved, first + 3, other - against)

    red_base = select(block.valid, red * (1.0 / 36.0), 0.0)
    red_run = [select(block.valid, part, 0.0) for part in red_run]
    block.store(reds, 0, red_base)
    block.store(reds, 1, red_base + red_run[0])
    block.store(reds, 2, red_base - red_run[0])
    block.store(reds, 3, red_run[1])
    block.store(reds, 4, red_run[2])


def arrive_stage(block, geometry, walls, state, fields):
    third = 1.0 / 3.0
    moved, reds = state
    own = [None] * MOVED

    def here(direction):
        if own[direction] is None:
            own[direction] = block.load(moved, direction)
        return own[direction]

    def arrived(direction, opposite):
        vel_x, vel_y, vel_z = VELOCITIES[direction]
        values = here(direction) if vel_x == 0 else block.load(moved, direction, -vel_x)
        if vel_y != 0:
            beside = block.load(moved, direction, -vel_x, -vel_y)
            leaving = geometry.last_lanes if vel_y == 1 else geometry.first_lanes
            values = select(leaving, beside, values)
        if vel_y != 0 or vel_z != 0:
            values = roll_lanes(values, TILE * vel_y + vel_z)
        masks = []
        if vel_x in block.x_walls:
            masks.append(block.x_walls[vel_x])
        if (vel_y, vel_z) in geometry.walls:
            masks.append(geometry.walls[vel_y, vel_z])
        if not masks:
            return values
        wall = functools.reduce(lambda one, two: one | two, masks)
        return select(wall, here(opposite), values)

    red = block.load(reds, 0)
    red_y = block.load(reds, 3)
    red_z = block.load(reds, 4)
    from_x = block.load(reds, 1, -1) + block.load(reds, 2, 1)
    spread = 2.0 * red + from_x
    spread_y = 2.0 * red_y + (block.load(reds, 3, -1) + block.load(reds, 3, 1))
    spread_z = 2.0 * red_z + (block.load(reds, 4, -1) + block.load(reds, 4, 1))
    up_y, down_y = red + red_y, red - red_y
    low_y = (
        (spread + spread_y)
        + geometry.from_low_z(up_y + red_z)
        + geometry.from_high_z(up_y - red_z)
    )
    high_y = (
        (spread - spread_y)
        + geometry.from_low_z(down_y + red_z)
        + geometry.from_high_z(down_y - red_z)
    )
    bounced = (
        block.wall_terms(walls, 3) * red
        - block.wall_terms(walls, 1) * red_y
        - block.wall_terms(walls, 2) * red_z
    )
    if not block.inner:
        bounced = bounced - block.wall_terms(walls, 0) * (block.load(reds, 1) - red)
    red_total = (
        12.0 * red
        + 2.0 * from_x
        + geometry.from_low_z(spread + spread_z)
        + geometry.from_high_z(spread - spread_z)
        + geometry.from_low_y(low_y)
        + geometry.from_high_y(high_y)
        + bounced
    )
    rest = here(0)
    sums, diffs = [], []
    for axis in range(3):
        up = arrived(1 + 2 * axis, 2 + 2 * axis)
        down = arrived(2 + 2 * axis, 1 + 2 * axis)
        sums.append(up + down)
        diffs.append(up - down)
    total = rest + sums[0] + sums[1] + sums[2]
    cross = []
    for plane, (a, b) in enumerate(((0, 1), (0, 2), (1, 2))):
        first = 7 + 4 * plane
        parts = [arrived(first + offset, first + (offset ^ 1)) for offset in range(4)]
        same, other = parts[0] + parts[1], parts[2] + parts[3]
        along, against = parts[0] - parts[1], parts[2] - parts[3]
        both = same + other
        cross.append(same - other)
        total = total + both
        sums[a], sums[b] = sums[a] + both, sums[b] + both
        diffs[a], diffs[b] = diffs[a] + (along + against), diffs[b] + (along - against)
    shared = third * total
    block.store(fields, 0, total)
    for axis in range(3):
        block.store(fields, 1 + axis, diffs[axis])
        block.store(fields, 4 + axis, sums[axis] - shared - diffs[axis] * diffs[axis])
    for plane, (a, b) in enumerate(((0, 1), (0, 2), (1, 2))):
        block.store(fields, 7 + plane, cross[plane] - diffs[a] * diffs[b])
    block.store(fields, 10, red_total)


def over_rows(geometry, first, size, blocks, stage):
    trip = size * blocks
    rest = -2 * first % trip
    assert TILE % trip == 0 and rest % min(size, rest or size) == 0

    def run(start, count, step_size):
        for offset in range(0, count, step_size):
            row = start + offset
            stage(Block(geometry, [(row, row, step_size)], inner=True))

    def step(index, carry):
        run(first + index * trip, trip, size)
        return carry

    trips = (geometry.live - 2 * first - rest) // trip
    lax.fori_loop(0, trips, step, 0)
    if rest:
        run(geometry.live - first - rest, rest, min(size, rest))


def block_tiles():
    return lax.broadcasted_iota(jnp.int32, (SUBLANES, LANES), 0)


def roll_tiles(block, amount):
    return pltpu.roll(block, amount % SUBLANES, 0)


def pack_blocks(blocks):
    tiles, rest = block_tiles(), blocks[GROUP - 1]
    packed = []
    for number, block in enumerate(blocks[: GROUP - 1]):
        low, high = 2 * number + 1, 2 * number + 2
        block = jnp.where(tiles == 0, roll_tiles(rest, -low), block)
        packed.append(jnp.where(tiles == SUBLANES - 1, roll_tiles(rest, SUBLANES - 1 - high), block))
    return packed


def unpack_blocks(packed):
    tiles, rest = block_tiles(), None
    for number, block in enumerate(packed):
        low, high = 2 * number + 1, 2 * number + 2
        part = jnp.where(tiles == low, roll_tiles(block, low), roll_tiles(block, high - SUBLANES + 1))
        rest = part if rest is None else jnp.where(tiles >= low, part, rest)
    return list(packed) + [rest]


def flat_view(ref):
    rows, width, lanes = ref.shape
    return ref.reshape(rows * width, lanes)


def spread_tile(raw, raw_solid, index, row, target, target_row):
    source = raw_solid if index == FIELDS else raw.at[index]
    width = target.shape[1]
    for tile in range(OWN_TILES):
        values = source[pl.ds(row, SUBLANES), pl.ds(tile * LANES, LANES)].astype(jnp.float32)
        start = target_row * width + index * SUBLANES + 1 + tile
        flat_view(target)[pl.ds(start, SUBLANES, stride=width), :] = values


def load_kernel(
    tiles_count, density, momentum, stress, red, solid, widths,
    info, raw, raw_solid, packet, mine,
    first_tile, last_tile, held_widths, sems,
):
    row_count, flat_count = raw_solid.shape
    own_tiles = flat_count // LANES
    copies = [
        pltpu.make_async_copy(widths, held_widths, sems.at[0]),
        pltpu.make_async_copy(density, raw.at[0], sems.at[1]),
        pltpu.make_async_copy(momentum, raw.at[pl.ds(1, 3)], sems.at[2]),
        pltpu.make_async_copy(red, raw.at[10], sems.at[3]),
        pltpu.make_async_copy(solid, raw_solid, sems.at[4]),
        pltpu.make_async_copy(stress.at[pl.ds(0, 3)], raw.at[pl.ds(4, 3)], sems.at[5]),
        pltpu.make_async_copy(stress.at[pl.ds(3, 3)], raw.at[pl.ds(7, 3)], sems.at[6]),
    ]
    for copy in copies:
        copy.start()
    tiles_index, sub_index = lax.axis_index("tiles"), lax.axis_index("sub")
    low_part = sub_index == 0
    edge_start = pl.multiple_of(jnp.where(low_part, (own_tiles - 1) * LANES, 0), LANES)

    copies[0].wait()
    live = held_widths[tiles_index] * TILE
    info[0] = live
    info[1] = (tiles_index == 0).astype(jnp.int32)
    info[2] = (tiles_index == tiles_count - 1).astype(jnp.int32)
    info[3] = sub_index

    near_cut = lax.broadcasted_iota(jnp.int32, (SUBLANES, LANES), 1) < HALF
    near_cut = near_cut == jnp.logical_not(low_part)
    near_last = pl.multiple_of(live - SUBLANES, SUBLANES)
    edges = pl.ds(edge_start, LANES)

    def plane_of(index):
        return raw_solid if index == FIELDS else raw.at[index]

    def pack_edges(pair):
        here, there = [plane_of(index) for index in ORDER[2 * pair : 2 * pair + 2]]
        for row in range(0, row_count, SUBLANES):
            rows = pl.ds(row, SUBLANES)
            beside = pltpu.roll(there[rows, edges].astype(jnp.float32), HALF, 1)
            both = jnp.where(near_cut, here[rows, edges].astype(jnp.float32), beside)
            packet[pl.ds(END_ROWS + pair * row_count + row, SUBLANES), :] = both

    targets = ((packet, jnp.logical_not(low_part)), (mine, low_part))

    def row_of(use_last, index, number_first, number_last):
        first = read_row(ByRow(first_tile), index, number_first)
        last = read_row(ByRow(last_tile), index, number_last)
        return jnp.where(use_last, last, first)

    def pack_ends(group):
        for target, use_last in targets:
            blocks = []
            for number in range(group * GROUP, (group + 1) * GROUP):
                place, extra = divmod(number, FULL)
                blocks.append(row_of(use_last, ORDER[place], extra, SUBLANES - FULL + extra))
            for number, block in enumerate(pack_blocks(blocks)):
                place = (group * (GROUP - 1) + number) * SUBLANES
                target[pl.ds(place, SUBLANES), :] = block

    place = 0
    for copy, count in zip(copies[1:], (1, 3, 1, 1, 3, 3)):
        copy.wait()
        before, place = place, place + count
        for index in ORDER[before:place]:
            for target, row in ((first_tile, 0), (last_tile, near_last)):
                spread_tile(raw, raw_solid, index, row, target, 0)
        for pair in range(before // 2, place // 2):
            pack_edges(pair)
        for group in range(before * FULL // GROUP, place * FULL // GROUP):
            pack_ends(group)
    for target, use_last in targets:
        red_row, density_row = [
            row_of(use_last, index, FULL, SUBLANES - HALO) for index in (10, 0)
        ]
        target[pl.ds(PACKED * SUBLANES, SUBLANES), :] = 2.0 * red_row - density_row


def load_inputs(arrays, widths, tiles_count):
    row_count, flat_count = arrays[0].shape
    return pl.pallas_call(
        functools.partial(load_kernel, tiles_count),
        out_shape=[
            pltpu.SMEM((4,), jnp.int32),
            jax.ShapeDtypeStruct((FIELDS, row_count, flat_count), jnp.float32),
            jax.ShapeDtypeStruct((row_count, flat_count), jnp.int32),
            jax.ShapeDtypeStruct((END_ROWS + PAIRS * row_count, LANES), jnp.float32),
            jax.ShapeDtypeStruct((END_ROWS, LANES), jnp.float32),
        ],
        in_specs=[HBM] * 6,
        out_specs=[SMEM] + [VMEM] * 4,
        scratch_shapes=[
            pltpu.VMEM((SUBLANES, PLACES * SUBLANES, LANES), jnp.float32),
            pltpu.VMEM((SUBLANES, PLACES * SUBLANES, LANES), jnp.float32),
            pltpu.SMEM(widths.shape, jnp.int32),
            pltpu.SemaphoreType.DMA((7,)),
        ],
        compiler_params=pltpu.CompilerParams(vmem_limit_bytes=16 * 1024 * 1024),
        name="load",
    )(*[pltpu.with_memory_space_constraint(array, pltpu.HBM) for array in (*arrays, widths)])


def spread_kernel(raw, raw_solid, spread):
    for index in range(PLANES):
        for row in range(0, raw_solid.shape[0], SUBLANES):
            spread_tile(raw, raw_solid, index, row, spread, row)


def spread_rows(raw, raw_solid):
    row_count = raw_solid.shape[0]
    return pl.pallas_call(
        spread_kernel,
        out_shape=by_row(row_count, PLACES),
        in_specs=[VMEM, VMEM],
        out_specs=VMEM,
        compiler_params=pltpu.CompilerParams(vmem_limit_bytes=16 * 1024 * 1024),
        cost_estimate=pl.CostEstimate(flops=1_000_000, bytes_accessed=4_000_000, transcendentals=0),
        name="spread",
    )(raw, raw_solid)


def join_kernel(mine, packet, spread, ends):
    ends[pl.ds(0, END_ROWS), :] = mine[...]
    ends[pl.ds(END_ROWS, END_ROWS), :] = packet[pl.ds(0, END_ROWS), :]


def join_ends(mine, packet, spread):
    return pl.pallas_call(
        join_kernel,
        out_shape=jax.ShapeDtypeStruct((2 * END_ROWS, LANES), jnp.float32),
        in_specs=[VMEM, VMEM, ANY],
        out_specs=VMEM,
        compiler_params=pltpu.CompilerParams(vmem_limit_bytes=8 * 1024 * 1024),
        name="join",
    )(mine, packet, spread)


def beside_kernel(info, spread, packet, whole):
    low_part = info[3] == 0
    row_count, width = spread.shape[:2]
    flat = flat_view(whole)
    for pair in range(PAIRS):
        for row in range(0, row_count, SUBLANES):
            both = packet[pl.ds(END_ROWS + pair * row_count + row, SUBLANES), :]
            for place, values in ((2 * pair, both), (2 * pair + 1, pltpu.roll(both, HALF, 1))):
                index = ORDER[place]
                start = row * width + index * SUBLANES
                below = jnp.where(low_part, 0.0, values)
                above = jnp.where(low_part, values, 0.0)
                flat[pl.ds(start, SUBLANES, stride=width), :] = below
                flat[pl.ds(start + SUBLANES - 1, SUBLANES, stride=width), :] = above


def put_beside(info, spread, packet):
    return pl.pallas_call(
        beside_kernel,
        out_shape=jax.ShapeDtypeStruct(spread.shape, jnp.float32),
        in_specs=[SMEM, VMEM, VMEM],
        out_specs=VMEM,
        input_output_aliases={1: 0},
        compiler_params=pltpu.CompilerParams(vmem_limit_bytes=16 * 1024 * 1024),
        name="beside",
    )(info, pltpu.with_memory_space_constraint(spread, pltpu.VMEM), packet)


def keep_rows(slab, source, first, size, live):
    for slab_row, row in slab_rows(live, first, size):
        for extra in range(size):
            slab[slab_row + extra] = source[row + extra]


def slab_rows(live, first, size):
    mirrored = SLAB - first - size
    return [(first, first - HALO), (SLAB + mirrored, live - 2 * RIM + mirrored)]


def collide_rows(geometry, before, whole, first, colours, walls, state):
    over_rows(geometry, first - 1, *COLOUR_BLOCK, lambda block: colour_stage(
        block, geometry, before, colours))
    over_rows(geometry, first, *COLLIDE_BLOCK, lambda block: collide_stage(
        block, geometry, before, whole, colours, walls, state))


def tile_copies(pieces, outs, held_row, out_row, sems):
    held, rows = pl.ds(held_row, SUBLANES), pl.ds(out_row, SUBLANES)
    parts = (
        (pieces.at[0, held], outs[0].at[rows]),
        (pieces.at[pl.ds(1, 3), held], outs[1].at[:, rows]),
        (pieces.at[pl.ds(4, 6), held], outs[2].at[:, rows]),
        (pieces.at[10, held], outs[3].at[rows]),
    )
    return [
        pltpu.make_async_copy(source, target, sems.at[number])
        for number, (source, target) in enumerate(parts)
    ]


def gather_tiles(final, row, pieces, held_row):
    width = final.shape[1]
    start = row * width
    if not isinstance(start, int):
        start = pl.multiple_of(start, SUBLANES)
    for index in range(FIELDS):
        for tile in range(OWN_TILES):
            place = start + index * SUBLANES + 1 + tile
            pieces[index, pl.ds(held_row, SUBLANES), pl.ds(tile * LANES, LANES)] = flat_view(final)[
                pl.ds(place, SUBLANES, stride=width), :
            ]


def first_kernel(
    info, whole, moved_later, reds_later, final,
    moved_slab, reds_slab, fields_slab, moved_later_slab, reds_later_slab, final_slab,
    colours, walls, moved, reds, fields,
):
    state, later = (ByRow(moved), ByRow(reds)), (ByRow(moved_later), ByRow(reds_later))
    geometry = Geometry(info, OWN_TILES)
    live = geometry.live
    fill_wall_table(walls, geometry)
    collide_rows(geometry, ByRow(whole), ByRow(whole), 1, ByRow(colours), walls, state)
    over_rows(geometry, 2, *ARRIVE_BLOCK, lambda block: arrive_stage(
        block, geometry, walls, state, ByRow(fields)))
    keep_rows(moved_slab, moved, HALO + 1, KEPT, live)
    keep_rows(reds_slab, reds, HALO + 1, KEPT, live)
    keep_rows(fields_slab, fields, HALO + 2, KEPT, live)
    collide_rows(geometry, ByRow(fields), ByRow(whole), 3, ByRow(colours), walls, later)
    keep_rows(moved_later_slab, moved_later, HALO + 3, KEPT, live)
    keep_rows(reds_later_slab, reds_later, HALO + 3, KEPT, live)
    edges = slab_rows(live, HALO + RIM, RIM)
    rim = Block(geometry, [(row, row, RIM) for _, row in edges], True, [at for at, _ in edges])
    arrive_stage(rim, geometry, walls, later, ByRow(final_slab))

    def arrive_tile(tile, carry):
        row = tile * SUBLANES
        block = Block(geometry, [(row, row, SUBLANES)], inner=True)
        arrive_stage(block, geometry, walls, later, ByRow(final))
        return carry

    lax.fori_loop(1, jnp.minimum(SPLIT, live // SUBLANES - 1), arrive_tile, 0)


def second_kernel(info, moved, reds, earlier, arrived, pieces, final, walls):
    state = (ByRow(moved), ByRow(reds))
    geometry = Geometry(info, OWN_TILES)
    last = geometry.live // SUBLANES - 1
    fill_wall_table(walls, geometry)

    def pass_on(tile, carry):
        row = pl.multiple_of(tile * SUBLANES, SUBLANES)
        gather_tiles(earlier, row, pieces, row)
        return carry

    def finish(tile, carry):
        row = pl.multiple_of(tile * SUBLANES, SUBLANES)
        block = Block(geometry, [(row, row, SUBLANES)], inner=True)
        arrive_stage(block, geometry, walls, state, ByRow(final))
        gather_tiles(final, row, pieces, row)
        return carry

    lax.fori_loop(1, jnp.minimum(SPLIT, last), pass_on, 0)
    lax.fori_loop(SPLIT, last, finish, 0)


def scratch_of(shape):
    return pltpu.VMEM(shape.shape, shape.dtype)


def pieces_of(rows, flat_count):
    return pltpu.VMEM((FIELDS, rows, flat_count), jnp.float32)


def run_first(info, whole):
    rows = whole.shape[0]
    shapes = [by_row(rows, count) for count in (HELD, REDS, FIELDS)]
    slabs = [by_row(2 * SLAB, count) for count in (HELD, REDS, FIELDS, HELD, REDS, FIELDS)]
    scratch = [by_row(rows, 4), by_row(4, 3)]
    scratch = scratch + [by_row(rows, count) for count in (HELD, REDS, FIELDS)]
    return pl.pallas_call(
        first_kernel,
        out_shape=shapes + slabs,
        in_specs=[SMEM, VMEM],
        out_specs=[VMEM] * 9,
        scratch_shapes=[scratch_of(shape) for shape in scratch],
        compiler_params=pltpu.CompilerParams(vmem_limit_bytes=24 * 1024 * 1024),
        cost_estimate=pl.CostEstimate(flops=20_000_000, bytes_accessed=8_000_000, transcendentals=0),
        name="first",
    )(info, whole)


def run_second(info, state, earlier, arrived, arrays):
    row_count, flat_count = arrays[0].shape
    return pl.pallas_call(
        second_kernel,
        out_shape=jax.ShapeDtypeStruct((FIELDS, row_count, flat_count), jnp.float32),
        in_specs=[SMEM] + [VMEM] * 3 + [ANY],
        out_specs=VMEM,
        scratch_shapes=[scratch_of(by_row(row_count, FIELDS)), scratch_of(by_row(4, 3))],
        compiler_params=pltpu.CompilerParams(vmem_limit_bytes=16 * 1024 * 1024),
        cost_estimate=pl.CostEstimate(flops=20_000_000, bytes_accessed=8_000_000, transcendentals=0),
        name="second",
    )(info, *state, earlier, arrived)


def follow_kernel(ends, kept, out):
    out[pl.ds(PACKED * SUBLANES, 1), :] = jnp.zeros((1, LANES), jnp.float32)


def follow(ends, kept):
    return pl.pallas_call(
        follow_kernel,
        out_shape=jax.ShapeDtypeStruct(ends.shape, jnp.float32),
        in_specs=[VMEM, ANY],
        out_specs=VMEM,
        input_output_aliases={0: 0},
        compiler_params=pltpu.CompilerParams(vmem_limit_bytes=8 * 1024 * 1024),
        name="follow",
    )(pltpu.with_memory_space_constraint(ends, pltpu.VMEM), kept)


def outer_kernel(info, whole, arrived, passed, inner_pieces, *refs):
    outs = refs[6:10]
    moved, reds, fields, moved_later, reds_later, final = refs[10:16]
    start_fields, colours, walls, pieces, zeros, sems = refs[16:]
    row_tiles = inner_pieces.shape[1] // SUBLANES
    state, later = (ByRow(moved), ByRow(reds)), (ByRow(moved_later), ByRow(reds_later))
    geometry = Geometry(info, OWN_TILES)
    live = geometry.live
    low_part = info[3] == 0

    def for_tiles(operation):
        for tile in range(1, row_tiles):
            row = tile * SUBLANES
            inner = tile_copies(inner_pieces, outs, row, row, sems.at[tile])
            dead = tile_copies(zeros, outs, 0, row, sems.at[tile])

            @pl.when(row + SUBLANES < live)
            def _():
                for copy in inner:
                    operation(copy)

            @pl.when(row >= live)
            def _():
                for copy in dead:
                    operation(copy)

    zeros[...] = jnp.zeros(zeros.shape, zeros.dtype)
    for_tiles(lambda copy: copy.start())
    fill_wall_table(walls, geometry)

    def ends_of(ref, half):
        blocks = []
        for group in range(FULL * PLANES // GROUP):
            first = half * (PACKED + 1) + group * (GROUP - 1)
            packed = [ref[pl.ds((first + k) * SUBLANES, SUBLANES), :] for k in range(GROUP - 1)]
            blocks = blocks + unpack_blocks(packed)
        last = half * (PACKED + 1) + PACKED
        return blocks + [ref[pl.ds(last * SUBLANES, SUBLANES), :]]

    tiles = block_tiles()
    middle = (tiles >= 1) & (tiles <= OWN_TILES)

    def widened(own, other):
        beside = jnp.where(tiles == 0, roll_tiles(other, -OWN_TILES), roll_tiles(other, OWN_TILES))
        return jnp.where(geometry.domain, jnp.where(middle, own, beside), 0.0)

    straight = [widened(*pair) for pair in zip(ends_of(arrived, 0), ends_of(arrived, 1))]
    crossed = [widened(*pair) for pair in zip(ends_of(passed, 1), ends_of(passed, 0))]
    below = [jnp.where(low_part, *pair) for pair in zip(straight, crossed)]
    above = [jnp.where(low_part, *pair) for pair in zip(crossed, straight)]

    for number in range(FULL * PLANES):
        place, extra = divmod(number, FULL)
        index = ORDER[place]
        write_row(ByRow(start_fields), index, 1 + extra, below[number])
        write_row(ByRow(start_fields), index, 2 * SLAB - HALO + extra, above[number])
    for row, colour in ((0, below[-1]), (2 * SLAB - 1, above[-1])):
        write_row(ByRow(start_fields), 0, row, jnp.zeros((SUBLANES, LANES), jnp.float32))
        write_row(ByRow(start_fields), 10, row, 0.5 * colour)
    for slab_row, row in slab_rows(live, HALO, FULL):
        for extra in range(FULL):
            start_fields[slab_row + extra] = whole[row + extra]

    def block(first, count):
        return Block(geometry, [(row, at, count) for at, row in slab_rows(live, first, count)])

    held, solids, marks = ByRow(fields), ByRow(start_fields), ByRow(colours)
    colour_stage(block(0, 6), geometry, solids, marks)
    collide_stage(block(1, 4), geometry, solids, solids, marks, walls, state)
    arrive_stage(block(2, 4), geometry, walls, state, held)
    colour_stage(block(2, 6), geometry, held, marks)
    collide_stage(block(3, 4), geometry, held, solids, marks, walls, later)
    arrive_stage(block(4, 4), geometry, walls, later, ByRow(final))

    copies = []
    for side, row, out_row in ((0, HALO, 0), (1, SLAB, live - SUBLANES)):
        gather_tiles(final, row, pieces, side * SUBLANES)
        out_row = pl.multiple_of(out_row, SUBLANES)
        copies = copies + tile_copies(pieces, outs, side * SUBLANES, out_row, sems.at[row_tiles + side])
    for copy in copies:
        copy.start()
    for copy in copies:
        copy.wait()
    for_tiles(lambda copy: copy.wait())


def run_outer(info, whole, arrived, passed, inner_pieces, slabs, arrays):
    row_count, flat_count = arrays[0].shape
    shapes = [jax.ShapeDtypeStruct(array.shape, jnp.float32) for array in (*arrays[:4], *slabs)]
    slabs = [pltpu.with_memory_space_constraint(slab, pltpu.VMEM) for slab in slabs]
    return pl.pallas_call(
        outer_kernel,
        out_shape=shapes,
        in_specs=[SMEM] + [VMEM] * 10,
        out_specs=[ANY] * 4 + [VMEM] * 6,
        scratch_shapes=[
            scratch_of(by_row(2 * SLAB, PLACES)),
            scratch_of(by_row(2 * SLAB, 4)),
            scratch_of(by_row(4, 3)),
            pieces_of(2 * SUBLANES, flat_count),
            pieces_of(SUBLANES, flat_count),
            pltpu.SemaphoreType.DMA((row_count // SUBLANES + 2, 4)),
        ],
        input_output_aliases={5 + number: 4 + number for number in range(6)},
        compiler_params=pltpu.CompilerParams(vmem_limit_bytes=24 * 1024 * 1024),
        name="outer",
    )(info, whole, arrived, passed, inner_pieces, *slabs)


def body(density, momentum, stress, red_density, solid, widths):
    tiles_count = lax.axis_size("tiles")
    arrays = (density, momentum, stress, red_density, solid)
    info, raw, raw_solid, packet, mine = load_inputs(arrays, widths, tiles_count)
    info = pltpu.with_memory_space_constraint(info, pltpu.SMEM)
    swap = [(0, 1), (1, 0)]
    packet = lax.ppermute(packet, "sub", swap)
    spread = spread_rows(raw, raw_solid)
    ends = join_ends(mine, packet, spread)
    route = [(2 * k, 2 * k + 2) for k in range(tiles_count - 1)]
    route = route + [(2 * k + 3, 2 * k + 1) for k in range(tiles_count - 1)]
    arrived = lax.ppermute(ends, ("tiles", "sub"), route)
    whole = put_beside(info, spread, packet)
    moved, reds, earlier, *slabs = run_first(info, whole)
    arrived = follow(arrived, slabs[-1])
    passed = lax.ppermute(arrived, "sub", swap)
    pieces = run_second(info, (moved, reds), earlier, arrived, arrays)
    return tuple(run_outer(info, whole, arrived, passed, pieces, slabs, arrays)[:4])


def solution(mesh):
    in_specs = (
        P(("groups", "tiles"), "sub"),
        P(None, ("groups", "tiles"), "sub"),
        P(None, ("groups", "tiles"), "sub"),
        P(("groups", "tiles"), "sub"),
        P(("groups", "tiles"), "sub"),
        P("groups"),
    )
    out_specs = (
        P(("groups", "tiles"), "sub"),
        P(None, ("groups", "tiles"), "sub"),
        P(None, ("groups", "tiles"), "sub"),
        P(("groups", "tiles"), "sub"),
    )
    return jax.shard_map(body, mesh=mesh, in_specs=in_specs, out_specs=out_specs, check_vma=False)
```

```python
import functools

import jax
import jax.numpy as jnp
from jax import lax
from jax.experimental import pallas as pl
from jax.experimental.pallas import tpu as pltpu
from jax.sharding import PartitionSpec as P

TILE = 16
STEPS = 2
RELAX_TIME = 0.8
SURFACE = 0.1
SEPARATION = 0.7

LANES = 128
SUBLANES = 8
FULL = 3
HALO = FULL + 1
FIELDS = 11
PLANES = FIELDS + 1
MOVED = 19
REDS = 5
HELD = MOVED + 1
RIM = 4
SLAB = HALO + 2 * RIM
OWN_TILES = SUBLANES - 2
GROUP = 4
PACKED = FULL * PLANES // GROUP * (GROUP - 1)
END_ROWS = (PACKED + 1) * SUBLANES
HALF = LANES // 2
ORDER = (0, 1, 2, 3, 10, 11, 4, 5, 6, 7, 8, 9)
PAIRS = PLANES // 2
PLACES = PLANES + 1
SPLIT = 3
KEPT = 2
COLOUR_BLOCK = (8, 1)
COLLIDE_BLOCK = (1, 8)
ARRIVE_BLOCK = (2, 4)
VMEM = pl.BlockSpec(memory_space=pltpu.VMEM)
SMEM = pl.BlockSpec(memory_space=pltpu.SMEM)
ANY = pl.BlockSpec(memory_space=pl.ANY)
HBM = pl.BlockSpec(memory_space=pltpu.HBM)


class Rows:
    def __init__(self, parts):
        self.parts = parts

    def _with(self, other, operation):
        others = other.parts if isinstance(other, Rows) else [other] * len(self.parts)
        return Rows([operation(one, two) for one, two in zip(self.parts, others)])

    def __add__(self, other):
        return self._with(other, lambda one, two: one + two)

    def __sub__(self, other):
        return self._with(other, lambda one, two: one - two)

    def __rsub__(self, other):
        return self._with(other, lambda one, two: two - one)

    def __mul__(self, other):
        return self._with(other, lambda one, two: one * two)

    def __or__(self, other):
        return self._with(other, lambda one, two: one | two)

    def __eq__(self, other):
        return self._with(other, lambda one, two: one == two)

    __radd__, __rmul__, __ror__ = __add__, __mul__, __or__

    def each(self, operation):
        return Rows([operation(part) for part in self.parts])


def select(mask, yes, no):
    count = max(len(item.parts) for item in (mask, yes, no) if isinstance(item, Rows))
    columns = [
        item.parts if isinstance(item, Rows) else [item] * count for item in (mask, yes, no)
    ]
    return Rows([jnp.where(*row) for row in zip(*columns)])


def roll_lanes(values, amount):
    return values.each(lambda part: pltpu.roll(part, amount % LANES, 1))


def roll_sublanes(values, amount):
    return values.each(lambda part: pltpu.roll(part, amount % SUBLANES, 0))


class Geometry:
    def __init__(self, info, own_tiles):
        live, first, last, sub_index = info[0], info[1], info[2], info[3]
        self.live = live
        self.low_row = jnp.where(first == 1, 0, -1000)
        self.high_row = jnp.where(last == 1, live, 1000)
        shape = (SUBLANES, LANES)
        lane = lax.broadcasted_iota(jnp.int32, shape, 1)
        tile = lax.broadcasted_iota(jnp.int32, shape, 0)
        depth = lane & (TILE - 1)
        low_part = sub_index == 0
        high_part = sub_index == 1
        z_walls = {1: depth == 0, -1: depth == TILE - 1}
        y_walls = {
            1: (tile == 1) & (lane < TILE) & low_part,
            -1: (tile == own_tiles) & (lane >= LANES - TILE) & high_part,
        }
        self.walls = {(0, vel_z): wall for vel_z, wall in z_walls.items()}
        for vel_y, y_wall in y_walls.items():
            self.walls[vel_y, 0] = y_wall
            for vel_z, z_wall in z_walls.items():
                self.walls[vel_y, vel_z] = y_wall | z_wall
        own = (tile >= 1) & (tile <= own_tiles)
        self.domain = own | ((tile == own_tiles + 1) & low_part) | ((tile == 0) & high_part)
        self.first_lanes = lane < TILE
        self.last_lanes = lane >= LANES - TILE

    def from_low_y(self, values):
        return roll_lanes(select(self.last_lanes, roll_sublanes(values, 1), values), TILE)

    def from_high_y(self, values):
        return roll_lanes(select(self.first_lanes, roll_sublanes(values, -1), values), -TILE)

    def from_low_z(self, values):
        return select(self.walls[0, 1], 0.0, roll_lanes(values, 1))

    def from_high_z(self, values):
        return select(self.walls[0, -1], 0.0, roll_lanes(values, -1))


def flat_rows(row, count, tile_offset=0):
    start = row * SUBLANES
    if not isinstance(start, int):
        start = pl.multiple_of(start, SUBLANES)
    return pl.ds(start + tile_offset, count * SUBLANES)


class ByRow:
    def __init__(self, ref):
        self.ref = ref


def by_row(rows, count):
    return jax.ShapeDtypeStruct((rows, count * SUBLANES, LANES), jnp.float32)


def place_of(ref, index, row, tile_offset=0):
    if isinstance(ref, ByRow):
        return ref.ref, row, pl.ds(index * SUBLANES + tile_offset, SUBLANES)
    return ref, index, flat_rows(row, 1, tile_offset)


def read_row(ref, index, row, tile_offset=0):
    ref, first, second = place_of(ref, index, row, tile_offset)
    return ref[first, second, :]


def write_row(ref, index, row, values):
    ref, first, second = place_of(ref, index, row)
    ref[first, second, :] = values


class Block:
    def __init__(self, geometry, spans, inner=False, store_rows=None):
        self.spans = spans
        self.store_rows = store_rows or [local for row, local, count in spans]
        rows = [row + extra for row, local, count in spans for extra in range(count)]
        self.inner = inner
        rows = [row + extra for row, local, count in spans for extra in range(count)]
        if inner:
            self.x_walls = {}
            self.valid = geometry.domain
            self.kinds = [0]
            return
        ids = Rows([row + jnp.zeros((SUBLANES, LANES), jnp.int32) for row in rows])
        self.x_walls = {1: ids == geometry.low_row, -1: ids == geometry.high_row - 1}
        self.valid = ids.each(
            lambda part: geometry.domain & (part >= geometry.low_row) & (part < geometry.high_row)
        )
        self.kinds = [
            jnp.where(row == geometry.low_row, 1, 0) + jnp.where(row == geometry.high_row - 1, 2, 0)
            for row in rows
        ]

    def load(self, ref, index, offset=0, tile_offset=0):
        return Rows([
            read_row(ref, index, local + offset + extra, tile_offset)
            for row, local, count in self.spans
            for extra in range(count)
        ])

    def store(self, ref, index, values):
        targets = [
            target + extra
            for (row, local, count), target in zip(self.spans, self.store_rows)
            for extra in range(count)
        ]
        for target, part in zip(targets, values.parts):
            write_row(ref, index, target, part)

    def wall_terms(self, walls, position):
        terms = [walls[position, flat_rows(kind, 1), :] for kind in self.kinds]
        return terms[0] if self.inner else Rows(terms)


def fill_wall_table(walls, geometry):
    one = jnp.ones((SUBLANES, LANES), jnp.float32)
    up_y, down_y, up_z, down_z = [
        jnp.where(geometry.walls[key], 0.0, one) for key in ((-1, 0), (1, 0), (0, -1), (0, 1))
    ]
    sum_y, sum_z = up_y + down_y, up_z + down_z
    for kind, (up_x, down_x) in enumerate(((1.0, 1.0), (1.0, 0.0), (0.0, 1.0))):
        sum_x = up_x + down_x
        around_x = 2.0 + sum_y + sum_z
        total = 12.0 + 2.0 * (sum_x + sum_y + sum_z) + sum_x * (sum_y + sum_z) + sum_y * sum_z
        rows = (
            (up_x - down_x) * around_x,
            (up_y - down_y) * (2.0 + sum_x + sum_z),
            (up_z - down_z) * (2.0 + sum_x + sum_y),
            36.0 - total,
        )
        for position, row in enumerate(rows):
            walls[position, flat_rows(kind, 1), :] = row


VELOCITIES = tuple(
    tuple(sign if axis == place else 0 for place in range(3)) for axis in range(3) for sign in (1, -1)
) + tuple(
    tuple({a: one, b: two}.get(place, 0) for place in range(3))
    for a, b in ((0, 1), (0, 2), (1, 2))
    for one, two in ((1, 1), (-1, -1), (1, -1), (-1, 1))
)
VELOCITIES = ((0, 0, 0),) + VELOCITIES


def colour_stage(block, geometry, fields, colours):
    density = block.load(fields, 0)
    red = block.load(fields, 10)
    colour = select(block.valid, 2.0 * red - density, 0.0)
    along_y = geometry.from_low_y(colour) + geometry.from_high_y(colour)
    along_z = geometry.from_low_z(colour) + geometry.from_high_z(colour)
    block.store(colours, 0, colour)
    block.store(colours, 1, 2.0 * colour + (along_y + along_z))
    block.store(colours, 2, along_y)
    block.store(colours, 3, along_z)


def collide_stage(block, geometry, fields, solids, colours, walls, state):
    relaxing = 1.0 - 1.0 / RELAX_TIME
    third = 1.0 / 3.0
    colour = block.load(colours, 0)
    doubled = 2.0 * colour + (block.load(colours, 0, -1) + block.load(colours, 0, 1))
    term_y = doubled + block.load(colours, 3)
    term_z = doubled + block.load(colours, 2)
    grad_x = block.load(colours, 1, 1) - block.load(colours, 1, -1)
    grad_y = geometry.from_high_y(term_y) - geometry.from_low_y(term_y)
    grad_z = geometry.from_high_z(term_z) - geometry.from_low_z(term_z)
    if not block.inner:
        grad_x = grad_x - block.wall_terms(walls, 0) * colour
    grad_y = grad_y - block.wall_terms(walls, 1) * colour
    grad_z = grad_z - block.wall_terms(walls, 2) * colour

    fluid = block.load(solids, PLANES - 1) == 0.0
    density = block.load(fields, 0)
    red = block.load(fields, 10)
    flux = [block.load(fields, 1 + axis) for axis in range(3)]
    stress = [block.load(fields, 4 + part) for part in range(6)]
    square_xx, square_yy, square_zz = grad_x * grad_x, grad_y * grad_y, grad_z * grad_z
    square = square_xx + square_yy + square_zz
    inverse = select(fluid, (1.0 + square * (1.0 / 144.0)).each(lax.rsqrt), 0.0)
    trace = third * square
    strength = (SURFACE / (8.0 * 144.0)) * inverse
    keep = select(fluid, relaxing / 8.0, 1.0 / 8.0)
    eighths = [0.125 * part for part in flux]
    own = [
        eighths[axis] * flux[axis] + (keep * stress[axis] + strength * (squared - trace))
        for axis, squared in enumerate((square_xx, square_yy, square_zz))
    ]
    strength, keep = 2.0 * strength, 2.0 * keep
    quarters = [2.0 * part for part in eighths[:2]]
    grads = (grad_x, grad_y, grad_z)
    cross = [
        quarters[a] * flux[b] + (keep * stress[3 + plane] + strength * (grads[a] * grads[b]))
        for plane, (a, b) in enumerate(((0, 1), (0, 2), (1, 2)))
    ]
    base = density * (1.0 / 36.0) - third * (own[0] + own[1] + own[2])
    sign = select(fluid, 1.0 / 12.0, -1.0 / 12.0)
    run = [sign * part for part in flux]
    mixing = ((SEPARATION / 144.0) * red) * ((density - red) * inverse)
    red_run = [0.5 * part + mixing * grad for part, grad in zip(run, grads)]
    moved, reds = state
    block.store(moved, 0, 12.0 * base)
    straight = [base + part for part in own]
    for axis in range(3):
        middle = 2.0 * straight[axis]
        swing = 2.0 * run[axis]
        block.store(moved, 1 + 2 * axis, middle + swing)
        block.store(moved, 2 + 2 * axis, middle - swing)
    for plane, (a, b) in enumerate(((0, 1), (0, 2), (1, 2))):
        middle = straight[a] + own[b]
        same, other = middle + cross[plane], middle - cross[plane]
        along, against = run[a] + run[b], run[a] - run[b]
        first = 7 + 4 * plane
        block.store(moved, first, same + along)
        block.store(moved, first + 1, same - along)
        block.store(moved, first + 2, other + against)
        block.store(moved, first + 3, other - against)

    red_base = select(block.valid, red * (1.0 / 36.0), 0.0)
    red_run = [select(block.valid, part, 0.0) for part in red_run]
    block.store(reds, 0, red_base)
    block.store(reds, 1, red_base + red_run[0])
    block.store(reds, 2, red_base - red_run[0])
    block.store(reds, 3, red_run[1])
    block.store(reds, 4, red_run[2])


def arrive_stage(block, geometry, walls, state, fields):
    third = 1.0 / 3.0
    moved, reds = state
    own = [None] * MOVED

    def here(direction):
        if own[direction] is None:
            own[direction] = block.load(moved, direction)
        return own[direction]

    def arrived(direction, opposite):
        vel_x, vel_y, vel_z = VELOCITIES[direction]
        values = here(direction) if vel_x == 0 else block.load(moved, direction, -vel_x)
        if vel_y != 0:
            beside = block.load(moved, direction, -vel_x, -vel_y)
            leaving = geometry.last_lanes if vel_y == 1 else geometry.first_lanes
            values = select(leaving, beside, values)
        if vel_y != 0 or vel_z != 0:
            values = roll_lanes(values, TILE * vel_y + vel_z)
        masks = []
        if vel_x in block.x_walls:
            masks.append(block.x_walls[vel_x])
        if (vel_y, vel_z) in geometry.walls:
            masks.append(geometry.walls[vel_y, vel_z])
        if not masks:
            return values
        wall = functools.reduce(lambda one, two: one | two, masks)
        return select(wall, here(opposite), values)

    red = block.load(reds, 0)
    red_y = block.load(reds, 3)
    red_z = block.load(reds, 4)
    from_x = block.load(reds, 1, -1) + block.load(reds, 2, 1)
    spread = 2.0 * red + from_x
    spread_y = 2.0 * red_y + (block.load(reds, 3, -1) + block.load(reds, 3, 1))
    spread_z = 2.0 * red_z + (block.load(reds, 4, -1) + block.load(reds, 4, 1))
    up_y, down_y = red + red_y, red - red_y
    low_y = (
        (spread + spread_y)
        + geometry.from_low_z(up_y + red_z)
        + geometry.from_high_z(up_y - red_z)
    )
    high_y = (
        (spread - spread_y)
        + geometry.from_low_z(down_y + red_z)
        + geometry.from_high_z(down_y - red_z)
    )
    bounced = (
        block.wall_terms(walls, 3) * red
        - block.wall_terms(walls, 1) * red_y
        - block.wall_terms(walls, 2) * red_z
    )
    if not block.inner:
        bounced = bounced - block.wall_terms(walls, 0) * (block.load(reds, 1) - red)
    red_total = (
        12.0 * red
        + 2.0 * from_x
        + geometry.from_low_z(spread + spread_z)
        + geometry.from_high_z(spread - spread_z)
        + geometry.from_low_y(low_y)
        + geometry.from_high_y(high_y)
        + bounced
    )
    rest = here(0)
    sums, diffs = [], []
    for axis in range(3):
        up = arrived(1 + 2 * axis, 2 + 2 * axis)
        down = arrived(2 + 2 * axis, 1 + 2 * axis)
        sums.append(up + down)
        diffs.append(up - down)
    total = rest + sums[0] + sums[1] + sums[2]
    cross = []
    for plane, (a, b) in enumerate(((0, 1), (0, 2), (1, 2))):
        first = 7 + 4 * plane
        parts = [arrived(first + offset, first + (offset ^ 1)) for offset in range(4)]
        same, other = parts[0] + parts[1], parts[2] + parts[3]
        along, against = parts[0] - parts[1], parts[2] - parts[3]
        both = same + other
        cross.append(same - other)
        total = total + both
        sums[a], sums[b] = sums[a] + both, sums[b] + both
        diffs[a], diffs[b] = diffs[a] + (along + against), diffs[b] + (along - against)
    shared = third * total
    block.store(fields, 0, total)
    for axis in range(3):
        block.store(fields, 1 + axis, diffs[axis])
        block.store(fields, 4 + axis, sums[axis] - shared - diffs[axis] * diffs[axis])
    for plane, (a, b) in enumerate(((0, 1), (0, 2), (1, 2))):
        block.store(fields, 7 + plane, cross[plane] - diffs[a] * diffs[b])
    block.store(fields, 10, red_total)


def over_rows(geometry, first, size, blocks, stage):
    trip = size * blocks
    rest = -2 * first % trip
    assert TILE % trip == 0 and rest % min(size, rest or size) == 0

    def run(start, count, step_size):
        for offset in range(0, count, step_size):
            row = start + offset
            stage(Block(geometry, [(row, row, step_size)], inner=True))

    def step(index, carry):
        run(first + index * trip, trip, size)
        return carry

    trips = (geometry.live - 2 * first - rest) // trip
    lax.fori_loop(0, trips, step, 0)
    if rest:
        run(geometry.live - first - rest, rest, min(size, rest))


def block_tiles():
    return lax.broadcasted_iota(jnp.int32, (SUBLANES, LANES), 0)


def roll_tiles(block, amount):
    return pltpu.roll(block, amount % SUBLANES, 0)


def pack_blocks(blocks):
    tiles, rest = block_tiles(), blocks[GROUP - 1]
    packed = []
    for number, block in enumerate(blocks[: GROUP - 1]):
        low, high = 2 * number + 1, 2 * number + 2
        block = jnp.where(tiles == 0, roll_tiles(rest, -low), block)
        packed.append(jnp.where(tiles == SUBLANES - 1, roll_tiles(rest, SUBLANES - 1 - high), block))
    return packed


def unpack_blocks(packed):
    tiles, rest = block_tiles(), None
    for number, block in enumerate(packed):
        low, high = 2 * number + 1, 2 * number + 2
        part = jnp.where(tiles == low, roll_tiles(block, low), roll_tiles(block, high - SUBLANES + 1))
        rest = part if rest is None else jnp.where(tiles >= low, part, rest)
    return list(packed) + [rest]


def flat_view(ref):
    rows, width, lanes = ref.shape
    return ref.reshape(rows * width, lanes)


def spread_tile(raw, raw_solid, index, row, target, target_row):
    source = raw_solid if index == FIELDS else raw.at[index]
    width = target.shape[1]
    for tile in range(OWN_TILES):
        values = source[pl.ds(row, SUBLANES), pl.ds(tile * LANES, LANES)].astype(jnp.float32)
        start = target_row * width + index * SUBLANES + 1 + tile
        flat_view(target)[pl.ds(start, SUBLANES, stride=width), :] = values


def load_kernel(
    tiles_count, density, momentum, stress, red, solid, widths,
    info, raw, raw_solid, packet, mine,
    first_tile, last_tile, held_widths, sems,
):
    row_count, flat_count = raw_solid.shape
    own_tiles = flat_count // LANES
    copies = [
        pltpu.make_async_copy(widths, held_widths, sems.at[0]),
        pltpu.make_async_copy(density, raw.at[0], sems.at[1]),
        pltpu.make_async_copy(momentum, raw.at[pl.ds(1, 3)], sems.at[2]),
        pltpu.make_async_copy(red, raw.at[10], sems.at[3]),
        pltpu.make_async_copy(solid, raw_solid, sems.at[4]),
        pltpu.make_async_copy(stress.at[pl.ds(0, 3)], raw.at[pl.ds(4, 3)], sems.at[5]),
        pltpu.make_async_copy(stress.at[pl.ds(3, 3)], raw.at[pl.ds(7, 3)], sems.at[6]),
    ]
    for copy in copies:
        copy.start()
    tiles_index, sub_index = lax.axis_index("tiles"), lax.axis_index("sub")
    low_part = sub_index == 0
    edge_start = pl.multiple_of(jnp.where(low_part, (own_tiles - 1) * LANES, 0), LANES)

    copies[0].wait()
    live = held_widths[tiles_index] * TILE
    info[0] = live
    info[1] = (tiles_index == 0).astype(jnp.int32)
    info[2] = (tiles_index == tiles_count - 1).astype(jnp.int32)
    info[3] = sub_index

    near_cut = lax.broadcasted_iota(jnp.int32, (SUBLANES, LANES), 1) < HALF
    near_cut = near_cut == jnp.logical_not(low_part)
    near_last = pl.multiple_of(live - SUBLANES, SUBLANES)
    edges = pl.ds(edge_start, LANES)

    def plane_of(index):
        return raw_solid if index == FIELDS else raw.at[index]

    def pack_edges(pair):
        here, there = [plane_of(index) for index in ORDER[2 * pair : 2 * pair + 2]]
        for row in range(0, row_count, SUBLANES):
            rows = pl.ds(row, SUBLANES)
            beside = pltpu.roll(there[rows, edges].astype(jnp.float32), HALF, 1)
            both = jnp.where(near_cut, here[rows, edges].astype(jnp.float32), beside)
            packet[pl.ds(END_ROWS + pair * row_count + row, SUBLANES), :] = both

    targets = ((packet, jnp.logical_not(low_part)), (mine, low_part))

    def row_of(use_last, index, number_first, number_last):
        first = read_row(ByRow(first_tile), index, number_first)
        last = read_row(ByRow(last_tile), index, number_last)
        return jnp.where(use_last, last, first)

    def pack_ends(group):
        for target, use_last in targets:
            blocks = []
            for number in range(group * GROUP, (group + 1) * GROUP):
                place, extra = divmod(number, FULL)
                blocks.append(row_of(use_last, ORDER[place], extra, SUBLANES - FULL + extra))
            for number, block in enumerate(pack_blocks(blocks)):
                place = (group * (GROUP - 1) + number) * SUBLANES
                target[pl.ds(place, SUBLANES), :] = block

    place = 0
    for copy, count in zip(copies[1:], (1, 3, 1, 1, 3, 3)):
        copy.wait()
        before, place = place, place + count
        for index in ORDER[before:place]:
            for target, row in ((first_tile, 0), (last_tile, near_last)):
                spread_tile(raw, raw_solid, index, row, target, 0)
        for pair in range(before // 2, place // 2):
            pack_edges(pair)
        for group in range(before * FULL // GROUP, place * FULL // GROUP):
            pack_ends(group)
    for target, use_last in targets:
        red_row, density_row = [
            row_of(use_last, index, FULL, SUBLANES - HALO) for index in (10, 0)
        ]
        target[pl.ds(PACKED * SUBLANES, SUBLANES), :] = 2.0 * red_row - density_row


def load_inputs(arrays, widths, tiles_count):
    row_count, flat_count = arrays[0].shape
    return pl.pallas_call(
        functools.partial(load_kernel, tiles_count),
        out_shape=[
            pltpu.SMEM((4,), jnp.int32),
            jax.ShapeDtypeStruct((FIELDS, row_count, flat_count), jnp.float32),
            jax.ShapeDtypeStruct((row_count, flat_count), jnp.int32),
            jax.ShapeDtypeStruct((END_ROWS + PAIRS * row_count, LANES), jnp.float32),
            jax.ShapeDtypeStruct((END_ROWS, LANES), jnp.float32),
        ],
        in_specs=[HBM] * 6,
        out_specs=[SMEM] + [VMEM] * 4,
        scratch_shapes=[
            pltpu.VMEM((SUBLANES, PLACES * SUBLANES, LANES), jnp.float32),
            pltpu.VMEM((SUBLANES, PLACES * SUBLANES, LANES), jnp.float32),
            pltpu.SMEM(widths.shape, jnp.int32),
            pltpu.SemaphoreType.DMA((7,)),
        ],
        compiler_params=pltpu.CompilerParams(vmem_limit_bytes=16 * 1024 * 1024),
        name="load",
    )(*[pltpu.with_memory_space_constraint(array, pltpu.HBM) for array in (*arrays, widths)])


def spread_kernel(raw, raw_solid, spread):
    for index in range(PLANES):
        for row in range(0, raw_solid.shape[0], SUBLANES):
            spread_tile(raw, raw_solid, index, row, spread, row)


def spread_rows(raw, raw_solid):
    row_count = raw_solid.shape[0]
    return pl.pallas_call(
        spread_kernel,
        out_shape=by_row(row_count, PLACES),
        in_specs=[VMEM, VMEM],
        out_specs=VMEM,
        compiler_params=pltpu.CompilerParams(vmem_limit_bytes=16 * 1024 * 1024),
        cost_estimate=pl.CostEstimate(flops=1_000_000, bytes_accessed=4_000_000, transcendentals=0),
        name="spread",
    )(raw, raw_solid)


def join_kernel(mine, packet, spread, ends):
    ends[pl.ds(0, END_ROWS), :] = mine[...]
    ends[pl.ds(END_ROWS, END_ROWS), :] = packet[pl.ds(0, END_ROWS), :]


def join_ends(mine, packet, spread):
    return pl.pallas_call(
        join_kernel,
        out_shape=jax.ShapeDtypeStruct((2 * END_ROWS, LANES), jnp.float32),
        in_specs=[VMEM, VMEM, ANY],
        out_specs=VMEM,
        compiler_params=pltpu.CompilerParams(vmem_limit_bytes=8 * 1024 * 1024),
        name="join",
    )(mine, packet, spread)


def beside_kernel(info, spread, packet, whole):
    low_part = info[3] == 0
    row_count, width = spread.shape[:2]
    flat = flat_view(whole)
    for pair in range(PAIRS):
        for row in range(0, row_count, SUBLANES):
            both = packet[pl.ds(END_ROWS + pair * row_count + row, SUBLANES), :]
            for place, values in ((2 * pair, both), (2 * pair + 1, pltpu.roll(both, HALF, 1))):
                index = ORDER[place]
                start = row * width + index * SUBLANES
                below = jnp.where(low_part, 0.0, values)
                above = jnp.where(low_part, values, 0.0)
                flat[pl.ds(start, SUBLANES, stride=width), :] = below
                flat[pl.ds(start + SUBLANES - 1, SUBLANES, stride=width), :] = above


def put_beside(info, spread, packet):
    return pl.pallas_call(
        beside_kernel,
        out_shape=jax.ShapeDtypeStruct(spread.shape, jnp.float32),
        in_specs=[SMEM, VMEM, VMEM],
        out_specs=VMEM,
        input_output_aliases={1: 0},
        compiler_params=pltpu.CompilerParams(vmem_limit_bytes=16 * 1024 * 1024),
        name="beside",
    )(info, pltpu.with_memory_space_constraint(spread, pltpu.VMEM), packet)


def keep_rows(slab, source, first, size, live):
    for slab_row, row in slab_rows(live, first, size):
        for extra in range(size):
            slab[slab_row + extra] = source[row + extra]


def slab_rows(live, first, size):
    mirrored = SLAB - first - size
    return [(first, first - HALO), (SLAB + mirrored, live - 2 * RIM + mirrored)]


def collide_rows(geometry, before, whole, first, colours, walls, state):
    over_rows(geometry, first - 1, *COLOUR_BLOCK, lambda block: colour_stage(
        block, geometry, before, colours))
    over_rows(geometry, first, *COLLIDE_BLOCK, lambda block: collide_stage(
        block, geometry, before, whole, colours, walls, state))


def split_fields(pieces):
    return pieces.at[0], pieces.at[pl.ds(1, 3)], pieces.at[pl.ds(4, 6)], pieces.at[10]


def tile_copies(pieces, outs, held_row, out_row, sems):
    held, rows = pl.ds(held_row, SUBLANES), pl.ds(out_row, SUBLANES)
    parts = (
        (pieces.at[0, held], outs[0].at[rows]),
        (pieces.at[pl.ds(1, 3), held], outs[1].at[:, rows]),
        (pieces.at[pl.ds(4, 6), held], outs[2].at[:, rows]),
        (pieces.at[10, held], outs[3].at[rows]),
    )
    return [
        pltpu.make_async_copy(source, target, sems.at[number])
        for number, (source, target) in enumerate(parts)
    ]


def gather_tiles(final, row, pieces, held_row):
    width = final.shape[1]
    start = row * width
    if not isinstance(start, int):
        start = pl.multiple_of(start, SUBLANES)
    for index in range(FIELDS):
        for tile in range(OWN_TILES):
            place = start + index * SUBLANES + 1 + tile
            pieces[index, pl.ds(held_row, SUBLANES), pl.ds(tile * LANES, LANES)] = flat_view(final)[
                pl.ds(place, SUBLANES, stride=width), :
            ]


def first_kernel(
    info, whole, moved_later, reds_later, final,
    moved_slab, reds_slab, fields_slab, moved_later_slab, reds_later_slab, final_slab,
    colours, walls, moved, reds, fields,
):
    state, later = (ByRow(moved), ByRow(reds)), (ByRow(moved_later), ByRow(reds_later))
    geometry = Geometry(info, OWN_TILES)
    live = geometry.live
    fill_wall_table(walls, geometry)
    collide_rows(geometry, ByRow(whole), ByRow(whole), 1, ByRow(colours), walls, state)
    over_rows(geometry, 2, *ARRIVE_BLOCK, lambda block: arrive_stage(
        block, geometry, walls, state, ByRow(fields)))
    keep_rows(moved_slab, moved, HALO + 1, KEPT, live)
    keep_rows(reds_slab, reds, HALO + 1, KEPT, live)
    keep_rows(fields_slab, fields, HALO + 2, KEPT, live)
    collide_rows(geometry, ByRow(fields), ByRow(whole), 3, ByRow(colours), walls, later)
    keep_rows(moved_later_slab, moved_later, HALO + 3, KEPT, live)
    keep_rows(reds_later_slab, reds_later, HALO + 3, KEPT, live)
    edges = slab_rows(live, HALO + RIM, RIM)
    rim = Block(geometry, [(row, row, RIM) for _, row in edges], True, [at for at, _ in edges])
    arrive_stage(rim, geometry, walls, later, ByRow(final_slab))

    def arrive_one(tile, carry):
        arrive_tile(geometry, walls, later, final, tile)
        return carry

    lax.fori_loop(1, jnp.minimum(SPLIT, live // SUBLANES - 1), arrive_one, 0)


def arrive_tile(geometry, walls, state, final, tile):
    size = ARRIVE_BLOCK[0]
    for offset in range(0, SUBLANES, size):
        row = tile * SUBLANES + offset
        block = Block(geometry, [(row, row, size)], inner=True)
        arrive_stage(block, geometry, walls, state, ByRow(final))


def second_kernel(info, moved, reds, earlier, arrived, pieces, final, walls):
    state = (ByRow(moved), ByRow(reds))
    geometry = Geometry(info, OWN_TILES)
    last = geometry.live // SUBLANES - 1
    fill_wall_table(walls, geometry)

    def pass_on(tile, carry):
        row = pl.multiple_of(tile * SUBLANES, SUBLANES)
        gather_tiles(earlier, row, pieces, row)
        return carry

    def finish(tile, carry):
        row = pl.multiple_of(tile * SUBLANES, SUBLANES)
        arrive_tile(geometry, walls, state, final, tile)
        gather_tiles(final, row, pieces, row)
        return carry

    lax.fori_loop(1, jnp.minimum(SPLIT, last), pass_on, 0)
    lax.fori_loop(SPLIT, last, finish, 0)
    for row in range(0, pieces.shape[1], SUBLANES):

        @pl.when(row >= geometry.live)
        def _():
            rows = pl.ds(row, SUBLANES)
            pieces[:, rows, :] = jnp.zeros((FIELDS, SUBLANES, pieces.shape[2]), jnp.float32)


def scratch_of(shape):
    return pltpu.VMEM(shape.shape, shape.dtype)


def pieces_of(rows, flat_count):
    return pltpu.VMEM((FIELDS, rows, flat_count), jnp.float32)


def run_first(info, whole):
    rows = whole.shape[0]
    shapes = [by_row(rows, count) for count in (HELD, REDS, FIELDS)]
    slabs = [by_row(2 * SLAB, count) for count in (HELD, REDS, FIELDS, HELD, REDS, FIELDS)]
    scratch = [by_row(rows, 4), by_row(4, 3)]
    scratch = scratch + [by_row(rows, count) for count in (HELD, REDS, FIELDS)]
    return pl.pallas_call(
        first_kernel,
        out_shape=shapes + slabs,
        in_specs=[SMEM, VMEM],
        out_specs=[VMEM] * 9,
        scratch_shapes=[scratch_of(shape) for shape in scratch],
        compiler_params=pltpu.CompilerParams(vmem_limit_bytes=24 * 1024 * 1024),
        cost_estimate=pl.CostEstimate(flops=20_000_000, bytes_accessed=8_000_000, transcendentals=0),
        name="first",
    )(info, whole)


def run_second(info, state, earlier, arrived, arrays):
    row_count, flat_count = arrays[0].shape
    return pl.pallas_call(
        second_kernel,
        out_shape=jax.ShapeDtypeStruct((FIELDS, row_count, flat_count), jnp.float32),
        in_specs=[SMEM] + [VMEM] * 3 + [ANY],
        out_specs=VMEM,
        scratch_shapes=[scratch_of(by_row(row_count, FIELDS)), scratch_of(by_row(4, 3))],
        compiler_params=pltpu.CompilerParams(vmem_limit_bytes=16 * 1024 * 1024),
        cost_estimate=pl.CostEstimate(flops=20_000_000, bytes_accessed=8_000_000, transcendentals=0),
        name="second",
    )(info, *state, earlier, arrived)


def follow_kernel(ends, kept, out):
    out[pl.ds(PACKED * SUBLANES, 1), :] = jnp.zeros((1, LANES), jnp.float32)


def follow(ends, kept):
    return pl.pallas_call(
        follow_kernel,
        out_shape=jax.ShapeDtypeStruct(ends.shape, jnp.float32),
        in_specs=[VMEM, ANY],
        out_specs=VMEM,
        input_output_aliases={0: 0},
        compiler_params=pltpu.CompilerParams(vmem_limit_bytes=8 * 1024 * 1024),
        name="follow",
    )(pltpu.with_memory_space_constraint(ends, pltpu.VMEM), kept)


def outer_kernel(info, whole, arrived, passed, inner_pieces, *refs):
    outs = refs[6:10]
    moved, reds, fields, moved_later, reds_later, final = refs[10:16]
    start_fields, colours, walls, pieces, sems = refs[16:]
    state, later = (ByRow(moved), ByRow(reds)), (ByRow(moved_later), ByRow(reds_later))
    geometry = Geometry(info, OWN_TILES)
    live = geometry.live
    low_part = info[3] == 0

    inner_copies = [
        pltpu.make_async_copy(source, out, sems.at[2, number])
        for number, (source, out) in enumerate(zip(split_fields(inner_pieces), outs))
    ]
    for copy in inner_copies:
        copy.start()
    fill_wall_table(walls, geometry)

    def ends_of(ref, half):
        blocks = []
        for group in range(FULL * PLANES // GROUP):
            first = half * (PACKED + 1) + group * (GROUP - 1)
            packed = [ref[pl.ds((first + k) * SUBLANES, SUBLANES), :] for k in range(GROUP - 1)]
            blocks = blocks + unpack_blocks(packed)
        last = half * (PACKED + 1) + PACKED
        return blocks + [ref[pl.ds(last * SUBLANES, SUBLANES), :]]

    tiles = block_tiles()
    middle = (tiles >= 1) & (tiles <= OWN_TILES)

    def widened(own, other):
        beside = jnp.where(tiles == 0, roll_tiles(other, -OWN_TILES), roll_tiles(other, OWN_TILES))
        return jnp.where(geometry.domain, jnp.where(middle, own, beside), 0.0)

    straight = [widened(*pair) for pair in zip(ends_of(arrived, 0), ends_of(arrived, 1))]
    crossed = [widened(*pair) for pair in zip(ends_of(passed, 1), ends_of(passed, 0))]
    below = [jnp.where(low_part, *pair) for pair in zip(straight, crossed)]
    above = [jnp.where(low_part, *pair) for pair in zip(crossed, straight)]

    for number in range(FULL * PLANES):
        place, extra = divmod(number, FULL)
        index = ORDER[place]
        write_row(ByRow(start_fields), index, 1 + extra, below[number])
        write_row(ByRow(start_fields), index, 2 * SLAB - HALO + extra, above[number])
    for row, colour in ((0, below[-1]), (2 * SLAB - 1, above[-1])):
        write_row(ByRow(start_fields), 0, row, jnp.zeros((SUBLANES, LANES), jnp.float32))
        write_row(ByRow(start_fields), 10, row, 0.5 * colour)
    for slab_row, row in slab_rows(live, HALO, FULL):
        for extra in range(FULL):
            start_fields[slab_row + extra] = whole[row + extra]

    def block(first, count):
        return Block(geometry, [(row, at, count) for at, row in slab_rows(live, first, count)])

    held, solids, marks = ByRow(fields), ByRow(start_fields), ByRow(colours)
    colour_stage(block(0, 6), geometry, solids, marks)
    collide_stage(block(1, 4), geometry, solids, solids, marks, walls, state)
    arrive_stage(block(2, 4), geometry, walls, state, held)
    colour_stage(block(2, 6), geometry, held, marks)
    collide_stage(block(3, 4), geometry, held, solids, marks, walls, later)
    arrive_stage(block(4, 4), geometry, walls, later, ByRow(final))

    copies = []
    for side, row, out_row in ((0, HALO, 0), (1, SLAB, live - SUBLANES)):
        gather_tiles(final, row, pieces, side * SUBLANES)
        out_row = pl.multiple_of(out_row, SUBLANES)
        copies = copies + tile_copies(pieces, outs, side * SUBLANES, out_row, sems.at[side])
    for copy in inner_copies:
        copy.wait()
    for copy in copies:
        copy.start()
    for copy in copies:
        copy.wait()


def run_outer(info, whole, arrived, passed, inner_pieces, slabs, arrays):
    row_count, flat_count = arrays[0].shape
    shapes = [jax.ShapeDtypeStruct(array.shape, jnp.float32) for array in (*arrays[:4], *slabs)]
    slabs = [pltpu.with_memory_space_constraint(slab, pltpu.VMEM) for slab in slabs]
    return pl.pallas_call(
        outer_kernel,
        out_shape=shapes,
        in_specs=[SMEM] + [VMEM] * 10,
        out_specs=[ANY] * 4 + [VMEM] * 6,
        scratch_shapes=[
            scratch_of(by_row(2 * SLAB, PLACES)),
            scratch_of(by_row(2 * SLAB, 4)),
            scratch_of(by_row(4, 3)),
            pieces_of(2 * SUBLANES, flat_count),
            pltpu.SemaphoreType.DMA((3, 4)),
        ],
        input_output_aliases={5 + number: 4 + number for number in range(6)},
        compiler_params=pltpu.CompilerParams(vmem_limit_bytes=24 * 1024 * 1024),
        name="outer",
    )(info, whole, arrived, passed, inner_pieces, *slabs)


def body(density, momentum, stress, red_density, solid, widths):
    tiles_count = lax.axis_size("tiles")
    arrays = (density, momentum, stress, red_density, solid)
    info, raw, raw_solid, packet, mine = load_inputs(arrays, widths, tiles_count)
    info = pltpu.with_memory_space_constraint(info, pltpu.SMEM)
    swap = [(0, 1), (1, 0)]
    packet = lax.ppermute(packet, "sub", swap)
    spread = spread_rows(raw, raw_solid)
    ends = join_ends(mine, packet, spread)
    route = [(2 * k, 2 * k + 2) for k in range(tiles_count - 1)]
    route = route + [(2 * k + 3, 2 * k + 1) for k in range(tiles_count - 1)]
    arrived = lax.ppermute(ends, ("tiles", "sub"), route)
    whole = put_beside(info, spread, packet)
    moved, reds, earlier, *slabs = run_first(info, whole)
    arrived = follow(arrived, slabs[-1])
    passed = lax.ppermute(arrived, "sub", swap)
    pieces = run_second(info, (moved, reds), earlier, arrived, arrays)
    return tuple(run_outer(info, whole, arrived, passed, pieces, slabs, arrays)[:4])


def solution(mesh):
    in_specs = (
        P(("groups", "tiles"), "sub"),
        P(None, ("groups", "tiles"), "sub"),
        P(None, ("groups", "tiles"), "sub"),
        P(("groups", "tiles"), "sub"),
        P(("groups", "tiles"), "sub"),
        P("groups"),
    )
    out_specs = (
        P(("groups", "tiles"), "sub"),
        P(None, ("groups", "tiles"), "sub"),
        P(None, ("groups", "tiles"), "sub"),
        P(("groups", "tiles"), "sub"),
    )
    return jax.shard_map(body, mesh=mesh, in_specs=in_specs, out_specs=out_specs, check_vma=False)
```

```python
import functools

import jax
import jax.numpy as jnp
from jax import lax
from jax.experimental import pallas as pl
from jax.experimental.pallas import tpu as pltpu
from jax.sharding import PartitionSpec as P

TILE = 16
STEPS = 2
RELAX_TIME = 0.8
SURFACE = 0.1
SEPARATION = 0.7

LANES = 128
SUBLANES = 8
FULL = 3
HALO = FULL + 1
FIELDS = 11
PLANES = FIELDS + 1
MOVED = 19
REDS = 5
HELD = MOVED + 1
RIM = 4
SLAB = HALO + 2 * RIM
OWN_TILES = SUBLANES - 2
GROUP = 4
PACKED = FULL * PLANES // GROUP * (GROUP - 1)
END_ROWS = (PACKED + 1) * SUBLANES
HALF = LANES // 2
ORDER = (0, 1, 2, 3, 10, 11, 4, 5, 6, 7, 8, 9)
PAIRS = PLANES // 2
PLACES = PLANES + 1
SPLIT = 4
KEPT = 2
COLOUR_BLOCK = (16, 1)
COLLIDE_BLOCK = (8, 1)
ARRIVE_BLOCK = (8, 1)
VMEM = pl.BlockSpec(memory_space=pltpu.VMEM)
SMEM = pl.BlockSpec(memory_space=pltpu.SMEM)
ANY = pl.BlockSpec(memory_space=pl.ANY)
HBM = pl.BlockSpec(memory_space=pltpu.HBM)


class Rows:
    def __init__(self, parts):
        self.parts = parts

    def _with(self, other, operation):
        others = other.parts if isinstance(other, Rows) else [other] * len(self.parts)
        return Rows([operation(one, two) for one, two in zip(self.parts, others)])

    def __add__(self, other):
        return self._with(other, lambda one, two: one + two)

    def __sub__(self, other):
        return self._with(other, lambda one, two: one - two)

    def __rsub__(self, other):
        return self._with(other, lambda one, two: two - one)

    def __mul__(self, other):
        return self._with(other, lambda one, two: one * two)

    def __or__(self, other):
        return self._with(other, lambda one, two: one | two)

    def __eq__(self, other):
        return self._with(other, lambda one, two: one == two)

    __radd__, __rmul__, __ror__ = __add__, __mul__, __or__

    def each(self, operation):
        return Rows([operation(part) for part in self.parts])


def select(mask, yes, no):
    count = max(len(item.parts) for item in (mask, yes, no) if isinstance(item, Rows))
    columns = [
        item.parts if isinstance(item, Rows) else [item] * count for item in (mask, yes, no)
    ]
    return Rows([jnp.where(*row) for row in zip(*columns)])


def roll_lanes(values, amount):
    return values.each(lambda part: pltpu.roll(part, amount % LANES, 1))


def roll_sublanes(values, amount):
    return values.each(lambda part: pltpu.roll(part, amount % SUBLANES, 0))


class Geometry:
    def __init__(self, info, own_tiles):
        live, first, last, sub_index = info[0], info[1], info[2], info[3]
        self.live = live
        self.low_row = jnp.where(first == 1, 0, -1000)
        self.high_row = jnp.where(last == 1, live, 1000)
        shape = (SUBLANES, LANES)
        lane = lax.broadcasted_iota(jnp.int32, shape, 1)
        tile = lax.broadcasted_iota(jnp.int32, shape, 0)
        depth = lane & (TILE - 1)
        low_part = sub_index == 0
        high_part = sub_index == 1
        z_walls = {1: depth == 0, -1: depth == TILE - 1}
        y_walls = {
            1: (tile == 1) & (lane < TILE) & low_part,
            -1: (tile == own_tiles) & (lane >= LANES - TILE) & high_part,
        }
        self.walls = {(0, vel_z): wall for vel_z, wall in z_walls.items()}
        for vel_y, y_wall in y_walls.items():
            self.walls[vel_y, 0] = y_wall
            for vel_z, z_wall in z_walls.items():
                self.walls[vel_y, vel_z] = y_wall | z_wall
        own = (tile >= 1) & (tile <= own_tiles)
        self.domain = own | ((tile == own_tiles + 1) & low_part) | ((tile == 0) & high_part)
        self.first_lanes = lane < TILE
        self.last_lanes = lane >= LANES - TILE

    def from_low_y(self, values):
        return roll_lanes(select(self.last_lanes, roll_sublanes(values, 1), values), TILE)

    def from_high_y(self, values):
        return roll_lanes(select(self.first_lanes, roll_sublanes(values, -1), values), -TILE)

    def from_low_z(self, values):
        return select(self.walls[0, 1], 0.0, roll_lanes(values, 1))

    def from_high_z(self, values):
        return select(self.walls[0, -1], 0.0, roll_lanes(values, -1))


def flat_rows(row, count, tile_offset=0):
    start = row * SUBLANES
    if not isinstance(start, int):
        start = pl.multiple_of(start, SUBLANES)
    return pl.ds(start + tile_offset, count * SUBLANES)


class ByRow:
    def __init__(self, ref):
        self.ref = ref


def by_row(rows, count):
    return jax.ShapeDtypeStruct((rows, count * SUBLANES, LANES), jnp.float32)


def place_of(ref, index, row, tile_offset=0):
    if isinstance(ref, ByRow):
        return ref.ref, row, pl.ds(index * SUBLANES + tile_offset, SUBLANES)
    return ref, index, flat_rows(row, 1, tile_offset)


def read_row(ref, index, row, tile_offset=0):
    ref, first, second = place_of(ref, index, row, tile_offset)
    return ref[first, second, :]


def write_row(ref, index, row, values):
    ref, first, second = place_of(ref, index, row)
    ref[first, second, :] = values


class Block:
    def __init__(self, geometry, spans, inner=False, store_rows=None):
        self.spans = spans
        self.store_rows = store_rows or [local for row, local, count in spans]
        rows = [row + extra for row, local, count in spans for extra in range(count)]
        self.inner = inner
        rows = [row + extra for row, local, count in spans for extra in range(count)]
        if inner:
            self.x_walls = {}
            self.valid = geometry.domain
            self.kinds = [0]
            return
        ids = Rows([row + jnp.zeros((SUBLANES, LANES), jnp.int32) for row in rows])
        self.x_walls = {1: ids == geometry.low_row, -1: ids == geometry.high_row - 1}
        self.valid = ids.each(
            lambda part: geometry.domain & (part >= geometry.low_row) & (part < geometry.high_row)
        )
        self.kinds = [
            jnp.where(row == geometry.low_row, 1, 0) + jnp.where(row == geometry.high_row - 1, 2, 0)
            for row in rows
        ]

    def load(self, ref, index, offset=0, tile_offset=0):
        return Rows([
            read_row(ref, index, local + offset + extra, tile_offset)
            for row, local, count in self.spans
            for extra in range(count)
        ])

    def store(self, ref, index, values):
        targets = [
            target + extra
            for (row, local, count), target in zip(self.spans, self.store_rows)
            for extra in range(count)
        ]
        for target, part in zip(targets, values.parts):
            write_row(ref, index, target, part)

    def wall_terms(self, walls, position):
        terms = [walls[position, flat_rows(kind, 1), :] for kind in self.kinds]
        return terms[0] if self.inner else Rows(terms)


def fill_wall_table(walls, geometry):
    one = jnp.ones((SUBLANES, LANES), jnp.float32)
    up_y, down_y, up_z, down_z = [
        jnp.where(geometry.walls[key], 0.0, one) for key in ((-1, 0), (1, 0), (0, -1), (0, 1))
    ]
    sum_y, sum_z = up_y + down_y, up_z + down_z
    for kind, (up_x, down_x) in enumerate(((1.0, 1.0), (1.0, 0.0), (0.0, 1.0))):
        sum_x = up_x + down_x
        around_x = 2.0 + sum_y + sum_z
        total = 12.0 + 2.0 * (sum_x + sum_y + sum_z) + sum_x * (sum_y + sum_z) + sum_y * sum_z
        rows = (
            (up_x - down_x) * around_x,
            (up_y - down_y) * (2.0 + sum_x + sum_z),
            (up_z - down_z) * (2.0 + sum_x + sum_y),
            36.0 - total,
        )
        for position, row in enumerate(rows):
            walls[position, flat_rows(kind, 1), :] = row


VELOCITIES = tuple(
    tuple(sign if axis == place else 0 for place in range(3)) for axis in range(3) for sign in (1, -1)
) + tuple(
    tuple({a: one, b: two}.get(place, 0) for place in range(3))
    for a, b in ((0, 1), (0, 2), (1, 2))
    for one, two in ((1, 1), (-1, -1), (1, -1), (-1, 1))
)
VELOCITIES = ((0, 0, 0),) + VELOCITIES


def colour_stage(block, geometry, fields, colours):
    density = block.load(fields, 0)
    red = block.load(fields, 10)
    colour = select(block.valid, 2.0 * red - density, 0.0)
    along_y = geometry.from_low_y(colour) + geometry.from_high_y(colour)
    along_z = geometry.from_low_z(colour) + geometry.from_high_z(colour)
    block.store(colours, 0, colour)
    block.store(colours, 1, 2.0 * colour + (along_y + along_z))
    block.store(colours, 2, along_y)
    block.store(colours, 3, along_z)


def collide_stage(block, geometry, fields, solids, colours, walls, state):
    relaxing = 1.0 - 1.0 / RELAX_TIME
    third = 1.0 / 3.0
    colour = block.load(colours, 0)
    doubled = 2.0 * colour + (block.load(colours, 0, -1) + block.load(colours, 0, 1))
    term_y = doubled + block.load(colours, 3)
    term_z = doubled + block.load(colours, 2)
    grad_x = block.load(colours, 1, 1) - block.load(colours, 1, -1)
    grad_y = geometry.from_high_y(term_y) - geometry.from_low_y(term_y)
    grad_z = geometry.from_high_z(term_z) - geometry.from_low_z(term_z)
    if not block.inner:
        grad_x = grad_x - block.wall_terms(walls, 0) * colour
    grad_y = grad_y - block.wall_terms(walls, 1) * colour
    grad_z = grad_z - block.wall_terms(walls, 2) * colour

    fluid = block.load(solids, PLANES - 1) == 0.0
    density = block.load(fields, 0)
    red = block.load(fields, 10)
    flux = [block.load(fields, 1 + axis) for axis in range(3)]
    stress = [block.load(fields, 4 + part) for part in range(6)]
    square_xx, square_yy, square_zz = grad_x * grad_x, grad_y * grad_y, grad_z * grad_z
    square = square_xx + square_yy + square_zz
    inverse = select(fluid, (1.0 + square * (1.0 / 144.0)).each(lax.rsqrt), 0.0)
    trace = third * square
    strength = (SURFACE / (8.0 * 144.0)) * inverse
    keep = select(fluid, relaxing / 8.0, 1.0 / 8.0)
    eighths = [0.125 * part for part in flux]
    own = [
        eighths[axis] * flux[axis] + (keep * stress[axis] + strength * (squared - trace))
        for axis, squared in enumerate((square_xx, square_yy, square_zz))
    ]
    strength, keep = 2.0 * strength, 2.0 * keep
    quarters = [2.0 * part for part in eighths[:2]]
    grads = (grad_x, grad_y, grad_z)
    cross = [
        quarters[a] * flux[b] + (keep * stress[3 + plane] + strength * (grads[a] * grads[b]))
        for plane, (a, b) in enumerate(((0, 1), (0, 2), (1, 2)))
    ]
    base = density * (1.0 / 36.0) - third * (own[0] + own[1] + own[2])
    sign = select(fluid, 1.0 / 12.0, -1.0 / 12.0)
    run = [sign * part for part in flux]
    mixing = ((SEPARATION / 144.0) * red) * ((density - red) * inverse)
    red_run = [0.5 * part + mixing * grad for part, grad in zip(run, grads)]
    moved, reds = state
    block.store(moved, 0, 12.0 * base)
    straight = [base + part for part in own]
    for axis in range(3):
        middle = 2.0 * straight[axis]
        swing = 2.0 * run[axis]
        block.store(moved, 1 + 2 * axis, middle + swing)
        block.store(moved, 2 + 2 * axis, middle - swing)
    for plane, (a, b) in enumerate(((0, 1), (0, 2), (1, 2))):
        middle = straight[a] + own[b]
        same, other = middle + cross[plane], middle - cross[plane]
        along, against = run[a] + run[b], run[a] - run[b]
        first = 7 + 4 * plane
        block.store(moved, first, same + along)
        block.store(moved, first + 1, same - along)
        block.store(moved, first + 2, other + against)
        block.store(moved, first + 3, other - against)

    red_base = select(block.valid, red * (1.0 / 36.0), 0.0)
    red_run = [select(block.valid, part, 0.0) for part in red_run]
    block.store(reds, 0, red_base)
    block.store(reds, 1, red_base + red_run[0])
    block.store(reds, 2, red_base - red_run[0])
    block.store(reds, 3, red_run[1])
    block.store(reds, 4, red_run[2])


def arrive_stage(block, geometry, walls, state, fields):
    third = 1.0 / 3.0
    moved, reds = state
    own = [None] * MOVED

    def here(direction):
        if own[direction] is None:
            own[direction] = block.load(moved, direction)
        return own[direction]

    def arrived(direction, opposite):
        vel_x, vel_y, vel_z = VELOCITIES[direction]
        values = here(direction) if vel_x == 0 else block.load(moved, direction, -vel_x)
        if vel_y != 0:
            beside = block.load(moved, direction, -vel_x, -vel_y)
            leaving = geometry.last_lanes if vel_y == 1 else geometry.first_lanes
            values = select(leaving, beside, values)
        if vel_y != 0 or vel_z != 0:
            values = roll_lanes(values, TILE * vel_y + vel_z)
        masks = []
        if vel_x in block.x_walls:
            masks.append(block.x_walls[vel_x])
        if (vel_y, vel_z) in geometry.walls:
            masks.append(geometry.walls[vel_y, vel_z])
        if not masks:
            return values
        wall = functools.reduce(lambda one, two: one | two, masks)
        return select(wall, here(opposite), values)

    red = block.load(reds, 0)
    red_y = block.load(reds, 3)
    red_z = block.load(reds, 4)
    from_x = block.load(reds, 1, -1) + block.load(reds, 2, 1)
    spread = 2.0 * red + from_x
    spread_y = 2.0 * red_y + (block.load(reds, 3, -1) + block.load(reds, 3, 1))
    spread_z = 2.0 * red_z + (block.load(reds, 4, -1) + block.load(reds, 4, 1))
    up_y, down_y = red + red_y, red - red_y
    low_y = (
        (spread + spread_y)
        + geometry.from_low_z(up_y + red_z)
        + geometry.from_high_z(up_y - red_z)
    )
    high_y = (
        (spread - spread_y)
        + geometry.from_low_z(down_y + red_z)
        + geometry.from_high_z(down_y - red_z)
    )
    bounced = (
        block.wall_terms(walls, 3) * red
        - block.wall_terms(walls, 1) * red_y
        - block.wall_terms(walls, 2) * red_z
    )
    if not block.inner:
        bounced = bounced - block.wall_terms(walls, 0) * (block.load(reds, 1) - red)
    red_total = (
        12.0 * red
        + 2.0 * from_x
        + geometry.from_low_z(spread + spread_z)
        + geometry.from_high_z(spread - spread_z)
        + geometry.from_low_y(low_y)
        + geometry.from_high_y(high_y)
        + bounced
    )
    rest = here(0)
    sums, diffs = [], []
    for axis in range(3):
        up = arrived(1 + 2 * axis, 2 + 2 * axis)
        down = arrived(2 + 2 * axis, 1 + 2 * axis)
        sums.append(up + down)
        diffs.append(up - down)
    total = rest + sums[0] + sums[1] + sums[2]
    cross = []
    for plane, (a, b) in enumerate(((0, 1), (0, 2), (1, 2))):
        first = 7 + 4 * plane
        parts = [arrived(first + offset, first + (offset ^ 1)) for offset in range(4)]
        same, other = parts[0] + parts[1], parts[2] + parts[3]
        along, against = parts[0] - parts[1], parts[2] - parts[3]
        both = same + other
        cross.append(same - other)
        total = total + both
        sums[a], sums[b] = sums[a] + both, sums[b] + both
        diffs[a], diffs[b] = diffs[a] + (along + against), diffs[b] + (along - against)
    shared = third * total
    block.store(fields, 0, total)
    for axis in range(3):
        block.store(fields, 1 + axis, diffs[axis])
        block.store(fields, 4 + axis, sums[axis] - shared - diffs[axis] * diffs[axis])
    for plane, (a, b) in enumerate(((0, 1), (0, 2), (1, 2))):
        block.store(fields, 7 + plane, cross[plane] - diffs[a] * diffs[b])
    block.store(fields, 10, red_total)


def over_rows(geometry, first, size, blocks, stage):
    trip = size * blocks
    rest = -2 * first % trip
    assert TILE % trip == 0 and rest % min(size, rest or size) == 0

    def run(start, count, step_size):
        for offset in range(0, count, step_size):
            row = start + offset
            stage(Block(geometry, [(row, row, step_size)], inner=True))

    def step(index, carry):
        run(first + index * trip, trip, size)
        return carry

    trips = (geometry.live - 2 * first - rest) // trip
    lax.fori_loop(0, trips, step, 0)
    if rest:
        run(geometry.live - first - rest, rest, min(size, rest))


def block_tiles():
    return lax.broadcasted_iota(jnp.int32, (SUBLANES, LANES), 0)


def roll_tiles(block, amount):
    return pltpu.roll(block, amount % SUBLANES, 0)


def pack_blocks(blocks):
    tiles, rest = block_tiles(), blocks[GROUP - 1]
    packed = []
    for number, block in enumerate(blocks[: GROUP - 1]):
        low, high = 2 * number + 1, 2 * number + 2
        block = jnp.where(tiles == 0, roll_tiles(rest, -low), block)
        packed.append(jnp.where(tiles == SUBLANES - 1, roll_tiles(rest, SUBLANES - 1 - high), block))
    return packed


def unpack_blocks(packed):
    tiles, rest = block_tiles(), None
    for number, block in enumerate(packed):
        low, high = 2 * number + 1, 2 * number + 2
        part = jnp.where(tiles == low, roll_tiles(block, low), roll_tiles(block, high - SUBLANES + 1))
        rest = part if rest is None else jnp.where(tiles >= low, part, rest)
    return list(packed) + [rest]


def flat_view(ref):
    rows, width, lanes = ref.shape
    return ref.reshape(rows * width, lanes)


def spread_tile(raw, raw_solid, index, row, target, target_row):
    source = raw_solid if index == FIELDS else raw.at[index]
    width = target.shape[1]
    for tile in range(OWN_TILES):
        values = source[pl.ds(row, SUBLANES), pl.ds(tile * LANES, LANES)].astype(jnp.float32)
        start = target_row * width + index * SUBLANES + 1 + tile
        flat_view(target)[pl.ds(start, SUBLANES, stride=width), :] = values


def load_kernel(
    tiles_count, density, momentum, stress, red, solid, widths,
    info, raw, raw_solid, packet, mine,
    first_tile, last_tile, held_widths, sems,
):
    row_count, flat_count = raw_solid.shape
    own_tiles = flat_count // LANES
    copies = [
        pltpu.make_async_copy(widths, held_widths, sems.at[0]),
        pltpu.make_async_copy(density, raw.at[0], sems.at[1]),
        pltpu.make_async_copy(momentum, raw.at[pl.ds(1, 3)], sems.at[2]),
        pltpu.make_async_copy(red, raw.at[10], sems.at[3]),
        pltpu.make_async_copy(solid, raw_solid, sems.at[4]),
        pltpu.make_async_copy(stress.at[pl.ds(0, 3)], raw.at[pl.ds(4, 3)], sems.at[5]),
        pltpu.make_async_copy(stress.at[pl.ds(3, 3)], raw.at[pl.ds(7, 3)], sems.at[6]),
    ]
    for copy in copies:
        copy.start()
    tiles_index, sub_index = lax.axis_index("tiles"), lax.axis_index("sub")
    low_part = sub_index == 0
    edge_start = pl.multiple_of(jnp.where(low_part, (own_tiles - 1) * LANES, 0), LANES)

    copies[0].wait()
    live = held_widths[tiles_index] * TILE
    info[0] = live
    info[1] = (tiles_index == 0).astype(jnp.int32)
    info[2] = (tiles_index == tiles_count - 1).astype(jnp.int32)
    info[3] = sub_index

    near_cut = lax.broadcasted_iota(jnp.int32, (SUBLANES, LANES), 1) < HALF
    near_cut = near_cut == jnp.logical_not(low_part)
    near_last = pl.multiple_of(live - SUBLANES, SUBLANES)
    edges = pl.ds(edge_start, LANES)

    def plane_of(index):
        return raw_solid if index == FIELDS else raw.at[index]

    def pack_edges(pair):
        here, there = [plane_of(index) for index in ORDER[2 * pair : 2 * pair + 2]]
        for row in range(0, row_count, SUBLANES):
            rows = pl.ds(row, SUBLANES)
            beside = pltpu.roll(there[rows, edges].astype(jnp.float32), HALF, 1)
            both = jnp.where(near_cut, here[rows, edges].astype(jnp.float32), beside)
            packet[pl.ds(END_ROWS + pair * row_count + row, SUBLANES), :] = both

    targets = ((packet, jnp.logical_not(low_part)), (mine, low_part))

    def row_of(use_last, index, number_first, number_last):
        first = read_row(ByRow(first_tile), index, number_first)
        last = read_row(ByRow(last_tile), index, number_last)
        return jnp.where(use_last, last, first)

    def pack_ends(group):
        for target, use_last in targets:
            blocks = []
            for number in range(group * GROUP, (group + 1) * GROUP):
                place, extra = divmod(number, FULL)
                blocks.append(row_of(use_last, ORDER[place], extra, SUBLANES - FULL + extra))
            for number, block in enumerate(pack_blocks(blocks)):
                place = (group * (GROUP - 1) + number) * SUBLANES
                target[pl.ds(place, SUBLANES), :] = block

    place = 0
    for copy, count in zip(copies[1:], (1, 3, 1, 1, 3, 3)):
        copy.wait()
        before, place = place, place + count
        for index in ORDER[before:place]:
            for target, row in ((first_tile, 0), (last_tile, near_last)):
                spread_tile(raw, raw_solid, index, row, target, 0)
        for pair in range(before // 2, place // 2):
            pack_edges(pair)
        for group in range(before * FULL // GROUP, place * FULL // GROUP):
            pack_ends(group)
    for target, use_last in targets:
        red_row, density_row = [
            row_of(use_last, index, FULL, SUBLANES - HALO) for index in (10, 0)
        ]
        target[pl.ds(PACKED * SUBLANES, SUBLANES), :] = 2.0 * red_row - density_row


def load_inputs(arrays, widths, tiles_count):
    row_count, flat_count = arrays[0].shape
    return pl.pallas_call(
        functools.partial(load_kernel, tiles_count),
        out_shape=[
            pltpu.SMEM((4,), jnp.int32),
            jax.ShapeDtypeStruct((FIELDS, row_count, flat_count), jnp.float32),
            jax.ShapeDtypeStruct((row_count, flat_count), jnp.int32),
            jax.ShapeDtypeStruct((END_ROWS + PAIRS * row_count, LANES), jnp.float32),
            jax.ShapeDtypeStruct((END_ROWS, LANES), jnp.float32),
        ],
        in_specs=[HBM] * 6,
        out_specs=[SMEM] + [VMEM] * 4,
        scratch_shapes=[
            pltpu.VMEM((SUBLANES, PLACES * SUBLANES, LANES), jnp.float32),
            pltpu.VMEM((SUBLANES, PLACES * SUBLANES, LANES), jnp.float32),
            pltpu.SMEM(widths.shape, jnp.int32),
            pltpu.SemaphoreType.DMA((7,)),
        ],
        compiler_params=pltpu.CompilerParams(vmem_limit_bytes=16 * 1024 * 1024),
        name="load",
    )(*[pltpu.with_memory_space_constraint(array, pltpu.HBM) for array in (*arrays, widths)])


def spread_kernel(raw, raw_solid, spread):
    for index in range(PLANES):
        for row in range(0, raw_solid.shape[0], SUBLANES):
            spread_tile(raw, raw_solid, index, row, spread, row)


def spread_rows(raw, raw_solid):
    row_count = raw_solid.shape[0]
    return pl.pallas_call(
        spread_kernel,
        out_shape=by_row(row_count, PLACES),
        in_specs=[VMEM, VMEM],
        out_specs=VMEM,
        compiler_params=pltpu.CompilerParams(vmem_limit_bytes=16 * 1024 * 1024),
        cost_estimate=pl.CostEstimate(flops=1_000_000, bytes_accessed=4_000_000, transcendentals=0),
        name="spread",
    )(raw, raw_solid)


def join_kernel(mine, packet, spread, ends):
    ends[pl.ds(0, END_ROWS), :] = mine[...]
    ends[pl.ds(END_ROWS, END_ROWS), :] = packet[pl.ds(0, END_ROWS), :]


def join_ends(mine, packet, spread):
    return pl.pallas_call(
        join_kernel,
        out_shape=jax.ShapeDtypeStruct((2 * END_ROWS, LANES), jnp.float32),
        in_specs=[VMEM, VMEM, ANY],
        out_specs=VMEM,
        compiler_params=pltpu.CompilerParams(vmem_limit_bytes=8 * 1024 * 1024),
        name="join",
    )(mine, packet, spread)


def beside_kernel(info, spread, packet, whole):
    low_part = info[3] == 0
    row_count, width = spread.shape[:2]
    flat = flat_view(whole)
    for pair in range(PAIRS):
        for row in range(0, row_count, SUBLANES):
            both = packet[pl.ds(END_ROWS + pair * row_count + row, SUBLANES), :]
            for place, values in ((2 * pair, both), (2 * pair + 1, pltpu.roll(both, HALF, 1))):
                index = ORDER[place]
                start = row * width + index * SUBLANES
                below = jnp.where(low_part, 0.0, values)
                above = jnp.where(low_part, values, 0.0)
                flat[pl.ds(start, SUBLANES, stride=width), :] = below
                flat[pl.ds(start + SUBLANES - 1, SUBLANES, stride=width), :] = above


def put_beside(info, spread, packet):
    return pl.pallas_call(
        beside_kernel,
        out_shape=jax.ShapeDtypeStruct(spread.shape, jnp.float32),
        in_specs=[SMEM, VMEM, VMEM],
        out_specs=VMEM,
        input_output_aliases={1: 0},
        compiler_params=pltpu.CompilerParams(vmem_limit_bytes=16 * 1024 * 1024),
        name="beside",
    )(info, pltpu.with_memory_space_constraint(spread, pltpu.VMEM), packet)


def keep_rows(slab, source, first, size, live):
    for slab_row, row in slab_rows(live, first, size):
        for extra in range(size):
            slab[slab_row + extra] = source[row + extra]


def slab_rows(live, first, size):
    mirrored = SLAB - first - size
    return [(first, first - HALO), (SLAB + mirrored, live - 2 * RIM + mirrored)]


def collide_rows(geometry, before, whole, first, colours, walls, state):
    over_rows(geometry, first - 1, *COLOUR_BLOCK, lambda block: colour_stage(
        block, geometry, before, colours))
    over_rows(geometry, first, *COLLIDE_BLOCK, lambda block: collide_stage(
        block, geometry, before, whole, colours, walls, state))


def tile_copies(pieces, outs, held_row, out_row, sems):
    held, rows = pl.ds(held_row, SUBLANES), pl.ds(out_row, SUBLANES)
    parts = (
        (pieces.at[0, held], outs[0].at[rows]),
        (pieces.at[pl.ds(1, 3), held], outs[1].at[:, rows]),
        (pieces.at[pl.ds(4, 6), held], outs[2].at[:, rows]),
        (pieces.at[10, held], outs[3].at[rows]),
    )
    return [
        pltpu.make_async_copy(source, target, sems.at[number])
        for number, (source, target) in enumerate(parts)
    ]


def gather_tiles(final, row, pieces, held_row):
    width = final.shape[1]
    start = row * width
    if not isinstance(start, int):
        start = pl.multiple_of(start, SUBLANES)
    for index in range(FIELDS):
        for tile in range(OWN_TILES):
            place = start + index * SUBLANES + 1 + tile
            pieces[index, pl.ds(held_row, SUBLANES), pl.ds(tile * LANES, LANES)] = flat_view(final)[
                pl.ds(place, SUBLANES, stride=width), :
            ]


def first_kernel(
    info, whole, moved_later, reds_later, final,
    moved_slab, reds_slab, fields_slab, moved_later_slab, reds_later_slab, final_slab,
    colours, walls, moved, reds, fields,
):
    state, later = (ByRow(moved), ByRow(reds)), (ByRow(moved_later), ByRow(reds_later))
    geometry = Geometry(info, OWN_TILES)
    live = geometry.live
    fill_wall_table(walls, geometry)
    collide_rows(geometry, ByRow(whole), ByRow(whole), 1, ByRow(colours), walls, state)
    over_rows(geometry, 2, *ARRIVE_BLOCK, lambda block: arrive_stage(
        block, geometry, walls, state, ByRow(fields)))
    keep_rows(moved_slab, moved, HALO + 1, KEPT, live)
    keep_rows(reds_slab, reds, HALO + 1, KEPT, live)
    keep_rows(fields_slab, fields, HALO + 2, KEPT, live)
    collide_rows(geometry, ByRow(fields), ByRow(whole), 3, ByRow(colours), walls, later)
    keep_rows(moved_later_slab, moved_later, HALO + 3, KEPT, live)
    keep_rows(reds_later_slab, reds_later, HALO + 3, KEPT, live)
    edges = slab_rows(live, HALO + RIM, RIM)
    rim = Block(geometry, [(row, row, RIM) for _, row in edges], True, [at for at, _ in edges])
    arrive_stage(rim, geometry, walls, later, ByRow(final_slab))

    def arrive_tile(tile, carry):
        row = tile * SUBLANES
        block = Block(geometry, [(row, row, SUBLANES)], inner=True)
        arrive_stage(block, geometry, walls, later, ByRow(final))
        return carry

    lax.fori_loop(1, jnp.minimum(SPLIT, live // SUBLANES - 1), arrive_tile, 0)


def second_kernel(
    info, moved, reds, earlier, arrived, density_out, momentum_out, stress_out, red_out,
    final, walls, pieces, zeros, sems,
):
    outs = (density_out, momentum_out, stress_out, red_out)
    row_tiles = density_out.shape[0] // SUBLANES
    state = (ByRow(moved), ByRow(reds))
    geometry = Geometry(info, OWN_TILES)
    live = geometry.live
    last = live // SUBLANES - 1
    fill_wall_table(walls, geometry)

    def copies_of(tile):
        row = pl.multiple_of(tile * SUBLANES, SUBLANES)
        return tile_copies(pieces, outs, row, row, sems.at[tile])

    def send_out(tile, source):
        row = pl.multiple_of(tile * SUBLANES, SUBLANES)
        gather_tiles(source, row, pieces, row)
        for copy in copies_of(tile):
            copy.start()

    def pass_on(tile, carry):
        send_out(tile, earlier)
        return carry

    def finish(tile, carry):
        row = tile * SUBLANES
        block = Block(geometry, [(row, row, SUBLANES)], inner=True)
        arrive_stage(block, geometry, walls, state, ByRow(final))
        send_out(tile, final)
        return carry

    def settle(tile, carry):
        for copy in copies_of(tile):
            copy.wait()
        return carry

    lax.fori_loop(1, jnp.minimum(SPLIT, last), pass_on, 0)
    zeros[...] = jnp.zeros(zeros.shape, zeros.dtype)
    dead = {}
    for tile in range(row_tiles):
        dead[tile] = tile_copies(zeros, outs, 0, tile * SUBLANES, sems.at[tile])

        @pl.when(tile * SUBLANES >= live)
        def _():
            for copy in dead[tile]:
                copy.start()

    lax.fori_loop(SPLIT, last, finish, 0)
    lax.fori_loop(1, last, settle, 0)
    for tile in range(row_tiles):

        @pl.when(tile * SUBLANES >= live)
        def _():
            for copy in dead[tile]:
                copy.wait()


def scratch_of(shape):
    return pltpu.VMEM(shape.shape, shape.dtype)


def pieces_of(rows, flat_count):
    return pltpu.VMEM((FIELDS, rows, flat_count), jnp.float32)


def run_first(info, whole):
    rows = whole.shape[0]
    shapes = [by_row(rows, count) for count in (HELD, REDS, FIELDS)]
    slabs = [by_row(2 * SLAB, count) for count in (HELD, REDS, FIELDS, HELD, REDS, FIELDS)]
    scratch = [by_row(rows, 4), by_row(4, 3)]
    scratch = scratch + [by_row(rows, count) for count in (HELD, REDS, FIELDS)]
    return pl.pallas_call(
        first_kernel,
        out_shape=shapes + slabs,
        in_specs=[SMEM, VMEM],
        out_specs=[VMEM] * 9,
        scratch_shapes=[scratch_of(shape) for shape in scratch],
        compiler_params=pltpu.CompilerParams(vmem_limit_bytes=24 * 1024 * 1024),
        cost_estimate=pl.CostEstimate(flops=20_000_000, bytes_accessed=8_000_000, transcendentals=0),
        name="first",
    )(info, whole)


def run_second(info, state, earlier, arrived, arrays):
    row_count, flat_count = arrays[0].shape
    return pl.pallas_call(
        second_kernel,
        out_shape=[jax.ShapeDtypeStruct(array.shape, jnp.float32) for array in arrays[:4]],
        in_specs=[SMEM] + [VMEM] * 3 + [ANY],
        out_specs=[ANY] * 4,
        scratch_shapes=[
            scratch_of(by_row(row_count, FIELDS)),
            scratch_of(by_row(4, 3)),
            pieces_of(row_count, flat_count),
            pieces_of(SUBLANES, flat_count),
            pltpu.SemaphoreType.DMA((row_count // SUBLANES, 4)),
        ],
        compiler_params=pltpu.CompilerParams(vmem_limit_bytes=24 * 1024 * 1024),
        cost_estimate=pl.CostEstimate(flops=20_000_000, bytes_accessed=8_000_000, transcendentals=0),
        name="second",
    )(info, *state, earlier, arrived)


def follow_kernel(ends, kept, out):
    out[pl.ds(PACKED * SUBLANES, 1), :] = jnp.zeros((1, LANES), jnp.float32)


def follow(ends, kept):
    return pl.pallas_call(
        follow_kernel,
        out_shape=jax.ShapeDtypeStruct(ends.shape, jnp.float32),
        in_specs=[VMEM, ANY],
        out_specs=VMEM,
        input_output_aliases={0: 0},
        compiler_params=pltpu.CompilerParams(vmem_limit_bytes=8 * 1024 * 1024),
        name="follow",
    )(pltpu.with_memory_space_constraint(ends, pltpu.VMEM), kept)


def outer_kernel(info, whole, arrived, passed, *refs):
    outs = refs[10:14]
    moved, reds, fields, moved_later, reds_later, final = refs[14:20]
    start_fields, colours, walls, pieces, sems = refs[20:]
    state, later = (ByRow(moved), ByRow(reds)), (ByRow(moved_later), ByRow(reds_later))
    geometry = Geometry(info, OWN_TILES)
    live = geometry.live
    low_part = info[3] == 0
    fill_wall_table(walls, geometry)

    def ends_of(ref, half):
        blocks = []
        for group in range(FULL * PLANES // GROUP):
            first = half * (PACKED + 1) + group * (GROUP - 1)
            packed = [ref[pl.ds((first + k) * SUBLANES, SUBLANES), :] for k in range(GROUP - 1)]
            blocks = blocks + unpack_blocks(packed)
        last = half * (PACKED + 1) + PACKED
        return blocks + [ref[pl.ds(last * SUBLANES, SUBLANES), :]]

    tiles = block_tiles()
    middle = (tiles >= 1) & (tiles <= OWN_TILES)

    def widened(own, other):
        beside = jnp.where(tiles == 0, roll_tiles(other, -OWN_TILES), roll_tiles(other, OWN_TILES))
        return jnp.where(geometry.domain, jnp.where(middle, own, beside), 0.0)

    straight = [widened(*pair) for pair in zip(ends_of(arrived, 0), ends_of(arrived, 1))]
    crossed = [widened(*pair) for pair in zip(ends_of(passed, 1), ends_of(passed, 0))]
    below = [jnp.where(low_part, *pair) for pair in zip(straight, crossed)]
    above = [jnp.where(low_part, *pair) for pair in zip(crossed, straight)]

    for number in range(FULL * PLANES):
        place, extra = divmod(number, FULL)
        index = ORDER[place]
        write_row(ByRow(start_fields), index, 1 + extra, below[number])
        write_row(ByRow(start_fields), index, 2 * SLAB - HALO + extra, above[number])
    for row, colour in ((0, below[-1]), (2 * SLAB - 1, above[-1])):
        write_row(ByRow(start_fields), 0, row, jnp.zeros((SUBLANES, LANES), jnp.float32))
        write_row(ByRow(start_fields), 10, row, 0.5 * colour)
    for slab_row, row in slab_rows(live, HALO, FULL):
        for extra in range(FULL):
            start_fields[slab_row + extra] = whole[row + extra]

    def block(first, count):
        return Block(geometry, [(row, at, count) for at, row in slab_rows(live, first, count)])

    held, solids, marks = ByRow(fields), ByRow(start_fields), ByRow(colours)
    colour_stage(block(0, 6), geometry, solids, marks)
    collide_stage(block(1, 4), geometry, solids, solids, marks, walls, state)
    arrive_stage(block(2, 4), geometry, walls, state, held)
    colour_stage(block(2, 6), geometry, held, marks)
    collide_stage(block(3, 4), geometry, held, solids, marks, walls, later)
    arrive_stage(block(4, 4), geometry, walls, later, ByRow(final))

    copies = []
    for side, row, out_row in ((0, HALO, 0), (1, SLAB, live - SUBLANES)):
        gather_tiles(final, row, pieces, side * SUBLANES)
        out_row = pl.multiple_of(out_row, SUBLANES)
        copies = copies + tile_copies(pieces, outs, side * SUBLANES, out_row, sems.at[side])
    for copy in copies:
        copy.start()
    for copy in copies:
        copy.wait()


def run_outer(info, whole, arrived, passed, slabs, outs):
    flat_count = outs[0].shape[1]
    shapes = [jax.ShapeDtypeStruct(array.shape, jnp.float32) for array in (*outs, *slabs)]
    slabs = [pltpu.with_memory_space_constraint(slab, pltpu.VMEM) for slab in slabs]
    aliases = {4 + number: 4 + number for number in range(6)}
    aliases.update({10 + number: number for number in range(4)})
    return pl.pallas_call(
        outer_kernel,
        out_shape=shapes,
        in_specs=[SMEM] + [VMEM] * 9 + [ANY] * 4,
        out_specs=[ANY] * 4 + [VMEM] * 6,
        scratch_shapes=[
            scratch_of(by_row(2 * SLAB, PLACES)),
            scratch_of(by_row(2 * SLAB, 4)),
            scratch_of(by_row(4, 3)),
            pieces_of(2 * SUBLANES, flat_count),
            pltpu.SemaphoreType.DMA((2, 4)),
        ],
        input_output_aliases=aliases,
        compiler_params=pltpu.CompilerParams(vmem_limit_bytes=24 * 1024 * 1024),
        name="outer",
    )(info, whole, arrived, passed, *slabs, *outs)


def body(density, momentum, stress, red_density, solid, widths):
    tiles_count = lax.axis_size("tiles")
    arrays = (density, momentum, stress, red_density, solid)
    info, raw, raw_solid, packet, mine = load_inputs(arrays, widths, tiles_count)
    info = pltpu.with_memory_space_constraint(info, pltpu.SMEM)
    swap = [(0, 1), (1, 0)]
    packet = lax.ppermute(packet, "sub", swap)
    spread = spread_rows(raw, raw_solid)
    ends = join_ends(mine, packet, spread)
    route = [(2 * k, 2 * k + 2) for k in range(tiles_count - 1)]
    route = route + [(2 * k + 3, 2 * k + 1) for k in range(tiles_count - 1)]
    arrived = lax.ppermute(ends, ("tiles", "sub"), route)
    whole = put_beside(info, spread, packet)
    moved, reds, earlier, *slabs = run_first(info, whole)
    arrived = follow(arrived, slabs[-1])
    passed = lax.ppermute(arrived, "sub", swap)
    outs = run_second(info, (moved, reds), earlier, arrived, arrays)
    return tuple(run_outer(info, whole, arrived, passed, slabs, outs)[:4])


def solution(mesh):
    in_specs = (
        P(("groups", "tiles"), "sub"),
        P(None, ("groups", "tiles"), "sub"),
        P(None, ("groups", "tiles"), "sub"),
        P(("groups", "tiles"), "sub"),
        P(("groups", "tiles"), "sub"),
        P("groups"),
    )
    out_specs = (
        P(("groups", "tiles"), "sub"),
        P(None, ("groups", "tiles"), "sub"),
        P(None, ("groups", "tiles"), "sub"),
        P(("groups", "tiles"), "sub"),
    )
    return jax.shard_map(body, mesh=mesh, in_specs=in_specs, out_specs=out_specs, check_vma=False)
```

```python
import functools

import jax
import jax.numpy as jnp
from jax import lax
from jax.experimental import pallas as pl
from jax.experimental.pallas import tpu as pltpu
from jax.sharding import PartitionSpec as P

TILE = 16
STEPS = 2
RELAX_TIME = 0.8
SURFACE = 0.1
SEPARATION = 0.7

LANES = 128
SUBLANES = 8
FULL = 3
HALO = FULL + 1
FIELDS = 11
PLANES = FIELDS + 1
MOVED = 19
REDS = 5
HELD = MOVED + 1
RIM = 4
SLAB = HALO + 2 * RIM
OWN_TILES = SUBLANES - 2
GROUP = 4
PACKED = FULL * PLANES // GROUP * (GROUP - 1)
END_ROWS = (PACKED + 1) * SUBLANES
HALF = LANES // 2
ORDER = (0, 1, 2, 3, 10, 11, 4, 5, 6, 7, 8, 9)
PAIRS = PLANES // 2
PLACES = PLANES + 1
SPLIT = 5
KEPT = 2
OUT_COPIES = 5
COLOUR_BLOCK = (16, 1)
COLLIDE_BLOCK = (8, 1)
ARRIVE_BLOCK = (16, 1)
VMEM = pl.BlockSpec(memory_space=pltpu.VMEM)
SMEM = pl.BlockSpec(memory_space=pltpu.SMEM)
ANY = pl.BlockSpec(memory_space=pl.ANY)
HBM = pl.BlockSpec(memory_space=pltpu.HBM)


class Rows:
    def __init__(self, parts):
        self.parts = parts

    def _with(self, other, operation):
        others = other.parts if isinstance(other, Rows) else [other] * len(self.parts)
        return Rows([operation(one, two) for one, two in zip(self.parts, others)])

    def __add__(self, other):
        return self._with(other, lambda one, two: one + two)

    def __sub__(self, other):
        return self._with(other, lambda one, two: one - two)

    def __rsub__(self, other):
        return self._with(other, lambda one, two: two - one)

    def __mul__(self, other):
        return self._with(other, lambda one, two: one * two)

    def __or__(self, other):
        return self._with(other, lambda one, two: one | two)

    def __eq__(self, other):
        return self._with(other, lambda one, two: one == two)

    __radd__, __rmul__, __ror__ = __add__, __mul__, __or__

    def each(self, operation):
        return Rows([operation(part) for part in self.parts])


def select(mask, yes, no):
    count = max(len(item.parts) for item in (mask, yes, no) if isinstance(item, Rows))
    columns = [
        item.parts if isinstance(item, Rows) else [item] * count for item in (mask, yes, no)
    ]
    return Rows([jnp.where(*row) for row in zip(*columns)])


def roll_lanes(values, amount):
    return values.each(lambda part: pltpu.roll(part, amount % LANES, 1))


def roll_sublanes(values, amount):
    return values.each(lambda part: pltpu.roll(part, amount % SUBLANES, 0))


class Geometry:
    def __init__(self, info, own_tiles):
        live, first, last, sub_index = info[0], info[1], info[2], info[3]
        self.live = live
        self.low_row = jnp.where(first == 1, 0, -1000)
        self.high_row = jnp.where(last == 1, live, 1000)
        shape = (SUBLANES, LANES)
        lane = lax.broadcasted_iota(jnp.int32, shape, 1)
        tile = lax.broadcasted_iota(jnp.int32, shape, 0)
        depth = lane & (TILE - 1)
        low_part = sub_index == 0
        high_part = sub_index == 1
        z_walls = {1: depth == 0, -1: depth == TILE - 1}
        y_walls = {
            1: (tile == 1) & (lane < TILE) & low_part,
            -1: (tile == own_tiles) & (lane >= LANES - TILE) & high_part,
        }
        self.walls = {(0, vel_z): wall for vel_z, wall in z_walls.items()}
        for vel_y, y_wall in y_walls.items():
            self.walls[vel_y, 0] = y_wall
            for vel_z, z_wall in z_walls.items():
                self.walls[vel_y, vel_z] = y_wall | z_wall
        own = (tile >= 1) & (tile <= own_tiles)
        self.domain = own | ((tile == own_tiles + 1) & low_part) | ((tile == 0) & high_part)
        self.first_lanes = lane < TILE
        self.last_lanes = lane >= LANES - TILE

    def from_low_y(self, values):
        return roll_lanes(select(self.last_lanes, roll_sublanes(values, 1), values), TILE)

    def from_high_y(self, values):
        return roll_lanes(select(self.first_lanes, roll_sublanes(values, -1), values), -TILE)

    def from_low_z(self, values):
        return select(self.walls[0, 1], 0.0, roll_lanes(values, 1))

    def from_high_z(self, values):
        return select(self.walls[0, -1], 0.0, roll_lanes(values, -1))


def flat_rows(row, count, tile_offset=0):
    start = row * SUBLANES
    if not isinstance(start, int):
        start = pl.multiple_of(start, SUBLANES)
    return pl.ds(start + tile_offset, count * SUBLANES)


class ByRow:
    def __init__(self, ref):
        self.ref = ref


def by_row(rows, count):
    return jax.ShapeDtypeStruct((rows, count * SUBLANES, LANES), jnp.float32)


def place_of(ref, index, row, tile_offset=0):
    if isinstance(ref, ByRow):
        return ref.ref, row, pl.ds(index * SUBLANES + tile_offset, SUBLANES)
    return ref, index, flat_rows(row, 1, tile_offset)


def read_row(ref, index, row, tile_offset=0):
    ref, first, second = place_of(ref, index, row, tile_offset)
    return ref[first, second, :]


def write_row(ref, index, row, values):
    ref, first, second = place_of(ref, index, row)
    ref[first, second, :] = values


class Block:
    def __init__(self, geometry, spans, inner=False, store_rows=None):
        self.spans = spans
        self.store_rows = store_rows or [local for row, local, count in spans]
        rows = [row + extra for row, local, count in spans for extra in range(count)]
        self.inner = inner
        rows = [row + extra for row, local, count in spans for extra in range(count)]
        if inner:
            self.x_walls = {}
            self.valid = geometry.domain
            self.kinds = [0]
            return
        ids = Rows([row + jnp.zeros((SUBLANES, LANES), jnp.int32) for row in rows])
        self.x_walls = {1: ids == geometry.low_row, -1: ids == geometry.high_row - 1}
        self.valid = ids.each(
            lambda part: geometry.domain & (part >= geometry.low_row) & (part < geometry.high_row)
        )
        self.kinds = [
            jnp.where(row == geometry.low_row, 1, 0) + jnp.where(row == geometry.high_row - 1, 2, 0)
            for row in rows
        ]

    def load(self, ref, index, offset=0, tile_offset=0):
        return Rows([
            read_row(ref, index, local + offset + extra, tile_offset)
            for row, local, count in self.spans
            for extra in range(count)
        ])

    def store(self, ref, index, values):
        targets = [
            target + extra
            for (row, local, count), target in zip(self.spans, self.store_rows)
            for extra in range(count)
        ]
        for target, part in zip(targets, values.parts):
            write_row(ref, index, target, part)

    def wall_terms(self, walls, position):
        terms = [walls[position, flat_rows(kind, 1), :] for kind in self.kinds]
        return terms[0] if self.inner else Rows(terms)


def fill_wall_table(walls, geometry):
    one = jnp.ones((SUBLANES, LANES), jnp.float32)
    up_y, down_y, up_z, down_z = [
        jnp.where(geometry.walls[key], 0.0, one) for key in ((-1, 0), (1, 0), (0, -1), (0, 1))
    ]
    sum_y, sum_z = up_y + down_y, up_z + down_z
    for kind, (up_x, down_x) in enumerate(((1.0, 1.0), (1.0, 0.0), (0.0, 1.0))):
        sum_x = up_x + down_x
        around_x = 2.0 + sum_y + sum_z
        total = 12.0 + 2.0 * (sum_x + sum_y + sum_z) + sum_x * (sum_y + sum_z) + sum_y * sum_z
        rows = (
            (up_x - down_x) * around_x,
            (up_y - down_y) * (2.0 + sum_x + sum_z),
            (up_z - down_z) * (2.0 + sum_x + sum_y),
            36.0 - total,
        )
        for position, row in enumerate(rows):
            walls[position, flat_rows(kind, 1), :] = row


VELOCITIES = tuple(
    tuple(sign if axis == place else 0 for place in range(3)) for axis in range(3) for sign in (1, -1)
) + tuple(
    tuple({a: one, b: two}.get(place, 0) for place in range(3))
    for a, b in ((0, 1), (0, 2), (1, 2))
    for one, two in ((1, 1), (-1, -1), (1, -1), (-1, 1))
)
VELOCITIES = ((0, 0, 0),) + VELOCITIES


def colour_stage(block, geometry, fields, colours):
    density = block.load(fields, 0)
    red = block.load(fields, 10)
    colour = select(block.valid, 2.0 * red - density, 0.0)
    along_y = geometry.from_low_y(colour) + geometry.from_high_y(colour)
    along_z = geometry.from_low_z(colour) + geometry.from_high_z(colour)
    block.store(colours, 0, colour)
    block.store(colours, 1, 2.0 * colour + (along_y + along_z))
    block.store(colours, 2, along_y)
    block.store(colours, 3, along_z)


def collide_stage(block, geometry, fields, solids, colours, walls, state):
    relaxing = 1.0 - 1.0 / RELAX_TIME
    third = 1.0 / 3.0
    colour = block.load(colours, 0)
    doubled = 2.0 * colour + (block.load(colours, 0, -1) + block.load(colours, 0, 1))
    term_y = doubled + block.load(colours, 3)
    term_z = doubled + block.load(colours, 2)
    grad_x = block.load(colours, 1, 1) - block.load(colours, 1, -1)
    grad_y = geometry.from_high_y(term_y) - geometry.from_low_y(term_y)
    grad_z = geometry.from_high_z(term_z) - geometry.from_low_z(term_z)
    if not block.inner:
        grad_x = grad_x - block.wall_terms(walls, 0) * colour
    grad_y = grad_y - block.wall_terms(walls, 1) * colour
    grad_z = grad_z - block.wall_terms(walls, 2) * colour

    fluid = block.load(solids, PLANES - 1) == 0.0
    density = block.load(fields, 0)
    red = block.load(fields, 10)
    flux = [block.load(fields, 1 + axis) for axis in range(3)]
    stress = [block.load(fields, 4 + part) for part in range(6)]
    square_xx, square_yy, square_zz = grad_x * grad_x, grad_y * grad_y, grad_z * grad_z
    square = square_xx + square_yy + square_zz
    inverse = select(fluid, (1.0 + square * (1.0 / 144.0)).each(lax.rsqrt), 0.0)
    trace = third * square
    strength = (SURFACE / (8.0 * 144.0)) * inverse
    keep = select(fluid, relaxing / 8.0, 1.0 / 8.0)
    eighths = [0.125 * part for part in flux]
    own = [
        eighths[axis] * flux[axis] + (keep * stress[axis] + strength * (squared - trace))
        for axis, squared in enumerate((square_xx, square_yy, square_zz))
    ]
    strength, keep = 2.0 * strength, 2.0 * keep
    quarters = [2.0 * part for part in eighths[:2]]
    grads = (grad_x, grad_y, grad_z)
    cross = [
        quarters[a] * flux[b] + (keep * stress[3 + plane] + strength * (grads[a] * grads[b]))
        for plane, (a, b) in enumerate(((0, 1), (0, 2), (1, 2)))
    ]
    base = density * (1.0 / 36.0) - third * (own[0] + own[1] + own[2])
    sign = select(fluid, 1.0 / 12.0, -1.0 / 12.0)
    run = [sign * part for part in flux]
    mixing = ((SEPARATION / 144.0) * red) * ((density - red) * inverse)
    red_run = [0.5 * part + mixing * grad for part, grad in zip(run, grads)]
    moved, reds = state
    block.store(moved, 0, 12.0 * base)
    straight = [base + part for part in own]
    for axis in range(3):
        middle = 2.0 * straight[axis]
        swing = 2.0 * run[axis]
        block.store(moved, 1 + 2 * axis, middle + swing)
        block.store(moved, 2 + 2 * axis, middle - swing)
    for plane, (a, b) in enumerate(((0, 1), (0, 2), (1, 2))):
        middle = straight[a] + own[b]
        same, other = middle + cross[plane], middle - cross[plane]
        along, against = run[a] + run[b], run[a] - run[b]
        first = 7 + 4 * plane
        block.store(moved, first, same + along)
        block.store(moved, first + 1, same - along)
        block.store(moved, first + 2, other + against)
        block.store(moved, first + 3, other - against)

    red_base = select(block.valid, red * (1.0 / 36.0), 0.0)
    red_run = [select(block.valid, part, 0.0) for part in red_run]
    block.store(reds, 0, red_base)
    block.store(reds, 1, red_base + red_run[0])
    block.store(reds, 2, red_base - red_run[0])
    block.store(reds, 3, red_run[1])
    block.store(reds, 4, red_run[2])


def arrive_stage(block, geometry, walls, state, fields):
    third = 1.0 / 3.0
    moved, reds = state
    own = [None] * MOVED

    def here(direction):
        if own[direction] is None:
            own[direction] = block.load(moved, direction)
        return own[direction]

    def arrived(direction, opposite):
        vel_x, vel_y, vel_z = VELOCITIES[direction]
        values = here(direction) if vel_x == 0 else block.load(moved, direction, -vel_x)
        if vel_y != 0:
            beside = block.load(moved, direction, -vel_x, -vel_y)
            leaving = geometry.last_lanes if vel_y == 1 else geometry.first_lanes
            values = select(leaving, beside, values)
        if vel_y != 0 or vel_z != 0:
            values = roll_lanes(values, TILE * vel_y + vel_z)
        masks = []
        if vel_x in block.x_walls:
            masks.append(block.x_walls[vel_x])
        if (vel_y, vel_z) in geometry.walls:
            masks.append(geometry.walls[vel_y, vel_z])
        if not masks:
            return values
        wall = functools.reduce(lambda one, two: one | two, masks)
        return select(wall, here(opposite), values)

    red = block.load(reds, 0)
    red_y = block.load(reds, 3)
    red_z = block.load(reds, 4)
    from_x = block.load(reds, 1, -1) + block.load(reds, 2, 1)
    spread = 2.0 * red + from_x
    spread_y = 2.0 * red_y + (block.load(reds, 3, -1) + block.load(reds, 3, 1))
    spread_z = 2.0 * red_z + (block.load(reds, 4, -1) + block.load(reds, 4, 1))
    up_y, down_y = red + red_y, red - red_y
    low_y = (
        (spread + spread_y)
        + geometry.from_low_z(up_y + red_z)
        + geometry.from_high_z(up_y - red_z)
    )
    high_y = (
        (spread - spread_y)
        + geometry.from_low_z(down_y + red_z)
        + geometry.from_high_z(down_y - red_z)
    )
    bounced = (
        block.wall_terms(walls, 3) * red
        - block.wall_terms(walls, 1) * red_y
        - block.wall_terms(walls, 2) * red_z
    )
    if not block.inner:
        bounced = bounced - block.wall_terms(walls, 0) * (block.load(reds, 1) - red)
    red_total = (
        12.0 * red
        + 2.0 * from_x
        + geometry.from_low_z(spread + spread_z)
        + geometry.from_high_z(spread - spread_z)
        + geometry.from_low_y(low_y)
        + geometry.from_high_y(high_y)
        + bounced
    )
    rest = here(0)
    sums, diffs = [], []
    for axis in range(3):
        up = arrived(1 + 2 * axis, 2 + 2 * axis)
        down = arrived(2 + 2 * axis, 1 + 2 * axis)
        sums.append(up + down)
        diffs.append(up - down)
    total = rest + sums[0] + sums[1] + sums[2]
    cross = []
    for plane, (a, b) in enumerate(((0, 1), (0, 2), (1, 2))):
        first = 7 + 4 * plane
        parts = [arrived(first + offset, first + (offset ^ 1)) for offset in range(4)]
        same, other = parts[0] + parts[1], parts[2] + parts[3]
        along, against = parts[0] - parts[1], parts[2] - parts[3]
        both = same + other
        cross.append(same - other)
        total = total + both
        sums[a], sums[b] = sums[a] + both, sums[b] + both
        diffs[a], diffs[b] = diffs[a] + (along + against), diffs[b] + (along - against)
    shared = third * total
    block.store(fields, 0, total)
    for axis in range(3):
        block.store(fields, 1 + axis, diffs[axis])
        block.store(fields, 4 + axis, sums[axis] - shared - diffs[axis] * diffs[axis])
    for plane, (a, b) in enumerate(((0, 1), (0, 2), (1, 2))):
        block.store(fields, 7 + plane, cross[plane] - diffs[a] * diffs[b])
    block.store(fields, 10, red_total)


def over_rows(geometry, first, size, blocks, stage):
    trip = size * blocks
    rest = -2 * first % trip
    assert TILE % trip == 0 and rest % min(size, rest or size) == 0

    def run(start, count, step_size):
        for offset in range(0, count, step_size):
            row = start + offset
            stage(Block(geometry, [(row, row, step_size)], inner=True))

    def step(index, carry):
        run(first + index * trip, trip, size)
        return carry

    trips = (geometry.live - 2 * first - rest) // trip
    lax.fori_loop(0, trips, step, 0)
    if rest:
        run(geometry.live - first - rest, rest, min(size, rest))


def block_tiles():
    return lax.broadcasted_iota(jnp.int32, (SUBLANES, LANES), 0)


def roll_tiles(block, amount):
    return pltpu.roll(block, amount % SUBLANES, 0)


def pack_blocks(blocks):
    tiles, rest = block_tiles(), blocks[GROUP - 1]
    packed = []
    for number, block in enumerate(blocks[: GROUP - 1]):
        low, high = 2 * number + 1, 2 * number + 2
        block = jnp.where(tiles == 0, roll_tiles(rest, -low), block)
        packed.append(jnp.where(tiles == SUBLANES - 1, roll_tiles(rest, SUBLANES - 1 - high), block))
    return packed


def unpack_blocks(packed):
    tiles, rest = block_tiles(), None
    for number, block in enumerate(packed):
        low, high = 2 * number + 1, 2 * number + 2
        part = jnp.where(tiles == low, roll_tiles(block, low), roll_tiles(block, high - SUBLANES + 1))
        rest = part if rest is None else jnp.where(tiles >= low, part, rest)
    return list(packed) + [rest]


def flat_view(ref):
    rows, width, lanes = ref.shape
    return ref.reshape(rows * width, lanes)


def spread_tile(raw, raw_solid, index, row, target, target_row):
    source = raw_solid if index == FIELDS else raw.at[index]
    width = target.shape[1]
    for tile in range(OWN_TILES):
        values = source[pl.ds(row, SUBLANES), pl.ds(tile * LANES, LANES)].astype(jnp.float32)
        start = target_row * width + index * SUBLANES + 1 + tile
        flat_view(target)[pl.ds(start, SUBLANES, stride=width), :] = values


def load_kernel(
    tiles_count, density, momentum, stress, red, solid, widths,
    info, raw, raw_solid, packet, mine,
    first_tile, last_tile, held_widths, sems,
):
    row_count, flat_count = raw_solid.shape
    own_tiles = flat_count // LANES
    planes = [density] + [momentum.at[axis] for axis in range(3)]
    planes = planes + [stress.at[part] for part in range(6)] + [red, solid]
    copies = [pltpu.make_async_copy(widths, held_widths, sems.at[PLANES])]
    for index in ORDER:
        target = raw_solid if index == FIELDS else raw.at[index]
        copies.append(pltpu.make_async_copy(planes[index], target, sems.at[index]))
    for copy in copies:
        copy.start()
    tiles_index, sub_index = lax.axis_index("tiles"), lax.axis_index("sub")
    low_part = sub_index == 0
    edge_start = pl.multiple_of(jnp.where(low_part, (own_tiles - 1) * LANES, 0), LANES)

    copies[0].wait()
    live = held_widths[tiles_index] * TILE
    info[0] = live
    info[1] = (tiles_index == 0).astype(jnp.int32)
    info[2] = (tiles_index == tiles_count - 1).astype(jnp.int32)
    info[3] = sub_index

    near_cut = lax.broadcasted_iota(jnp.int32, (SUBLANES, LANES), 1) < HALF
    near_cut = near_cut == jnp.logical_not(low_part)
    near_last = pl.multiple_of(live - SUBLANES, SUBLANES)
    edges = pl.ds(edge_start, LANES)

    def plane_of(index):
        return raw_solid if index == FIELDS else raw.at[index]

    def pack_edges(pair):
        here, there = [plane_of(index) for index in ORDER[2 * pair : 2 * pair + 2]]
        for row in range(0, row_count, SUBLANES):
            rows = pl.ds(row, SUBLANES)
            beside = pltpu.roll(there[rows, edges].astype(jnp.float32), HALF, 1)
            both = jnp.where(near_cut, here[rows, edges].astype(jnp.float32), beside)
            packet[pl.ds(END_ROWS + pair * row_count + row, SUBLANES), :] = both

    targets = ((packet, jnp.logical_not(low_part)), (mine, low_part))

    def row_of(use_last, index, number_first, number_last):
        first = read_row(ByRow(first_tile), index, number_first)
        last = read_row(ByRow(last_tile), index, number_last)
        return jnp.where(use_last, last, first)

    def pack_ends(group):
        for target, use_last in targets:
            blocks = []
            for number in range(group * GROUP, (group + 1) * GROUP):
                place, extra = divmod(number, FULL)
                blocks.append(row_of(use_last, ORDER[place], extra, SUBLANES - FULL + extra))
            for number, block in enumerate(pack_blocks(blocks)):
                place = (group * (GROUP - 1) + number) * SUBLANES
                target[pl.ds(place, SUBLANES), :] = block

    for before, (copy, index) in enumerate(zip(copies[1:], ORDER)):
        place = before + 1
        copy.wait()
        for target, row in ((first_tile, 0), (last_tile, near_last)):
            spread_tile(raw, raw_solid, index, row, target, 0)
        for pair in range(before // 2, place // 2):
            pack_edges(pair)
        for group in range(before * FULL // GROUP, place * FULL // GROUP):
            pack_ends(group)
    for target, use_last in targets:
        red_row, density_row = [
            row_of(use_last, index, FULL, SUBLANES - HALO) for index in (10, 0)
        ]
        target[pl.ds(PACKED * SUBLANES, SUBLANES), :] = 2.0 * red_row - density_row


def load_inputs(arrays, widths, tiles_count):
    row_count, flat_count = arrays[0].shape
    return pl.pallas_call(
        functools.partial(load_kernel, tiles_count),
        out_shape=[
            pltpu.SMEM((4,), jnp.int32),
            jax.ShapeDtypeStruct((FIELDS, row_count, flat_count), jnp.float32),
            jax.ShapeDtypeStruct((row_count, flat_count), jnp.int32),
            jax.ShapeDtypeStruct((END_ROWS + PAIRS * row_count, LANES), jnp.float32),
            jax.ShapeDtypeStruct((END_ROWS, LANES), jnp.float32),
        ],
        in_specs=[HBM] * 6,
        out_specs=[SMEM] + [VMEM] * 4,
        scratch_shapes=[
            pltpu.VMEM((SUBLANES, PLACES * SUBLANES, LANES), jnp.float32),
            pltpu.VMEM((SUBLANES, PLACES * SUBLANES, LANES), jnp.float32),
            pltpu.SMEM(widths.shape, jnp.int32),
            pltpu.SemaphoreType.DMA((PLANES + 1,)),
        ],
        compiler_params=pltpu.CompilerParams(vmem_limit_bytes=16 * 1024 * 1024),
        name="load",
    )(*[pltpu.with_memory_space_constraint(array, pltpu.HBM) for array in (*arrays, widths)])


def spread_kernel(raw, raw_solid, spread):
    for index in range(PLANES):
        for row in range(0, raw_solid.shape[0], SUBLANES):
            spread_tile(raw, raw_solid, index, row, spread, row)


def spread_rows(raw, raw_solid):
    row_count = raw_solid.shape[0]
    return pl.pallas_call(
        spread_kernel,
        out_shape=by_row(row_count, PLACES),
        in_specs=[VMEM, VMEM],
        out_specs=VMEM,
        compiler_params=pltpu.CompilerParams(vmem_limit_bytes=16 * 1024 * 1024),
        cost_estimate=pl.CostEstimate(flops=1_000_000, bytes_accessed=4_000_000, transcendentals=0),
        name="spread",
    )(raw, raw_solid)


def join_kernel(mine, packet, spread, ends):
    ends[pl.ds(0, END_ROWS), :] = mine[...]
    ends[pl.ds(END_ROWS, END_ROWS), :] = packet[pl.ds(0, END_ROWS), :]


def join_ends(mine, packet, spread):
    return pl.pallas_call(
        join_kernel,
        out_shape=jax.ShapeDtypeStruct((2 * END_ROWS, LANES), jnp.float32),
        in_specs=[VMEM, VMEM, ANY],
        out_specs=VMEM,
        compiler_params=pltpu.CompilerParams(vmem_limit_bytes=8 * 1024 * 1024),
        name="join",
    )(mine, packet, spread)


def beside_kernel(info, spread, packet, whole):
    low_part = info[3] == 0
    row_count, width = spread.shape[:2]
    flat = flat_view(whole)
    for pair in range(PAIRS):
        for row in range(0, row_count, SUBLANES):
            both = packet[pl.ds(END_ROWS + pair * row_count + row, SUBLANES), :]
            for place, values in ((2 * pair, both), (2 * pair + 1, pltpu.roll(both, HALF, 1))):
                index = ORDER[place]
                start = row * width + index * SUBLANES
                below = jnp.where(low_part, 0.0, values)
                above = jnp.where(low_part, values, 0.0)
                flat[pl.ds(start, SUBLANES, stride=width), :] = below
                flat[pl.ds(start + SUBLANES - 1, SUBLANES, stride=width), :] = above


def put_beside(info, spread, packet):
    return pl.pallas_call(
        beside_kernel,
        out_shape=jax.ShapeDtypeStruct(spread.shape, jnp.float32),
        in_specs=[SMEM, VMEM, VMEM],
        out_specs=VMEM,
        input_output_aliases={1: 0},
        compiler_params=pltpu.CompilerParams(vmem_limit_bytes=16 * 1024 * 1024),
        name="beside",
    )(info, pltpu.with_memory_space_constraint(spread, pltpu.VMEM), packet)


def keep_rows(slab, source, first, size, live):
    for slab_row, row in slab_rows(live, first, size):
        for extra in range(size):
            slab[slab_row + extra] = source[row + extra]


def slab_rows(live, first, size):
    mirrored = SLAB - first - size
    return [(first, first - HALO), (SLAB + mirrored, live - 2 * RIM + mirrored)]


def collide_rows(geometry, before, whole, first, colours, walls, state):
    over_rows(geometry, first - 1, *COLOUR_BLOCK, lambda block: colour_stage(
        block, geometry, before, colours))
    over_rows(geometry, first, *COLLIDE_BLOCK, lambda block: collide_stage(
        block, geometry, before, whole, colours, walls, state))


def tile_copies(pieces, outs, held_row, out_row, sems):
    held, rows = pl.ds(held_row, SUBLANES), pl.ds(out_row, SUBLANES)
    parts = (
        (pieces.at[0, held], outs[0].at[rows]),
        (pieces.at[pl.ds(1, 3), held], outs[1].at[:, rows]),
        (pieces.at[pl.ds(4, 3), held], outs[2].at[pl.ds(0, 3), rows]),
        (pieces.at[pl.ds(7, 3), held], outs[2].at[pl.ds(3, 3), rows]),
        (pieces.at[10, held], outs[3].at[rows]),
    )
    return [
        pltpu.make_async_copy(source, target, sems.at[number])
        for number, (source, target) in enumerate(parts)
    ]


def gather_tiles(final, row, pieces, held_row):
    width = final.shape[1]
    start = row * width
    if not isinstance(start, int):
        start = pl.multiple_of(start, SUBLANES)
    for index in range(FIELDS):
        for tile in range(OWN_TILES):
            place = start + index * SUBLANES + 1 + tile
            pieces[index, pl.ds(held_row, SUBLANES), pl.ds(tile * LANES, LANES)] = flat_view(final)[
                pl.ds(place, SUBLANES, stride=width), :
            ]


def first_kernel(
    info, whole, moved_later, reds_later, final,
    moved_slab, reds_slab, fields_slab, moved_later_slab, reds_later_slab, final_slab,
    colours, walls, moved, reds, fields,
):
    state, later = (ByRow(moved), ByRow(reds)), (ByRow(moved_later), ByRow(reds_later))
    geometry = Geometry(info, OWN_TILES)
    live = geometry.live
    fill_wall_table(walls, geometry)
    collide_rows(geometry, ByRow(whole), ByRow(whole), 1, ByRow(colours), walls, state)
    over_rows(geometry, 2, *ARRIVE_BLOCK, lambda block: arrive_stage(
        block, geometry, walls, state, ByRow(fields)))
    keep_rows(moved_slab, moved, HALO + 1, KEPT, live)
    keep_rows(reds_slab, reds, HALO + 1, KEPT, live)
    keep_rows(fields_slab, fields, HALO + 2, KEPT, live)
    collide_rows(geometry, ByRow(fields), ByRow(whole), 3, ByRow(colours), walls, later)
    keep_rows(moved_later_slab, moved_later, HALO + 3, KEPT, live)
    keep_rows(reds_later_slab, reds_later, HALO + 3, KEPT, live)
    edges = slab_rows(live, HALO + RIM, RIM)
    rim = Block(geometry, [(row, row, RIM) for _, row in edges], True, [at for at, _ in edges])
    arrive_stage(rim, geometry, walls, later, ByRow(final_slab))

    def arrive_tile(tile, carry):
        row = tile * SUBLANES
        block = Block(geometry, [(row, row, SUBLANES)], inner=True)
        arrive_stage(block, geometry, walls, later, ByRow(final))
        return carry

    lax.fori_loop(1, jnp.minimum(SPLIT, live // SUBLANES - 1), arrive_tile, 0)


def second_kernel(
    info, moved, reds, earlier, arrived, density_out, momentum_out, stress_out, red_out,
    final, walls, pieces, zeros, sems,
):
    outs = (density_out, momentum_out, stress_out, red_out)
    row_tiles = density_out.shape[0] // SUBLANES
    state = (ByRow(moved), ByRow(reds))
    geometry = Geometry(info, OWN_TILES)
    live = geometry.live
    last = live // SUBLANES - 1
    fill_wall_table(walls, geometry)

    def copies_of(tile):
        row = pl.multiple_of(tile * SUBLANES, SUBLANES)
        return tile_copies(pieces, outs, row, row, sems.at[tile])

    def send_out(tile, source):
        row = pl.multiple_of(tile * SUBLANES, SUBLANES)
        gather_tiles(source, row, pieces, row)
        for copy in copies_of(tile):
            copy.start()

    def pass_on(tile, carry):
        send_out(tile, earlier)
        return carry

    def finish(tile, carry):
        row = tile * SUBLANES
        block = Block(geometry, [(row, row, SUBLANES)], inner=True)
        arrive_stage(block, geometry, walls, state, ByRow(final))
        send_out(tile, final)
        return carry

    def settle(tile, carry):
        for copy in copies_of(tile):
            copy.wait()
        return carry

    lax.fori_loop(1, jnp.minimum(SPLIT, last), pass_on, 0)
    zeros[...] = jnp.zeros(zeros.shape, zeros.dtype)
    dead = {}
    for tile in range(row_tiles):
        dead[tile] = tile_copies(zeros, outs, 0, tile * SUBLANES, sems.at[tile])

        @pl.when(tile * SUBLANES >= live)
        def _():
            for copy in dead[tile]:
                copy.start()

    lax.fori_loop(SPLIT, last, finish, 0)
    lax.fori_loop(1, last, settle, 0)
    for tile in range(row_tiles):

        @pl.when(tile * SUBLANES >= live)
        def _():
            for copy in dead[tile]:
                copy.wait()


def scratch_of(shape):
    return pltpu.VMEM(shape.shape, shape.dtype)


def pieces_of(rows, flat_count):
    return pltpu.VMEM((FIELDS, rows, flat_count), jnp.float32)


def run_first(info, whole):
    rows = whole.shape[0]
    shapes = [by_row(rows, count) for count in (HELD, REDS, FIELDS)]
    slabs = [by_row(2 * SLAB, count) for count in (HELD, REDS, FIELDS, HELD, REDS, FIELDS)]
    scratch = [by_row(rows, 4), by_row(4, 3)]
    scratch = scratch + [by_row(rows, count) for count in (HELD, REDS, FIELDS)]
    return pl.pallas_call(
        first_kernel,
        out_shape=shapes + slabs,
        in_specs=[SMEM, VMEM],
        out_specs=[VMEM] * 9,
        scratch_shapes=[scratch_of(shape) for shape in scratch],
        compiler_params=pltpu.CompilerParams(vmem_limit_bytes=24 * 1024 * 1024),
        cost_estimate=pl.CostEstimate(flops=20_000_000, bytes_accessed=8_000_000, transcendentals=0),
        name="first",
    )(info, whole)


def run_second(info, state, earlier, arrived, arrays):
    row_count, flat_count = arrays[0].shape
    return pl.pallas_call(
        second_kernel,
        out_shape=[jax.ShapeDtypeStruct(array.shape, jnp.float32) for array in arrays[:4]],
        in_specs=[SMEM] + [VMEM] * 3 + [ANY],
        out_specs=[ANY] * 4,
        scratch_shapes=[
            scratch_of(by_row(row_count, FIELDS)),
            scratch_of(by_row(4, 3)),
            pieces_of(row_count, flat_count),
            pieces_of(SUBLANES, flat_count),
            pltpu.SemaphoreType.DMA((row_count // SUBLANES, OUT_COPIES)),
        ],
        compiler_params=pltpu.CompilerParams(vmem_limit_bytes=24 * 1024 * 1024),
        cost_estimate=pl.CostEstimate(flops=20_000_000, bytes_accessed=8_000_000, transcendentals=0),
        name="second",
    )(info, *state, earlier, arrived)


def follow_kernel(ends, kept, out):
    out[pl.ds(PACKED * SUBLANES, 1), :] = jnp.zeros((1, LANES), jnp.float32)


def follow(ends, kept):
    return pl.pallas_call(
        follow_kernel,
        out_shape=jax.ShapeDtypeStruct(ends.shape, jnp.float32),
        in_specs=[VMEM, ANY],
        out_specs=VMEM,
        input_output_aliases={0: 0},
        compiler_params=pltpu.CompilerParams(vmem_limit_bytes=8 * 1024 * 1024),
        name="follow",
    )(pltpu.with_memory_space_constraint(ends, pltpu.VMEM), kept)


def outer_kernel(info, whole, arrived, passed, *refs):
    outs = refs[10:14]
    moved, reds, fields, moved_later, reds_later, final = refs[14:20]
    start_fields, colours, walls, pieces, sems = refs[20:]
    state, later = (ByRow(moved), ByRow(reds)), (ByRow(moved_later), ByRow(reds_later))
    geometry = Geometry(info, OWN_TILES)
    live = geometry.live
    low_part = info[3] == 0
    fill_wall_table(walls, geometry)

    def ends_of(ref, half):
        blocks = []
        for group in range(FULL * PLANES // GROUP):
            first = half * (PACKED + 1) + group * (GROUP - 1)
            packed = [ref[pl.ds((first + k) * SUBLANES, SUBLANES), :] for k in range(GROUP - 1)]
            blocks = blocks + unpack_blocks(packed)
        last = half * (PACKED + 1) + PACKED
        return blocks + [ref[pl.ds(last * SUBLANES, SUBLANES), :]]

    tiles = block_tiles()
    middle = (tiles >= 1) & (tiles <= OWN_TILES)

    def widened(own, other):
        beside = jnp.where(tiles == 0, roll_tiles(other, -OWN_TILES), roll_tiles(other, OWN_TILES))
        return jnp.where(geometry.domain, jnp.where(middle, own, beside), 0.0)

    straight = [widened(*pair) for pair in zip(ends_of(arrived, 0), ends_of(arrived, 1))]
    crossed = [widened(*pair) for pair in zip(ends_of(passed, 1), ends_of(passed, 0))]
    below = [jnp.where(low_part, *pair) for pair in zip(straight, crossed)]
    above = [jnp.where(low_part, *pair) for pair in zip(crossed, straight)]

    for number in range(FULL * PLANES):
        place, extra = divmod(number, FULL)
        index = ORDER[place]
        write_row(ByRow(start_fields), index, 1 + extra, below[number])
        write_row(ByRow(start_fields), index, 2 * SLAB - HALO + extra, above[number])
    for row, colour in ((0, below[-1]), (2 * SLAB - 1, above[-1])):
        write_row(ByRow(start_fields), 0, row, jnp.zeros((SUBLANES, LANES), jnp.float32))
        write_row(ByRow(start_fields), 10, row, 0.5 * colour)
    for slab_row, row in slab_rows(live, HALO, FULL):
        for extra in range(FULL):
            start_fields[slab_row + extra] = whole[row + extra]

    def block(first, count):
        return Block(geometry, [(row, at, count) for at, row in slab_rows(live, first, count)])

    held, solids, marks = ByRow(fields), ByRow(start_fields), ByRow(colours)
    colour_stage(block(0, 6), geometry, solids, marks)
    collide_stage(block(1, 4), geometry, solids, solids, marks, walls, state)
    arrive_stage(block(2, 4), geometry, walls, state, held)
    colour_stage(block(2, 6), geometry, held, marks)
    collide_stage(block(3, 4), geometry, held, solids, marks, walls, later)
    arrive_stage(block(4, 4), geometry, walls, later, ByRow(final))

    copies = []
    for side, row, out_row in ((0, HALO, 0), (1, SLAB, live - SUBLANES)):
        gather_tiles(final, row, pieces, side * SUBLANES)
        out_row = pl.multiple_of(out_row, SUBLANES)
        copies = copies + tile_copies(pieces, outs, side * SUBLANES, out_row, sems.at[side])
    for copy in copies:
        copy.start()
    for copy in copies:
        copy.wait()


def run_outer(info, whole, arrived, passed, slabs, outs):
    flat_count = outs[0].shape[1]
    shapes = [jax.ShapeDtypeStruct(array.shape, jnp.float32) for array in (*outs, *slabs)]
    slabs = [pltpu.with_memory_space_constraint(slab, pltpu.VMEM) for slab in slabs]
    aliases = {4 + number: 4 + number for number in range(6)}
    aliases.update({10 + number: number for number in range(4)})
    return pl.pallas_call(
        outer_kernel,
        out_shape=shapes,
        in_specs=[SMEM] + [VMEM] * 9 + [ANY] * 4,
        out_specs=[ANY] * 4 + [VMEM] * 6,
        scratch_shapes=[
            scratch_of(by_row(2 * SLAB, PLACES)),
            scratch_of(by_row(2 * SLAB, 4)),
            scratch_of(by_row(4, 3)),
            pieces_of(2 * SUBLANES, flat_count),
            pltpu.SemaphoreType.DMA((2, OUT_COPIES)),
        ],
        input_output_aliases=aliases,
        compiler_params=pltpu.CompilerParams(vmem_limit_bytes=24 * 1024 * 1024),
        name="outer",
    )(info, whole, arrived, passed, *slabs, *outs)


def body(density, momentum, stress, red_density, solid, widths):
    tiles_count = lax.axis_size("tiles")
    arrays = (density, momentum, stress, red_density, solid)
    info, raw, raw_solid, packet, mine = load_inputs(arrays, widths, tiles_count)
    info = pltpu.with_memory_space_constraint(info, pltpu.SMEM)
    swap = [(0, 1), (1, 0)]
    packet = lax.ppermute(packet, "sub", swap)
    spread = spread_rows(raw, raw_solid)
    ends = join_ends(mine, packet, spread)
    route = [(2 * k, 2 * k + 2) for k in range(tiles_count - 1)]
    route = route + [(2 * k + 3, 2 * k + 1) for k in range(tiles_count - 1)]
    arrived = lax.ppermute(ends, ("tiles", "sub"), route)
    whole = put_beside(info, spread, packet)
    moved, reds, earlier, *slabs = run_first(info, whole)
    arrived = follow(arrived, slabs[-1])
    passed = lax.ppermute(arrived, "sub", swap)
    outs = run_second(info, (moved, reds), earlier, arrived, arrays)
    return tuple(run_outer(info, whole, arrived, passed, slabs, outs)[:4])


def solution(mesh):
    in_specs = (
        P(("groups", "tiles"), "sub"),
        P(None, ("groups", "tiles"), "sub"),
        P(None, ("groups", "tiles"), "sub"),
        P(("groups", "tiles"), "sub"),
        P(("groups", "tiles"), "sub"),
        P("groups"),
    )
    out_specs = (
        P(("groups", "tiles"), "sub"),
        P(None, ("groups", "tiles"), "sub"),
        P(None, ("groups", "tiles"), "sub"),
        P(("groups", "tiles"), "sub"),
    )
    return jax.shard_map(body, mesh=mesh, in_specs=in_specs, out_specs=out_specs, check_vma=False)
```

```python
import functools

import jax
import jax.numpy as jnp
from jax import lax
from jax.experimental import pallas as pl
from jax.experimental.pallas import tpu as pltpu
from jax.sharding import PartitionSpec as P

TILE = 16
STEPS = 2
RELAX_TIME = 0.8
SURFACE = 0.1
SEPARATION = 0.7

LANES = 128
SUBLANES = 8
FULL = 3
HALO = FULL + 1
FIELDS = 11
PLANES = FIELDS + 1
MOVED = 19
REDS = 5
HELD = MOVED + 1
RIM = 4
SLAB = HALO + 2 * RIM
OWN_TILES = SUBLANES - 2
GROUP = 4
PACKED = FULL * PLANES // GROUP * (GROUP - 1)
END_ROWS = (PACKED + 1) * SUBLANES
HALF = LANES // 2
ORDER = (0, 1, 2, 3, 10, 11, 4, 5, 6, 7, 8, 9)
PAIRS = PLANES // 2
PLACES = PLANES + 1
KEPT = 2
OUT_COPIES = 4
COLOUR_BLOCK = (16, 1)
COLLIDE_BLOCK = (8, 1)
ARRIVE_BLOCK = (16, 1)
VMEM = pl.BlockSpec(memory_space=pltpu.VMEM)
SMEM = pl.BlockSpec(memory_space=pltpu.SMEM)
ANY = pl.BlockSpec(memory_space=pl.ANY)
HBM = pl.BlockSpec(memory_space=pltpu.HBM)


class Rows:
    def __init__(self, parts):
        self.parts = parts

    def _with(self, other, operation):
        others = other.parts if isinstance(other, Rows) else [other] * len(self.parts)
        return Rows([operation(one, two) for one, two in zip(self.parts, others)])

    def __add__(self, other):
        return self._with(other, lambda one, two: one + two)

    def __sub__(self, other):
        return self._with(other, lambda one, two: one - two)

    def __rsub__(self, other):
        return self._with(other, lambda one, two: two - one)

    def __mul__(self, other):
        return self._with(other, lambda one, two: one * two)

    def __or__(self, other):
        return self._with(other, lambda one, two: one | two)

    def __eq__(self, other):
        return self._with(other, lambda one, two: one == two)

    __radd__, __rmul__, __ror__ = __add__, __mul__, __or__

    def each(self, operation):
        return Rows([operation(part) for part in self.parts])


def select(mask, yes, no):
    count = max(len(item.parts) for item in (mask, yes, no) if isinstance(item, Rows))
    columns = [
        item.parts if isinstance(item, Rows) else [item] * count for item in (mask, yes, no)
    ]
    return Rows([jnp.where(*row) for row in zip(*columns)])


def roll_lanes(values, amount):
    return values.each(lambda part: pltpu.roll(part, amount % LANES, 1))


def roll_sublanes(values, amount):
    return values.each(lambda part: pltpu.roll(part, amount % SUBLANES, 0))


class Geometry:
    def __init__(self, info, own_tiles):
        live, first, last, sub_index = info[0], info[1], info[2], info[3]
        self.live = live
        self.low_row = jnp.where(first == 1, 0, -1000)
        self.high_row = jnp.where(last == 1, live, 1000)
        shape = (SUBLANES, LANES)
        lane = lax.broadcasted_iota(jnp.int32, shape, 1)
        tile = lax.broadcasted_iota(jnp.int32, shape, 0)
        depth = lane & (TILE - 1)
        low_part = sub_index == 0
        high_part = sub_index == 1
        z_walls = {1: depth == 0, -1: depth == TILE - 1}
        y_walls = {
            1: (tile == 1) & (lane < TILE) & low_part,
            -1: (tile == own_tiles) & (lane >= LANES - TILE) & high_part,
        }
        self.walls = {(0, vel_z): wall for vel_z, wall in z_walls.items()}
        for vel_y, y_wall in y_walls.items():
            self.walls[vel_y, 0] = y_wall
            for vel_z, z_wall in z_walls.items():
                self.walls[vel_y, vel_z] = y_wall | z_wall
        own = (tile >= 1) & (tile <= own_tiles)
        self.domain = own | ((tile == own_tiles + 1) & low_part) | ((tile == 0) & high_part)
        self.first_lanes = lane < TILE
        self.last_lanes = lane >= LANES - TILE

    def from_low_y(self, values):
        return roll_lanes(select(self.last_lanes, roll_sublanes(values, 1), values), TILE)

    def from_high_y(self, values):
        return roll_lanes(select(self.first_lanes, roll_sublanes(values, -1), values), -TILE)

    def from_low_z(self, values):
        return select(self.walls[0, 1], 0.0, roll_lanes(values, 1))

    def from_high_z(self, values):
        return select(self.walls[0, -1], 0.0, roll_lanes(values, -1))


def flat_rows(row, count, tile_offset=0):
    start = row * SUBLANES
    if not isinstance(start, int):
        start = pl.multiple_of(start, SUBLANES)
    return pl.ds(start + tile_offset, count * SUBLANES)


class ByRow:
    def __init__(self, ref):
        self.ref = ref


def by_row(rows, count):
    return jax.ShapeDtypeStruct((rows, count * SUBLANES, LANES), jnp.float32)


def place_of(ref, index, row, tile_offset=0):
    if isinstance(ref, ByRow):
        return ref.ref, row, pl.ds(index * SUBLANES + tile_offset, SUBLANES)
    return ref, index, flat_rows(row, 1, tile_offset)


def read_row(ref, index, row, tile_offset=0):
    ref, first, second = place_of(ref, index, row, tile_offset)
    return ref[first, second, :]


def write_row(ref, index, row, values):
    ref, first, second = place_of(ref, index, row)
    ref[first, second, :] = values


class Block:
    def __init__(self, geometry, spans, inner=False, store_rows=None):
        self.spans = spans
        self.store_rows = store_rows or [local for row, local, count in spans]
        rows = [row + extra for row, local, count in spans for extra in range(count)]
        self.inner = inner
        rows = [row + extra for row, local, count in spans for extra in range(count)]
        if inner:
            self.x_walls = {}
            self.valid = geometry.domain
            self.kinds = [0]
            return
        ids = Rows([row + jnp.zeros((SUBLANES, LANES), jnp.int32) for row in rows])
        self.x_walls = {1: ids == geometry.low_row, -1: ids == geometry.high_row - 1}
        self.valid = ids.each(
            lambda part: geometry.domain & (part >= geometry.low_row) & (part < geometry.high_row)
        )
        self.kinds = [
            jnp.where(row == geometry.low_row, 1, 0) + jnp.where(row == geometry.high_row - 1, 2, 0)
            for row in rows
        ]

    def load(self, ref, index, offset=0, tile_offset=0):
        return Rows([
            read_row(ref, index, local + offset + extra, tile_offset)
            for row, local, count in self.spans
            for extra in range(count)
        ])

    def store(self, ref, index, values):
        targets = [
            target + extra
            for (row, local, count), target in zip(self.spans, self.store_rows)
            for extra in range(count)
        ]
        for target, part in zip(targets, values.parts):
            write_row(ref, index, target, part)

    def wall_terms(self, walls, position):
        terms = [walls[position, flat_rows(kind, 1), :] for kind in self.kinds]
        return terms[0] if self.inner else Rows(terms)


def fill_wall_table(walls, geometry):
    one = jnp.ones((SUBLANES, LANES), jnp.float32)
    up_y, down_y, up_z, down_z = [
        jnp.where(geometry.walls[key], 0.0, one) for key in ((-1, 0), (1, 0), (0, -1), (0, 1))
    ]
    sum_y, sum_z = up_y + down_y, up_z + down_z
    for kind, (up_x, down_x) in enumerate(((1.0, 1.0), (1.0, 0.0), (0.0, 1.0))):
        sum_x = up_x + down_x
        around_x = 2.0 + sum_y + sum_z
        total = 12.0 + 2.0 * (sum_x + sum_y + sum_z) + sum_x * (sum_y + sum_z) + sum_y * sum_z
        rows = (
            (up_x - down_x) * around_x,
            (up_y - down_y) * (2.0 + sum_x + sum_z),
            (up_z - down_z) * (2.0 + sum_x + sum_y),
            36.0 - total,
        )
        for position, row in enumerate(rows):
            walls[position, flat_rows(kind, 1), :] = row


VELOCITIES = tuple(
    tuple(sign if axis == place else 0 for place in range(3)) for axis in range(3) for sign in (1, -1)
) + tuple(
    tuple({a: one, b: two}.get(place, 0) for place in range(3))
    for a, b in ((0, 1), (0, 2), (1, 2))
    for one, two in ((1, 1), (-1, -1), (1, -1), (-1, 1))
)
VELOCITIES = ((0, 0, 0),) + VELOCITIES


def colour_stage(block, geometry, fields, colours):
    density = block.load(fields, 0)
    red = block.load(fields, 10)
    colour = select(block.valid, 2.0 * red - density, 0.0)
    along_y = geometry.from_low_y(colour) + geometry.from_high_y(colour)
    along_z = geometry.from_low_z(colour) + geometry.from_high_z(colour)
    block.store(colours, 0, colour)
    block.store(colours, 1, 2.0 * colour + (along_y + along_z))
    block.store(colours, 2, along_y)
    block.store(colours, 3, along_z)


def collide_stage(block, geometry, fields, solids, colours, walls, state):
    relaxing = 1.0 - 1.0 / RELAX_TIME
    third = 1.0 / 3.0
    colour = block.load(colours, 0)
    doubled = 2.0 * colour + (block.load(colours, 0, -1) + block.load(colours, 0, 1))
    term_y = doubled + block.load(colours, 3)
    term_z = doubled + block.load(colours, 2)
    grad_x = block.load(colours, 1, 1) - block.load(colours, 1, -1)
    grad_y = geometry.from_high_y(term_y) - geometry.from_low_y(term_y)
    grad_z = geometry.from_high_z(term_z) - geometry.from_low_z(term_z)
    if not block.inner:
        grad_x = grad_x - block.wall_terms(walls, 0) * colour
    grad_y = grad_y - block.wall_terms(walls, 1) * colour
    grad_z = grad_z - block.wall_terms(walls, 2) * colour

    fluid = block.load(solids, PLANES - 1) == 0.0
    density = block.load(fields, 0)
    red = block.load(fields, 10)
    flux = [block.load(fields, 1 + axis) for axis in range(3)]
    stress = [block.load(fields, 4 + part) for part in range(6)]
    square_xx, square_yy, square_zz = grad_x * grad_x, grad_y * grad_y, grad_z * grad_z
    square = square_xx + square_yy + square_zz
    inverse = select(fluid, (1.0 + square * (1.0 / 144.0)).each(lax.rsqrt), 0.0)
    trace = third * square
    strength = (SURFACE / (8.0 * 144.0)) * inverse
    keep = select(fluid, relaxing / 8.0, 1.0 / 8.0)
    eighths = [0.125 * part for part in flux]
    own = [
        eighths[axis] * flux[axis] + (keep * stress[axis] + strength * (squared - trace))
        for axis, squared in enumerate((square_xx, square_yy, square_zz))
    ]
    strength, keep = 2.0 * strength, 2.0 * keep
    quarters = [2.0 * part for part in eighths[:2]]
    grads = (grad_x, grad_y, grad_z)
    cross = [
        quarters[a] * flux[b] + (keep * stress[3 + plane] + strength * (grads[a] * grads[b]))
        for plane, (a, b) in enumerate(((0, 1), (0, 2), (1, 2)))
    ]
    base = density * (1.0 / 36.0) - third * (own[0] + own[1] + own[2])
    sign = select(fluid, 1.0 / 12.0, -1.0 / 12.0)
    run = [sign * part for part in flux]
    mixing = ((SEPARATION / 144.0) * red) * ((density - red) * inverse)
    red_run = [0.5 * part + mixing * grad for part, grad in zip(run, grads)]
    moved, reds = state
    block.store(moved, 0, 12.0 * base)
    straight = [base + part for part in own]
    for axis in range(3):
        middle = 2.0 * straight[axis]
        swing = 2.0 * run[axis]
        block.store(moved, 1 + 2 * axis, middle + swing)
        block.store(moved, 2 + 2 * axis, middle - swing)
    for plane, (a, b) in enumerate(((0, 1), (0, 2), (1, 2))):
        middle = straight[a] + own[b]
        same, other = middle + cross[plane], middle - cross[plane]
        along, against = run[a] + run[b], run[a] - run[b]
        first = 7 + 4 * plane
        block.store(moved, first, same + along)
        block.store(moved, first + 1, same - along)
        block.store(moved, first + 2, other + against)
        block.store(moved, first + 3, other - against)

    red_base = select(block.valid, red * (1.0 / 36.0), 0.0)
    red_run = [select(block.valid, part, 0.0) for part in red_run]
    block.store(reds, 0, red_base)
    block.store(reds, 1, red_base + red_run[0])
    block.store(reds, 2, red_base - red_run[0])
    block.store(reds, 3, red_run[1])
    block.store(reds, 4, red_run[2])


def arrive_stage(block, geometry, walls, state, fields):
    third = 1.0 / 3.0
    moved, reds = state
    own = [None] * MOVED

    def here(direction):
        if own[direction] is None:
            own[direction] = block.load(moved, direction)
        return own[direction]

    def arrived(direction, opposite):
        vel_x, vel_y, vel_z = VELOCITIES[direction]
        values = here(direction) if vel_x == 0 else block.load(moved, direction, -vel_x)
        if vel_y != 0:
            beside = block.load(moved, direction, -vel_x, -vel_y)
            leaving = geometry.last_lanes if vel_y == 1 else geometry.first_lanes
            values = select(leaving, beside, values)
        if vel_y != 0 or vel_z != 0:
            values = roll_lanes(values, TILE * vel_y + vel_z)
        masks = []
        if vel_x in block.x_walls:
            masks.append(block.x_walls[vel_x])
        if (vel_y, vel_z) in geometry.walls:
            masks.append(geometry.walls[vel_y, vel_z])
        if not masks:
            return values
        wall = functools.reduce(lambda one, two: one | two, masks)
        return select(wall, here(opposite), values)

    red = block.load(reds, 0)
    red_y = block.load(reds, 3)
    red_z = block.load(reds, 4)
    from_x = block.load(reds, 1, -1) + block.load(reds, 2, 1)
    spread = 2.0 * red + from_x
    spread_y = 2.0 * red_y + (block.load(reds, 3, -1) + block.load(reds, 3, 1))
    spread_z = 2.0 * red_z + (block.load(reds, 4, -1) + block.load(reds, 4, 1))
    up_y, down_y = red + red_y, red - red_y
    low_y = (
        (spread + spread_y)
        + geometry.from_low_z(up_y + red_z)
        + geometry.from_high_z(up_y - red_z)
    )
    high_y = (
        (spread - spread_y)
        + geometry.from_low_z(down_y + red_z)
        + geometry.from_high_z(down_y - red_z)
    )
    bounced = (
        block.wall_terms(walls, 3) * red
        - block.wall_terms(walls, 1) * red_y
        - block.wall_terms(walls, 2) * red_z
    )
    if not block.inner:
        bounced = bounced - block.wall_terms(walls, 0) * (block.load(reds, 1) - red)
    red_total = (
        12.0 * red
        + 2.0 * from_x
        + geometry.from_low_z(spread + spread_z)
        + geometry.from_high_z(spread - spread_z)
        + geometry.from_low_y(low_y)
        + geometry.from_high_y(high_y)
        + bounced
    )
    rest = here(0)
    sums, diffs = [], []
    for axis in range(3):
        up = arrived(1 + 2 * axis, 2 + 2 * axis)
        down = arrived(2 + 2 * axis, 1 + 2 * axis)
        sums.append(up + down)
        diffs.append(up - down)
    total = rest + sums[0] + sums[1] + sums[2]
    cross = []
    for plane, (a, b) in enumerate(((0, 1), (0, 2), (1, 2))):
        first = 7 + 4 * plane
        parts = [arrived(first + offset, first + (offset ^ 1)) for offset in range(4)]
        same, other = parts[0] + parts[1], parts[2] + parts[3]
        along, against = parts[0] - parts[1], parts[2] - parts[3]
        both = same + other
        cross.append(same - other)
        total = total + both
        sums[a], sums[b] = sums[a] + both, sums[b] + both
        diffs[a], diffs[b] = diffs[a] + (along + against), diffs[b] + (along - against)
    shared = third * total
    block.store(fields, 0, total)
    for axis in range(3):
        block.store(fields, 1 + axis, diffs[axis])
        block.store(fields, 4 + axis, sums[axis] - shared - diffs[axis] * diffs[axis])
    for plane, (a, b) in enumerate(((0, 1), (0, 2), (1, 2))):
        block.store(fields, 7 + plane, cross[plane] - diffs[a] * diffs[b])
    block.store(fields, 10, red_total)


def over_rows(geometry, first, size, blocks, stage):
    trip = size * blocks
    rest = -2 * first % trip
    assert TILE % trip == 0 and rest % min(size, rest or size) == 0

    def run(start, count, step_size):
        for offset in range(0, count, step_size):
            row = start + offset
            stage(Block(geometry, [(row, row, step_size)], inner=True))

    def step(index, carry):
        run(first + index * trip, trip, size)
        return carry

    trips = (geometry.live - 2 * first - rest) // trip
    lax.fori_loop(0, trips, step, 0)
    if rest:
        run(geometry.live - first - rest, rest, min(size, rest))


def block_tiles():
    return lax.broadcasted_iota(jnp.int32, (SUBLANES, LANES), 0)


def roll_tiles(block, amount):
    return pltpu.roll(block, amount % SUBLANES, 0)


def pack_blocks(blocks):
    tiles, rest = block_tiles(), blocks[GROUP - 1]
    packed = []
    for number, block in enumerate(blocks[: GROUP - 1]):
        low, high = 2 * number + 1, 2 * number + 2
        block = jnp.where(tiles == 0, roll_tiles(rest, -low), block)
        packed.append(jnp.where(tiles == SUBLANES - 1, roll_tiles(rest, SUBLANES - 1 - high), block))
    return packed


def unpack_blocks(packed):
    tiles, rest = block_tiles(), None
    for number, block in enumerate(packed):
        low, high = 2 * number + 1, 2 * number + 2
        part = jnp.where(tiles == low, roll_tiles(block, low), roll_tiles(block, high - SUBLANES + 1))
        rest = part if rest is None else jnp.where(tiles >= low, part, rest)
    return list(packed) + [rest]


def flat_view(ref):
    rows, width, lanes = ref.shape
    return ref.reshape(rows * width, lanes)


def spread_tile(raw, raw_solid, index, row, target, target_row):
    source = raw_solid if index == FIELDS else raw.at[index]
    width = target.shape[1]
    for tile in range(OWN_TILES):
        values = source[pl.ds(row, SUBLANES), pl.ds(tile * LANES, LANES)].astype(jnp.float32)
        start = target_row * width + index * SUBLANES + 1 + tile
        flat_view(target)[pl.ds(start, SUBLANES, stride=width), :] = values


def load_kernel(
    tiles_count, density, momentum, stress, red, solid, widths,
    info, raw, raw_solid, packet, mine,
    first_tile, last_tile, held_widths, sems,
):
    row_count, flat_count = raw_solid.shape
    own_tiles = flat_count // LANES
    copies = [
        pltpu.make_async_copy(widths, held_widths, sems.at[0]),
        pltpu.make_async_copy(density, raw.at[0], sems.at[1]),
        pltpu.make_async_copy(momentum, raw.at[pl.ds(1, 3)], sems.at[2]),
        pltpu.make_async_copy(red, raw.at[10], sems.at[3]),
        pltpu.make_async_copy(solid, raw_solid, sems.at[4]),
        pltpu.make_async_copy(stress.at[pl.ds(0, 3)], raw.at[pl.ds(4, 3)], sems.at[5]),
        pltpu.make_async_copy(stress.at[pl.ds(3, 3)], raw.at[pl.ds(7, 3)], sems.at[6]),
    ]
    for copy in copies:
        copy.start()
    tiles_index, sub_index = lax.axis_index("tiles"), lax.axis_index("sub")
    low_part = sub_index == 0
    edge_start = pl.multiple_of(jnp.where(low_part, (own_tiles - 1) * LANES, 0), LANES)

    copies[0].wait()
    live = held_widths[tiles_index] * TILE
    info[0] = live
    info[1] = (tiles_index == 0).astype(jnp.int32)
    info[2] = (tiles_index == tiles_count - 1).astype(jnp.int32)
    info[3] = sub_index

    near_cut = lax.broadcasted_iota(jnp.int32, (SUBLANES, LANES), 1) < HALF
    near_cut = near_cut == jnp.logical_not(low_part)
    near_last = pl.multiple_of(live - SUBLANES, SUBLANES)
    edges = pl.ds(edge_start, LANES)

    def plane_of(index):
        return raw_solid if index == FIELDS else raw.at[index]

    def pack_edges(pair):
        here, there = [plane_of(index) for index in ORDER[2 * pair : 2 * pair + 2]]
        for row in range(0, row_count, SUBLANES):
            rows = pl.ds(row, SUBLANES)
            beside = pltpu.roll(there[rows, edges].astype(jnp.float32), HALF, 1)
            both = jnp.where(near_cut, here[rows, edges].astype(jnp.float32), beside)
            packet[pl.ds(END_ROWS + pair * row_count + row, SUBLANES), :] = both

    targets = ((packet, jnp.logical_not(low_part)), (mine, low_part))

    def row_of(use_last, index, number_first, number_last):
        first = read_row(ByRow(first_tile), index, number_first)
        last = read_row(ByRow(last_tile), index, number_last)
        return jnp.where(use_last, last, first)

    def pack_ends(group):
        for target, use_last in targets:
            blocks = []
            for number in range(group * GROUP, (group + 1) * GROUP):
                place, extra = divmod(number, FULL)
                blocks.append(row_of(use_last, ORDER[place], extra, SUBLANES - FULL + extra))
            for number, block in enumerate(pack_blocks(blocks)):
                place = (group * (GROUP - 1) + number) * SUBLANES
                target[pl.ds(place, SUBLANES), :] = block

    place = 0
    for copy, count in zip(copies[1:], (1, 3, 1, 1, 3, 3)):
        copy.wait()
        before, place = place, place + count
        for index in ORDER[before:place]:
            for target, row in ((first_tile, 0), (last_tile, near_last)):
                spread_tile(raw, raw_solid, index, row, target, 0)
        for pair in range(before // 2, place // 2):
            pack_edges(pair)
        for group in range(before * FULL // GROUP, place * FULL // GROUP):
            pack_ends(group)
    for target, use_last in targets:
        red_row, density_row = [
            row_of(use_last, index, FULL, SUBLANES - HALO) for index in (10, 0)
        ]
        target[pl.ds(PACKED * SUBLANES, SUBLANES), :] = 2.0 * red_row - density_row


def load_inputs(arrays, widths, tiles_count):
    row_count, flat_count = arrays[0].shape
    return pl.pallas_call(
        functools.partial(load_kernel, tiles_count),
        out_shape=[
            pltpu.SMEM((4,), jnp.int32),
            jax.ShapeDtypeStruct((FIELDS, row_count, flat_count), jnp.float32),
            jax.ShapeDtypeStruct((row_count, flat_count), jnp.int32),
            jax.ShapeDtypeStruct((END_ROWS + PAIRS * row_count, LANES), jnp.float32),
            jax.ShapeDtypeStruct((END_ROWS, LANES), jnp.float32),
        ],
        in_specs=[HBM] * 6,
        out_specs=[SMEM] + [VMEM] * 4,
        scratch_shapes=[
            pltpu.VMEM((SUBLANES, PLACES * SUBLANES, LANES), jnp.float32),
            pltpu.VMEM((SUBLANES, PLACES * SUBLANES, LANES), jnp.float32),
            pltpu.SMEM(widths.shape, jnp.int32),
            pltpu.SemaphoreType.DMA((7,)),
        ],
        compiler_params=pltpu.CompilerParams(vmem_limit_bytes=16 * 1024 * 1024),
        name="load",
    )(*[pltpu.with_memory_space_constraint(array, pltpu.HBM) for array in (*arrays, widths)])


def spread_kernel(raw, raw_solid, spread):
    for index in range(PLANES):
        for row in range(0, raw_solid.shape[0], SUBLANES):
            spread_tile(raw, raw_solid, index, row, spread, row)


def spread_rows(raw, raw_solid):
    row_count = raw_solid.shape[0]
    return pl.pallas_call(
        spread_kernel,
        out_shape=by_row(row_count, PLACES),
        in_specs=[VMEM, VMEM],
        out_specs=VMEM,
        compiler_params=pltpu.CompilerParams(vmem_limit_bytes=16 * 1024 * 1024),
        cost_estimate=pl.CostEstimate(flops=1_000_000, bytes_accessed=4_000_000, transcendentals=0),
        name="spread",
    )(raw, raw_solid)


def join_kernel(mine, packet, spread, ends):
    ends[pl.ds(0, END_ROWS), :] = mine[...]
    ends[pl.ds(END_ROWS, END_ROWS), :] = packet[pl.ds(0, END_ROWS), :]


def join_ends(mine, packet, spread):
    return pl.pallas_call(
        join_kernel,
        out_shape=jax.ShapeDtypeStruct((2 * END_ROWS, LANES), jnp.float32),
        in_specs=[VMEM, VMEM, ANY],
        out_specs=VMEM,
        compiler_params=pltpu.CompilerParams(vmem_limit_bytes=8 * 1024 * 1024),
        name="join",
    )(mine, packet, spread)


def beside_kernel(info, spread, packet, whole):
    low_part = info[3] == 0
    row_count, width = spread.shape[:2]
    flat = flat_view(whole)
    for pair in range(PAIRS):
        for row in range(0, row_count, SUBLANES):
            both = packet[pl.ds(END_ROWS + pair * row_count + row, SUBLANES), :]
            for place, values in ((2 * pair, both), (2 * pair + 1, pltpu.roll(both, HALF, 1))):
                index = ORDER[place]
                start = row * width + index * SUBLANES
                below = jnp.where(low_part, 0.0, values)
                above = jnp.where(low_part, values, 0.0)
                flat[pl.ds(start, SUBLANES, stride=width), :] = below
                flat[pl.ds(start + SUBLANES - 1, SUBLANES, stride=width), :] = above


def put_beside(info, spread, packet):
    return pl.pallas_call(
        beside_kernel,
        out_shape=jax.ShapeDtypeStruct(spread.shape, jnp.float32),
        in_specs=[SMEM, VMEM, VMEM],
        out_specs=VMEM,
        input_output_aliases={1: 0},
        compiler_params=pltpu.CompilerParams(vmem_limit_bytes=16 * 1024 * 1024),
        name="beside",
    )(info, pltpu.with_memory_space_constraint(spread, pltpu.VMEM), packet)


def keep_rows(slab, source, first, size, live):
    for slab_row, row in slab_rows(live, first, size):
        for extra in range(size):
            slab[slab_row + extra] = source[row + extra]


def slab_rows(live, first, size):
    mirrored = SLAB - first - size
    return [(first, first - HALO), (SLAB + mirrored, live - 2 * RIM + mirrored)]


def collide_rows(geometry, before, whole, first, colours, walls, state):
    over_rows(geometry, first - 1, *COLOUR_BLOCK, lambda block: colour_stage(
        block, geometry, before, colours))
    over_rows(geometry, first, *COLLIDE_BLOCK, lambda block: collide_stage(
        block, geometry, before, whole, colours, walls, state))


def row_copies(pieces, outs, held_row, out_row, count, sems):
    held, rows = pl.ds(held_row, count), pl.ds(out_row, count)
    parts = (
        (pieces.at[0, held], outs[0].at[rows]),
        (pieces.at[pl.ds(1, 3), held], outs[1].at[:, rows]),
        (pieces.at[pl.ds(4, 6), held], outs[2].at[:, rows]),
        (pieces.at[10, held], outs[3].at[rows]),
    )
    return [
        pltpu.make_async_copy(source, target, sems.at[number])
        for number, (source, target) in enumerate(parts)
    ]


def gather_tiles(final, row, pieces, held_row):
    width = final.shape[1]
    start = row * width
    if not isinstance(start, int):
        start = pl.multiple_of(start, SUBLANES)
    for index in range(FIELDS):
        for tile in range(OWN_TILES):
            place = start + index * SUBLANES + 1 + tile
            pieces[index, pl.ds(held_row, SUBLANES), pl.ds(tile * LANES, LANES)] = flat_view(final)[
                pl.ds(place, SUBLANES, stride=width), :
            ]


def first_kernel(
    info, whole, pieces,
    moved_slab, reds_slab, fields_slab, moved_later_slab, reds_later_slab, final_slab,
    colours, walls, moved, reds, fields, moved_later, reds_later, final,
):
    state, later = (ByRow(moved), ByRow(reds)), (ByRow(moved_later), ByRow(reds_later))
    geometry = Geometry(info, OWN_TILES)
    live = geometry.live
    fill_wall_table(walls, geometry)
    collide_rows(geometry, ByRow(whole), ByRow(whole), 1, ByRow(colours), walls, state)
    over_rows(geometry, 2, *ARRIVE_BLOCK, lambda block: arrive_stage(
        block, geometry, walls, state, ByRow(fields)))
    keep_rows(moved_slab, moved, HALO + 1, KEPT, live)
    keep_rows(reds_slab, reds, HALO + 1, KEPT, live)
    keep_rows(fields_slab, fields, HALO + 2, KEPT, live)
    collide_rows(geometry, ByRow(fields), ByRow(whole), 3, ByRow(colours), walls, later)
    keep_rows(moved_later_slab, moved_later, HALO + 3, KEPT, live)
    keep_rows(reds_later_slab, reds_later, HALO + 3, KEPT, live)
    edges = slab_rows(live, HALO + RIM, RIM)
    rim = Block(geometry, [(row, row, RIM) for _, row in edges], True, [at for at, _ in edges])
    arrive_stage(rim, geometry, walls, later, ByRow(final_slab))

    def finish(tile, carry):
        row = pl.multiple_of(tile * SUBLANES, SUBLANES)
        block = Block(geometry, [(row, row, SUBLANES)], inner=True)
        arrive_stage(block, geometry, walls, later, ByRow(final))
        gather_tiles(final, row, pieces, row)
        return carry

    lax.fori_loop(1, live // SUBLANES - 1, finish, 0)
    for row in range(0, pieces.shape[1], SUBLANES):

        @pl.when(row >= live)
        def _():
            zeros = jnp.zeros((FIELDS, SUBLANES, pieces.shape[2]), jnp.float32)
            pieces[:, pl.ds(row, SUBLANES), :] = zeros


def scratch_of(shape):
    return pltpu.VMEM(shape.shape, shape.dtype)


def pieces_of(rows, flat_count):
    return pltpu.VMEM((FIELDS, rows, flat_count), jnp.float32)


def run_first(info, whole, arrays):
    rows, flat_count = arrays[0].shape
    pieces = jax.ShapeDtypeStruct((FIELDS, rows, flat_count), jnp.float32)
    slabs = [by_row(2 * SLAB, count) for count in (HELD, REDS, FIELDS, HELD, REDS, FIELDS)]
    scratch = [by_row(rows, 4), by_row(4, 3)]
    scratch = scratch + [by_row(rows, count) for count in (HELD, REDS, FIELDS, HELD, REDS, FIELDS)]
    return pl.pallas_call(
        first_kernel,
        out_shape=[pieces] + slabs,
        in_specs=[SMEM, VMEM],
        out_specs=[VMEM] * 7,
        scratch_shapes=[scratch_of(shape) for shape in scratch],
        compiler_params=pltpu.CompilerParams(vmem_limit_bytes=32 * 1024 * 1024),
        cost_estimate=pl.CostEstimate(flops=40_000_000, bytes_accessed=8_000_000, transcendentals=0),
        name="first",
    )(info, whole)


def follow_kernel(ends, kept, out):
    out[pl.ds(PACKED * SUBLANES, 1), :] = jnp.zeros((1, LANES), jnp.float32)


def follow(ends, kept):
    return pl.pallas_call(
        follow_kernel,
        out_shape=jax.ShapeDtypeStruct(ends.shape, jnp.float32),
        in_specs=[VMEM, ANY],
        out_specs=VMEM,
        input_output_aliases={0: 0},
        compiler_params=pltpu.CompilerParams(vmem_limit_bytes=8 * 1024 * 1024),
        name="follow",
    )(pltpu.with_memory_space_constraint(ends, pltpu.VMEM), kept)


def side_steps(straight, info, whole, ends, slabs, scratch, pieces):
    moved, reds, fields, moved_later, reds_later, final = slabs
    start_fields, colours, walls = scratch
    state, later = (ByRow(moved), ByRow(reds)), (ByRow(moved_later), ByRow(reds_later))
    geometry = Geometry(info, OWN_TILES)
    live = geometry.live
    is_low = info[3] == (0 if straight else 1)
    fill_wall_table(walls, geometry)

    def ends_of(half):
        blocks = []
        for group in range(FULL * PLANES // GROUP):
            first = half * (PACKED + 1) + group * (GROUP - 1)
            packed = [ends[pl.ds((first + k) * SUBLANES, SUBLANES), :] for k in range(GROUP - 1)]
            blocks = blocks + unpack_blocks(packed)
        last = half * (PACKED + 1) + PACKED
        return blocks + [ends[pl.ds(last * SUBLANES, SUBLANES), :]]

    tiles = block_tiles()
    middle = (tiles >= 1) & (tiles <= OWN_TILES)

    def widened(own, other):
        beside = jnp.where(tiles == 0, roll_tiles(other, -OWN_TILES), roll_tiles(other, OWN_TILES))
        return jnp.where(geometry.domain, jnp.where(middle, own, beside), 0.0)

    halves = (0, 1) if straight else (1, 0)
    halo = [widened(*pair) for pair in zip(*[ends_of(half) for half in halves])]

    def rows_at(first, count):
        mirrored = SLAB - first - count
        local = jnp.where(is_low, first, SLAB + mirrored)
        return local, jnp.where(is_low, first - HALO, live - 2 * RIM + mirrored)

    held_start = ByRow(start_fields)
    halo_row, _ = rows_at(1, FULL)
    for number in range(FULL * PLANES):
        place, extra = divmod(number, FULL)
        write_row(held_start, ORDER[place], halo_row + extra, halo[number])
    colour_row, _ = rows_at(0, 1)
    write_row(held_start, 0, colour_row, jnp.zeros((SUBLANES, LANES), jnp.float32))
    write_row(held_start, 10, colour_row, 0.5 * halo[-1])
    local, row = rows_at(HALO, FULL)
    for extra in range(FULL):
        start_fields[local + extra] = whole[row + extra]

    def block(first, count):
        local, row = rows_at(first, count)
        return Block(geometry, [(row, local, count)])

    held, marks = ByRow(fields), ByRow(colours)
    colour_stage(block(0, 6), geometry, held_start, marks)
    collide_stage(block(1, 4), geometry, held_start, held_start, marks, walls, state)
    arrive_stage(block(2, 4), geometry, walls, state, held)
    colour_stage(block(2, 6), geometry, held, marks)
    collide_stage(block(3, 4), geometry, held, held_start, marks, walls, later)
    arrive_stage(block(4, 4), geometry, walls, later, ByRow(final))
    gather_tiles(final, jnp.where(is_low, HALO, SLAB), pieces, 0)


def edge_row(info, straight):
    is_low = info[3] == (0 if straight else 1)
    return pl.multiple_of(jnp.where(is_low, 0, info[0] - SUBLANES), SUBLANES)


def straight_kernel(info, whole, ends, inner_pieces, *refs):
    outs, slabs, pieces = refs[6:10], refs[10:16], refs[16]
    scratch, sems = refs[17:20], refs[20]
    live = info[0]
    starts = (
        jnp.where(live == TILE, TILE, SUBLANES),
        jnp.where(live == 3 * TILE, TILE + SUBLANES, 2 * TILE),
    )
    copies = []
    for number, start in enumerate(starts):
        row = pl.multiple_of(start, SUBLANES)
        copies = copies + row_copies(inner_pieces, outs, row, row, TILE, sems.at[number])
    for copy in copies:
        copy.start()
    side_steps(True, info, whole, ends, slabs, scratch, pieces)
    for copy in copies:
        copy.wait()


def crossed_kernel(info, whole, ends, straight_pieces, *refs):
    outs, slabs = refs[10:14], refs[14:20]
    scratch, pieces, sems = refs[20:23], refs[23], refs[24]
    rows = [edge_row(info, straight) for straight in (True, False)]
    straight = row_copies(straight_pieces, outs, 0, rows[0], SUBLANES, sems.at[0])
    for copy in straight:
        copy.start()
    side_steps(False, info, whole, ends, slabs, scratch, pieces)
    crossed = row_copies(pieces, outs, 0, rows[1], SUBLANES, sems.at[1])
    for copy in crossed:
        copy.start()
    for copy in straight + crossed:
        copy.wait()


def run_side(straight, info, whole, ends, held_pieces, slabs, outs):
    flat_count = outs[0].shape[1]
    assert outs[0].shape[0] == 3 * TILE
    shapes = [jax.ShapeDtypeStruct(array.shape, jnp.float32) for array in (*outs, *slabs)]
    slabs = [pltpu.with_memory_space_constraint(slab, pltpu.VMEM) for slab in slabs]
    aliases = {4 + number: 4 + number for number in range(6)}
    scratch = [by_row(2 * SLAB, PLACES), by_row(2 * SLAB, 4), by_row(4, 3)]
    scratch = [scratch_of(shape) for shape in scratch]
    sems = pltpu.SemaphoreType.DMA((2, OUT_COPIES))
    edge = jax.ShapeDtypeStruct((FIELDS, SUBLANES, flat_count), jnp.float32)
    if straight:
        shapes, scratch = shapes + [edge], scratch + [sems]
    else:
        aliases.update({10 + number: number for number in range(4)})
        scratch = scratch + [scratch_of(edge), sems]
    return pl.pallas_call(
        straight_kernel if straight else crossed_kernel,
        out_shape=shapes,
        in_specs=[SMEM] + [VMEM] * 9 + ([] if straight else [ANY] * 4),
        out_specs=[ANY] * 4 + [VMEM] * (7 if straight else 6),
        scratch_shapes=scratch,
        input_output_aliases=aliases,
        compiler_params=pltpu.CompilerParams(vmem_limit_bytes=24 * 1024 * 1024),
        cost_estimate=pl.CostEstimate(flops=10_000_000, bytes_accessed=4_000_000, transcendentals=0),
        name="straight" if straight else "crossed",
    )(info, whole, ends, held_pieces, *slabs, *([] if straight else outs))


def body(density, momentum, stress, red_density, solid, widths):
    tiles_count = lax.axis_size("tiles")
    arrays = (density, momentum, stress, red_density, solid)
    info, raw, raw_solid, packet, mine = load_inputs(arrays, widths, tiles_count)
    info = pltpu.with_memory_space_constraint(info, pltpu.SMEM)
    swap = [(0, 1), (1, 0)]
    packet = lax.ppermute(packet, "sub", swap)
    spread = spread_rows(raw, raw_solid)
    ends = join_ends(mine, packet, spread)
    route = [(2 * k, 2 * k + 2) for k in range(tiles_count - 1)]
    route = route + [(2 * k + 3, 2 * k + 1) for k in range(tiles_count - 1)]
    arrived = lax.ppermute(ends, ("tiles", "sub"), route)
    whole = put_beside(info, spread, packet)
    pieces, *slabs = run_first(info, whole, arrays)
    arrived = follow(arrived, slabs[-1])
    passed = lax.ppermute(arrived, "sub", swap)
    results = run_side(True, info, whole, arrived, pieces, slabs, arrays[:4])
    outs, slabs, pieces = results[:4], results[4:10], results[10]
    return tuple(run_side(False, info, whole, passed, pieces, slabs, outs)[:4])


def solution(mesh):
    in_specs = (
        P(("groups", "tiles"), "sub"),
        P(None, ("groups", "tiles"), "sub"),
        P(None, ("groups", "tiles"), "sub"),
        P(("groups", "tiles"), "sub"),
        P(("groups", "tiles"), "sub"),
        P("groups"),
    )
    out_specs = (
        P(("groups", "tiles"), "sub"),
        P(None, ("groups", "tiles"), "sub"),
        P(None, ("groups", "tiles"), "sub"),
        P(("groups", "tiles"), "sub"),
    )
    return jax.shard_map(body, mesh=mesh, in_specs=in_specs, out_specs=out_specs, check_vma=False)
```

```python
import functools

import jax
import jax.numpy as jnp
from jax import lax
from jax.experimental import pallas as pl
from jax.experimental.pallas import tpu as pltpu
from jax.sharding import PartitionSpec as P

TILE = 16
STEPS = 2
RELAX_TIME = 0.8
SURFACE = 0.1
SEPARATION = 0.7

LANES = 128
SUBLANES = 8
FULL = 3
HALO = FULL + 1
FIELDS = 11
PLANES = FIELDS + 1
MOVED = 19
REDS = 5
HELD = MOVED + 1
RIM = 4
SLAB = HALO + 2 * RIM
OWN_TILES = SUBLANES - 2
GROUP = 4
PACKED = FULL * PLANES // GROUP * (GROUP - 1)
END_ROWS = (PACKED + 1) * SUBLANES
HALF = LANES // 2
ORDER = (0, 1, 2, 3, 10, 11, 4, 5, 6, 7, 8, 9)
PAIRS = PLANES // 2
PLACES = PLANES + 1
KEPT = 2
OUT_COPIES = 5
COLOUR_BLOCK = (16, 1)
COLLIDE_BLOCK = (8, 1)
ARRIVE_BLOCK = (16, 1)
VMEM = pl.BlockSpec(memory_space=pltpu.VMEM)
SMEM = pl.BlockSpec(memory_space=pltpu.SMEM)
ANY = pl.BlockSpec(memory_space=pl.ANY)
HBM = pl.BlockSpec(memory_space=pltpu.HBM)


class Rows:
    def __init__(self, parts):
        self.parts = parts

    def _with(self, other, operation):
        others = other.parts if isinstance(other, Rows) else [other] * len(self.parts)
        return Rows([operation(one, two) for one, two in zip(self.parts, others)])

    def __add__(self, other):
        return self._with(other, lambda one, two: one + two)

    def __sub__(self, other):
        return self._with(other, lambda one, two: one - two)

    def __rsub__(self, other):
        return self._with(other, lambda one, two: two - one)

    def __mul__(self, other):
        return self._with(other, lambda one, two: one * two)

    def __or__(self, other):
        return self._with(other, lambda one, two: one | two)

    def __eq__(self, other):
        return self._with(other, lambda one, two: one == two)

    __radd__, __rmul__, __ror__ = __add__, __mul__, __or__

    def each(self, operation):
        return Rows([operation(part) for part in self.parts])


def select(mask, yes, no):
    count = max(len(item.parts) for item in (mask, yes, no) if isinstance(item, Rows))
    columns = [
        item.parts if isinstance(item, Rows) else [item] * count for item in (mask, yes, no)
    ]
    return Rows([jnp.where(*row) for row in zip(*columns)])


def roll_lanes(values, amount):
    return values.each(lambda part: pltpu.roll(part, amount % LANES, 1))


def roll_sublanes(values, amount):
    return values.each(lambda part: pltpu.roll(part, amount % SUBLANES, 0))


class Geometry:
    def __init__(self, info, own_tiles):
        live, first, last, sub_index = info[0], info[1], info[2], info[3]
        self.live = live
        self.low_row = jnp.where(first == 1, 0, -1000)
        self.high_row = jnp.where(last == 1, live, 1000)
        shape = (SUBLANES, LANES)
        lane = lax.broadcasted_iota(jnp.int32, shape, 1)
        tile = lax.broadcasted_iota(jnp.int32, shape, 0)
        depth = lane & (TILE - 1)
        low_part = sub_index == 0
        high_part = sub_index == 1
        z_walls = {1: depth == 0, -1: depth == TILE - 1}
        y_walls = {
            1: (tile == 1) & (lane < TILE) & low_part,
            -1: (tile == own_tiles) & (lane >= LANES - TILE) & high_part,
        }
        self.walls = {(0, vel_z): wall for vel_z, wall in z_walls.items()}
        for vel_y, y_wall in y_walls.items():
            self.walls[vel_y, 0] = y_wall
            for vel_z, z_wall in z_walls.items():
                self.walls[vel_y, vel_z] = y_wall | z_wall
        own = (tile >= 1) & (tile <= own_tiles)
        self.domain = own | ((tile == own_tiles + 1) & low_part) | ((tile == 0) & high_part)
        self.first_lanes = lane < TILE
        self.last_lanes = lane >= LANES - TILE

    def from_low_y(self, values):
        return roll_lanes(select(self.last_lanes, roll_sublanes(values, 1), values), TILE)

    def from_high_y(self, values):
        return roll_lanes(select(self.first_lanes, roll_sublanes(values, -1), values), -TILE)

    def from_low_z(self, values):
        return select(self.walls[0, 1], 0.0, roll_lanes(values, 1))

    def from_high_z(self, values):
        return select(self.walls[0, -1], 0.0, roll_lanes(values, -1))


def flat_rows(row, count, tile_offset=0):
    start = row * SUBLANES
    if not isinstance(start, int):
        start = pl.multiple_of(start, SUBLANES)
    return pl.ds(start + tile_offset, count * SUBLANES)


class ByRow:
    def __init__(self, ref):
        self.ref = ref


def by_row(rows, count):
    return jax.ShapeDtypeStruct((rows, count * SUBLANES, LANES), jnp.float32)


def place_of(ref, index, row, tile_offset=0):
    if isinstance(ref, ByRow):
        return ref.ref, row, pl.ds(index * SUBLANES + tile_offset, SUBLANES)
    return ref, index, flat_rows(row, 1, tile_offset)


def read_row(ref, index, row, tile_offset=0):
    ref, first, second = place_of(ref, index, row, tile_offset)
    return ref[first, second, :]


def write_row(ref, index, row, values):
    ref, first, second = place_of(ref, index, row)
    ref[first, second, :] = values


class Block:
    def __init__(self, geometry, spans, inner=False, store_rows=None):
        self.spans = spans
        self.store_rows = store_rows or [local for row, local, count in spans]
        rows = [row + extra for row, local, count in spans for extra in range(count)]
        self.inner = inner
        rows = [row + extra for row, local, count in spans for extra in range(count)]
        if inner:
            self.x_walls = {}
            self.valid = geometry.domain
            self.kinds = [0]
            return
        ids = Rows([row + jnp.zeros((SUBLANES, LANES), jnp.int32) for row in rows])
        self.x_walls = {1: ids == geometry.low_row, -1: ids == geometry.high_row - 1}
        self.valid = ids.each(
            lambda part: geometry.domain & (part >= geometry.low_row) & (part < geometry.high_row)
        )
        self.kinds = [
            jnp.where(row == geometry.low_row, 1, 0) + jnp.where(row == geometry.high_row - 1, 2, 0)
            for row in rows
        ]

    def load(self, ref, index, offset=0, tile_offset=0):
        return Rows([
            read_row(ref, index, local + offset + extra, tile_offset)
            for row, local, count in self.spans
            for extra in range(count)
        ])

    def store(self, ref, index, values):
        targets = [
            target + extra
            for (row, local, count), target in zip(self.spans, self.store_rows)
            for extra in range(count)
        ]
        for target, part in zip(targets, values.parts):
            write_row(ref, index, target, part)

    def wall_terms(self, walls, position):
        terms = [walls[position, flat_rows(kind, 1), :] for kind in self.kinds]
        return terms[0] if self.inner else Rows(terms)


def fill_wall_table(walls, geometry):
    one = jnp.ones((SUBLANES, LANES), jnp.float32)
    up_y, down_y, up_z, down_z = [
        jnp.where(geometry.walls[key], 0.0, one) for key in ((-1, 0), (1, 0), (0, -1), (0, 1))
    ]
    sum_y, sum_z = up_y + down_y, up_z + down_z
    for kind, (up_x, down_x) in enumerate(((1.0, 1.0), (1.0, 0.0), (0.0, 1.0))):
        sum_x = up_x + down_x
        around_x = 2.0 + sum_y + sum_z
        total = 12.0 + 2.0 * (sum_x + sum_y + sum_z) + sum_x * (sum_y + sum_z) + sum_y * sum_z
        rows = (
            (up_x - down_x) * around_x,
            (up_y - down_y) * (2.0 + sum_x + sum_z),
            (up_z - down_z) * (2.0 + sum_x + sum_y),
            36.0 - total,
        )
        for position, row in enumerate(rows):
            walls[position, flat_rows(kind, 1), :] = row


VELOCITIES = tuple(
    tuple(sign if axis == place else 0 for place in range(3)) for axis in range(3) for sign in (1, -1)
) + tuple(
    tuple({a: one, b: two}.get(place, 0) for place in range(3))
    for a, b in ((0, 1), (0, 2), (1, 2))
    for one, two in ((1, 1), (-1, -1), (1, -1), (-1, 1))
)
VELOCITIES = ((0, 0, 0),) + VELOCITIES


def colour_stage(block, geometry, fields, colours):
    density = block.load(fields, 0)
    red = block.load(fields, 10)
    colour = select(block.valid, 2.0 * red - density, 0.0)
    along_y = geometry.from_low_y(colour) + geometry.from_high_y(colour)
    along_z = geometry.from_low_z(colour) + geometry.from_high_z(colour)
    block.store(colours, 0, colour)
    block.store(colours, 1, 2.0 * colour + (along_y + along_z))
    block.store(colours, 2, along_y)
    block.store(colours, 3, along_z)


def collide_stage(block, geometry, fields, solids, colours, walls, state):
    relaxing = 1.0 - 1.0 / RELAX_TIME
    third = 1.0 / 3.0
    colour = block.load(colours, 0)
    doubled = 2.0 * colour + (block.load(colours, 0, -1) + block.load(colours, 0, 1))
    term_y = doubled + block.load(colours, 3)
    term_z = doubled + block.load(colours, 2)
    grad_x = block.load(colours, 1, 1) - block.load(colours, 1, -1)
    grad_y = geometry.from_high_y(term_y) - geometry.from_low_y(term_y)
    grad_z = geometry.from_high_z(term_z) - geometry.from_low_z(term_z)
    if not block.inner:
        grad_x = grad_x - block.wall_terms(walls, 0) * colour
    grad_y = grad_y - block.wall_terms(walls, 1) * colour
    grad_z = grad_z - block.wall_terms(walls, 2) * colour

    fluid = block.load(solids, PLANES - 1) == 0.0
    density = block.load(fields, 0)
    red = block.load(fields, 10)
    flux = [block.load(fields, 1 + axis) for axis in range(3)]
    stress = [block.load(fields, 4 + part) for part in range(6)]
    square_xx, square_yy, square_zz = grad_x * grad_x, grad_y * grad_y, grad_z * grad_z
    square = square_xx + square_yy + square_zz
    inverse = select(fluid, (1.0 + square * (1.0 / 144.0)).each(lax.rsqrt), 0.0)
    trace = third * square
    strength = (SURFACE / (8.0 * 144.0)) * inverse
    keep = select(fluid, relaxing / 8.0, 1.0 / 8.0)
    eighths = [0.125 * part for part in flux]
    own = [
        eighths[axis] * flux[axis] + (keep * stress[axis] + strength * (squared - trace))
        for axis, squared in enumerate((square_xx, square_yy, square_zz))
    ]
    strength, keep = 2.0 * strength, 2.0 * keep
    quarters = [2.0 * part for part in eighths[:2]]
    grads = (grad_x, grad_y, grad_z)
    cross = [
        quarters[a] * flux[b] + (keep * stress[3 + plane] + strength * (grads[a] * grads[b]))
        for plane, (a, b) in enumerate(((0, 1), (0, 2), (1, 2)))
    ]
    base = density * (1.0 / 36.0) - third * (own[0] + own[1] + own[2])
    sign = select(fluid, 1.0 / 12.0, -1.0 / 12.0)
    run = [sign * part for part in flux]
    mixing = ((SEPARATION / 144.0) * red) * ((density - red) * inverse)
    red_run = [0.5 * part + mixing * grad for part, grad in zip(run, grads)]
    moved, reds = state
    block.store(moved, 0, 12.0 * base)
    straight = [base + part for part in own]
    for axis in range(3):
        middle = 2.0 * straight[axis]
        swing = 2.0 * run[axis]
        block.store(moved, 1 + 2 * axis, middle + swing)
        block.store(moved, 2 + 2 * axis, middle - swing)
    for plane, (a, b) in enumerate(((0, 1), (0, 2), (1, 2))):
        middle = straight[a] + own[b]
        same, other = middle + cross[plane], middle - cross[plane]
        along, against = run[a] + run[b], run[a] - run[b]
        first = 7 + 4 * plane
        block.store(moved, first, same + along)
        block.store(moved, first + 1, same - along)
        block.store(moved, first + 2, other + against)
        block.store(moved, first + 3, other - against)

    red_base = select(block.valid, red * (1.0 / 36.0), 0.0)
    red_run = [select(block.valid, part, 0.0) for part in red_run]
    block.store(reds, 0, red_base)
    block.store(reds, 1, red_base + red_run[0])
    block.store(reds, 2, red_base - red_run[0])
    block.store(reds, 3, red_run[1])
    block.store(reds, 4, red_run[2])


def arrive_stage(block, geometry, walls, state, fields):
    third = 1.0 / 3.0
    moved, reds = state
    own = [None] * MOVED

    def here(direction):
        if own[direction] is None:
            own[direction] = block.load(moved, direction)
        return own[direction]

    def arrived(direction, opposite):
        vel_x, vel_y, vel_z = VELOCITIES[direction]
        values = here(direction) if vel_x == 0 else block.load(moved, direction, -vel_x)
        if vel_y != 0:
            beside = block.load(moved, direction, -vel_x, -vel_y)
            leaving = geometry.last_lanes if vel_y == 1 else geometry.first_lanes
            values = select(leaving, beside, values)
        if vel_y != 0 or vel_z != 0:
            values = roll_lanes(values, TILE * vel_y + vel_z)
        masks = []
        if vel_x in block.x_walls:
            masks.append(block.x_walls[vel_x])
        if (vel_y, vel_z) in geometry.walls:
            masks.append(geometry.walls[vel_y, vel_z])
        if not masks:
            return values
        wall = functools.reduce(lambda one, two: one | two, masks)
        return select(wall, here(opposite), values)

    red = block.load(reds, 0)
    red_y = block.load(reds, 3)
    red_z = block.load(reds, 4)
    from_x = block.load(reds, 1, -1) + block.load(reds, 2, 1)
    spread = 2.0 * red + from_x
    spread_y = 2.0 * red_y + (block.load(reds, 3, -1) + block.load(reds, 3, 1))
    spread_z = 2.0 * red_z + (block.load(reds, 4, -1) + block.load(reds, 4, 1))
    up_y, down_y = red + red_y, red - red_y
    low_y = (
        (spread + spread_y)
        + geometry.from_low_z(up_y + red_z)
        + geometry.from_high_z(up_y - red_z)
    )
    high_y = (
        (spread - spread_y)
        + geometry.from_low_z(down_y + red_z)
        + geometry.from_high_z(down_y - red_z)
    )
    bounced = (
        block.wall_terms(walls, 3) * red
        - block.wall_terms(walls, 1) * red_y
        - block.wall_terms(walls, 2) * red_z
    )
    if not block.inner:
        bounced = bounced - block.wall_terms(walls, 0) * (block.load(reds, 1) - red)
    red_total = (
        12.0 * red
        + 2.0 * from_x
        + geometry.from_low_z(spread + spread_z)
        + geometry.from_high_z(spread - spread_z)
        + geometry.from_low_y(low_y)
        + geometry.from_high_y(high_y)
        + bounced
    )
    rest = here(0)
    sums, diffs = [], []
    for axis in range(3):
        up = arrived(1 + 2 * axis, 2 + 2 * axis)
        down = arrived(2 + 2 * axis, 1 + 2 * axis)
        sums.append(up + down)
        diffs.append(up - down)
    total = rest + sums[0] + sums[1] + sums[2]
    cross = []
    for plane, (a, b) in enumerate(((0, 1), (0, 2), (1, 2))):
        first = 7 + 4 * plane
        parts = [arrived(first + offset, first + (offset ^ 1)) for offset in range(4)]
        same, other = parts[0] + parts[1], parts[2] + parts[3]
        along, against = parts[0] - parts[1], parts[2] - parts[3]
        both = same + other
        cross.append(same - other)
        total = total + both
        sums[a], sums[b] = sums[a] + both, sums[b] + both
        diffs[a], diffs[b] = diffs[a] + (along + against), diffs[b] + (along - against)
    shared = third * total
    block.store(fields, 0, total)
    for axis in range(3):
        block.store(fields, 1 + axis, diffs[axis])
        block.store(fields, 4 + axis, sums[axis] - shared - diffs[axis] * diffs[axis])
    for plane, (a, b) in enumerate(((0, 1), (0, 2), (1, 2))):
        block.store(fields, 7 + plane, cross[plane] - diffs[a] * diffs[b])
    block.store(fields, 10, red_total)


def over_rows(geometry, first, size, blocks, stage):
    trip = size * blocks
    rest = -2 * first % trip
    assert TILE % trip == 0 and rest % min(size, rest or size) == 0

    def run(start, count, step_size):
        for offset in range(0, count, step_size):
            row = start + offset
            stage(Block(geometry, [(row, row, step_size)], inner=True))

    def step(index, carry):
        run(first + index * trip, trip, size)
        return carry

    trips = (geometry.live - 2 * first - rest) // trip
    lax.fori_loop(0, trips, step, 0)
    if rest:
        run(geometry.live - first - rest, rest, min(size, rest))


def block_tiles():
    return lax.broadcasted_iota(jnp.int32, (SUBLANES, LANES), 0)


def roll_tiles(block, amount):
    return pltpu.roll(block, amount % SUBLANES, 0)


def pack_blocks(blocks):
    tiles, rest = block_tiles(), blocks[GROUP - 1]
    packed = []
    for number, block in enumerate(blocks[: GROUP - 1]):
        low, high = 2 * number + 1, 2 * number + 2
        block = jnp.where(tiles == 0, roll_tiles(rest, -low), block)
        packed.append(jnp.where(tiles == SUBLANES - 1, roll_tiles(rest, SUBLANES - 1 - high), block))
    return packed


def unpack_blocks(packed):
    tiles, rest = block_tiles(), None
    for number, block in enumerate(packed):
        low, high = 2 * number + 1, 2 * number + 2
        part = jnp.where(tiles == low, roll_tiles(block, low), roll_tiles(block, high - SUBLANES + 1))
        rest = part if rest is None else jnp.where(tiles >= low, part, rest)
    return list(packed) + [rest]


def flat_view(ref):
    rows, width, lanes = ref.shape
    return ref.reshape(rows * width, lanes)


def spread_tile(raw, raw_solid, index, row, target, target_row):
    source = raw_solid if index == FIELDS else raw.at[index]
    width = target.shape[1]
    for tile in range(OWN_TILES):
        values = source[pl.ds(row, SUBLANES), pl.ds(tile * LANES, LANES)].astype(jnp.float32)
        start = target_row * width + index * SUBLANES + 1 + tile
        flat_view(target)[pl.ds(start, SUBLANES, stride=width), :] = values


def load_kernel(
    tiles_count, density, momentum, stress, red, solid, widths,
    info, raw, raw_solid, packet, mine,
    first_tile, last_tile, held_widths, sems,
):
    row_count, flat_count = raw_solid.shape
    own_tiles = flat_count // LANES
    copies = [
        pltpu.make_async_copy(widths, held_widths, sems.at[0]),
        pltpu.make_async_copy(density, raw.at[0], sems.at[1]),
        pltpu.make_async_copy(momentum, raw.at[pl.ds(1, 3)], sems.at[2]),
        pltpu.make_async_copy(red, raw.at[10], sems.at[3]),
        pltpu.make_async_copy(solid, raw_solid, sems.at[4]),
        pltpu.make_async_copy(stress.at[pl.ds(0, 3)], raw.at[pl.ds(4, 3)], sems.at[5]),
        pltpu.make_async_copy(stress.at[pl.ds(3, 3)], raw.at[pl.ds(7, 3)], sems.at[6]),
    ]
    for copy in copies:
        copy.start()
    tiles_index, sub_index = lax.axis_index("tiles"), lax.axis_index("sub")
    low_part = sub_index == 0
    edge_start = pl.multiple_of(jnp.where(low_part, (own_tiles - 1) * LANES, 0), LANES)

    copies[0].wait()
    live = held_widths[tiles_index] * TILE
    info[0] = live
    info[1] = (tiles_index == 0).astype(jnp.int32)
    info[2] = (tiles_index == tiles_count - 1).astype(jnp.int32)
    info[3] = sub_index

    near_cut = lax.broadcasted_iota(jnp.int32, (SUBLANES, LANES), 1) < HALF
    near_cut = near_cut == jnp.logical_not(low_part)
    near_last = pl.multiple_of(live - SUBLANES, SUBLANES)
    edges = pl.ds(edge_start, LANES)

    def plane_of(index):
        return raw_solid if index == FIELDS else raw.at[index]

    def pack_edges(pair):
        here, there = [plane_of(index) for index in ORDER[2 * pair : 2 * pair + 2]]
        for row in range(0, row_count, SUBLANES):
            rows = pl.ds(row, SUBLANES)
            beside = pltpu.roll(there[rows, edges].astype(jnp.float32), HALF, 1)
            both = jnp.where(near_cut, here[rows, edges].astype(jnp.float32), beside)
            packet[pl.ds(END_ROWS + pair * row_count + row, SUBLANES), :] = both

    targets = ((packet, jnp.logical_not(low_part)), (mine, low_part))

    def row_of(use_last, index, number_first, number_last):
        first = read_row(ByRow(first_tile), index, number_first)
        last = read_row(ByRow(last_tile), index, number_last)
        return jnp.where(use_last, last, first)

    def pack_ends(group):
        for target, use_last in targets:
            blocks = []
            for number in range(group * GROUP, (group + 1) * GROUP):
                place, extra = divmod(number, FULL)
                blocks.append(row_of(use_last, ORDER[place], extra, SUBLANES - FULL + extra))
            for number, block in enumerate(pack_blocks(blocks)):
                place = (group * (GROUP - 1) + number) * SUBLANES
                target[pl.ds(place, SUBLANES), :] = block

    place = 0
    for copy, count in zip(copies[1:], (1, 3, 1, 1, 3, 3)):
        copy.wait()
        before, place = place, place + count
        for index in ORDER[before:place]:
            for target, row in ((first_tile, 0), (last_tile, near_last)):
                spread_tile(raw, raw_solid, index, row, target, 0)
        for pair in range(before // 2, place // 2):
            pack_edges(pair)
        for group in range(before * FULL // GROUP, place * FULL // GROUP):
            pack_ends(group)
    for target, use_last in targets:
        red_row, density_row = [
            row_of(use_last, index, FULL, SUBLANES - HALO) for index in (10, 0)
        ]
        target[pl.ds(PACKED * SUBLANES, SUBLANES), :] = 2.0 * red_row - density_row


def load_inputs(arrays, widths, tiles_count):
    row_count, flat_count = arrays[0].shape
    return pl.pallas_call(
        functools.partial(load_kernel, tiles_count),
        out_shape=[
            pltpu.SMEM((4,), jnp.int32),
            jax.ShapeDtypeStruct((FIELDS, row_count, flat_count), jnp.float32),
            jax.ShapeDtypeStruct((row_count, flat_count), jnp.int32),
            jax.ShapeDtypeStruct((END_ROWS + PAIRS * row_count, LANES), jnp.float32),
            jax.ShapeDtypeStruct((END_ROWS, LANES), jnp.float32),
        ],
        in_specs=[HBM] * 6,
        out_specs=[SMEM] + [VMEM] * 4,
        scratch_shapes=[
            pltpu.VMEM((SUBLANES, PLACES * SUBLANES, LANES), jnp.float32),
            pltpu.VMEM((SUBLANES, PLACES * SUBLANES, LANES), jnp.float32),
            pltpu.SMEM(widths.shape, jnp.int32),
            pltpu.SemaphoreType.DMA((7,)),
        ],
        compiler_params=pltpu.CompilerParams(vmem_limit_bytes=16 * 1024 * 1024),
        name="load",
    )(*[pltpu.with_memory_space_constraint(array, pltpu.HBM) for array in (*arrays, widths)])


def spread_kernel(raw, raw_solid, spread):
    for index in range(PLANES):
        for row in range(0, raw_solid.shape[0], SUBLANES):
            spread_tile(raw, raw_solid, index, row, spread, row)


def spread_rows(raw, raw_solid):
    row_count = raw_solid.shape[0]
    return pl.pallas_call(
        spread_kernel,
        out_shape=by_row(row_count, PLACES),
        in_specs=[VMEM, VMEM],
        out_specs=VMEM,
        compiler_params=pltpu.CompilerParams(vmem_limit_bytes=16 * 1024 * 1024),
        cost_estimate=pl.CostEstimate(flops=1_000_000, bytes_accessed=4_000_000, transcendentals=0),
        name="spread",
    )(raw, raw_solid)


def join_kernel(mine, packet, spread, ends):
    ends[pl.ds(0, END_ROWS), :] = mine[...]
    ends[pl.ds(END_ROWS, END_ROWS), :] = packet[pl.ds(0, END_ROWS), :]


def join_ends(mine, packet, spread):
    return pl.pallas_call(
        join_kernel,
        out_shape=jax.ShapeDtypeStruct((2 * END_ROWS, LANES), jnp.float32),
        in_specs=[VMEM, VMEM, ANY],
        out_specs=VMEM,
        compiler_params=pltpu.CompilerParams(vmem_limit_bytes=8 * 1024 * 1024),
        name="join",
    )(mine, packet, spread)


def beside_kernel(info, spread, packet, whole):
    low_part = info[3] == 0
    row_count, width = spread.shape[:2]
    flat = flat_view(whole)
    for pair in range(PAIRS):
        for row in range(0, row_count, SUBLANES):
            both = packet[pl.ds(END_ROWS + pair * row_count + row, SUBLANES), :]
            for place, values in ((2 * pair, both), (2 * pair + 1, pltpu.roll(both, HALF, 1))):
                index = ORDER[place]
                start = row * width + index * SUBLANES
                below = jnp.where(low_part, 0.0, values)
                above = jnp.where(low_part, values, 0.0)
                flat[pl.ds(start, SUBLANES, stride=width), :] = below
                flat[pl.ds(start + SUBLANES - 1, SUBLANES, stride=width), :] = above


def put_beside(info, spread, packet):
    return pl.pallas_call(
        beside_kernel,
        out_shape=jax.ShapeDtypeStruct(spread.shape, jnp.float32),
        in_specs=[SMEM, VMEM, VMEM],
        out_specs=VMEM,
        input_output_aliases={1: 0},
        compiler_params=pltpu.CompilerParams(vmem_limit_bytes=16 * 1024 * 1024),
        name="beside",
    )(info, pltpu.with_memory_space_constraint(spread, pltpu.VMEM), packet)


def keep_rows(slab, source, first, size, live):
    for slab_row, row in slab_rows(live, first, size):
        for extra in range(size):
            slab[slab_row + extra] = source[row + extra]


def slab_rows(live, first, size):
    mirrored = SLAB - first - size
    return [(first, first - HALO), (SLAB + mirrored, live - 2 * RIM + mirrored)]


def collide_rows(geometry, before, whole, first, colours, walls, state):
    over_rows(geometry, first - 1, *COLOUR_BLOCK, lambda block: colour_stage(
        block, geometry, before, colours))
    over_rows(geometry, first, *COLLIDE_BLOCK, lambda block: collide_stage(
        block, geometry, before, whole, colours, walls, state))


def row_copies(pieces, outs, held_row, out_row, count, sems):
    held, rows = pl.ds(held_row, count), pl.ds(out_row, count)
    parts = (
        (pieces.at[0, held], outs[0].at[rows]),
        (pieces.at[pl.ds(1, 3), held], outs[1].at[:, rows]),
        (pieces.at[pl.ds(4, 3), held], outs[2].at[pl.ds(0, 3), rows]),
        (pieces.at[pl.ds(7, 3), held], outs[2].at[pl.ds(3, 3), rows]),
        (pieces.at[10, held], outs[3].at[rows]),
    )
    return [
        pltpu.make_async_copy(source, target, sems.at[number])
        for number, (source, target) in enumerate(parts)
    ]


def gather_tiles(final, row, pieces, held_row):
    width = final.shape[1]
    start = row * width
    if not isinstance(start, int):
        start = pl.multiple_of(start, SUBLANES)
    for index in range(FIELDS):
        for tile in range(OWN_TILES):
            place = start + index * SUBLANES + 1 + tile
            pieces[index, pl.ds(held_row, SUBLANES), pl.ds(tile * LANES, LANES)] = flat_view(final)[
                pl.ds(place, SUBLANES, stride=width), :
            ]


def first_kernel(
    info, whole, pieces,
    moved_slab, reds_slab, fields_slab, moved_later_slab, reds_later_slab, final_slab,
    colours, walls, moved, reds, fields, moved_later, reds_later, final,
):
    state, later = (ByRow(moved), ByRow(reds)), (ByRow(moved_later), ByRow(reds_later))
    geometry = Geometry(info, OWN_TILES)
    live = geometry.live
    fill_wall_table(walls, geometry)
    collide_rows(geometry, ByRow(whole), ByRow(whole), 1, ByRow(colours), walls, state)
    over_rows(geometry, 2, *ARRIVE_BLOCK, lambda block: arrive_stage(
        block, geometry, walls, state, ByRow(fields)))
    keep_rows(moved_slab, moved, HALO + 1, KEPT, live)
    keep_rows(reds_slab, reds, HALO + 1, KEPT, live)
    keep_rows(fields_slab, fields, HALO + 2, KEPT, live)
    collide_rows(geometry, ByRow(fields), ByRow(whole), 3, ByRow(colours), walls, later)
    keep_rows(moved_later_slab, moved_later, HALO + 3, KEPT, live)
    keep_rows(reds_later_slab, reds_later, HALO + 3, KEPT, live)
    edges = slab_rows(live, HALO + RIM, RIM)
    rim = Block(geometry, [(row, row, RIM) for _, row in edges], True, [at for at, _ in edges])
    arrive_stage(rim, geometry, walls, later, ByRow(final_slab))

    def finish(tile, carry):
        row = pl.multiple_of(tile * SUBLANES, SUBLANES)
        block = Block(geometry, [(row, row, SUBLANES)], inner=True)
        arrive_stage(block, geometry, walls, later, ByRow(final))
        gather_tiles(final, row, pieces, row)
        return carry

    lax.fori_loop(1, live // SUBLANES - 1, finish, 0)
    for row in range(0, pieces.shape[1], SUBLANES):

        @pl.when(row >= live)
        def _():
            zeros = jnp.zeros((FIELDS, SUBLANES, pieces.shape[2]), jnp.float32)
            pieces[:, pl.ds(row, SUBLANES), :] = zeros


def scratch_of(shape):
    return pltpu.VMEM(shape.shape, shape.dtype)


def pieces_of(rows, flat_count):
    return pltpu.VMEM((FIELDS, rows, flat_count), jnp.float32)


def run_first(info, whole, arrays):
    rows, flat_count = arrays[0].shape
    pieces = jax.ShapeDtypeStruct((FIELDS, rows, flat_count), jnp.float32)
    slabs = [by_row(2 * SLAB, count) for count in (HELD, REDS, FIELDS, HELD, REDS, FIELDS)]
    scratch = [by_row(rows, 4), by_row(4, 3)]
    scratch = scratch + [by_row(rows, count) for count in (HELD, REDS, FIELDS, HELD, REDS, FIELDS)]
    return pl.pallas_call(
        first_kernel,
        out_shape=[pieces] + slabs,
        in_specs=[SMEM, VMEM],
        out_specs=[VMEM] * 7,
        scratch_shapes=[scratch_of(shape) for shape in scratch],
        compiler_params=pltpu.CompilerParams(vmem_limit_bytes=32 * 1024 * 1024),
        cost_estimate=pl.CostEstimate(flops=40_000_000, bytes_accessed=8_000_000, transcendentals=0),
        name="first",
    )(info, whole)


def follow_kernel(ends, kept, out):
    out[pl.ds(PACKED * SUBLANES, 1), :] = jnp.zeros((1, LANES), jnp.float32)


def follow(ends, kept):
    return pl.pallas_call(
        follow_kernel,
        out_shape=jax.ShapeDtypeStruct(ends.shape, jnp.float32),
        in_specs=[VMEM, ANY],
        out_specs=VMEM,
        input_output_aliases={0: 0},
        compiler_params=pltpu.CompilerParams(vmem_limit_bytes=8 * 1024 * 1024),
        name="follow",
    )(pltpu.with_memory_space_constraint(ends, pltpu.VMEM), kept)


def side_steps(straight, info, whole, ends, slabs, scratch, pieces):
    moved, reds, fields, moved_later, reds_later, final = slabs
    start_fields, colours, walls = scratch
    state, later = (ByRow(moved), ByRow(reds)), (ByRow(moved_later), ByRow(reds_later))
    geometry = Geometry(info, OWN_TILES)
    live = geometry.live
    is_low = info[3] == (0 if straight else 1)
    fill_wall_table(walls, geometry)

    def ends_of(half):
        blocks = []
        for group in range(FULL * PLANES // GROUP):
            first = half * (PACKED + 1) + group * (GROUP - 1)
            packed = [ends[pl.ds((first + k) * SUBLANES, SUBLANES), :] for k in range(GROUP - 1)]
            blocks = blocks + unpack_blocks(packed)
        last = half * (PACKED + 1) + PACKED
        return blocks + [ends[pl.ds(last * SUBLANES, SUBLANES), :]]

    tiles = block_tiles()
    middle = (tiles >= 1) & (tiles <= OWN_TILES)

    def widened(own, other):
        beside = jnp.where(tiles == 0, roll_tiles(other, -OWN_TILES), roll_tiles(other, OWN_TILES))
        return jnp.where(geometry.domain, jnp.where(middle, own, beside), 0.0)

    halves = (0, 1) if straight else (1, 0)
    halo = [widened(*pair) for pair in zip(*[ends_of(half) for half in halves])]

    def rows_at(first, count):
        mirrored = SLAB - first - count
        local = jnp.where(is_low, first, SLAB + mirrored)
        return local, jnp.where(is_low, first - HALO, live - 2 * RIM + mirrored)

    held_start = ByRow(start_fields)
    halo_row, _ = rows_at(1, FULL)
    for number in range(FULL * PLANES):
        place, extra = divmod(number, FULL)
        write_row(held_start, ORDER[place], halo_row + extra, halo[number])
    colour_row, _ = rows_at(0, 1)
    write_row(held_start, 0, colour_row, jnp.zeros((SUBLANES, LANES), jnp.float32))
    write_row(held_start, 10, colour_row, 0.5 * halo[-1])
    local, row = rows_at(HALO, FULL)
    for extra in range(FULL):
        start_fields[local + extra] = whole[row + extra]

    def block(first, count):
        local, row = rows_at(first, count)
        return Block(geometry, [(row, local, count)])

    held, marks = ByRow(fields), ByRow(colours)
    colour_stage(block(0, 6), geometry, held_start, marks)
    collide_stage(block(1, 4), geometry, held_start, held_start, marks, walls, state)
    arrive_stage(block(2, 4), geometry, walls, state, held)
    colour_stage(block(2, 6), geometry, held, marks)
    collide_stage(block(3, 4), geometry, held, held_start, marks, walls, later)
    arrive_stage(block(4, 4), geometry, walls, later, ByRow(final))
    gather_tiles(final, jnp.where(is_low, HALO, SLAB), pieces, 0)


def edge_row(info, straight):
    is_low = info[3] == (0 if straight else 1)
    return pl.multiple_of(jnp.where(is_low, 0, info[0] - SUBLANES), SUBLANES)


def straight_kernel(info, whole, ends, inner_pieces, *refs):
    outs, slabs, pieces = refs[6:10], refs[10:16], refs[16]
    scratch, sems = refs[17:20], refs[20]
    live = info[0]
    starts = (
        jnp.where(live == TILE, TILE, SUBLANES),
        jnp.where(live == 3 * TILE, TILE + SUBLANES, 2 * TILE),
    )
    copies = []
    for number, start in enumerate(starts):
        row = pl.multiple_of(start, SUBLANES)
        copies = copies + row_copies(inner_pieces, outs, row, row, TILE, sems.at[number])
    for copy in copies:
        copy.start()
    side_steps(True, info, whole, ends, slabs, scratch, pieces)
    for copy in copies:
        copy.wait()


def crossed_kernel(info, whole, ends, straight_pieces, *refs):
    outs, slabs = refs[10:14], refs[14:20]
    scratch, pieces, sems = refs[20:23], refs[23], refs[24]
    rows = [edge_row(info, straight) for straight in (True, False)]
    straight = row_copies(straight_pieces, outs, 0, rows[0], SUBLANES, sems.at[0])
    for copy in straight:
        copy.start()
    side_steps(False, info, whole, ends, slabs, scratch, pieces)
    crossed = row_copies(pieces, outs, 0, rows[1], SUBLANES, sems.at[1])
    for copy in crossed:
        copy.start()
    for copy in straight + crossed:
        copy.wait()


def run_side(straight, info, whole, ends, held_pieces, slabs, outs):
    flat_count = outs[0].shape[1]
    assert outs[0].shape[0] == 3 * TILE
    shapes = [jax.ShapeDtypeStruct(array.shape, jnp.float32) for array in (*outs, *slabs)]
    slabs = [pltpu.with_memory_space_constraint(slab, pltpu.VMEM) for slab in slabs]
    aliases = {4 + number: 4 + number for number in range(6)}
    scratch = [by_row(2 * SLAB, PLACES), by_row(2 * SLAB, 4), by_row(4, 3)]
    scratch = [scratch_of(shape) for shape in scratch]
    sems = pltpu.SemaphoreType.DMA((2, OUT_COPIES))
    edge = jax.ShapeDtypeStruct((FIELDS, SUBLANES, flat_count), jnp.float32)
    if straight:
        shapes, scratch = shapes + [edge], scratch + [sems]
    else:
        aliases.update({10 + number: number for number in range(4)})
        scratch = scratch + [scratch_of(edge), sems]
    return pl.pallas_call(
        straight_kernel if straight else crossed_kernel,
        out_shape=shapes,
        in_specs=[SMEM] + [VMEM] * 9 + ([] if straight else [ANY] * 4),
        out_specs=[ANY] * 4 + [VMEM] * (7 if straight else 6),
        scratch_shapes=scratch,
        input_output_aliases=aliases,
        compiler_params=pltpu.CompilerParams(vmem_limit_bytes=24 * 1024 * 1024),
        cost_estimate=pl.CostEstimate(flops=10_000_000, bytes_accessed=4_000_000, transcendentals=0),
        name="straight" if straight else "crossed",
    )(info, whole, ends, held_pieces, *slabs, *([] if straight else outs))


def body(density, momentum, stress, red_density, solid, widths):
    tiles_count = lax.axis_size("tiles")
    arrays = (density, momentum, stress, red_density, solid)
    info, raw, raw_solid, packet, mine = load_inputs(arrays, widths, tiles_count)
    info = pltpu.with_memory_space_constraint(info, pltpu.SMEM)
    swap = [(0, 1), (1, 0)]
    packet = lax.ppermute(packet, "sub", swap)
    spread = spread_rows(raw, raw_solid)
    ends = join_ends(mine, packet, spread)
    route = [(2 * k, 2 * k + 2) for k in range(tiles_count - 1)]
    route = route + [(2 * k + 3, 2 * k + 1) for k in range(tiles_count - 1)]
    arrived = lax.ppermute(ends, ("tiles", "sub"), route)
    whole = put_beside(info, spread, packet)
    pieces, *slabs = run_first(info, whole, arrays)
    arrived = follow(arrived, slabs[-1])
    passed = lax.ppermute(arrived, "sub", swap)
    results = run_side(True, info, whole, arrived, pieces, slabs, arrays[:4])
    outs, slabs, pieces = results[:4], results[4:10], results[10]
    return tuple(run_side(False, info, whole, passed, pieces, slabs, outs)[:4])


def solution(mesh):
    in_specs = (
        P(("groups", "tiles"), "sub"),
        P(None, ("groups", "tiles"), "sub"),
        P(None, ("groups", "tiles"), "sub"),
        P(("groups", "tiles"), "sub"),
        P(("groups", "tiles"), "sub"),
        P("groups"),
    )
    out_specs = (
        P(("groups", "tiles"), "sub"),
        P(None, ("groups", "tiles"), "sub"),
        P(None, ("groups", "tiles"), "sub"),
        P(("groups", "tiles"), "sub"),
    )
    return jax.shard_map(body, mesh=mesh, in_specs=in_specs, out_specs=out_specs, check_vma=False)
```

```python
import functools

import jax
import jax.numpy as jnp
from jax import lax
from jax.experimental import pallas as pl
from jax.experimental.pallas import tpu as pltpu
from jax.sharding import PartitionSpec as P

TILE = 16
STEPS = 2
RELAX_TIME = 0.8
SURFACE = 0.1
SEPARATION = 0.7

LANES = 128
SUBLANES = 8
FULL = 3
HALO = FULL + 1
FIELDS = 11
PLANES = FIELDS + 1
MOVED = 19
REDS = 5
HELD = MOVED + 1
RIM = 4
SLAB = HALO + 2 * RIM
OWN_TILES = SUBLANES - 2
GROUP = 4
PACKED = FULL * PLANES // GROUP * (GROUP - 1)
END_ROWS = (PACKED + 1) * SUBLANES
HALF = LANES // 2
ORDER = (0, 1, 2, 3, 10, 11, 4, 5, 6, 7, 8, 9)
PAIRS = PLANES // 2
PLACES = PLANES + 1
KEPT = 2
OUT_COPIES = 5
COLOUR_BLOCK = (16, 1)
COLLIDE_BLOCK = (16, 1)
ARRIVE_BLOCK = (16, 1)
VMEM = pl.BlockSpec(memory_space=pltpu.VMEM)
SMEM = pl.BlockSpec(memory_space=pltpu.SMEM)
ANY = pl.BlockSpec(memory_space=pl.ANY)
HBM = pl.BlockSpec(memory_space=pltpu.HBM)


class Rows:
    def __init__(self, parts):
        self.parts = parts

    def _with(self, other, operation):
        others = other.parts if isinstance(other, Rows) else [other] * len(self.parts)
        return Rows([operation(one, two) for one, two in zip(self.parts, others)])

    def __add__(self, other):
        return self._with(other, lambda one, two: one + two)

    def __sub__(self, other):
        return self._with(other, lambda one, two: one - two)

    def __rsub__(self, other):
        return self._with(other, lambda one, two: two - one)

    def __mul__(self, other):
        return self._with(other, lambda one, two: one * two)

    def __or__(self, other):
        return self._with(other, lambda one, two: one | two)

    def __eq__(self, other):
        return self._with(other, lambda one, two: one == two)

    __radd__, __rmul__, __ror__ = __add__, __mul__, __or__

    def each(self, operation):
        return Rows([operation(part) for part in self.parts])


def select(mask, yes, no):
    count = max(len(item.parts) for item in (mask, yes, no) if isinstance(item, Rows))
    columns = [
        item.parts if isinstance(item, Rows) else [item] * count for item in (mask, yes, no)
    ]
    return Rows([jnp.where(*row) for row in zip(*columns)])


def roll_lanes(values, amount):
    return values.each(lambda part: pltpu.roll(part, amount % LANES, 1))


def roll_sublanes(values, amount):
    return values.each(lambda part: pltpu.roll(part, amount % SUBLANES, 0))


class Geometry:
    def __init__(self, info, own_tiles):
        live, first, last, sub_index = info[0], info[1], info[2], info[3]
        self.live = live
        self.low_row = jnp.where(first == 1, 0, -1000)
        self.high_row = jnp.where(last == 1, live, 1000)
        shape = (SUBLANES, LANES)
        lane = lax.broadcasted_iota(jnp.int32, shape, 1)
        tile = lax.broadcasted_iota(jnp.int32, shape, 0)
        depth = lane & (TILE - 1)
        low_part = sub_index == 0
        high_part = sub_index == 1
        z_walls = {1: depth == 0, -1: depth == TILE - 1}
        y_walls = {
            1: (tile == 1) & (lane < TILE) & low_part,
            -1: (tile == own_tiles) & (lane >= LANES - TILE) & high_part,
        }
        self.walls = {(0, vel_z): wall for vel_z, wall in z_walls.items()}
        for vel_y, y_wall in y_walls.items():
            self.walls[vel_y, 0] = y_wall
            for vel_z, z_wall in z_walls.items():
                self.walls[vel_y, vel_z] = y_wall | z_wall
        own = (tile >= 1) & (tile <= own_tiles)
        self.domain = own | ((tile == own_tiles + 1) & low_part) | ((tile == 0) & high_part)
        self.first_lanes = lane < TILE
        self.last_lanes = lane >= LANES - TILE

    def from_low_y(self, values):
        return roll_lanes(select(self.last_lanes, roll_sublanes(values, 1), values), TILE)

    def from_high_y(self, values):
        return roll_lanes(select(self.first_lanes, roll_sublanes(values, -1), values), -TILE)

    def from_low_z(self, values):
        return select(self.walls[0, 1], 0.0, roll_lanes(values, 1))

    def from_high_z(self, values):
        return select(self.walls[0, -1], 0.0, roll_lanes(values, -1))


def flat_rows(row, count, tile_offset=0):
    start = row * SUBLANES
    if not isinstance(start, int):
        start = pl.multiple_of(start, SUBLANES)
    return pl.ds(start + tile_offset, count * SUBLANES)


class ByRow:
    def __init__(self, ref):
        self.ref = ref


def by_row(rows, count):
    return jax.ShapeDtypeStruct((rows, count * SUBLANES, LANES), jnp.float32)


def place_of(ref, index, row, tile_offset=0):
    if isinstance(ref, ByRow):
        return ref.ref, row, pl.ds(index * SUBLANES + tile_offset, SUBLANES)
    return ref, index, flat_rows(row, 1, tile_offset)


def read_row(ref, index, row, tile_offset=0):
    ref, first, second = place_of(ref, index, row, tile_offset)
    return ref[first, second, :]


def write_row(ref, index, row, values):
    ref, first, second = place_of(ref, index, row)
    ref[first, second, :] = values


class Block:
    def __init__(self, geometry, spans, inner=False, store_rows=None):
        self.spans = spans
        self.store_rows = store_rows or [local for row, local, count in spans]
        rows = [row + extra for row, local, count in spans for extra in range(count)]
        self.inner = inner
        rows = [row + extra for row, local, count in spans for extra in range(count)]
        if inner:
            self.x_walls = {}
            self.valid = geometry.domain
            self.kinds = [0]
            return
        ids = Rows([row + jnp.zeros((SUBLANES, LANES), jnp.int32) for row in rows])
        self.x_walls = {1: ids == geometry.low_row, -1: ids == geometry.high_row - 1}
        self.valid = ids.each(
            lambda part: geometry.domain & (part >= geometry.low_row) & (part < geometry.high_row)
        )
        self.kinds = [
            jnp.where(row == geometry.low_row, 1, 0) + jnp.where(row == geometry.high_row - 1, 2, 0)
            for row in rows
        ]

    def load(self, ref, index, offset=0, tile_offset=0):
        return Rows([
            read_row(ref, index, local + offset + extra, tile_offset)
            for row, local, count in self.spans
            for extra in range(count)
        ])

    def store(self, ref, index, values):
        targets = [
            target + extra
            for (row, local, count), target in zip(self.spans, self.store_rows)
            for extra in range(count)
        ]
        for target, part in zip(targets, values.parts):
            write_row(ref, index, target, part)

    def wall_terms(self, walls, position):
        terms = [walls[position, flat_rows(kind, 1), :] for kind in self.kinds]
        return terms[0] if self.inner else Rows(terms)


def fill_wall_table(walls, geometry):
    one = jnp.ones((SUBLANES, LANES), jnp.float32)
    up_y, down_y, up_z, down_z = [
        jnp.where(geometry.walls[key], 0.0, one) for key in ((-1, 0), (1, 0), (0, -1), (0, 1))
    ]
    sum_y, sum_z = up_y + down_y, up_z + down_z
    for kind, (up_x, down_x) in enumerate(((1.0, 1.0), (1.0, 0.0), (0.0, 1.0))):
        sum_x = up_x + down_x
        around_x = 2.0 + sum_y + sum_z
        total = 12.0 + 2.0 * (sum_x + sum_y + sum_z) + sum_x * (sum_y + sum_z) + sum_y * sum_z
        rows = (
            (up_x - down_x) * around_x,
            (up_y - down_y) * (2.0 + sum_x + sum_z),
            (up_z - down_z) * (2.0 + sum_x + sum_y),
            36.0 - total,
        )
        for position, row in enumerate(rows):
            walls[position, flat_rows(kind, 1), :] = row


VELOCITIES = tuple(
    tuple(sign if axis == place else 0 for place in range(3)) for axis in range(3) for sign in (1, -1)
) + tuple(
    tuple({a: one, b: two}.get(place, 0) for place in range(3))
    for a, b in ((0, 1), (0, 2), (1, 2))
    for one, two in ((1, 1), (-1, -1), (1, -1), (-1, 1))
)
VELOCITIES = ((0, 0, 0),) + VELOCITIES


def colour_stage(block, geometry, fields, colours):
    density = block.load(fields, 0)
    red = block.load(fields, 10)
    colour = select(block.valid, 2.0 * red - density, 0.0)
    along_y = geometry.from_low_y(colour) + geometry.from_high_y(colour)
    along_z = geometry.from_low_z(colour) + geometry.from_high_z(colour)
    block.store(colours, 0, colour)
    block.store(colours, 1, 2.0 * colour + (along_y + along_z))
    block.store(colours, 2, along_y)
    block.store(colours, 3, along_z)


def collide_stage(block, geometry, fields, solids, colours, walls, state):
    relaxing = 1.0 - 1.0 / RELAX_TIME
    third = 1.0 / 3.0
    colour = block.load(colours, 0)
    doubled = 2.0 * colour + (block.load(colours, 0, -1) + block.load(colours, 0, 1))
    term_y = doubled + block.load(colours, 3)
    term_z = doubled + block.load(colours, 2)
    grad_x = block.load(colours, 1, 1) - block.load(colours, 1, -1)
    grad_y = geometry.from_high_y(term_y) - geometry.from_low_y(term_y)
    grad_z = geometry.from_high_z(term_z) - geometry.from_low_z(term_z)
    if not block.inner:
        grad_x = grad_x - block.wall_terms(walls, 0) * colour
    grad_y = grad_y - block.wall_terms(walls, 1) * colour
    grad_z = grad_z - block.wall_terms(walls, 2) * colour

    fluid = block.load(solids, PLANES - 1) == 0.0
    density = block.load(fields, 0)
    red = block.load(fields, 10)
    flux = [block.load(fields, 1 + axis) for axis in range(3)]
    stress = [block.load(fields, 4 + part) for part in range(6)]
    square_xx, square_yy, square_zz = grad_x * grad_x, grad_y * grad_y, grad_z * grad_z
    square = square_xx + square_yy + square_zz
    inverse = select(fluid, (1.0 + square * (1.0 / 144.0)).each(lax.rsqrt), 0.0)
    trace = third * square
    strength = (SURFACE / (8.0 * 144.0)) * inverse
    keep = select(fluid, relaxing / 8.0, 1.0 / 8.0)
    eighths = [0.125 * part for part in flux]
    own = [
        eighths[axis] * flux[axis] + (keep * stress[axis] + strength * (squared - trace))
        for axis, squared in enumerate((square_xx, square_yy, square_zz))
    ]
    strength, keep = 2.0 * strength, 2.0 * keep
    quarters = [2.0 * part for part in eighths[:2]]
    grads = (grad_x, grad_y, grad_z)
    cross = [
        quarters[a] * flux[b] + (keep * stress[3 + plane] + strength * (grads[a] * grads[b]))
        for plane, (a, b) in enumerate(((0, 1), (0, 2), (1, 2)))
    ]
    base = density * (1.0 / 36.0) - third * (own[0] + own[1] + own[2])
    sign = select(fluid, 1.0 / 12.0, -1.0 / 12.0)
    run = [sign * part for part in flux]
    mixing = ((SEPARATION / 144.0) * red) * ((density - red) * inverse)
    red_run = [0.5 * part + mixing * grad for part, grad in zip(run, grads)]
    moved, reds = state
    block.store(moved, 0, 12.0 * base)
    straight = [base + part for part in own]
    for axis in range(3):
        middle = 2.0 * straight[axis]
        swing = 2.0 * run[axis]
        block.store(moved, 1 + 2 * axis, middle + swing)
        block.store(moved, 2 + 2 * axis, middle - swing)
    for plane, (a, b) in enumerate(((0, 1), (0, 2), (1, 2))):
        middle = straight[a] + own[b]
        same, other = middle + cross[plane], middle - cross[plane]
        along, against = run[a] + run[b], run[a] - run[b]
        first = 7 + 4 * plane
        block.store(moved, first, same + along)
        block.store(moved, first + 1, same - along)
        block.store(moved, first + 2, other + against)
        block.store(moved, first + 3, other - against)

    red_base = select(block.valid, red * (1.0 / 36.0), 0.0)
    red_run = [select(block.valid, part, 0.0) for part in red_run]
    block.store(reds, 0, red_base)
    block.store(reds, 1, red_base + red_run[0])
    block.store(reds, 2, red_base - red_run[0])
    block.store(reds, 3, red_run[1])
    block.store(reds, 4, red_run[2])


def arrive_stage(block, geometry, walls, state, fields):
    third = 1.0 / 3.0
    moved, reds = state
    own = [None] * MOVED

    def here(direction):
        if own[direction] is None:
            own[direction] = block.load(moved, direction)
        return own[direction]

    def arrived(direction, opposite):
        vel_x, vel_y, vel_z = VELOCITIES[direction]
        values = here(direction) if vel_x == 0 else block.load(moved, direction, -vel_x)
        if vel_y != 0:
            beside = block.load(moved, direction, -vel_x, -vel_y)
            leaving = geometry.last_lanes if vel_y == 1 else geometry.first_lanes
            values = select(leaving, beside, values)
        if vel_y != 0 or vel_z != 0:
            values = roll_lanes(values, TILE * vel_y + vel_z)
        masks = []
        if vel_x in block.x_walls:
            masks.append(block.x_walls[vel_x])
        if (vel_y, vel_z) in geometry.walls:
            masks.append(geometry.walls[vel_y, vel_z])
        if not masks:
            return values
        wall = functools.reduce(lambda one, two: one | two, masks)
        return select(wall, here(opposite), values)

    red = block.load(reds, 0)
    red_y = block.load(reds, 3)
    red_z = block.load(reds, 4)
    from_x = block.load(reds, 1, -1) + block.load(reds, 2, 1)
    spread = 2.0 * red + from_x
    spread_y = 2.0 * red_y + (block.load(reds, 3, -1) + block.load(reds, 3, 1))
    spread_z = 2.0 * red_z + (block.load(reds, 4, -1) + block.load(reds, 4, 1))
    up_y, down_y = red + red_y, red - red_y
    low_y = (
        (spread + spread_y)
        + geometry.from_low_z(up_y + red_z)
        + geometry.from_high_z(up_y - red_z)
    )
    high_y = (
        (spread - spread_y)
        + geometry.from_low_z(down_y + red_z)
        + geometry.from_high_z(down_y - red_z)
    )
    bounced = (
        block.wall_terms(walls, 3) * red
        - block.wall_terms(walls, 1) * red_y
        - block.wall_terms(walls, 2) * red_z
    )
    if not block.inner:
        bounced = bounced - block.wall_terms(walls, 0) * (block.load(reds, 1) - red)
    red_total = (
        12.0 * red
        + 2.0 * from_x
        + geometry.from_low_z(spread + spread_z)
        + geometry.from_high_z(spread - spread_z)
        + geometry.from_low_y(low_y)
        + geometry.from_high_y(high_y)
        + bounced
    )
    rest = here(0)
    sums, diffs = [], []
    for axis in range(3):
        up = arrived(1 + 2 * axis, 2 + 2 * axis)
        down = arrived(2 + 2 * axis, 1 + 2 * axis)
        sums.append(up + down)
        diffs.append(up - down)
    total = rest + sums[0] + sums[1] + sums[2]
    cross = []
    for plane, (a, b) in enumerate(((0, 1), (0, 2), (1, 2))):
        first = 7 + 4 * plane
        parts = [arrived(first + offset, first + (offset ^ 1)) for offset in range(4)]
        same, other = parts[0] + parts[1], parts[2] + parts[3]
        along, against = parts[0] - parts[1], parts[2] - parts[3]
        both = same + other
        cross.append(same - other)
        total = total + both
        sums[a], sums[b] = sums[a] + both, sums[b] + both
        diffs[a], diffs[b] = diffs[a] + (along + against), diffs[b] + (along - against)
    shared = third * total
    block.store(fields, 0, total)
    for axis in range(3):
        block.store(fields, 1 + axis, diffs[axis])
        block.store(fields, 4 + axis, sums[axis] - shared - diffs[axis] * diffs[axis])
    for plane, (a, b) in enumerate(((0, 1), (0, 2), (1, 2))):
        block.store(fields, 7 + plane, cross[plane] - diffs[a] * diffs[b])
    block.store(fields, 10, red_total)


def over_rows(geometry, first, size, blocks, stage):
    trip = size * blocks
    rest = -2 * first % trip
    assert TILE % trip == 0 and rest % min(size, rest or size) == 0

    def run(start, count, step_size):
        for offset in range(0, count, step_size):
            row = start + offset
            stage(Block(geometry, [(row, row, step_size)], inner=True))

    def step(index, carry):
        run(first + index * trip, trip, size)
        return carry

    trips = (geometry.live - 2 * first - rest) // trip
    lax.fori_loop(0, trips, step, 0)
    if rest:
        run(geometry.live - first - rest, rest, min(size, rest))


def block_tiles():
    return lax.broadcasted_iota(jnp.int32, (SUBLANES, LANES), 0)


def roll_tiles(block, amount):
    return pltpu.roll(block, amount % SUBLANES, 0)


def pack_blocks(blocks):
    tiles, rest = block_tiles(), blocks[GROUP - 1]
    packed = []
    for number, block in enumerate(blocks[: GROUP - 1]):
        low, high = 2 * number + 1, 2 * number + 2
        block = jnp.where(tiles == 0, roll_tiles(rest, -low), block)
        packed.append(jnp.where(tiles == SUBLANES - 1, roll_tiles(rest, SUBLANES - 1 - high), block))
    return packed


def unpack_blocks(packed):
    tiles, rest = block_tiles(), None
    for number, block in enumerate(packed):
        low, high = 2 * number + 1, 2 * number + 2
        part = jnp.where(tiles == low, roll_tiles(block, low), roll_tiles(block, high - SUBLANES + 1))
        rest = part if rest is None else jnp.where(tiles >= low, part, rest)
    return list(packed) + [rest]


def flat_view(ref):
    rows, width, lanes = ref.shape
    return ref.reshape(rows * width, lanes)


def spread_tile(raw, raw_solid, index, row, target, target_row):
    source = raw_solid if index == FIELDS else raw.at[index]
    width = target.shape[1]
    for tile in range(OWN_TILES):
        values = source[pl.ds(row, SUBLANES), pl.ds(tile * LANES, LANES)].astype(jnp.float32)
        start = target_row * width + index * SUBLANES + 1 + tile
        flat_view(target)[pl.ds(start, SUBLANES, stride=width), :] = values


def load_kernel(
    tiles_count, density, momentum, stress, red, solid, widths,
    info, raw, raw_solid, packet, mine,
    first_tile, last_tile, held_widths, sems,
):
    row_count, flat_count = raw_solid.shape
    own_tiles = flat_count // LANES
    copies = [
        pltpu.make_async_copy(widths, held_widths, sems.at[0]),
        pltpu.make_async_copy(density, raw.at[0], sems.at[1]),
        pltpu.make_async_copy(momentum, raw.at[pl.ds(1, 3)], sems.at[2]),
        pltpu.make_async_copy(red, raw.at[10], sems.at[3]),
        pltpu.make_async_copy(solid, raw_solid, sems.at[4]),
        pltpu.make_async_copy(stress.at[pl.ds(0, 3)], raw.at[pl.ds(4, 3)], sems.at[5]),
        pltpu.make_async_copy(stress.at[pl.ds(3, 3)], raw.at[pl.ds(7, 3)], sems.at[6]),
    ]
    for copy in copies:
        copy.start()
    tiles_index, sub_index = lax.axis_index("tiles"), lax.axis_index("sub")
    low_part = sub_index == 0
    edge_start = pl.multiple_of(jnp.where(low_part, (own_tiles - 1) * LANES, 0), LANES)

    copies[0].wait()
    live = held_widths[tiles_index] * TILE
    info[0] = live
    info[1] = (tiles_index == 0).astype(jnp.int32)
    info[2] = (tiles_index == tiles_count - 1).astype(jnp.int32)
    info[3] = sub_index

    near_cut = lax.broadcasted_iota(jnp.int32, (SUBLANES, LANES), 1) < HALF
    near_cut = near_cut == jnp.logical_not(low_part)
    near_last = pl.multiple_of(live - SUBLANES, SUBLANES)
    edges = pl.ds(edge_start, LANES)

    def plane_of(index):
        return raw_solid if index == FIELDS else raw.at[index]

    def pack_edges(pair):
        here, there = [plane_of(index) for index in ORDER[2 * pair : 2 * pair + 2]]
        for row in range(0, row_count, SUBLANES):
            rows = pl.ds(row, SUBLANES)
            beside = pltpu.roll(there[rows, edges].astype(jnp.float32), HALF, 1)
            both = jnp.where(near_cut, here[rows, edges].astype(jnp.float32), beside)
            packet[pl.ds(END_ROWS + pair * row_count + row, SUBLANES), :] = both

    targets = ((packet, jnp.logical_not(low_part)), (mine, low_part))

    def row_of(use_last, index, number_first, number_last):
        first = read_row(ByRow(first_tile), index, number_first)
        last = read_row(ByRow(last_tile), index, number_last)
        return jnp.where(use_last, last, first)

    def pack_ends(group):
        for target, use_last in targets:
            blocks = []
            for number in range(group * GROUP, (group + 1) * GROUP):
                place, extra = divmod(number, FULL)
                blocks.append(row_of(use_last, ORDER[place], extra, SUBLANES - FULL + extra))
            for number, block in enumerate(pack_blocks(blocks)):
                place = (group * (GROUP - 1) + number) * SUBLANES
                target[pl.ds(place, SUBLANES), :] = block

    place = 0
    for copy, count in zip(copies[1:], (1, 3, 1, 1, 3, 3)):
        copy.wait()
        before, place = place, place + count
        for index in ORDER[before:place]:
            for target, row in ((first_tile, 0), (last_tile, near_last)):
                spread_tile(raw, raw_solid, index, row, target, 0)
        for pair in range(before // 2, place // 2):
            pack_edges(pair)
        for group in range(before * FULL // GROUP, place * FULL // GROUP):
            pack_ends(group)
    for target, use_last in targets:
        red_row, density_row = [
            row_of(use_last, index, FULL, SUBLANES - HALO) for index in (10, 0)
        ]
        target[pl.ds(PACKED * SUBLANES, SUBLANES), :] = 2.0 * red_row - density_row


def load_inputs(arrays, widths, tiles_count):
    row_count, flat_count = arrays[0].shape
    return pl.pallas_call(
        functools.partial(load_kernel, tiles_count),
        out_shape=[
            pltpu.SMEM((4,), jnp.int32),
            jax.ShapeDtypeStruct((FIELDS, row_count, flat_count), jnp.float32),
            jax.ShapeDtypeStruct((row_count, flat_count), jnp.int32),
            jax.ShapeDtypeStruct((END_ROWS + PAIRS * row_count, LANES), jnp.float32),
            jax.ShapeDtypeStruct((END_ROWS, LANES), jnp.float32),
        ],
        in_specs=[HBM] * 6,
        out_specs=[SMEM] + [VMEM] * 4,
        scratch_shapes=[
            pltpu.VMEM((SUBLANES, PLACES * SUBLANES, LANES), jnp.float32),
            pltpu.VMEM((SUBLANES, PLACES * SUBLANES, LANES), jnp.float32),
            pltpu.SMEM(widths.shape, jnp.int32),
            pltpu.SemaphoreType.DMA((7,)),
        ],
        compiler_params=pltpu.CompilerParams(vmem_limit_bytes=16 * 1024 * 1024),
        name="load",
    )(*[pltpu.with_memory_space_constraint(array, pltpu.HBM) for array in (*arrays, widths)])


def spread_kernel(raw, raw_solid, spread):
    for index in range(PLANES):
        for row in range(0, raw_solid.shape[0], SUBLANES):
            spread_tile(raw, raw_solid, index, row, spread, row)


def spread_rows(raw, raw_solid):
    row_count = raw_solid.shape[0]
    return pl.pallas_call(
        spread_kernel,
        out_shape=by_row(row_count, PLACES),
        in_specs=[VMEM, VMEM],
        out_specs=VMEM,
        compiler_params=pltpu.CompilerParams(vmem_limit_bytes=16 * 1024 * 1024),
        cost_estimate=pl.CostEstimate(flops=1_000_000, bytes_accessed=4_000_000, transcendentals=0),
        name="spread",
    )(raw, raw_solid)


def join_kernel(mine, packet, spread, ends):
    ends[pl.ds(0, END_ROWS), :] = mine[...]
    ends[pl.ds(END_ROWS, END_ROWS), :] = packet[pl.ds(0, END_ROWS), :]


def join_ends(mine, packet, spread):
    return pl.pallas_call(
        join_kernel,
        out_shape=jax.ShapeDtypeStruct((2 * END_ROWS, LANES), jnp.float32),
        in_specs=[VMEM, VMEM, ANY],
        out_specs=VMEM,
        compiler_params=pltpu.CompilerParams(vmem_limit_bytes=8 * 1024 * 1024),
        name="join",
    )(mine, packet, spread)


def beside_kernel(info, spread, packet, whole):
    low_part = info[3] == 0
    row_count, width = spread.shape[:2]
    flat = flat_view(whole)
    for pair in range(PAIRS):
        for row in range(0, row_count, SUBLANES):
            both = packet[pl.ds(END_ROWS + pair * row_count + row, SUBLANES), :]
            for place, values in ((2 * pair, both), (2 * pair + 1, pltpu.roll(both, HALF, 1))):
                index = ORDER[place]
                start = row * width + index * SUBLANES
                below = jnp.where(low_part, 0.0, values)
                above = jnp.where(low_part, values, 0.0)
                flat[pl.ds(start, SUBLANES, stride=width), :] = below
                flat[pl.ds(start + SUBLANES - 1, SUBLANES, stride=width), :] = above


def put_beside(info, spread, packet):
    return pl.pallas_call(
        beside_kernel,
        out_shape=jax.ShapeDtypeStruct(spread.shape, jnp.float32),
        in_specs=[SMEM, VMEM, VMEM],
        out_specs=VMEM,
        input_output_aliases={1: 0},
        compiler_params=pltpu.CompilerParams(vmem_limit_bytes=16 * 1024 * 1024),
        name="beside",
    )(info, pltpu.with_memory_space_constraint(spread, pltpu.VMEM), packet)


def keep_rows(slab, source, first, size, live):
    for slab_row, row in slab_rows(live, first, size):
        for extra in range(size):
            slab[slab_row + extra] = source[row + extra]


def slab_rows(live, first, size):
    mirrored = SLAB - first - size
    return [(first, first - HALO), (SLAB + mirrored, live - 2 * RIM + mirrored)]


def collide_rows(geometry, before, whole, first, colours, walls, state):
    over_rows(geometry, first - 1, *COLOUR_BLOCK, lambda block: colour_stage(
        block, geometry, before, colours))
    over_rows(geometry, first, *COLLIDE_BLOCK, lambda block: collide_stage(
        block, geometry, before, whole, colours, walls, state))


def row_copies(pieces, outs, held_row, out_row, count, sems):
    held, rows = pl.ds(held_row, count), pl.ds(out_row, count)
    parts = (
        (pieces.at[0, held], outs[0].at[rows]),
        (pieces.at[pl.ds(1, 3), held], outs[1].at[:, rows]),
        (pieces.at[pl.ds(4, 3), held], outs[2].at[pl.ds(0, 3), rows]),
        (pieces.at[pl.ds(7, 3), held], outs[2].at[pl.ds(3, 3), rows]),
        (pieces.at[10, held], outs[3].at[rows]),
    )
    return [
        pltpu.make_async_copy(source, target, sems.at[number])
        for number, (source, target) in enumerate(parts)
    ]


def gather_tiles(final, row, pieces, held_row):
    width = final.shape[1]
    start = row * width
    if not isinstance(start, int):
        start = pl.multiple_of(start, SUBLANES)
    for index in range(FIELDS):
        for tile in range(OWN_TILES):
            place = start + index * SUBLANES + 1 + tile
            pieces[index, pl.ds(held_row, SUBLANES), pl.ds(tile * LANES, LANES)] = flat_view(final)[
                pl.ds(place, SUBLANES, stride=width), :
            ]


def first_kernel(
    info, whole, final,
    moved_slab, reds_slab, fields_slab, moved_later_slab, reds_later_slab, final_slab,
    colours, walls, moved, reds, fields, moved_later, reds_later,
):
    state, later = (ByRow(moved), ByRow(reds)), (ByRow(moved_later), ByRow(reds_later))
    geometry = Geometry(info, OWN_TILES)
    live = geometry.live
    fill_wall_table(walls, geometry)
    collide_rows(geometry, ByRow(whole), ByRow(whole), 1, ByRow(colours), walls, state)
    over_rows(geometry, 2, *ARRIVE_BLOCK, lambda block: arrive_stage(
        block, geometry, walls, state, ByRow(fields)))
    keep_rows(moved_slab, moved, HALO + 1, KEPT, live)
    keep_rows(reds_slab, reds, HALO + 1, KEPT, live)
    keep_rows(fields_slab, fields, HALO + 2, KEPT, live)
    collide_rows(geometry, ByRow(fields), ByRow(whole), 3, ByRow(colours), walls, later)
    keep_rows(moved_later_slab, moved_later, HALO + 3, KEPT, live)
    keep_rows(reds_later_slab, reds_later, HALO + 3, KEPT, live)
    edges = slab_rows(live, HALO + RIM, RIM)
    rim = Block(geometry, [(row, row, RIM) for _, row in edges], True, [at for at, _ in edges])
    arrive_stage(rim, geometry, walls, later, ByRow(final_slab))

    def finish(index, carry):
        row = SUBLANES + index * TILE
        block = Block(geometry, [(row, row, TILE)], inner=True)
        arrive_stage(block, geometry, walls, later, ByRow(final))
        return carry

    lax.fori_loop(0, live // TILE - 1, finish, 0)


def second_kernel(info, final, arrived, density_out, momentum_out, stress_out, red_out, pieces, sems):
    outs = (density_out, momentum_out, stress_out, red_out)
    live = info[0]
    copies = []
    for number, (least, inner_row, dead_row) in enumerate(
        ((2 * TILE, SUBLANES, TILE), (3 * TILE, SUBLANES + TILE, 2 * TILE))
    ):
        held_row = number * TILE

        @pl.when(live >= least)
        def _():
            for extra in range(0, TILE, SUBLANES):
                gather_tiles(final, inner_row + extra, pieces, held_row + extra)

        @pl.when(live < least)
        def _():
            zeros = jnp.zeros((FIELDS, TILE, pieces.shape[2]), jnp.float32)
            pieces[:, pl.ds(held_row, TILE), :] = zeros

        row = pl.multiple_of(jnp.where(live >= least, inner_row, dead_row), SUBLANES)
        started = row_copies(pieces, outs, held_row, row, TILE, sems.at[number])
        for copy in started:
            copy.start()
        copies = copies + started
    for copy in copies:
        copy.wait()


def scratch_of(shape):
    return pltpu.VMEM(shape.shape, shape.dtype)


def pieces_of(rows, flat_count):
    return pltpu.VMEM((FIELDS, rows, flat_count), jnp.float32)


def run_first(info, whole):
    rows = whole.shape[0]
    slabs = [by_row(2 * SLAB, count) for count in (HELD, REDS, FIELDS, HELD, REDS, FIELDS)]
    scratch = [by_row(rows, 4), by_row(4, 3)]
    scratch = scratch + [by_row(rows, count) for count in (HELD, REDS, FIELDS, HELD, REDS)]
    return pl.pallas_call(
        first_kernel,
        out_shape=[by_row(rows, FIELDS)] + slabs,
        in_specs=[SMEM, VMEM],
        out_specs=[VMEM] * 7,
        scratch_shapes=[scratch_of(shape) for shape in scratch],
        compiler_params=pltpu.CompilerParams(vmem_limit_bytes=32 * 1024 * 1024),
        cost_estimate=pl.CostEstimate(flops=40_000_000, bytes_accessed=8_000_000, transcendentals=0),
        name="first",
    )(info, whole)


def run_second(info, final, arrived, arrays):
    row_count, flat_count = arrays[0].shape
    assert row_count == 3 * TILE
    return pl.pallas_call(
        second_kernel,
        out_shape=[jax.ShapeDtypeStruct(array.shape, jnp.float32) for array in arrays[:4]],
        in_specs=[SMEM, VMEM, ANY],
        out_specs=[ANY] * 4,
        scratch_shapes=[
            pieces_of(2 * TILE, flat_count),
            pltpu.SemaphoreType.DMA((2, OUT_COPIES)),
        ],
        compiler_params=pltpu.CompilerParams(vmem_limit_bytes=16 * 1024 * 1024),
        cost_estimate=pl.CostEstimate(flops=20_000_000, bytes_accessed=8_000_000, transcendentals=0),
        name="second",
    )(info, final, arrived)


def follow_kernel(ends, kept, out):
    out[pl.ds(PACKED * SUBLANES, 1), :] = jnp.zeros((1, LANES), jnp.float32)


def follow(ends, kept):
    return pl.pallas_call(
        follow_kernel,
        out_shape=jax.ShapeDtypeStruct(ends.shape, jnp.float32),
        in_specs=[VMEM, ANY],
        out_specs=VMEM,
        input_output_aliases={0: 0},
        compiler_params=pltpu.CompilerParams(vmem_limit_bytes=8 * 1024 * 1024),
        name="follow",
    )(pltpu.with_memory_space_constraint(ends, pltpu.VMEM), kept)


def outer_kernel(info, whole, arrived, passed, *refs):
    outs = refs[10:14]
    moved, reds, fields, moved_later, reds_later, final = refs[14:20]
    start_fields, colours, walls, pieces, sems = refs[20:]
    state, later = (ByRow(moved), ByRow(reds)), (ByRow(moved_later), ByRow(reds_later))
    geometry = Geometry(info, OWN_TILES)
    live = geometry.live
    low_part = info[3] == 0
    fill_wall_table(walls, geometry)

    def ends_of(ref, half):
        blocks = []
        for group in range(FULL * PLANES // GROUP):
            first = half * (PACKED + 1) + group * (GROUP - 1)
            packed = [ref[pl.ds((first + k) * SUBLANES, SUBLANES), :] for k in range(GROUP - 1)]
            blocks = blocks + unpack_blocks(packed)
        last = half * (PACKED + 1) + PACKED
        return blocks + [ref[pl.ds(last * SUBLANES, SUBLANES), :]]

    tiles = block_tiles()
    middle = (tiles >= 1) & (tiles <= OWN_TILES)

    def widened(own, other):
        beside = jnp.where(tiles == 0, roll_tiles(other, -OWN_TILES), roll_tiles(other, OWN_TILES))
        return jnp.where(geometry.domain, jnp.where(middle, own, beside), 0.0)

    straight = [widened(*pair) for pair in zip(ends_of(arrived, 0), ends_of(arrived, 1))]
    crossed = [widened(*pair) for pair in zip(ends_of(passed, 1), ends_of(passed, 0))]
    below = [jnp.where(low_part, *pair) for pair in zip(straight, crossed)]
    above = [jnp.where(low_part, *pair) for pair in zip(crossed, straight)]

    for number in range(FULL * PLANES):
        place, extra = divmod(number, FULL)
        index = ORDER[place]
        write_row(ByRow(start_fields), index, 1 + extra, below[number])
        write_row(ByRow(start_fields), index, 2 * SLAB - HALO + extra, above[number])
    for row, colour in ((0, below[-1]), (2 * SLAB - 1, above[-1])):
        write_row(ByRow(start_fields), 0, row, jnp.zeros((SUBLANES, LANES), jnp.float32))
        write_row(ByRow(start_fields), 10, row, 0.5 * colour)
    for slab_row, row in slab_rows(live, HALO, FULL):
        for extra in range(FULL):
            start_fields[slab_row + extra] = whole[row + extra]

    def block(first, count):
        return Block(geometry, [(row, at, count) for at, row in slab_rows(live, first, count)])

    held, solids, marks = ByRow(fields), ByRow(start_fields), ByRow(colours)
    colour_stage(block(0, 6), geometry, solids, marks)
    collide_stage(block(1, 4), geometry, solids, solids, marks, walls, state)
    arrive_stage(block(2, 4), geometry, walls, state, held)
    colour_stage(block(2, 6), geometry, held, marks)
    collide_stage(block(3, 4), geometry, held, solids, marks, walls, later)
    arrive_stage(block(4, 4), geometry, walls, later, ByRow(final))

    copies = []
    for side, row, out_row in ((0, HALO, 0), (1, SLAB, live - SUBLANES)):
        gather_tiles(final, row, pieces, side * SUBLANES)
        out_row = pl.multiple_of(out_row, SUBLANES)
        copies = copies + row_copies(
            pieces, outs, side * SUBLANES, out_row, SUBLANES, sems.at[side]
        )
    for copy in copies:
        copy.start()
    for copy in copies:
        copy.wait()


def run_outer(info, whole, arrived, passed, slabs, outs):
    flat_count = outs[0].shape[1]
    shapes = [jax.ShapeDtypeStruct(array.shape, jnp.float32) for array in (*outs, *slabs)]
    slabs = [pltpu.with_memory_space_constraint(slab, pltpu.VMEM) for slab in slabs]
    aliases = {4 + number: 4 + number for number in range(6)}
    aliases.update({10 + number: number for number in range(4)})
    return pl.pallas_call(
        outer_kernel,
        out_shape=shapes,
        in_specs=[SMEM] + [VMEM] * 9 + [ANY] * 4,
        out_specs=[ANY] * 4 + [VMEM] * 6,
        scratch_shapes=[
            scratch_of(by_row(2 * SLAB, PLACES)),
            scratch_of(by_row(2 * SLAB, 4)),
            scratch_of(by_row(4, 3)),
            pieces_of(2 * SUBLANES, flat_count),
            pltpu.SemaphoreType.DMA((2, OUT_COPIES)),
        ],
        input_output_aliases=aliases,
        compiler_params=pltpu.CompilerParams(vmem_limit_bytes=24 * 1024 * 1024),
        name="outer",
    )(info, whole, arrived, passed, *slabs, *outs)


def body(density, momentum, stress, red_density, solid, widths):
    tiles_count = lax.axis_size("tiles")
    arrays = (density, momentum, stress, red_density, solid)
    info, raw, raw_solid, packet, mine = load_inputs(arrays, widths, tiles_count)
    info = pltpu.with_memory_space_constraint(info, pltpu.SMEM)
    swap = [(0, 1), (1, 0)]
    packet = lax.ppermute(packet, "sub", swap)
    spread = spread_rows(raw, raw_solid)
    ends = join_ends(mine, packet, spread)
    route = [(2 * k, 2 * k + 2) for k in range(tiles_count - 1)]
    route = route + [(2 * k + 3, 2 * k + 1) for k in range(tiles_count - 1)]
    arrived = lax.ppermute(ends, ("tiles", "sub"), route)
    whole = put_beside(info, spread, packet)
    final, *slabs = run_first(info, whole)
    arrived = follow(arrived, slabs[-1])
    passed = lax.ppermute(arrived, "sub", swap)
    outs = run_second(info, final, arrived, arrays)
    return tuple(run_outer(info, whole, arrived, passed, slabs, outs)[:4])


def solution(mesh):
    in_specs = (
        P(("groups", "tiles"), "sub"),
        P(None, ("groups", "tiles"), "sub"),
        P(None, ("groups", "tiles"), "sub"),
        P(("groups", "tiles"), "sub"),
        P(("groups", "tiles"), "sub"),
        P("groups"),
    )
    out_specs = (
        P(("groups", "tiles"), "sub"),
        P(None, ("groups", "tiles"), "sub"),
        P(None, ("groups", "tiles"), "sub"),
        P(("groups", "tiles"), "sub"),
    )
    return jax.shard_map(body, mesh=mesh, in_specs=in_specs, out_specs=out_specs, check_vma=False)
```

```python
import functools

import jax
import jax.numpy as jnp
from jax import lax
from jax.experimental import pallas as pl
from jax.experimental.pallas import tpu as pltpu
from jax.sharding import PartitionSpec as P

TILE = 16
STEPS = 2
RELAX_TIME = 0.8
SURFACE = 0.1
SEPARATION = 0.7

LANES = 128
SUBLANES = 8
FULL = 3
HALO = FULL + 1
FIELDS = 11
PLANES = FIELDS + 1
MOVED = 19
REDS = 5
HELD = MOVED + 1
RIM = 4
SLAB = HALO + 2 * RIM
OWN_TILES = SUBLANES - 2
GROUP = 4
PACKED = FULL * PLANES // GROUP * (GROUP - 1)
END_ROWS = PACKED * SUBLANES
SPARE = 9
HALF = LANES // 2
ORDER = (0, 1, 2, 3, 10, 11, 4, 5, 6, 7, 8, 9)
PAIRS = PLANES // 2
PLACES = PLANES + 1
KEPT = 2
OUT_COPIES = 5
COLOUR_BLOCK = (16, 1)
COLLIDE_BLOCK = (16, 1)
ARRIVE_BLOCK = (16, 1)
VMEM = pl.BlockSpec(memory_space=pltpu.VMEM)
SMEM = pl.BlockSpec(memory_space=pltpu.SMEM)
ANY = pl.BlockSpec(memory_space=pl.ANY)
HBM = pl.BlockSpec(memory_space=pltpu.HBM)


class Rows:
    def __init__(self, parts):
        self.parts = parts

    def _with(self, other, operation):
        others = other.parts if isinstance(other, Rows) else [other] * len(self.parts)
        return Rows([operation(one, two) for one, two in zip(self.parts, others)])

    def __add__(self, other):
        return self._with(other, lambda one, two: one + two)

    def __sub__(self, other):
        return self._with(other, lambda one, two: one - two)

    def __rsub__(self, other):
        return self._with(other, lambda one, two: two - one)

    def __mul__(self, other):
        return self._with(other, lambda one, two: one * two)

    def __or__(self, other):
        return self._with(other, lambda one, two: one | two)

    def __eq__(self, other):
        return self._with(other, lambda one, two: one == two)

    __radd__, __rmul__, __ror__ = __add__, __mul__, __or__

    def each(self, operation):
        return Rows([operation(part) for part in self.parts])


def select(mask, yes, no):
    count = max(len(item.parts) for item in (mask, yes, no) if isinstance(item, Rows))
    columns = [
        item.parts if isinstance(item, Rows) else [item] * count for item in (mask, yes, no)
    ]
    return Rows([jnp.where(*row) for row in zip(*columns)])


def roll_lanes(values, amount):
    return values.each(lambda part: pltpu.roll(part, amount % LANES, 1))


def roll_sublanes(values, amount):
    return values.each(lambda part: pltpu.roll(part, amount % SUBLANES, 0))


class Geometry:
    def __init__(self, info, own_tiles):
        live, first, last, sub_index = info[0], info[1], info[2], info[3]
        self.live = live
        self.low_row = jnp.where(first == 1, 0, -1000)
        self.high_row = jnp.where(last == 1, live, 1000)
        shape = (SUBLANES, LANES)
        lane = lax.broadcasted_iota(jnp.int32, shape, 1)
        tile = lax.broadcasted_iota(jnp.int32, shape, 0)
        depth = lane & (TILE - 1)
        low_part = sub_index == 0
        high_part = sub_index == 1
        z_walls = {1: depth == 0, -1: depth == TILE - 1}
        y_walls = {
            1: (tile == 1) & (lane < TILE) & low_part,
            -1: (tile == own_tiles) & (lane >= LANES - TILE) & high_part,
        }
        self.walls = {(0, vel_z): wall for vel_z, wall in z_walls.items()}
        for vel_y, y_wall in y_walls.items():
            self.walls[vel_y, 0] = y_wall
            for vel_z, z_wall in z_walls.items():
                self.walls[vel_y, vel_z] = y_wall | z_wall
        own = (tile >= 1) & (tile <= own_tiles)
        self.domain = own | ((tile == own_tiles + 1) & low_part) | ((tile == 0) & high_part)
        self.first_lanes = lane < TILE
        self.last_lanes = lane >= LANES - TILE

    def from_low_y(self, values):
        return roll_lanes(select(self.last_lanes, roll_sublanes(values, 1), values), TILE)

    def from_high_y(self, values):
        return roll_lanes(select(self.first_lanes, roll_sublanes(values, -1), values), -TILE)

    def from_low_z(self, values):
        return select(self.walls[0, 1], 0.0, roll_lanes(values, 1))

    def from_high_z(self, values):
        return select(self.walls[0, -1], 0.0, roll_lanes(values, -1))


def flat_rows(row, count, tile_offset=0):
    start = row * SUBLANES
    if not isinstance(start, int):
        start = pl.multiple_of(start, SUBLANES)
    return pl.ds(start + tile_offset, count * SUBLANES)


class ByRow:
    def __init__(self, ref):
        self.ref = ref


def by_row(rows, count):
    return jax.ShapeDtypeStruct((rows, count * SUBLANES, LANES), jnp.float32)


def place_of(ref, index, row, tile_offset=0):
    if isinstance(ref, ByRow):
        return ref.ref, row, pl.ds(index * SUBLANES + tile_offset, SUBLANES)
    return ref, index, flat_rows(row, 1, tile_offset)


def read_row(ref, index, row, tile_offset=0):
    ref, first, second = place_of(ref, index, row, tile_offset)
    return ref[first, second, :]


def write_row(ref, index, row, values):
    ref, first, second = place_of(ref, index, row)
    ref[first, second, :] = values


class Block:
    def __init__(self, geometry, spans, inner=False, store_rows=None):
        self.spans = spans
        self.store_rows = store_rows or [local for row, local, count in spans]
        rows = [row + extra for row, local, count in spans for extra in range(count)]
        self.inner = inner
        rows = [row + extra for row, local, count in spans for extra in range(count)]
        if inner:
            self.x_walls = {}
            self.valid = geometry.domain
            self.kinds = [0]
            return
        ids = Rows([row + jnp.zeros((SUBLANES, LANES), jnp.int32) for row in rows])
        self.x_walls = {1: ids == geometry.low_row, -1: ids == geometry.high_row - 1}
        self.valid = ids.each(
            lambda part: geometry.domain & (part >= geometry.low_row) & (part < geometry.high_row)
        )
        self.kinds = [
            jnp.where(row == geometry.low_row, 1, 0) + jnp.where(row == geometry.high_row - 1, 2, 0)
            for row in rows
        ]

    def load(self, ref, index, offset=0, tile_offset=0):
        return Rows([
            read_row(ref, index, local + offset + extra, tile_offset)
            for row, local, count in self.spans
            for extra in range(count)
        ])

    def store(self, ref, index, values):
        targets = [
            target + extra
            for (row, local, count), target in zip(self.spans, self.store_rows)
            for extra in range(count)
        ]
        for target, part in zip(targets, values.parts):
            write_row(ref, index, target, part)

    def wall_terms(self, walls, position):
        terms = [walls[position, flat_rows(kind, 1), :] for kind in self.kinds]
        return terms[0] if self.inner else Rows(terms)


def fill_wall_table(walls, geometry):
    one = jnp.ones((SUBLANES, LANES), jnp.float32)
    up_y, down_y, up_z, down_z = [
        jnp.where(geometry.walls[key], 0.0, one) for key in ((-1, 0), (1, 0), (0, -1), (0, 1))
    ]
    sum_y, sum_z = up_y + down_y, up_z + down_z
    for kind, (up_x, down_x) in enumerate(((1.0, 1.0), (1.0, 0.0), (0.0, 1.0))):
        sum_x = up_x + down_x
        around_x = 2.0 + sum_y + sum_z
        total = 12.0 + 2.0 * (sum_x + sum_y + sum_z) + sum_x * (sum_y + sum_z) + sum_y * sum_z
        rows = (
            (up_x - down_x) * around_x,
            (up_y - down_y) * (2.0 + sum_x + sum_z),
            (up_z - down_z) * (2.0 + sum_x + sum_y),
            36.0 - total,
        )
        for position, row in enumerate(rows):
            walls[position, flat_rows(kind, 1), :] = row


VELOCITIES = tuple(
    tuple(sign if axis == place else 0 for place in range(3)) for axis in range(3) for sign in (1, -1)
) + tuple(
    tuple({a: one, b: two}.get(place, 0) for place in range(3))
    for a, b in ((0, 1), (0, 2), (1, 2))
    for one, two in ((1, 1), (-1, -1), (1, -1), (-1, 1))
)
VELOCITIES = ((0, 0, 0),) + VELOCITIES


def colour_stage(block, geometry, fields, colours):
    density = block.load(fields, 0)
    red = block.load(fields, 10)
    colour = select(block.valid, 2.0 * red - density, 0.0)
    along_y = geometry.from_low_y(colour) + geometry.from_high_y(colour)
    along_z = geometry.from_low_z(colour) + geometry.from_high_z(colour)
    block.store(colours, 0, colour)
    block.store(colours, 1, 2.0 * colour + (along_y + along_z))
    block.store(colours, 2, along_y)
    block.store(colours, 3, along_z)


def collide_stage(block, geometry, fields, solids, colours, walls, state):
    relaxing = 1.0 - 1.0 / RELAX_TIME
    third = 1.0 / 3.0
    colour = block.load(colours, 0)
    doubled = 2.0 * colour + (block.load(colours, 0, -1) + block.load(colours, 0, 1))
    term_y = doubled + block.load(colours, 3)
    term_z = doubled + block.load(colours, 2)
    grad_x = block.load(colours, 1, 1) - block.load(colours, 1, -1)
    grad_y = geometry.from_high_y(term_y) - geometry.from_low_y(term_y)
    grad_z = geometry.from_high_z(term_z) - geometry.from_low_z(term_z)
    if not block.inner:
        grad_x = grad_x - block.wall_terms(walls, 0) * colour
    grad_y = grad_y - block.wall_terms(walls, 1) * colour
    grad_z = grad_z - block.wall_terms(walls, 2) * colour

    fluid = block.load(solids, PLANES - 1) == 0.0
    density = block.load(fields, 0)
    red = block.load(fields, 10)
    flux = [block.load(fields, 1 + axis) for axis in range(3)]
    stress = [block.load(fields, 4 + part) for part in range(6)]
    square_xx, square_yy, square_zz = grad_x * grad_x, grad_y * grad_y, grad_z * grad_z
    square = square_xx + square_yy + square_zz
    inverse = select(fluid, (1.0 + square * (1.0 / 144.0)).each(lax.rsqrt), 0.0)
    trace = third * square
    strength = (SURFACE / (8.0 * 144.0)) * inverse
    keep = select(fluid, relaxing / 8.0, 1.0 / 8.0)
    eighths = [0.125 * part for part in flux]
    own = [
        eighths[axis] * flux[axis] + (keep * stress[axis] + strength * (squared - trace))
        for axis, squared in enumerate((square_xx, square_yy, square_zz))
    ]
    strength, keep = 2.0 * strength, 2.0 * keep
    quarters = [2.0 * part for part in eighths[:2]]
    grads = (grad_x, grad_y, grad_z)
    cross = [
        quarters[a] * flux[b] + (keep * stress[3 + plane] + strength * (grads[a] * grads[b]))
        for plane, (a, b) in enumerate(((0, 1), (0, 2), (1, 2)))
    ]
    base = density * (1.0 / 36.0) - third * (own[0] + own[1] + own[2])
    sign = select(fluid, 1.0 / 12.0, -1.0 / 12.0)
    run = [sign * part for part in flux]
    mixing = ((SEPARATION / 144.0) * red) * ((density - red) * inverse)
    red_run = [0.5 * part + mixing * grad for part, grad in zip(run, grads)]
    moved, reds = state
    block.store(moved, 0, 12.0 * base)
    straight = [base + part for part in own]
    for axis in range(3):
        middle = 2.0 * straight[axis]
        swing = 2.0 * run[axis]
        block.store(moved, 1 + 2 * axis, middle + swing)
        block.store(moved, 2 + 2 * axis, middle - swing)
    for plane, (a, b) in enumerate(((0, 1), (0, 2), (1, 2))):
        middle = straight[a] + own[b]
        same, other = middle + cross[plane], middle - cross[plane]
        along, against = run[a] + run[b], run[a] - run[b]
        first = 7 + 4 * plane
        block.store(moved, first, same + along)
        block.store(moved, first + 1, same - along)
        block.store(moved, first + 2, other + against)
        block.store(moved, first + 3, other - against)

    red_base = select(block.valid, red * (1.0 / 36.0), 0.0)
    red_run = [select(block.valid, part, 0.0) for part in red_run]
    block.store(reds, 0, red_base)
    block.store(reds, 1, red_base + red_run[0])
    block.store(reds, 2, red_base - red_run[0])
    block.store(reds, 3, red_run[1])
    block.store(reds, 4, red_run[2])


def arrive_stage(block, geometry, walls, state, fields):
    third = 1.0 / 3.0
    moved, reds = state
    own = [None] * MOVED

    def here(direction):
        if own[direction] is None:
            own[direction] = block.load(moved, direction)
        return own[direction]

    def arrived(direction, opposite):
        vel_x, vel_y, vel_z = VELOCITIES[direction]
        values = here(direction) if vel_x == 0 else block.load(moved, direction, -vel_x)
        if vel_y != 0:
            beside = block.load(moved, direction, -vel_x, -vel_y)
            leaving = geometry.last_lanes if vel_y == 1 else geometry.first_lanes
            values = select(leaving, beside, values)
        if vel_y != 0 or vel_z != 0:
            values = roll_lanes(values, TILE * vel_y + vel_z)
        masks = []
        if vel_x in block.x_walls:
            masks.append(block.x_walls[vel_x])
        if (vel_y, vel_z) in geometry.walls:
            masks.append(geometry.walls[vel_y, vel_z])
        if not masks:
            return values
        wall = functools.reduce(lambda one, two: one | two, masks)
        return select(wall, here(opposite), values)

    red = block.load(reds, 0)
    red_y = block.load(reds, 3)
    red_z = block.load(reds, 4)
    from_x = block.load(reds, 1, -1) + block.load(reds, 2, 1)
    spread = 2.0 * red + from_x
    spread_y = 2.0 * red_y + (block.load(reds, 3, -1) + block.load(reds, 3, 1))
    spread_z = 2.0 * red_z + (block.load(reds, 4, -1) + block.load(reds, 4, 1))
    up_y, down_y = red + red_y, red - red_y
    low_y = (
        (spread + spread_y)
        + geometry.from_low_z(up_y + red_z)
        + geometry.from_high_z(up_y - red_z)
    )
    high_y = (
        (spread - spread_y)
        + geometry.from_low_z(down_y + red_z)
        + geometry.from_high_z(down_y - red_z)
    )
    bounced = (
        block.wall_terms(walls, 3) * red
        - block.wall_terms(walls, 1) * red_y
        - block.wall_terms(walls, 2) * red_z
    )
    if not block.inner:
        bounced = bounced - block.wall_terms(walls, 0) * (block.load(reds, 1) - red)
    red_total = (
        12.0 * red
        + 2.0 * from_x
        + geometry.from_low_z(spread + spread_z)
        + geometry.from_high_z(spread - spread_z)
        + geometry.from_low_y(low_y)
        + geometry.from_high_y(high_y)
        + bounced
    )
    rest = here(0)
    sums, diffs = [], []
    for axis in range(3):
        up = arrived(1 + 2 * axis, 2 + 2 * axis)
        down = arrived(2 + 2 * axis, 1 + 2 * axis)
        sums.append(up + down)
        diffs.append(up - down)
    total = rest + sums[0] + sums[1] + sums[2]
    cross = []
    for plane, (a, b) in enumerate(((0, 1), (0, 2), (1, 2))):
        first = 7 + 4 * plane
        parts = [arrived(first + offset, first + (offset ^ 1)) for offset in range(4)]
        same, other = parts[0] + parts[1], parts[2] + parts[3]
        along, against = parts[0] - parts[1], parts[2] - parts[3]
        both = same + other
        cross.append(same - other)
        total = total + both
        sums[a], sums[b] = sums[a] + both, sums[b] + both
        diffs[a], diffs[b] = diffs[a] + (along + against), diffs[b] + (along - against)
    shared = third * total
    block.store(fields, 0, total)
    for axis in range(3):
        block.store(fields, 1 + axis, diffs[axis])
        block.store(fields, 4 + axis, sums[axis] - shared - diffs[axis] * diffs[axis])
    for plane, (a, b) in enumerate(((0, 1), (0, 2), (1, 2))):
        block.store(fields, 7 + plane, cross[plane] - diffs[a] * diffs[b])
    block.store(fields, 10, red_total)


def over_rows(geometry, first, size, blocks, stage):
    trip = size * blocks
    rest = -2 * first % trip
    assert TILE % trip == 0 and rest % min(size, rest or size) == 0

    def run(start, count, step_size):
        for offset in range(0, count, step_size):
            row = start + offset
            stage(Block(geometry, [(row, row, step_size)], inner=True))

    def step(index, carry):
        run(first + index * trip, trip, size)
        return carry

    trips = (geometry.live - 2 * first - rest) // trip
    lax.fori_loop(0, trips, step, 0)
    if rest:
        run(geometry.live - first - rest, rest, min(size, rest))


def block_tiles():
    return lax.broadcasted_iota(jnp.int32, (SUBLANES, LANES), 0)


def roll_tiles(block, amount):
    return pltpu.roll(block, amount % SUBLANES, 0)


def pack_blocks(blocks):
    tiles, rest = block_tiles(), blocks[GROUP - 1]
    packed = []
    for number, block in enumerate(blocks[: GROUP - 1]):
        low, high = 2 * number + 1, 2 * number + 2
        block = jnp.where(tiles == 0, roll_tiles(rest, -low), block)
        packed.append(jnp.where(tiles == SUBLANES - 1, roll_tiles(rest, SUBLANES - 1 - high), block))
    return packed


def unpack_blocks(packed):
    tiles, rest = block_tiles(), None
    for number, block in enumerate(packed):
        low, high = 2 * number + 1, 2 * number + 2
        part = jnp.where(tiles == low, roll_tiles(block, low), roll_tiles(block, high - SUBLANES + 1))
        rest = part if rest is None else jnp.where(tiles >= low, part, rest)
    return list(packed) + [rest]


def flat_view(ref):
    rows, width, lanes = ref.shape
    return ref.reshape(rows * width, lanes)


def spread_tile(raw, raw_solid, index, row, target, target_row):
    source = raw_solid if index == FIELDS else raw.at[index]
    width = target.shape[1]
    for tile in range(OWN_TILES):
        values = source[pl.ds(row, SUBLANES), pl.ds(tile * LANES, LANES)].astype(jnp.float32)
        start = target_row * width + index * SUBLANES + 1 + tile
        flat_view(target)[pl.ds(start, SUBLANES, stride=width), :] = values


def load_kernel(
    tiles_count, density, momentum, stress, red, solid, widths,
    info, raw, raw_solid, packet, mine,
    first_tile, last_tile, held_widths, sems,
):
    row_count, flat_count = raw_solid.shape
    own_tiles = flat_count // LANES
    copies = [
        pltpu.make_async_copy(widths, held_widths, sems.at[0]),
        pltpu.make_async_copy(density, raw.at[0], sems.at[1]),
        pltpu.make_async_copy(momentum, raw.at[pl.ds(1, 3)], sems.at[2]),
        pltpu.make_async_copy(red, raw.at[10], sems.at[3]),
        pltpu.make_async_copy(solid, raw_solid, sems.at[4]),
        pltpu.make_async_copy(stress.at[pl.ds(0, 3)], raw.at[pl.ds(4, 3)], sems.at[5]),
        pltpu.make_async_copy(stress.at[pl.ds(3, 3)], raw.at[pl.ds(7, 3)], sems.at[6]),
    ]
    for copy in copies:
        copy.start()
    tiles_index, sub_index = lax.axis_index("tiles"), lax.axis_index("sub")
    low_part = sub_index == 0
    edge_start = pl.multiple_of(jnp.where(low_part, (own_tiles - 1) * LANES, 0), LANES)

    copies[0].wait()
    live = held_widths[tiles_index] * TILE
    info[0] = live
    info[1] = (tiles_index == 0).astype(jnp.int32)
    info[2] = (tiles_index == tiles_count - 1).astype(jnp.int32)
    info[3] = sub_index

    near_cut = lax.broadcasted_iota(jnp.int32, (SUBLANES, LANES), 1) < HALF
    near_cut = near_cut == jnp.logical_not(low_part)
    near_last = pl.multiple_of(live - SUBLANES, SUBLANES)
    edges = pl.ds(edge_start, LANES)

    def plane_of(index):
        return raw_solid if index == FIELDS else raw.at[index]

    def pack_edges(pair):
        here, there = [plane_of(index) for index in ORDER[2 * pair : 2 * pair + 2]]
        for row in range(0, row_count, SUBLANES):
            rows = pl.ds(row, SUBLANES)
            beside = pltpu.roll(there[rows, edges].astype(jnp.float32), HALF, 1)
            both = jnp.where(near_cut, here[rows, edges].astype(jnp.float32), beside)
            packet[pl.ds(END_ROWS + pair * row_count + row, SUBLANES), :] = both

    targets = ((packet, jnp.logical_not(low_part)), (mine, low_part))

    def row_of(use_last, index, number_first, number_last):
        first = read_row(ByRow(first_tile), index, number_first)
        last = read_row(ByRow(last_tile), index, number_last)
        return jnp.where(use_last, last, first)

    def colour_of(use_last):
        red_row, density_row = [
            row_of(use_last, index, FULL, SUBLANES - HALO) for index in (10, 0)
        ]
        return 2.0 * red_row - density_row

    def pack_ends(group):
        for target, use_last in targets:
            blocks = []
            for number in range(group * GROUP, (group + 1) * GROUP):
                place, extra = divmod(number, FULL)
                block = row_of(use_last, ORDER[place], extra, SUBLANES - FULL + extra)
                if ORDER[place] == SPARE and extra == 0:
                    block = jnp.where(use_last, colour_of(use_last), block)
                if ORDER[place] == SPARE and extra == FULL - 1:
                    block = jnp.where(use_last, block, colour_of(use_last))
                blocks.append(block)
            for number, block in enumerate(pack_blocks(blocks)):
                place = (group * (GROUP - 1) + number) * SUBLANES
                target[pl.ds(place, SUBLANES), :] = block

    place = 0
    for copy, count in zip(copies[1:], (1, 3, 1, 1, 3, 3)):
        copy.wait()
        before, place = place, place + count
        for index in ORDER[before:place]:
            for target, row in ((first_tile, 0), (last_tile, near_last)):
                spread_tile(raw, raw_solid, index, row, target, 0)
        for pair in range(before // 2, place // 2):
            pack_edges(pair)
        for group in range(before * FULL // GROUP, place * FULL // GROUP):
            pack_ends(group)


def load_inputs(arrays, widths, tiles_count):
    row_count, flat_count = arrays[0].shape
    return pl.pallas_call(
        functools.partial(load_kernel, tiles_count),
        out_shape=[
            pltpu.SMEM((4,), jnp.int32),
            jax.ShapeDtypeStruct((FIELDS, row_count, flat_count), jnp.float32),
            jax.ShapeDtypeStruct((row_count, flat_count), jnp.int32),
            jax.ShapeDtypeStruct((END_ROWS + PAIRS * row_count, LANES), jnp.float32),
            jax.ShapeDtypeStruct((END_ROWS, LANES), jnp.float32),
        ],
        in_specs=[HBM] * 6,
        out_specs=[SMEM] + [VMEM] * 4,
        scratch_shapes=[
            pltpu.VMEM((SUBLANES, PLACES * SUBLANES, LANES), jnp.float32),
            pltpu.VMEM((SUBLANES, PLACES * SUBLANES, LANES), jnp.float32),
            pltpu.SMEM(widths.shape, jnp.int32),
            pltpu.SemaphoreType.DMA((7,)),
        ],
        compiler_params=pltpu.CompilerParams(vmem_limit_bytes=16 * 1024 * 1024),
        name="load",
    )(*[pltpu.with_memory_space_constraint(array, pltpu.HBM) for array in (*arrays, widths)])


def spread_kernel(raw, raw_solid, spread):
    for index in range(PLANES):
        for row in range(0, raw_solid.shape[0], SUBLANES):
            spread_tile(raw, raw_solid, index, row, spread, row)


def spread_rows(raw, raw_solid):
    row_count = raw_solid.shape[0]
    return pl.pallas_call(
        spread_kernel,
        out_shape=by_row(row_count, PLACES),
        in_specs=[VMEM, VMEM],
        out_specs=VMEM,
        compiler_params=pltpu.CompilerParams(vmem_limit_bytes=16 * 1024 * 1024),
        cost_estimate=pl.CostEstimate(flops=1_000_000, bytes_accessed=4_000_000, transcendentals=0),
        name="spread",
    )(raw, raw_solid)


def join_kernel(mine, packet, spread, ends):
    ends[pl.ds(0, END_ROWS), :] = mine[...]
    ends[pl.ds(END_ROWS, END_ROWS), :] = packet[pl.ds(0, END_ROWS), :]


def join_ends(mine, packet, spread):
    return pl.pallas_call(
        join_kernel,
        out_shape=jax.ShapeDtypeStruct((2 * END_ROWS, LANES), jnp.float32),
        in_specs=[VMEM, VMEM, ANY],
        out_specs=VMEM,
        compiler_params=pltpu.CompilerParams(vmem_limit_bytes=8 * 1024 * 1024),
        name="join",
    )(mine, packet, spread)


def beside_kernel(info, spread, packet, whole):
    low_part = info[3] == 0
    row_count, width = spread.shape[:2]
    flat = flat_view(whole)
    for pair in range(PAIRS):
        for row in range(0, row_count, SUBLANES):
            both = packet[pl.ds(END_ROWS + pair * row_count + row, SUBLANES), :]
            for place, values in ((2 * pair, both), (2 * pair + 1, pltpu.roll(both, HALF, 1))):
                index = ORDER[place]
                start = row * width + index * SUBLANES
                below = jnp.where(low_part, 0.0, values)
                above = jnp.where(low_part, values, 0.0)
                flat[pl.ds(start, SUBLANES, stride=width), :] = below
                flat[pl.ds(start + SUBLANES - 1, SUBLANES, stride=width), :] = above


def put_beside(info, spread, packet):
    return pl.pallas_call(
        beside_kernel,
        out_shape=jax.ShapeDtypeStruct(spread.shape, jnp.float32),
        in_specs=[SMEM, VMEM, VMEM],
        out_specs=VMEM,
        input_output_aliases={1: 0},
        compiler_params=pltpu.CompilerParams(vmem_limit_bytes=16 * 1024 * 1024),
        name="beside",
    )(info, pltpu.with_memory_space_constraint(spread, pltpu.VMEM), packet)


def keep_rows(slab, source, first, size, live):
    for slab_row, row in slab_rows(live, first, size):
        for extra in range(size):
            slab[slab_row + extra] = source[row + extra]


def slab_rows(live, first, size):
    mirrored = SLAB - first - size
    return [(first, first - HALO), (SLAB + mirrored, live - 2 * RIM + mirrored)]


def collide_rows(geometry, before, whole, first, colours, walls, state):
    over_rows(geometry, first - 1, *COLOUR_BLOCK, lambda block: colour_stage(
        block, geometry, before, colours))
    over_rows(geometry, first, *COLLIDE_BLOCK, lambda block: collide_stage(
        block, geometry, before, whole, colours, walls, state))


def row_copies(pieces, outs, held_row, out_row, count, sems):
    held, rows = pl.ds(held_row, count), pl.ds(out_row, count)
    parts = (
        (pieces.at[0, held], outs[0].at[rows]),
        (pieces.at[pl.ds(1, 3), held], outs[1].at[:, rows]),
        (pieces.at[pl.ds(4, 3), held], outs[2].at[pl.ds(0, 3), rows]),
        (pieces.at[pl.ds(7, 3), held], outs[2].at[pl.ds(3, 3), rows]),
        (pieces.at[10, held], outs[3].at[rows]),
    )
    return [
        pltpu.make_async_copy(source, target, sems.at[number])
        for number, (source, target) in enumerate(parts)
    ]


def gather_tiles(final, row, pieces, held_row):
    width = final.shape[1]
    start = row * width
    if not isinstance(start, int):
        start = pl.multiple_of(start, SUBLANES)
    for index in range(FIELDS):
        for tile in range(OWN_TILES):
            place = start + index * SUBLANES + 1 + tile
            pieces[index, pl.ds(held_row, SUBLANES), pl.ds(tile * LANES, LANES)] = flat_view(final)[
                pl.ds(place, SUBLANES, stride=width), :
            ]


def first_kernel(
    info, whole, final,
    moved_slab, reds_slab, fields_slab, moved_later_slab, reds_later_slab, final_slab,
    colours, walls, moved, reds, fields, moved_later, reds_later,
):
    state, later = (ByRow(moved), ByRow(reds)), (ByRow(moved_later), ByRow(reds_later))
    geometry = Geometry(info, OWN_TILES)
    live = geometry.live
    fill_wall_table(walls, geometry)
    collide_rows(geometry, ByRow(whole), ByRow(whole), 1, ByRow(colours), walls, state)
    over_rows(geometry, 2, *ARRIVE_BLOCK, lambda block: arrive_stage(
        block, geometry, walls, state, ByRow(fields)))
    keep_rows(moved_slab, moved, HALO + 1, KEPT, live)
    keep_rows(reds_slab, reds, HALO + 1, KEPT, live)
    keep_rows(fields_slab, fields, HALO + 2, KEPT, live)
    collide_rows(geometry, ByRow(fields), ByRow(whole), 3, ByRow(colours), walls, later)
    keep_rows(moved_later_slab, moved_later, HALO + 3, KEPT, live)
    keep_rows(reds_later_slab, reds_later, HALO + 3, KEPT, live)
    edges = slab_rows(live, HALO + RIM, RIM)
    rim = Block(geometry, [(row, row, RIM) for _, row in edges], True, [at for at, _ in edges])
    arrive_stage(rim, geometry, walls, later, ByRow(final_slab))

    def finish(index, carry):
        row = SUBLANES + index * TILE
        block = Block(geometry, [(row, row, TILE)], inner=True)
        arrive_stage(block, geometry, walls, later, ByRow(final))
        return carry

    lax.fori_loop(0, live // TILE - 1, finish, 0)


def second_kernel(info, final, arrived, density_out, momentum_out, stress_out, red_out, pieces, sems):
    outs = (density_out, momentum_out, stress_out, red_out)
    live = info[0]
    copies = []
    for number, (least, inner_row, dead_row) in enumerate(
        ((2 * TILE, SUBLANES, TILE), (3 * TILE, SUBLANES + TILE, 2 * TILE))
    ):
        held_row = number * TILE

        @pl.when(live >= least)
        def _():
            for extra in range(0, TILE, SUBLANES):
                gather_tiles(final, inner_row + extra, pieces, held_row + extra)

        @pl.when(live < least)
        def _():
            zeros = jnp.zeros((FIELDS, TILE, pieces.shape[2]), jnp.float32)
            pieces[:, pl.ds(held_row, TILE), :] = zeros

        row = pl.multiple_of(jnp.where(live >= least, inner_row, dead_row), SUBLANES)
        started = row_copies(pieces, outs, held_row, row, TILE, sems.at[number])
        for copy in started:
            copy.start()
        copies = copies + started
    for copy in copies:
        copy.wait()


def scratch_of(shape):
    return pltpu.VMEM(shape.shape, shape.dtype)


def pieces_of(rows, flat_count):
    return pltpu.VMEM((FIELDS, rows, flat_count), jnp.float32)


def run_first(info, whole):
    rows = whole.shape[0]
    slabs = [by_row(2 * SLAB, count) for count in (HELD, REDS, FIELDS, HELD, REDS, FIELDS)]
    scratch = [by_row(rows, 4), by_row(4, 3)]
    scratch = scratch + [by_row(rows, count) for count in (HELD, REDS, FIELDS, HELD, REDS)]
    return pl.pallas_call(
        first_kernel,
        out_shape=[by_row(rows, FIELDS)] + slabs,
        in_specs=[SMEM, VMEM],
        out_specs=[VMEM] * 7,
        scratch_shapes=[scratch_of(shape) for shape in scratch],
        compiler_params=pltpu.CompilerParams(vmem_limit_bytes=32 * 1024 * 1024),
        cost_estimate=pl.CostEstimate(flops=40_000_000, bytes_accessed=8_000_000, transcendentals=0),
        name="first",
    )(info, whole)


def run_second(info, final, arrived, arrays):
    row_count, flat_count = arrays[0].shape
    assert row_count == 3 * TILE
    return pl.pallas_call(
        second_kernel,
        out_shape=[jax.ShapeDtypeStruct(array.shape, jnp.float32) for array in arrays[:4]],
        in_specs=[SMEM, VMEM, ANY],
        out_specs=[ANY] * 4,
        scratch_shapes=[
            pieces_of(2 * TILE, flat_count),
            pltpu.SemaphoreType.DMA((2, OUT_COPIES)),
        ],
        compiler_params=pltpu.CompilerParams(vmem_limit_bytes=16 * 1024 * 1024),
        cost_estimate=pl.CostEstimate(flops=20_000_000, bytes_accessed=8_000_000, transcendentals=0),
        name="second",
    )(info, final, arrived)


def follow_kernel(ends, kept, out):
    out[pl.ds(0, 1), :] = ends[pl.ds(0, 1), :]


def follow(ends, kept):
    return pl.pallas_call(
        follow_kernel,
        out_shape=jax.ShapeDtypeStruct(ends.shape, jnp.float32),
        in_specs=[VMEM, ANY],
        out_specs=VMEM,
        input_output_aliases={0: 0},
        compiler_params=pltpu.CompilerParams(vmem_limit_bytes=8 * 1024 * 1024),
        name="follow",
    )(pltpu.with_memory_space_constraint(ends, pltpu.VMEM), kept)


def outer_kernel(info, whole, arrived, passed, *refs):
    outs = refs[10:14]
    moved, reds, fields, moved_later, reds_later, final = refs[14:20]
    start_fields, colours, walls, pieces, sems = refs[20:]
    state, later = (ByRow(moved), ByRow(reds)), (ByRow(moved_later), ByRow(reds_later))
    geometry = Geometry(info, OWN_TILES)
    live = geometry.live
    low_part = info[3] == 0
    fill_wall_table(walls, geometry)

    def ends_of(ref, half):
        blocks = []
        for group in range(FULL * PLANES // GROUP):
            first = half * PACKED + group * (GROUP - 1)
            packed = [ref[pl.ds((first + k) * SUBLANES, SUBLANES), :] for k in range(GROUP - 1)]
            blocks = blocks + unpack_blocks(packed)
        return blocks

    tiles = block_tiles()
    middle = (tiles >= 1) & (tiles <= OWN_TILES)

    def widened(own, other):
        beside = jnp.where(tiles == 0, roll_tiles(other, -OWN_TILES), roll_tiles(other, OWN_TILES))
        return jnp.where(geometry.domain, jnp.where(middle, own, beside), 0.0)

    straight = [widened(*pair) for pair in zip(ends_of(arrived, 0), ends_of(arrived, 1))]
    crossed = [widened(*pair) for pair in zip(ends_of(passed, 1), ends_of(passed, 0))]
    below = [jnp.where(low_part, *pair) for pair in zip(straight, crossed)]
    above = [jnp.where(low_part, *pair) for pair in zip(crossed, straight)]

    for number in range(FULL * PLANES):
        place, extra = divmod(number, FULL)
        index = ORDER[place]
        write_row(ByRow(start_fields), index, 1 + extra, below[number])
        write_row(ByRow(start_fields), index, 2 * SLAB - HALO + extra, above[number])
    spare = FULL * ORDER.index(SPARE)
    ends_at = ((0, 1, below[spare]), (2 * SLAB - 1, 2 * SLAB - 2, above[spare + FULL - 1]))
    for row, next_row, colour in ends_at:
        write_row(ByRow(start_fields), SPARE, next_row, jnp.zeros((SUBLANES, LANES), jnp.float32))
        write_row(ByRow(start_fields), 0, row, jnp.zeros((SUBLANES, LANES), jnp.float32))
        write_row(ByRow(start_fields), 10, row, 0.5 * colour)
    for slab_row, row in slab_rows(live, HALO, FULL):
        for extra in range(FULL):
            start_fields[slab_row + extra] = whole[row + extra]

    def block(first, count):
        return Block(geometry, [(row, at, count) for at, row in slab_rows(live, first, count)])

    held, solids, marks = ByRow(fields), ByRow(start_fields), ByRow(colours)
    colour_stage(block(0, 6), geometry, solids, marks)
    collide_stage(block(1, 4), geometry, solids, solids, marks, walls, state)
    arrive_stage(block(2, 4), geometry, walls, state, held)
    colour_stage(block(2, 6), geometry, held, marks)
    collide_stage(block(3, 4), geometry, held, solids, marks, walls, later)
    arrive_stage(block(4, 4), geometry, walls, later, ByRow(final))

    copies = []
    for side, row, out_row in ((0, HALO, 0), (1, SLAB, live - SUBLANES)):
        gather_tiles(final, row, pieces, side * SUBLANES)
        out_row = pl.multiple_of(out_row, SUBLANES)
        copies = copies + row_copies(
            pieces, outs, side * SUBLANES, out_row, SUBLANES, sems.at[side]
        )
    for copy in copies:
        copy.start()
    for copy in copies:
        copy.wait()


def run_outer(info, whole, arrived, passed, slabs, outs):
    flat_count = outs[0].shape[1]
    shapes = [jax.ShapeDtypeStruct(array.shape, jnp.float32) for array in (*outs, *slabs)]
    slabs = [pltpu.with_memory_space_constraint(slab, pltpu.VMEM) for slab in slabs]
    aliases = {4 + number: 4 + number for number in range(6)}
    aliases.update({10 + number: number for number in range(4)})
    return pl.pallas_call(
        outer_kernel,
        out_shape=shapes,
        in_specs=[SMEM] + [VMEM] * 9 + [ANY] * 4,
        out_specs=[ANY] * 4 + [VMEM] * 6,
        scratch_shapes=[
            scratch_of(by_row(2 * SLAB, PLACES)),
            scratch_of(by_row(2 * SLAB, 4)),
            scratch_of(by_row(4, 3)),
            pieces_of(2 * SUBLANES, flat_count),
            pltpu.SemaphoreType.DMA((2, OUT_COPIES)),
        ],
        input_output_aliases=aliases,
        compiler_params=pltpu.CompilerParams(vmem_limit_bytes=24 * 1024 * 1024),
        name="outer",
    )(info, whole, arrived, passed, *slabs, *outs)


def body(density, momentum, stress, red_density, solid, widths):
    tiles_count = lax.axis_size("tiles")
    arrays = (density, momentum, stress, red_density, solid)
    info, raw, raw_solid, packet, mine = load_inputs(arrays, widths, tiles_count)
    info = pltpu.with_memory_space_constraint(info, pltpu.SMEM)
    swap = [(0, 1), (1, 0)]
    packet = lax.ppermute(packet, "sub", swap)
    spread = spread_rows(raw, raw_solid)
    ends = join_ends(mine, packet, spread)
    route = [(2 * k, 2 * k + 2) for k in range(tiles_count - 1)]
    route = route + [(2 * k + 3, 2 * k + 1) for k in range(tiles_count - 1)]
    arrived = lax.ppermute(ends, ("tiles", "sub"), route)
    whole = put_beside(info, spread, packet)
    final, *slabs = run_first(info, whole)
    arrived = follow(arrived, slabs[-1])
    passed = lax.ppermute(arrived, "sub", swap)
    outs = run_second(info, final, arrived, arrays)
    return tuple(run_outer(info, whole, arrived, passed, slabs, outs)[:4])


def solution(mesh):
    in_specs = (
        P(("groups", "tiles"), "sub"),
        P(None, ("groups", "tiles"), "sub"),
        P(None, ("groups", "tiles"), "sub"),
        P(("groups", "tiles"), "sub"),
        P(("groups", "tiles"), "sub"),
        P("groups"),
    )
    out_specs = (
        P(("groups", "tiles"), "sub"),
        P(None, ("groups", "tiles"), "sub"),
        P(None, ("groups", "tiles"), "sub"),
        P(("groups", "tiles"), "sub"),
    )
    return jax.shard_map(body, mesh=mesh, in_specs=in_specs, out_specs=out_specs, check_vma=False)
```

```python
import functools

import jax
import jax.numpy as jnp
from jax import lax
from jax.experimental import pallas as pl
from jax.experimental.pallas import tpu as pltpu
from jax.sharding import PartitionSpec as P

TILE = 16
STEPS = 2
RELAX_TIME = 0.8
SURFACE = 0.1
SEPARATION = 0.7

LANES = 128
SUBLANES = 8
FULL = 3
HALO = FULL + 1
FIELDS = 11
PLANES = FIELDS + 1
MOVED = 19
REDS = 5
HELD = MOVED + 1
RIM = 4
SLAB = HALO + 2 * RIM
OWN_TILES = SUBLANES - 2
GROUP = 4
PACKED = FULL * PLANES // GROUP * (GROUP - 1)
END_ROWS = PACKED * SUBLANES
SPARE = 9
HALF = LANES // 2
ORDER = (0, 1, 2, 3, 10, 11, 4, 5, 6, 7, 8, 9)
PAIRS = PLANES // 2
PLACES = PLANES + 1
KEPT = 2
OUT_COPIES = 5
COLOUR_BLOCK = (16, 1)
COLLIDE_BLOCK = (16, 1)
ARRIVE_BLOCK = (16, 1)
VMEM = pl.BlockSpec(memory_space=pltpu.VMEM)
SMEM = pl.BlockSpec(memory_space=pltpu.SMEM)
ANY = pl.BlockSpec(memory_space=pl.ANY)
HBM = pl.BlockSpec(memory_space=pltpu.HBM)


class Rows:
    def __init__(self, parts):
        self.parts = parts

    def _with(self, other, operation):
        others = other.parts if isinstance(other, Rows) else [other] * len(self.parts)
        return Rows([operation(one, two) for one, two in zip(self.parts, others)])

    def __add__(self, other):
        return self._with(other, lambda one, two: one + two)

    def __sub__(self, other):
        return self._with(other, lambda one, two: one - two)

    def __rsub__(self, other):
        return self._with(other, lambda one, two: two - one)

    def __mul__(self, other):
        return self._with(other, lambda one, two: one * two)

    def __or__(self, other):
        return self._with(other, lambda one, two: one | two)

    def __eq__(self, other):
        return self._with(other, lambda one, two: one == two)

    __radd__, __rmul__, __ror__ = __add__, __mul__, __or__

    def each(self, operation):
        return Rows([operation(part) for part in self.parts])


def select(mask, yes, no):
    count = max(len(item.parts) for item in (mask, yes, no) if isinstance(item, Rows))
    columns = [
        item.parts if isinstance(item, Rows) else [item] * count for item in (mask, yes, no)
    ]
    return Rows([jnp.where(*row) for row in zip(*columns)])


def roll_lanes(values, amount):
    return values.each(lambda part: pltpu.roll(part, amount % LANES, 1))


def roll_sublanes(values, amount):
    return values.each(lambda part: pltpu.roll(part, amount % SUBLANES, 0))


class Geometry:
    def __init__(self, info, own_tiles):
        live, first, last, sub_index = info[0], info[1], info[2], info[3]
        self.live = live
        self.low_row = jnp.where(first == 1, 0, -1000)
        self.high_row = jnp.where(last == 1, live, 1000)
        shape = (SUBLANES, LANES)
        lane = lax.broadcasted_iota(jnp.int32, shape, 1)
        tile = lax.broadcasted_iota(jnp.int32, shape, 0)
        depth = lane & (TILE - 1)
        low_part = sub_index == 0
        high_part = sub_index == 1
        z_walls = {1: depth == 0, -1: depth == TILE - 1}
        y_walls = {
            1: (tile == 1) & (lane < TILE) & low_part,
            -1: (tile == own_tiles) & (lane >= LANES - TILE) & high_part,
        }
        self.walls = {(0, vel_z): wall for vel_z, wall in z_walls.items()}
        for vel_y, y_wall in y_walls.items():
            self.walls[vel_y, 0] = y_wall
            for vel_z, z_wall in z_walls.items():
                self.walls[vel_y, vel_z] = y_wall | z_wall
        own = (tile >= 1) & (tile <= own_tiles)
        self.domain = own | ((tile == own_tiles + 1) & low_part) | ((tile == 0) & high_part)
        self.first_lanes = lane < TILE
        self.last_lanes = lane >= LANES - TILE

    def from_low_y(self, values):
        return roll_lanes(select(self.last_lanes, roll_sublanes(values, 1), values), TILE)

    def from_high_y(self, values):
        return roll_lanes(select(self.first_lanes, roll_sublanes(values, -1), values), -TILE)

    def from_low_z(self, values):
        return select(self.walls[0, 1], 0.0, roll_lanes(values, 1))

    def from_high_z(self, values):
        return select(self.walls[0, -1], 0.0, roll_lanes(values, -1))


def flat_rows(row, count, tile_offset=0):
    start = row * SUBLANES
    if not isinstance(start, int):
        start = pl.multiple_of(start, SUBLANES)
    return pl.ds(start + tile_offset, count * SUBLANES)


class ByRow:
    def __init__(self, ref):
        self.ref = ref


def by_row(rows, count):
    return jax.ShapeDtypeStruct((rows, count * SUBLANES, LANES), jnp.float32)


def place_of(ref, index, row, tile_offset=0):
    if isinstance(ref, ByRow):
        return ref.ref, row, pl.ds(index * SUBLANES + tile_offset, SUBLANES)
    return ref, index, flat_rows(row, 1, tile_offset)


def read_row(ref, index, row, tile_offset=0):
    ref, first, second = place_of(ref, index, row, tile_offset)
    return ref[first, second, :]


def write_row(ref, index, row, values):
    ref, first, second = place_of(ref, index, row)
    ref[first, second, :] = values


class Block:
    def __init__(self, geometry, spans, inner=False, store_rows=None):
        self.spans = spans
        self.store_rows = store_rows or [local for row, local, count in spans]
        rows = [row + extra for row, local, count in spans for extra in range(count)]
        self.inner = inner
        rows = [row + extra for row, local, count in spans for extra in range(count)]
        if inner:
            self.x_walls = {}
            self.valid = geometry.domain
            self.kinds = [0]
            return
        ids = Rows([row + jnp.zeros((SUBLANES, LANES), jnp.int32) for row in rows])
        self.x_walls = {1: ids == geometry.low_row, -1: ids == geometry.high_row - 1}
        self.valid = ids.each(
            lambda part: geometry.domain & (part >= geometry.low_row) & (part < geometry.high_row)
        )
        self.kinds = [
            jnp.where(row == geometry.low_row, 1, 0) + jnp.where(row == geometry.high_row - 1, 2, 0)
            for row in rows
        ]

    def load(self, ref, index, offset=0, tile_offset=0):
        return Rows([
            read_row(ref, index, local + offset + extra, tile_offset)
            for row, local, count in self.spans
            for extra in range(count)
        ])

    def store(self, ref, index, values):
        targets = [
            target + extra
            for (row, local, count), target in zip(self.spans, self.store_rows)
            for extra in range(count)
        ]
        for target, part in zip(targets, values.parts):
            write_row(ref, index, target, part)

    def wall_terms(self, walls, position):
        terms = [walls[position, flat_rows(kind, 1), :] for kind in self.kinds]
        return terms[0] if self.inner else Rows(terms)


def fill_wall_table(walls, geometry):
    one = jnp.ones((SUBLANES, LANES), jnp.float32)
    up_y, down_y, up_z, down_z = [
        jnp.where(geometry.walls[key], 0.0, one) for key in ((-1, 0), (1, 0), (0, -1), (0, 1))
    ]
    sum_y, sum_z = up_y + down_y, up_z + down_z
    for kind, (up_x, down_x) in enumerate(((1.0, 1.0), (1.0, 0.0), (0.0, 1.0))):
        sum_x = up_x + down_x
        around_x = 2.0 + sum_y + sum_z
        total = 12.0 + 2.0 * (sum_x + sum_y + sum_z) + sum_x * (sum_y + sum_z) + sum_y * sum_z
        rows = (
            (up_x - down_x) * around_x,
            (up_y - down_y) * (2.0 + sum_x + sum_z),
            (up_z - down_z) * (2.0 + sum_x + sum_y),
            36.0 - total,
        )
        for position, row in enumerate(rows):
            walls[position, flat_rows(kind, 1), :] = row


VELOCITIES = tuple(
    tuple(sign if axis == place else 0 for place in range(3)) for axis in range(3) for sign in (1, -1)
) + tuple(
    tuple({a: one, b: two}.get(place, 0) for place in range(3))
    for a, b in ((0, 1), (0, 2), (1, 2))
    for one, two in ((1, 1), (-1, -1), (1, -1), (-1, 1))
)
VELOCITIES = ((0, 0, 0),) + VELOCITIES


def colour_stage(block, geometry, fields, colours):
    density = block.load(fields, 0)
    red = block.load(fields, 10)
    colour = select(block.valid, 2.0 * red - density, 0.0)
    along_y = geometry.from_low_y(colour) + geometry.from_high_y(colour)
    along_z = geometry.from_low_z(colour) + geometry.from_high_z(colour)
    block.store(colours, 0, colour)
    block.store(colours, 1, 2.0 * colour + (along_y + along_z))
    block.store(colours, 2, along_y)
    block.store(colours, 3, along_z)


def collide_stage(block, geometry, fields, solids, colours, walls, state):
    relaxing = 1.0 - 1.0 / RELAX_TIME
    third = 1.0 / 3.0
    colour = block.load(colours, 0)
    doubled = 2.0 * colour + (block.load(colours, 0, -1) + block.load(colours, 0, 1))
    term_y = doubled + block.load(colours, 3)
    term_z = doubled + block.load(colours, 2)
    grad_x = block.load(colours, 1, 1) - block.load(colours, 1, -1)
    grad_y = geometry.from_high_y(term_y) - geometry.from_low_y(term_y)
    grad_z = geometry.from_high_z(term_z) - geometry.from_low_z(term_z)
    if not block.inner:
        grad_x = grad_x - block.wall_terms(walls, 0) * colour
    grad_y = grad_y - block.wall_terms(walls, 1) * colour
    grad_z = grad_z - block.wall_terms(walls, 2) * colour

    fluid = block.load(solids, PLANES - 1) == 0.0
    density = block.load(fields, 0)
    red = block.load(fields, 10)
    flux = [block.load(fields, 1 + axis) for axis in range(3)]
    stress = [block.load(fields, 4 + part) for part in range(6)]
    square_xx, square_yy, square_zz = grad_x * grad_x, grad_y * grad_y, grad_z * grad_z
    square = square_xx + square_yy + square_zz
    inverse = select(fluid, (1.0 + square * (1.0 / 144.0)).each(lax.rsqrt), 0.0)
    trace = third * square
    strength = (SURFACE / (8.0 * 144.0)) * inverse
    keep = select(fluid, relaxing / 8.0, 1.0 / 8.0)
    eighths = [0.125 * part for part in flux]
    own = [
        eighths[axis] * flux[axis] + (keep * stress[axis] + strength * (squared - trace))
        for axis, squared in enumerate((square_xx, square_yy, square_zz))
    ]
    strength, keep = 2.0 * strength, 2.0 * keep
    quarters = [2.0 * part for part in eighths[:2]]
    grads = (grad_x, grad_y, grad_z)
    cross = [
        quarters[a] * flux[b] + (keep * stress[3 + plane] + strength * (grads[a] * grads[b]))
        for plane, (a, b) in enumerate(((0, 1), (0, 2), (1, 2)))
    ]
    base = density * (1.0 / 36.0) - third * (own[0] + own[1] + own[2])
    sign = select(fluid, 1.0 / 12.0, -1.0 / 12.0)
    run = [sign * part for part in flux]
    mixing = ((SEPARATION / 144.0) * red) * ((density - red) * inverse)
    red_run = [0.5 * part + mixing * grad for part, grad in zip(run, grads)]
    moved, reds = state
    block.store(moved, 0, 12.0 * base)
    straight = [base + part for part in own]
    for axis in range(3):
        middle = 2.0 * straight[axis]
        swing = 2.0 * run[axis]
        block.store(moved, 1 + 2 * axis, middle + swing)
        block.store(moved, 2 + 2 * axis, middle - swing)
    for plane, (a, b) in enumerate(((0, 1), (0, 2), (1, 2))):
        middle = straight[a] + own[b]
        same, other = middle + cross[plane], middle - cross[plane]
        along, against = run[a] + run[b], run[a] - run[b]
        first = 7 + 4 * plane
        block.store(moved, first, same + along)
        block.store(moved, first + 1, same - along)
        block.store(moved, first + 2, other + against)
        block.store(moved, first + 3, other - against)

    red_base = select(block.valid, red * (1.0 / 36.0), 0.0)
    red_run = [select(block.valid, part, 0.0) for part in red_run]
    block.store(reds, 0, red_base)
    block.store(reds, 1, red_base + red_run[0])
    block.store(reds, 2, red_base - red_run[0])
    block.store(reds, 3, red_run[1])
    block.store(reds, 4, red_run[2])


def arrive_stage(block, geometry, walls, state, fields):
    third = 1.0 / 3.0
    moved, reds = state
    own = [None] * MOVED

    def here(direction):
        if own[direction] is None:
            own[direction] = block.load(moved, direction)
        return own[direction]

    def arrived(direction, opposite):
        vel_x, vel_y, vel_z = VELOCITIES[direction]
        values = here(direction) if vel_x == 0 else block.load(moved, direction, -vel_x)
        if vel_y != 0:
            beside = block.load(moved, direction, -vel_x, -vel_y)
            leaving = geometry.last_lanes if vel_y == 1 else geometry.first_lanes
            values = select(leaving, beside, values)
        if vel_y != 0 or vel_z != 0:
            values = roll_lanes(values, TILE * vel_y + vel_z)
        masks = []
        if vel_x in block.x_walls:
            masks.append(block.x_walls[vel_x])
        if (vel_y, vel_z) in geometry.walls:
            masks.append(geometry.walls[vel_y, vel_z])
        if not masks:
            return values
        wall = functools.reduce(lambda one, two: one | two, masks)
        return select(wall, here(opposite), values)

    red = block.load(reds, 0)
    red_y = block.load(reds, 3)
    red_z = block.load(reds, 4)
    from_x = block.load(reds, 1, -1) + block.load(reds, 2, 1)
    spread = 2.0 * red + from_x
    spread_y = 2.0 * red_y + (block.load(reds, 3, -1) + block.load(reds, 3, 1))
    spread_z = 2.0 * red_z + (block.load(reds, 4, -1) + block.load(reds, 4, 1))
    up_y, down_y = red + red_y, red - red_y
    low_y = (
        (spread + spread_y)
        + geometry.from_low_z(up_y + red_z)
        + geometry.from_high_z(up_y - red_z)
    )
    high_y = (
        (spread - spread_y)
        + geometry.from_low_z(down_y + red_z)
        + geometry.from_high_z(down_y - red_z)
    )
    bounced = (
        block.wall_terms(walls, 3) * red
        - block.wall_terms(walls, 1) * red_y
        - block.wall_terms(walls, 2) * red_z
    )
    if not block.inner:
        bounced = bounced - block.wall_terms(walls, 0) * (block.load(reds, 1) - red)
    red_total = (
        12.0 * red
        + 2.0 * from_x
        + geometry.from_low_z(spread + spread_z)
        + geometry.from_high_z(spread - spread_z)
        + geometry.from_low_y(low_y)
        + geometry.from_high_y(high_y)
        + bounced
    )
    rest = here(0)
    sums, diffs = [], []
    for axis in range(3):
        up = arrived(1 + 2 * axis, 2 + 2 * axis)
        down = arrived(2 + 2 * axis, 1 + 2 * axis)
        sums.append(up + down)
        diffs.append(up - down)
    total = rest + sums[0] + sums[1] + sums[2]
    cross = []
    for plane, (a, b) in enumerate(((0, 1), (0, 2), (1, 2))):
        first = 7 + 4 * plane
        parts = [arrived(first + offset, first + (offset ^ 1)) for offset in range(4)]
        same, other = parts[0] + parts[1], parts[2] + parts[3]
        along, against = parts[0] - parts[1], parts[2] - parts[3]
        both = same + other
        cross.append(same - other)
        total = total + both
        sums[a], sums[b] = sums[a] + both, sums[b] + both
        diffs[a], diffs[b] = diffs[a] + (along + against), diffs[b] + (along - against)
    shared = third * total
    block.store(fields, 0, total)
    for axis in range(3):
        block.store(fields, 1 + axis, diffs[axis])
        block.store(fields, 4 + axis, sums[axis] - shared - diffs[axis] * diffs[axis])
    for plane, (a, b) in enumerate(((0, 1), (0, 2), (1, 2))):
        block.store(fields, 7 + plane, cross[plane] - diffs[a] * diffs[b])
    block.store(fields, 10, red_total)


def over_rows(geometry, first, size, blocks, stage):
    trip = size * blocks
    rest = -2 * first % trip
    assert TILE % trip == 0 and rest % min(size, rest or size) == 0

    def run(start, count, step_size):
        for offset in range(0, count, step_size):
            row = start + offset
            stage(Block(geometry, [(row, row, step_size)], inner=True))

    def step(index, carry):
        run(first + index * trip, trip, size)
        return carry

    trips = (geometry.live - 2 * first - rest) // trip
    lax.fori_loop(0, trips, step, 0)
    if rest:
        run(geometry.live - first - rest, rest, min(size, rest))


def block_tiles():
    return lax.broadcasted_iota(jnp.int32, (SUBLANES, LANES), 0)


def roll_tiles(block, amount):
    return pltpu.roll(block, amount % SUBLANES, 0)


def pack_blocks(blocks):
    tiles, rest = block_tiles(), blocks[GROUP - 1]
    packed = []
    for number, block in enumerate(blocks[: GROUP - 1]):
        low, high = 2 * number + 1, 2 * number + 2
        block = jnp.where(tiles == 0, roll_tiles(rest, -low), block)
        packed.append(jnp.where(tiles == SUBLANES - 1, roll_tiles(rest, SUBLANES - 1 - high), block))
    return packed


def unpack_blocks(packed):
    tiles, rest = block_tiles(), None
    for number, block in enumerate(packed):
        low, high = 2 * number + 1, 2 * number + 2
        part = jnp.where(tiles == low, roll_tiles(block, low), roll_tiles(block, high - SUBLANES + 1))
        rest = part if rest is None else jnp.where(tiles >= low, part, rest)
    return list(packed) + [rest]


def flat_view(ref):
    rows, width, lanes = ref.shape
    return ref.reshape(rows * width, lanes)


def spread_tile(raw, raw_solid, index, row, target, target_row):
    source = raw_solid if index == FIELDS else raw.at[index]
    width = target.shape[1]
    for tile in range(OWN_TILES):
        values = source[pl.ds(row, SUBLANES), pl.ds(tile * LANES, LANES)].astype(jnp.float32)
        start = target_row * width + index * SUBLANES + 1 + tile
        flat_view(target)[pl.ds(start, SUBLANES, stride=width), :] = values


def load_kernel(
    tiles_count, density, momentum, stress, red, solid, widths,
    info, raw, raw_solid, packet, mine,
    first_tile, last_tile, held_widths, sems,
):
    row_count, flat_count = raw_solid.shape
    own_tiles = flat_count // LANES
    copies = [
        pltpu.make_async_copy(widths, held_widths, sems.at[0]),
        pltpu.make_async_copy(density, raw.at[0], sems.at[1]),
        pltpu.make_async_copy(momentum, raw.at[pl.ds(1, 3)], sems.at[2]),
        pltpu.make_async_copy(red, raw.at[10], sems.at[3]),
        pltpu.make_async_copy(solid, raw_solid, sems.at[4]),
        pltpu.make_async_copy(stress.at[pl.ds(0, 3)], raw.at[pl.ds(4, 3)], sems.at[5]),
        pltpu.make_async_copy(stress.at[pl.ds(3, 3)], raw.at[pl.ds(7, 3)], sems.at[6]),
    ]
    for copy in copies:
        copy.start()
    tiles_index, sub_index = lax.axis_index("tiles"), lax.axis_index("sub")
    low_part = sub_index == 0
    edge_start = pl.multiple_of(jnp.where(low_part, (own_tiles - 1) * LANES, 0), LANES)

    copies[0].wait()
    live = held_widths[tiles_index] * TILE
    info[0] = live
    info[1] = (tiles_index == 0).astype(jnp.int32)
    info[2] = (tiles_index == tiles_count - 1).astype(jnp.int32)
    info[3] = sub_index

    near_cut = lax.broadcasted_iota(jnp.int32, (SUBLANES, LANES), 1) < HALF
    near_cut = near_cut == jnp.logical_not(low_part)
    near_last = pl.multiple_of(live - SUBLANES, SUBLANES)
    edges = pl.ds(edge_start, LANES)

    def plane_of(index):
        return raw_solid if index == FIELDS else raw.at[index]

    def pack_edges(pair):
        here, there = [plane_of(index) for index in ORDER[2 * pair : 2 * pair + 2]]
        for row in range(0, row_count, SUBLANES):
            rows = pl.ds(row, SUBLANES)
            beside = pltpu.roll(there[rows, edges].astype(jnp.float32), HALF, 1)
            both = jnp.where(near_cut, here[rows, edges].astype(jnp.float32), beside)
            packet[pl.ds(END_ROWS + pair * row_count + row, SUBLANES), :] = both

    targets = ((packet, jnp.logical_not(low_part)), (mine, low_part))

    def row_of(use_last, index, number_first, number_last):
        first = read_row(ByRow(first_tile), index, number_first)
        last = read_row(ByRow(last_tile), index, number_last)
        return jnp.where(use_last, last, first)

    def colour_of(use_last):
        red_row, density_row = [
            row_of(use_last, index, FULL, SUBLANES - HALO) for index in (10, 0)
        ]
        return 2.0 * red_row - density_row

    def pack_ends(group):
        for target, use_last in targets:
            blocks = []
            for number in range(group * GROUP, (group + 1) * GROUP):
                place, extra = divmod(number, FULL)
                block = row_of(use_last, ORDER[place], extra, SUBLANES - FULL + extra)
                if ORDER[place] == SPARE and extra == 0:
                    block = jnp.where(use_last, colour_of(use_last), block)
                if ORDER[place] == SPARE and extra == FULL - 1:
                    block = jnp.where(use_last, block, colour_of(use_last))
                blocks.append(block)
            for number, block in enumerate(pack_blocks(blocks)):
                place = (group * (GROUP - 1) + number) * SUBLANES
                target[pl.ds(place, SUBLANES), :] = block

    place = 0
    for copy, count in zip(copies[1:], (1, 3, 1, 1, 3, 3)):
        copy.wait()
        before, place = place, place + count
        for index in ORDER[before:place]:
            for target, row in ((first_tile, 0), (last_tile, near_last)):
                spread_tile(raw, raw_solid, index, row, target, 0)
        for pair in range(before // 2, place // 2):
            pack_edges(pair)
        for group in range(before * FULL // GROUP, place * FULL // GROUP):
            pack_ends(group)


def load_inputs(arrays, widths, tiles_count):
    row_count, flat_count = arrays[0].shape
    return pl.pallas_call(
        functools.partial(load_kernel, tiles_count),
        out_shape=[
            pltpu.SMEM((4,), jnp.int32),
            jax.ShapeDtypeStruct((FIELDS, row_count, flat_count), jnp.float32),
            jax.ShapeDtypeStruct((row_count, flat_count), jnp.int32),
            jax.ShapeDtypeStruct((END_ROWS + PAIRS * row_count, LANES), jnp.float32),
            jax.ShapeDtypeStruct((END_ROWS, LANES), jnp.float32),
        ],
        in_specs=[HBM] * 6,
        out_specs=[SMEM] + [VMEM] * 4,
        scratch_shapes=[
            pltpu.VMEM((SUBLANES, PLACES * SUBLANES, LANES), jnp.float32),
            pltpu.VMEM((SUBLANES, PLACES * SUBLANES, LANES), jnp.float32),
            pltpu.SMEM(widths.shape, jnp.int32),
            pltpu.SemaphoreType.DMA((7,)),
        ],
        compiler_params=pltpu.CompilerParams(vmem_limit_bytes=16 * 1024 * 1024),
        name="load",
    )(*[pltpu.with_memory_space_constraint(array, pltpu.HBM) for array in (*arrays, widths)])


def spread_kernel(raw, raw_solid, spread):
    for index in range(PLANES):
        for row in range(0, raw_solid.shape[0], SUBLANES):
            spread_tile(raw, raw_solid, index, row, spread, row)


def spread_rows(raw, raw_solid):
    row_count = raw_solid.shape[0]
    return pl.pallas_call(
        spread_kernel,
        out_shape=by_row(row_count, PLACES),
        in_specs=[VMEM, VMEM],
        out_specs=VMEM,
        compiler_params=pltpu.CompilerParams(vmem_limit_bytes=16 * 1024 * 1024),
        cost_estimate=pl.CostEstimate(flops=1_000_000, bytes_accessed=4_000_000, transcendentals=0),
        name="spread",
    )(raw, raw_solid)


def join_kernel(mine, packet, spread, ends):
    ends[pl.ds(0, END_ROWS), :] = mine[...]
    ends[pl.ds(END_ROWS, END_ROWS), :] = packet[pl.ds(0, END_ROWS), :]


def join_ends(mine, packet, spread):
    return pl.pallas_call(
        join_kernel,
        out_shape=jax.ShapeDtypeStruct((2 * END_ROWS, LANES), jnp.float32),
        in_specs=[VMEM, VMEM, ANY],
        out_specs=VMEM,
        compiler_params=pltpu.CompilerParams(vmem_limit_bytes=8 * 1024 * 1024),
        name="join",
    )(mine, packet, spread)


def beside_kernel(info, spread, packet, whole):
    low_part = info[3] == 0
    row_count, width = spread.shape[:2]
    flat = flat_view(whole)
    for pair in range(PAIRS):
        for row in range(0, row_count, SUBLANES):
            both = packet[pl.ds(END_ROWS + pair * row_count + row, SUBLANES), :]
            for place, values in ((2 * pair, both), (2 * pair + 1, pltpu.roll(both, HALF, 1))):
                index = ORDER[place]
                start = row * width + index * SUBLANES
                below = jnp.where(low_part, 0.0, values)
                above = jnp.where(low_part, values, 0.0)
                flat[pl.ds(start, SUBLANES, stride=width), :] = below
                flat[pl.ds(start + SUBLANES - 1, SUBLANES, stride=width), :] = above


def put_beside(info, spread, packet):
    return pl.pallas_call(
        beside_kernel,
        out_shape=jax.ShapeDtypeStruct(spread.shape, jnp.float32),
        in_specs=[SMEM, VMEM, VMEM],
        out_specs=VMEM,
        input_output_aliases={1: 0},
        compiler_params=pltpu.CompilerParams(vmem_limit_bytes=16 * 1024 * 1024),
        name="beside",
    )(info, pltpu.with_memory_space_constraint(spread, pltpu.VMEM), packet)


def keep_rows(slab, source, first, size, live):
    for slab_row, row in slab_rows(live, first, size):
        for extra in range(size):
            slab[slab_row + extra] = source[row + extra]


def slab_rows(live, first, size):
    mirrored = SLAB - first - size
    return [(first, first - HALO), (SLAB + mirrored, live - 2 * RIM + mirrored)]


def collide_rows(geometry, before, whole, first, colours, walls, state):
    over_rows(geometry, first - 1, *COLOUR_BLOCK, lambda block: colour_stage(
        block, geometry, before, colours))
    over_rows(geometry, first, *COLLIDE_BLOCK, lambda block: collide_stage(
        block, geometry, before, whole, colours, walls, state))


def row_copies(pieces, outs, held_row, out_row, count, sems):
    held, rows = pl.ds(held_row, count), pl.ds(out_row, count)
    parts = (
        (pieces.at[0, held], outs[0].at[rows]),
        (pieces.at[pl.ds(1, 3), held], outs[1].at[:, rows]),
        (pieces.at[pl.ds(4, 3), held], outs[2].at[pl.ds(0, 3), rows]),
        (pieces.at[pl.ds(7, 3), held], outs[2].at[pl.ds(3, 3), rows]),
        (pieces.at[10, held], outs[3].at[rows]),
    )
    return [
        pltpu.make_async_copy(source, target, sems.at[number])
        for number, (source, target) in enumerate(parts)
    ]


def gather_tiles(final, row, pieces, held_row):
    width = final.shape[1]
    start = row * width
    if not isinstance(start, int):
        start = pl.multiple_of(start, SUBLANES)
    for index in range(FIELDS):
        for tile in range(OWN_TILES):
            place = start + index * SUBLANES + 1 + tile
            pieces[index, pl.ds(held_row, SUBLANES), pl.ds(tile * LANES, LANES)] = flat_view(final)[
                pl.ds(place, SUBLANES, stride=width), :
            ]


def first_kernel(
    info, whole, final,
    moved_slab, reds_slab, fields_slab, moved_later_slab, reds_later_slab, start_slab, walls, final_slab,
    colours, moved, reds, fields, moved_later, reds_later,
):
    state, later = (ByRow(moved), ByRow(reds)), (ByRow(moved_later), ByRow(reds_later))
    geometry = Geometry(info, OWN_TILES)
    live = geometry.live
    fill_wall_table(walls, geometry)
    collide_rows(geometry, ByRow(whole), ByRow(whole), 1, ByRow(colours), walls, state)
    over_rows(geometry, 2, *ARRIVE_BLOCK, lambda block: arrive_stage(
        block, geometry, walls, state, ByRow(fields)))
    keep_rows(start_slab, whole, HALO, FULL, live)
    keep_rows(moved_slab, moved, HALO + 1, KEPT, live)
    keep_rows(reds_slab, reds, HALO + 1, KEPT, live)
    keep_rows(fields_slab, fields, HALO + 2, KEPT, live)
    collide_rows(geometry, ByRow(fields), ByRow(whole), 3, ByRow(colours), walls, later)
    keep_rows(moved_later_slab, moved_later, HALO + 3, KEPT, live)
    keep_rows(reds_later_slab, reds_later, HALO + 3, KEPT, live)
    edges = slab_rows(live, HALO + RIM, RIM)
    rim = Block(geometry, [(row, row, RIM) for _, row in edges], True, [at for at, _ in edges])
    arrive_stage(rim, geometry, walls, later, ByRow(final_slab))

    def finish(index, carry):
        row = SUBLANES + index * TILE
        block = Block(geometry, [(row, row, TILE)], inner=True)
        arrive_stage(block, geometry, walls, later, ByRow(final))
        return carry

    lax.fori_loop(0, live // TILE - 1, finish, 0)


def second_kernel(info, final, arrived, density_out, momentum_out, stress_out, red_out, pieces, sems):
    outs = (density_out, momentum_out, stress_out, red_out)
    live = info[0]
    copies = []
    for number, (least, inner_row, dead_row) in enumerate(
        ((2 * TILE, SUBLANES, TILE), (3 * TILE, SUBLANES + TILE, 2 * TILE))
    ):
        held_row = number * TILE

        @pl.when(live >= least)
        def _():
            for extra in range(0, TILE, SUBLANES):
                gather_tiles(final, inner_row + extra, pieces, held_row + extra)

        @pl.when(live < least)
        def _():
            zeros = jnp.zeros((FIELDS, TILE, pieces.shape[2]), jnp.float32)
            pieces[:, pl.ds(held_row, TILE), :] = zeros

        row = pl.multiple_of(jnp.where(live >= least, inner_row, dead_row), SUBLANES)
        started = row_copies(pieces, outs, held_row, row, TILE, sems.at[number])
        for copy in started:
            copy.start()
        copies = copies + started
    for copy in copies:
        copy.wait()


def scratch_of(shape):
    return pltpu.VMEM(shape.shape, shape.dtype)


def pieces_of(rows, flat_count):
    return pltpu.VMEM((FIELDS, rows, flat_count), jnp.float32)


def run_first(info, whole):
    rows = whole.shape[0]
    slabs = [by_row(2 * SLAB, count) for count in (HELD, REDS, FIELDS, HELD, REDS, PLACES)]
    slabs = slabs + [by_row(4, 3), by_row(2 * SLAB, FIELDS)]
    scratch = [by_row(rows, 4)]
    scratch = scratch + [by_row(rows, count) for count in (HELD, REDS, FIELDS, HELD, REDS)]
    return pl.pallas_call(
        first_kernel,
        out_shape=[by_row(rows, FIELDS)] + slabs,
        in_specs=[SMEM, VMEM],
        out_specs=[VMEM] * 9,
        scratch_shapes=[scratch_of(shape) for shape in scratch],
        compiler_params=pltpu.CompilerParams(vmem_limit_bytes=32 * 1024 * 1024),
        cost_estimate=pl.CostEstimate(flops=40_000_000, bytes_accessed=8_000_000, transcendentals=0),
        name="first",
    )(info, whole)


def run_second(info, final, arrived, arrays):
    row_count, flat_count = arrays[0].shape
    assert row_count == 3 * TILE
    return pl.pallas_call(
        second_kernel,
        out_shape=[jax.ShapeDtypeStruct(array.shape, jnp.float32) for array in arrays[:4]],
        in_specs=[SMEM, VMEM, ANY],
        out_specs=[ANY] * 4,
        scratch_shapes=[
            pieces_of(2 * TILE, flat_count),
            pltpu.SemaphoreType.DMA((2, OUT_COPIES)),
        ],
        compiler_params=pltpu.CompilerParams(vmem_limit_bytes=16 * 1024 * 1024),
        cost_estimate=pl.CostEstimate(flops=20_000_000, bytes_accessed=8_000_000, transcendentals=0),
        name="second",
    )(info, final, arrived)


def follow_kernel(ends, kept, out):
    out[pl.ds(0, 1), :] = ends[pl.ds(0, 1), :]


def follow(ends, kept):
    return pl.pallas_call(
        follow_kernel,
        out_shape=jax.ShapeDtypeStruct(ends.shape, jnp.float32),
        in_specs=[VMEM, ANY],
        out_specs=VMEM,
        input_output_aliases={0: 0},
        compiler_params=pltpu.CompilerParams(vmem_limit_bytes=8 * 1024 * 1024),
        name="follow",
    )(pltpu.with_memory_space_constraint(ends, pltpu.VMEM), kept)


def outer_kernel(info, arrived, passed, *refs):
    outs = refs[12:16]
    moved, reds, fields, moved_later, reds_later, start_fields, walls, final = refs[16:24]
    colours, pieces, sems = refs[24:]
    state, later = (ByRow(moved), ByRow(reds)), (ByRow(moved_later), ByRow(reds_later))
    geometry = Geometry(info, OWN_TILES)
    live = geometry.live
    low_part = info[3] == 0

    def ends_of(ref, half):
        blocks = []
        for group in range(FULL * PLANES // GROUP):
            first = half * PACKED + group * (GROUP - 1)
            packed = [ref[pl.ds((first + k) * SUBLANES, SUBLANES), :] for k in range(GROUP - 1)]
            blocks = blocks + unpack_blocks(packed)
        return blocks

    tiles = block_tiles()
    middle = (tiles >= 1) & (tiles <= OWN_TILES)

    def widened(own, other):
        beside = jnp.where(tiles == 0, roll_tiles(other, -OWN_TILES), roll_tiles(other, OWN_TILES))
        return jnp.where(geometry.domain, jnp.where(middle, own, beside), 0.0)

    straight = [widened(*pair) for pair in zip(ends_of(arrived, 0), ends_of(arrived, 1))]
    crossed = [widened(*pair) for pair in zip(ends_of(passed, 1), ends_of(passed, 0))]
    below = [jnp.where(low_part, *pair) for pair in zip(straight, crossed)]
    above = [jnp.where(low_part, *pair) for pair in zip(crossed, straight)]

    for number in range(FULL * PLANES):
        place, extra = divmod(number, FULL)
        index = ORDER[place]
        write_row(ByRow(start_fields), index, 1 + extra, below[number])
        write_row(ByRow(start_fields), index, 2 * SLAB - HALO + extra, above[number])
    spare = FULL * ORDER.index(SPARE)
    ends_at = ((0, 1, below[spare]), (2 * SLAB - 1, 2 * SLAB - 2, above[spare + FULL - 1]))
    for row, next_row, colour in ends_at:
        write_row(ByRow(start_fields), SPARE, next_row, jnp.zeros((SUBLANES, LANES), jnp.float32))
        write_row(ByRow(start_fields), 0, row, jnp.zeros((SUBLANES, LANES), jnp.float32))
        write_row(ByRow(start_fields), 10, row, 0.5 * colour)
    def block(first, count):
        return Block(geometry, [(row, at, count) for at, row in slab_rows(live, first, count)])

    held, solids, marks = ByRow(fields), ByRow(start_fields), ByRow(colours)
    colour_stage(block(0, 6), geometry, solids, marks)
    collide_stage(block(1, 4), geometry, solids, solids, marks, walls, state)
    arrive_stage(block(2, 4), geometry, walls, state, held)
    colour_stage(block(2, 6), geometry, held, marks)
    collide_stage(block(3, 4), geometry, held, solids, marks, walls, later)
    arrive_stage(block(4, 4), geometry, walls, later, ByRow(final))

    copies = []
    for side, row, out_row in ((0, HALO, 0), (1, SLAB, live - SUBLANES)):
        gather_tiles(final, row, pieces, side * SUBLANES)
        out_row = pl.multiple_of(out_row, SUBLANES)
        started = row_copies(pieces, outs, side * SUBLANES, out_row, SUBLANES, sems.at[side])
        for copy in started:
            copy.start()
        copies = copies + started
    for copy in copies:
        copy.wait()


def run_outer(info, arrived, passed, slabs, outs):
    flat_count = outs[0].shape[1]
    shapes = [jax.ShapeDtypeStruct(array.shape, jnp.float32) for array in (*outs, *slabs)]
    slabs = [pltpu.with_memory_space_constraint(slab, pltpu.VMEM) for slab in slabs]
    aliases = {3 + number: 4 + number for number in range(8)}
    aliases.update({11 + number: number for number in range(4)})
    return pl.pallas_call(
        outer_kernel,
        out_shape=shapes,
        in_specs=[SMEM] + [VMEM] * 10 + [ANY] * 4,
        out_specs=[ANY] * 4 + [VMEM] * 8,
        scratch_shapes=[
            scratch_of(by_row(2 * SLAB, 4)),
            pieces_of(2 * SUBLANES, flat_count),
            pltpu.SemaphoreType.DMA((2, OUT_COPIES)),
        ],
        input_output_aliases=aliases,
        compiler_params=pltpu.CompilerParams(vmem_limit_bytes=24 * 1024 * 1024),
        name="outer",
    )(info, arrived, passed, *slabs, *outs)


def body(density, momentum, stress, red_density, solid, widths):
    tiles_count = lax.axis_size("tiles")
    arrays = (density, momentum, stress, red_density, solid)
    info, raw, raw_solid, packet, mine = load_inputs(arrays, widths, tiles_count)
    info = pltpu.with_memory_space_constraint(info, pltpu.SMEM)
    swap = [(0, 1), (1, 0)]
    packet = lax.ppermute(packet, "sub", swap)
    spread = spread_rows(raw, raw_solid)
    ends = join_ends(mine, packet, spread)
    route = [(2 * k, 2 * k + 2) for k in range(tiles_count - 1)]
    route = route + [(2 * k + 3, 2 * k + 1) for k in range(tiles_count - 1)]
    arrived = lax.ppermute(ends, ("tiles", "sub"), route)
    whole = put_beside(info, spread, packet)
    final, *slabs = run_first(info, whole)
    arrived = follow(arrived, slabs[-1])
    passed = lax.ppermute(arrived, "sub", swap)
    outs = run_second(info, final, arrived, arrays)
    return tuple(run_outer(info, arrived, passed, slabs, outs)[:4])


def solution(mesh):
    in_specs = (
        P(("groups", "tiles"), "sub"),
        P(None, ("groups", "tiles"), "sub"),
        P(None, ("groups", "tiles"), "sub"),
        P(("groups", "tiles"), "sub"),
        P(("groups", "tiles"), "sub"),
        P("groups"),
    )
    out_specs = (
        P(("groups", "tiles"), "sub"),
        P(None, ("groups", "tiles"), "sub"),
        P(None, ("groups", "tiles"), "sub"),
        P(("groups", "tiles"), "sub"),
    )
    return jax.shard_map(body, mesh=mesh, in_specs=in_specs, out_specs=out_specs, check_vma=False)
```
